128 devices in a mesh: ulysses: 8 (over z, core), ctx: 16 (over x, y).
Axes of the slice: x: 4, y: 4, z: 4, core: 2. Of those that a mesh axis runs over, the one named last changes fastest.
Arguments:
- queries: bfloat16 [8192, 4096], P(('ulysses', 'ctx')), may hold values from -160 to 160
- keys: bfloat16 [8192, 1024], P(('ulysses', 'ctx')), may hold values from -6 to 6
- values: bfloat16 [8192, 1024], P(('ulysses', 'ctx')), may hold values from -6 to 6
- attn_out: bfloat16 [8192, 4096], P(('ulysses', 'ctx')), may hold values from -4 to 4
- out_grad: bfloat16 [8192, 4096], P(('ulysses', 'ctx')), may hold values from -6 to 6
- segment: int32 [8192], replicated, may hold values from 0 to 2, as said below
- span_order: int32 [32], replicated, may hold values from 0 to 31, as said below
Outputs:
- query_grad: bfloat16 [8192, 4096], P(('ulysses', 'ctx'))
- key_grad: bfloat16 [8192, 1024], P(('ulysses', 'ctx'))
- value_grad: bfloat16 [8192, 1024], P(('ulysses', 'ctx'))
The draws below stay inside these ranges and needn't reach their ends.
Inputs may be any that keep to these rules, and one draw needn't show every extreme that they name: `segment`: 0 marks the prompt, 1 the chosen response, 2 the rejected response; in order of position the prompt comes first, then the chosen, then the rejected response, each of them non-empty. `span_order`: a permutation of 0 to 31.
All inputs are finite; a program needn't handle non-finite values.
Results may differ from the reference program's by a relative error of at most 0.005.
Values may be sent and summed in bfloat16 or wider, within the bound.
No kernel may reach another device: no remote copies, remote signals or barrier semaphores. Data moves between devices by JAX's collectives and lax.ppermute only.
A program may use at most 64 MiB of HBM per device.

```python
import jax
import jax.numpy as jnp
from jax import lax

QHEADS = 32
KVHEADS = 8
HEAD_DIM = 128
SEQ = 8192
BLK = 64
HALF = 256
SPANS = 32
GROUP = 4
N_ULYSSES = 8
N_CTX = 16


def span_layout(key):
    return jax.random.permutation(jax.random.fold_in(key, 901), SPANS).astype(jnp.int32)


def stored_positions(order):
    stored = jnp.arange(SEQ, dtype=jnp.int32)
    blocks = stored // BLK
    local = blocks // N_CTX * BLK + stored % BLK
    which = order[2 * (blocks % N_CTX) + local // HALF]
    return which * HALF + local % HALF


def base_keys(key):
    return jnp.clip(jax.random.normal(jax.random.fold_in(key, 303), (SEQ, KVHEADS * HEAD_DIM), jnp.float32), -6.0, 6.0)


def draw_span_order(key, part):
    order = span_layout(key)
    return order


def draw_segment(key, part):
    order = span_layout(key)
    key = jax.random.fold_in(key, 2)
    prompt = jax.random.randint(jax.random.fold_in(key, 1), (), SEQ // 8, SEQ // 4 + 1)
    remaining = SEQ - prompt
    chosen = jax.random.randint(jax.random.fold_in(key, 2), (), remaining * 3 // 8, remaining * 5 // 8 + 1)
    position = stored_positions(order)
    return jnp.where(position < prompt, 0, jnp.where(position < prompt + chosen, 1, 2)).astype(jnp.int32)


def draw_keys(key, part):
    shaped = base_keys(key)
    return shaped.astype(jnp.bfloat16)


def draw_queries(key, part):
    own_key = jax.random.fold_in(key, 4)
    drawn = jnp.clip(jax.random.normal(own_key, (SEQ, QHEADS * HEAD_DIM), jnp.float32), -6.0, 6.0)
    row_scale = jnp.exp(jax.random.uniform(jax.random.fold_in(own_key, 7), (SEQ, QHEADS, 1), jnp.float32, 0.0, 1.3862944))
    drawn = (drawn.reshape(SEQ, QHEADS, HEAD_DIM) * row_scale).reshape(SEQ, QHEADS * HEAD_DIM)
    return drawn.astype(jnp.bfloat16)


def shard_levels(stream_key, shape, cuts, smallest, largest):
    loudness, own = 1.0, jax.random.fold_in(stream_key, 6)
    for dim, parts in cuts:
        draws = jnp.exp(jax.random.uniform(jax.random.fold_in(own, dim), (parts,), jnp.float32, smallest / len(cuts), largest / len(cuts)))
        loudness = loudness * jnp.repeat(draws, shape[dim] // parts).reshape([-1 if axis == dim else 1 for axis in range(len(shape))])
    return loudness


def noise(rng, shape, width, most, pieces=(), held_as=jnp.bfloat16):
    factor_of = shard_levels(rng, shape, pieces, -0.22, 0.18) if pieces else 1.0
    drawn = jax.random.normal(rng, shape, jnp.float32) * width * factor_of
    return jnp.minimum(jnp.maximum(drawn, -most), most).astype(held_as)


def setup_inputs(seed: int = 0) -> dict:
    key_list = jax.random.split(jax.random.key(seed), 8)
    return {
        "queries": draw_queries(jax.random.fold_in(key_list[7], 71), 0),
        "keys": draw_keys(jax.random.fold_in(key_list[7], 71), 0),
        "values": noise(key_list[2], (SEQ, KVHEADS * HEAD_DIM), 1.0, 6.0, ((0, 128),)),
        "attn_out": noise(key_list[3], (SEQ, QHEADS * HEAD_DIM), 0.5, 4.0, ((0, 128),)),
        "out_grad": noise(key_list[4], (SEQ, QHEADS * HEAD_DIM), 1.0, 6.0, ((0, 128),)),
        "segment": draw_segment(jax.random.fold_in(key_list[7], 71), 0),
        "span_order": draw_span_order(jax.random.fold_in(key_list[7], 71), 0),
    }


masked_score = -1e30


def to_context(array):
    columns = array.shape[-1]
    return array.reshape(N_ULYSSES, N_CTX, BLK, columns).transpose(1, 0, 2, 3).reshape(SEQ, columns)


def from_context(array):
    columns = array.shape[-1]
    return array.reshape(N_CTX, N_ULYSSES, BLK, columns).transpose(1, 0, 2, 3).reshape(SEQ, columns)


def reference(queries, keys, values, attn_out, out_grad, segment, span_order):
    positions = (span_order[:, None] * HALF + jnp.arange(HALF, dtype=jnp.int32)[None, :]).reshape(SEQ)
    segments = to_context(segment[:, None])[:, 0]
    visible = (positions[None, :] <= positions[:, None]) & ((segments[None, :] == segments[:, None]) | (segments[None, :] == 0))
    scale_factor = HEAD_DIM ** -0.5

    def heads_first(array):
        return to_context(array).reshape(SEQ, KVHEADS, GROUP, HEAD_DIM).transpose(1, 2, 0, 3)

    def kv_first(array):
        return to_context(array).reshape(SEQ, KVHEADS, HEAD_DIM).transpose(1, 0, 2)

    def one_group(operands):
        query_heads, saved_heads, grad_heads, key_head, value_head = operands

        def one_head(sums, head):
            query_one, saved_one, grad_one = head
            scores = jnp.dot(query_one, key_head.T, preferred_element_type=jnp.float32) * scale_factor
            masked = jnp.where(visible, scores, masked_score)
            row_max = jnp.max(masked, axis=1)
            row_total = jnp.sum(jnp.where(visible, jnp.exp(masked - row_max[:, None]), 0.0), axis=1)
            logsum = row_max + jnp.log(row_total)
            weights = jnp.where(visible, jnp.exp(scores - logsum[:, None]), 0.0)
            row_dot = jnp.sum(grad_one.astype(jnp.float32) * saved_one.astype(jnp.float32), axis=1)
            prob_grad = jnp.dot(grad_one, value_head.T, preferred_element_type=jnp.float32)
            score_grad = (weights * (prob_grad - row_dot[:, None])).astype(jnp.bfloat16)
            query_part = jnp.dot(score_grad, key_head, preferred_element_type=jnp.float32) * scale_factor
            key_sum = sums[0] + jnp.dot(score_grad.T, query_one, preferred_element_type=jnp.float32) * scale_factor
            value_sum = sums[1] + jnp.dot(weights.astype(jnp.bfloat16).T, grad_one, preferred_element_type=jnp.float32)
            return (key_sum, value_sum), query_part

        zeros = jnp.zeros((SEQ, HEAD_DIM), jnp.float32)
        (key_sum, value_sum), query_parts = lax.scan(one_head, (zeros, zeros), (query_heads, saved_heads, grad_heads))
        return query_parts, key_sum, value_sum

    query_parts, key_sums, value_sums = lax.map(one_group, (heads_first(queries), heads_first(attn_out), heads_first(out_grad), kv_first(keys), kv_first(values)))
    query_grad = from_context(query_parts.transpose(2, 0, 1, 3).reshape(SEQ, QHEADS * HEAD_DIM)).astype(jnp.bfloat16)
    key_grad = from_context(key_sums.transpose(1, 0, 2).reshape(SEQ, KVHEADS * HEAD_DIM)).astype(jnp.bfloat16)
    value_grad = from_context(value_sums.transpose(1, 0, 2).reshape(SEQ, KVHEADS * HEAD_DIM)).astype(jnp.bfloat16)
    return query_grad, key_grad, value_grad
```

```python
import functools
import math

import jax
import jax.numpy as jnp
from jax import lax
from jax.experimental import pallas as pl
from jax.experimental.pallas import tpu as pltpu
from jax.sharding import Mesh, PartitionSpec as P

D = 128
G = 4
R = 64
SPAN = 256
NT = 32
QR = G * R
C = 2 * QR
SCALE = D**-0.5
LOG2E = math.log2(math.e)
EXP_SCALE = SCALE * LOG2E
HIDDEN = -1e30
F32 = jnp.float32
BF16 = jnp.bfloat16
AXES = ("z", "core", "xh", "xl", "y")
HEADS = ("xh", "z")
NT_DIMS = (((1,), (1,)), ((), ()))


def pack_kv_kernel(keys, values, out):
    for g in range(8):
        out[g, :R] = keys[:, g * D : (g + 1) * D]
        out[g, R:] = values[:, g * D : (g + 1) * D]


def pack_q_kernel(queries, saved, grads, out):
    ones = jnp.ones((8, D), BF16)
    row = lax.broadcasted_iota(jnp.int32, (16, D), 0)
    for g in range(8):
        dots = []
        for pair in range(2):
            prods = []
            for h in (2 * pair, 2 * pair + 1):
                cols = slice((g * G + h) * D, (g * G + h + 1) * D)
                grad = grads[:, cols]
                out[g, h * R : (h + 1) * R] = queries[:, cols]
                out[g, QR + h * R : QR + (h + 1) * R] = grad
                prods.append(grad.astype(F32) * saved[:, cols].astype(F32))
            prod = jnp.concatenate(prods, axis=0)
            high = prod.astype(BF16)
            low = (prod - high.astype(F32)).astype(BF16)
            dots.append(
                lax.dot_general(ones, high, NT_DIMS, preferred_element_type=F32)
                + lax.dot_general(ones, low, NT_DIMS, preferred_element_type=F32)
            )
        values = []
        for dot in dots:
            both = jnp.concatenate([dot, dot], axis=0)
            high = both.astype(BF16).astype(F32)
            values.append((high, both - high))
        block = jnp.where(
            row == 0,
            values[0][0],
            jnp.where(row == 1, values[1][0], jnp.where(row == 2, values[0][1], values[1][1])),
        )
        out[g, 2 * QR :] = block.astype(BF16)


def attention_kernel(meta, qpay, *refs):
    pieces = refs[:10]
    dq_out, mine_0, mine_p, mine_m, mine_2, other_0, other_p, other_m, other_2 = refs[10:19]
    q_s, do_s, d_s, k_s, v_s, stash, m_blk, m_run, l_run, dk_s, dv_s, dq_s, sem = refs[19:]
    n0 = meta[64]
    n1 = meta[65]
    xl = meta[66]
    y = meta[67]
    core = meta[68]

    copies = []
    for s in range(8):
        for part, dst in ((0, q_s), (1, do_s)):
            copies.append(
                pltpu.make_async_copy(
                    qpay.at[s, pl.ds(part * QR, QR)], dst.at[s // 2, pl.ds((s % 2) * QR, QR)], sem
                )
            )
    copies.append(pltpu.make_async_copy(qpay.at[:, pl.ds(2 * QR, 16)], d_s, sem))
    for number, piece in enumerate(pieces):
        which = number % 5
        from_core = core if number < 5 else 1 - core
        dy = (0, 3, 1, 2, 2)[which]
        flips = ((0, 1), (0, 1), (0, 1), (0,), (1,))[which]
        for place, flip in enumerate(flips):
            slot = jnp.where(xl == flip, 0, 1) * 4 + (y + dy) % 4
            source = piece.at[place] if len(flips) > 1 else piece
            copies.append(
                pltpu.make_async_copy(source.at[:, pl.ds(0, R)], k_s.at[slot, :, from_core], sem)
            )
            copies.append(
                pltpu.make_async_copy(source.at[:, pl.ds(R, R)], v_s.at[slot, :, from_core], sem)
            )
    for copy in copies:
        copy.start()
    dk_s[...] = jnp.zeros_like(dk_s)
    dv_s[...] = jnp.zeros_like(dv_s)
    for copy in copies:
        copy.wait()

    def tile_of(ref, tile):
        return ref[tile // 4, pl.ds((tile % 4) * 2, 2)].reshape(SPAN, D)

    def add_to(ref, tile, term):
        place = (tile // 4, pl.ds((tile % 4) * 2, 2))
        ref[place] += term.reshape(2, 2, R, D)

    def chunk_step(c, unused):
        tile_q = (xl * 4 + y) * 4 + c
        span_q = meta[tile_q]
        first = span_q * SPAN
        has_second = first + (SPAN - 1) >= n1
        all_second = first >= n1
        lo = jnp.where(has_second, n0 // SPAN, 0)
        hi = jnp.where(has_second, (n1 + (SPAN - 1)) // SPAN, 0)
        hi = jnp.minimum(hi, span_q)
        lo = jnp.minimum(lo, hi)
        skip_at = (n0 + (SPAN - 1)) // SPAN
        skip_to = n1 // SPAN
        skip = jnp.where(all_second, jnp.maximum(skip_to - skip_at, 0), 0)
        n_masked = 1 + hi - lo - skip
        n_plain = span_q - (hi - lo)

        def masked_at(i):
            at = lo + i - 1
            at = jnp.where(at >= skip_at, at + skip, at)
            return jnp.where(i == 0, span_q, at)

        def plain_at(i):
            return jnp.where(i < lo, i, i + (hi - lo))

        q = q_s[c]
        grads = do_s[c]
        m_run[...] = jnp.full_like(m_run, HIDDEN)
        l_run[...] = jnp.zeros_like(l_run)
        dq_s[...] = jnp.zeros_like(dq_s)

        def weigh(at, masked):
            tile = meta[32 + at]
            scores = lax.dot_general(tile_of(k_s, tile), q, NT_DIMS, preferred_element_type=F32)
            scores = scores * EXP_SCALE
            if masked:
                lane = lax.broadcasted_iota(jnp.int32, (1, C), 1)
                query_pos = first + core * R + (lane // QR) * (2 * R) + lane % R
                key_pos = at * SPAN + lax.broadcasted_iota(jnp.int32, (SPAN, 1), 0)
                low = jnp.where(query_pos >= n1, n0, n1)
                seen = (key_pos <= query_pos) & ((key_pos < low) | (key_pos >= n1))
                scores = jnp.where(seen, scores, HIDDEN)
            old = m_run[...]
            new = jnp.maximum(old, jnp.max(scores, axis=0, keepdims=True))
            weights = jnp.exp2(scores - new)
            part = jnp.sum(weights.reshape(SPAN // 8, 8, C), axis=0)
            l_run[...] = l_run[...] * jnp.exp2(old - new) + part
            m_run[...] = new
            m_blk[at] = new
            stash[at] = weights.astype(BF16)

        def masked_step(i, carry):
            weigh(masked_at(i), True)
            return carry

        def plain_step(i, carry):
            weigh(plain_at(i), False)
            return carry

        lax.fori_loop(0, n_masked, masked_step, 0)
        lax.fori_loop(0, n_plain, plain_step, 0)

        logsum = m_run[...] + jnp.log2(jnp.sum(l_run[...], axis=0, keepdims=True))
        dots = []
        for half in range(2):
            block = d_s[2 * c + half].astype(F32)
            dots += [block[0:1] + block[2:3], block[1:2] + block[3:4]]
        row_dot = jnp.concatenate(dots, axis=1)

        def grad_step(i, carry):
            at = jnp.where(i < n_plain, plain_at(i), masked_at(i - n_plain))
            tile = meta[32 + at]
            keys = tile_of(k_s, tile)
            values = tile_of(v_s, tile)
            weights = stash[at].astype(F32) * jnp.exp2(m_blk[at] - logsum)
            prob_grad = lax.dot_general(values, grads, NT_DIMS, preferred_element_type=F32)
            score_grad = (weights * (prob_grad - row_dot)).astype(BF16)
            add_to(dv_s, tile, jnp.dot(weights.astype(BF16), grads, preferred_element_type=F32))
            add_to(dk_s, tile, jnp.dot(score_grad, q, preferred_element_type=F32))
            dq_s[...] += jnp.dot(keys.T, score_grad, preferred_element_type=F32)
            return carry

        lax.fori_loop(0, n_plain + n_masked, grad_step, 0)
        dq = (dq_s[...] * SCALE).T.astype(BF16)
        dq_out[2 * c] = dq[:QR]
        dq_out[2 * c + 1] = dq[QR:]
        return unused

    lax.fori_loop(0, 4, chunk_step, 0)

    for from_core, outs in ((core, (mine_0, mine_p, mine_m, mine_2)), (1 - core, (other_0, other_p, other_m, other_2))):
        for dy, out in zip((0, 1, 3, 2), outs):
            for flip in range(2):
                slot = jnp.where(xl == flip, 0, 1) * 4 + (y + dy) % 4
                out[flip, :, :R] = (dk_s[slot, :, from_core] * SCALE).astype(BF16)
                out[flip, :, R:] = dv_s[slot, :, from_core].astype(BF16)


def unpack_q_kernel(got, out):
    for g in range(8):
        for h in range(G):
            out[:, (g * G + h) * D : (g * G + h + 1) * D] = got[g, h * R : (h + 1) * R]


def unpack_kv_kernel(got, key_grad, value_grad):
    for g in range(8):
        key_grad[:, g * D : (g + 1) * D] = got[g, :R]
        value_grad[:, g * D : (g + 1) * D] = got[g, R:]


def on_vmem(kernel, outs, *args):
    return pl.pallas_call(
        kernel,
        out_shape=outs,
        compiler_params=pltpu.CompilerParams(vmem_limit_bytes=16 << 20),
    )(*args)


def exchange(array):
    return lax.all_to_all(array, HEADS, split_axis=0, concat_axis=0, tiled=True)


def shift(array, by):
    return lax.ppermute(array, "y", [(i, (i + by) % 4) for i in range(4)])


def flip(array, axis):
    return lax.ppermute(array, axis, [(0, 1), (1, 0)])


def gather_kv(own):
    both = jnp.stack([own, flip(own, "xl")])
    behind = shift(both, 1)
    ahead = shift(both, -1)
    far_same = shift(behind[0], 1)
    far_flip = shift(ahead[1], -1)
    mine = (both, behind, ahead, far_same, far_flip)
    return mine + tuple(flip(array, "core") for array in mine)


def add(*terms):
    total = terms[0].astype(F32)
    for term in terms[1:]:
        total = total + term.astype(F32)
    return total


def reduce_kv(mine, other):
    got_0, got_p, got_m, got_2 = [flip(array, "core") for array in other]
    mine_0, mine_p, mine_m, mine_2 = mine
    far = add(mine_2, got_2).astype(BF16)
    from_behind = shift(far[0], 1)
    from_ahead = shift(far[1], -1)
    to_ahead = jnp.stack([add(mine_p[0], got_p[0], from_behind), add(mine_p[1], got_p[1])])
    to_behind = jnp.stack([add(mine_m[0], got_m[0]), add(mine_m[1], got_m[1], from_ahead)])
    near_behind = shift(to_ahead.astype(BF16), 1)
    near_ahead = shift(to_behind.astype(BF16), -1)
    total = add(mine_0, got_0, near_behind, near_ahead)
    return add(total[0], flip(total[1].astype(BF16), "xl")).astype(BF16)


def body(queries, keys, values, attn_out, out_grad, segment, span_order):
    kv_own = exchange(on_vmem(pack_kv_kernel, jax.ShapeDtypeStruct((8, 2 * R, D), BF16), keys, values))
    q_own = exchange(
        on_vmem(
            pack_q_kernel,
            jax.ShapeDtypeStruct((8, 2 * QR + 16, D), BF16),
            queries,
            attn_out,
            out_grad,
        )
    )
    span_of_tile = span_order.reshape(2, 2, 4, 2).transpose(1, 2, 0, 3).reshape(NT)
    number = jnp.arange(NT, dtype=jnp.int32)
    tile_of_span = jnp.sum(
        jnp.where(span_of_tile[None, :] == number[:, None], number[None, :], 0), axis=1
    ).astype(jnp.int32)
    n0 = jnp.sum((segment == 0).astype(jnp.int32))
    n1 = jnp.sum((segment != 2).astype(jnp.int32))
    scalars = jnp.stack(
        [n0, n1, lax.axis_index("xl"), lax.axis_index("y"), lax.axis_index("core")]
    ).astype(jnp.int32)
    meta = jnp.concatenate([span_of_tile, tile_of_span, scalars])

    pieces = gather_kv(kv_own)
    group = jax.ShapeDtypeStruct((2, 8, 2 * R, D), BF16)
    outs = pl.pallas_call(
        attention_kernel,
        out_shape=[jax.ShapeDtypeStruct((8, QR, D), BF16)] + [group] * 8,
        in_specs=[pl.BlockSpec(memory_space=pltpu.SMEM)] + [pl.BlockSpec(memory_space=pl.ANY)] * 11,
        scratch_shapes=[
            pltpu.VMEM((4, C, D), BF16),
            pltpu.VMEM((4, C, D), BF16),
            pltpu.VMEM((8, 16, D), BF16),
            pltpu.VMEM((8, 8, 2, R, D), BF16),
            pltpu.VMEM((8, 8, 2, R, D), BF16),
            pltpu.VMEM((NT, SPAN, C), BF16),
            pltpu.VMEM((NT, 1, C), F32),
            pltpu.VMEM((1, C), F32),
            pltpu.VMEM((8, C), F32),
            pltpu.VMEM((8, 8, 2, R, D), F32),
            pltpu.VMEM((8, 8, 2, R, D), F32),
            pltpu.VMEM((D, C), F32),
            pltpu.SemaphoreType.DMA,
        ],
        compiler_params=pltpu.CompilerParams(vmem_limit_bytes=48 << 20),
    )(meta, q_own, *pieces)
    dq = exchange(outs[0])
    dkv = exchange(reduce_kv(outs[1:5], outs[5:9]))
    query_grad = on_vmem(unpack_q_kernel, jax.ShapeDtypeStruct((R, 8 * G * D), BF16), dq)
    key_grad, value_grad = on_vmem(
        unpack_kv_kernel, [jax.ShapeDtypeStruct((R, 8 * D), BF16)] * 2, dkv
    )
    return query_grad, key_grad, value_grad


def solution(mesh):
    fine = Mesh(mesh.devices.reshape(4, 2, 2, 2, 4), AXES)
    rows = P(AXES, None)
    return jax.shard_map(
        body,
        mesh=fine,
        in_specs=(rows,) * 5 + (P(), P()),
        out_specs=(rows,) * 3,
        check_vma=False,
    )
```

```python
import functools
import math

import jax
import jax.numpy as jnp
from jax import lax
from jax.experimental import pallas as pl
from jax.experimental.pallas import tpu as pltpu
from jax.sharding import Mesh, PartitionSpec as P

D = 128
G = 4
R = 64
SPAN = 256
NT = 32
HR = R // 2
QR = G * HR
C = 2 * QR
SCALE = D**-0.5
LOG2E = math.log2(math.e)
EXP_SCALE = SCALE * LOG2E
HIDDEN = -1e30
F32 = jnp.float32
BF16 = jnp.bfloat16
AXES = ("z", "core", "xh", "xl", "y")
HEADS = ("xh", "z")
SPREAD = ("xh", "xl", "z")
NT_DIMS = (((1,), (1,)), ((), ()))


def pack_kv_kernel(keys, values, out):
    for g in range(8):
        out[g, :R] = keys[:, g * D : (g + 1) * D]
        out[g, R:] = values[:, g * D : (g + 1) * D]


def pack_q_kernel(queries, saved, grads, out):
    ones = jnp.ones((8, D), BF16)
    row = lax.broadcasted_iota(jnp.int32, (16, D), 0)
    for g in range(8):
        for half in range(2):
            dest = (g // 4 * 2 + half) * 4 + g % 4
            rows = slice(half * HR, (half + 1) * HR)
            prods = []
            for h in range(G):
                cols = slice((g * G + h) * D, (g * G + h + 1) * D)
                grad = grads[rows, cols]
                out[dest, h * HR : (h + 1) * HR] = queries[rows, cols]
                out[dest, QR + h * HR : QR + (h + 1) * HR] = grad
                prods.append(grad.astype(F32) * saved[rows, cols].astype(F32))
            prod = jnp.concatenate(prods, axis=0)
            high = prod.astype(BF16)
            low = (prod - high.astype(F32)).astype(BF16)
            dot = lax.dot_general(ones, high, NT_DIMS, preferred_element_type=F32)
            dot = dot + lax.dot_general(ones, low, NT_DIMS, preferred_element_type=F32)
            both = jnp.concatenate([dot, dot], axis=0)
            rounded = both.astype(BF16).astype(F32)
            out[dest, 2 * QR :] = jnp.where(row == 0, rounded, both - rounded).astype(BF16)


def attention_kernel(meta, qpay, *refs):
    pieces = refs[:10]
    dq_out, mine_0, mine_p, mine_m, mine_2, other_0, other_p, other_m, other_2 = refs[10:19]
    q_s, do_s, d_s, k_s, v_s, kt_s, stash, m_blk, m_run, l_run, dk_s, dv_s, dq_s, sem = refs[19:]
    n0 = meta[64]
    n1 = meta[65]
    xl = meta[66]
    y = meta[67]
    core = meta[68]

    copies = []
    for s in range(16):
        for part, dst in ((0, q_s), (1, do_s)):
            copies.append(
                pltpu.make_async_copy(
                    qpay.at[s, pl.ds(part * QR, QR)], dst.at[s // 2, pl.ds((s % 2) * QR, QR)], sem
                )
            )
    copies.append(pltpu.make_async_copy(qpay.at[:, pl.ds(2 * QR, 16)], d_s, sem))
    for number, piece in enumerate(pieces):
        which = number % 5
        from_core = core if number < 5 else 1 - core
        dy = (0, 3, 1, 2, 2)[which]
        flips = ((0, 1), (0, 1), (0, 1), (0,), (1,))[which]
        for place, flip in enumerate(flips):
            slot = jnp.where(xl == flip, 0, 1) * 4 + (y + dy) % 4
            source = piece.at[place] if len(flips) > 1 else piece
            copies.append(
                pltpu.make_async_copy(source.at[:, pl.ds(0, R)], k_s.at[slot, :, from_core], sem)
            )
            copies.append(
                pltpu.make_async_copy(source.at[:, pl.ds(R, R)], v_s.at[slot, :, from_core], sem)
            )
    for copy in copies:
        copy.start()
    dk_s[...] = jnp.zeros_like(dk_s)
    dv_s[...] = jnp.zeros_like(dv_s)
    for copy in copies:
        copy.wait()

    def tile_of(ref, tile):
        return ref[tile // 4, pl.ds((tile % 4) * 2, 2)].reshape(SPAN, D)

    def add_to(ref, tile, term):
        place = (tile // 4, pl.ds((tile % 4) * 2, 2))
        ref[place] += term.reshape(2, 2, R, D)

    def turn(tile, carry):
        kt_s[tile] = tile_of(k_s, tile).T
        return carry

    lax.fori_loop(0, NT, turn, 0)

    def chunk_step(c, unused):
        tile_q = (((c // 2) % 2 * 4 + y) * 2 + c // 4) * 2 + c % 2
        span_q = meta[tile_q]
        first = span_q * SPAN
        has_second = first + (SPAN - 1) >= n1
        all_second = first >= n1
        lo = jnp.where(has_second, n0 // SPAN, 0)
        hi = jnp.where(has_second, (n1 + (SPAN - 1)) // SPAN, 0)
        hi = jnp.minimum(hi, span_q)
        lo = jnp.minimum(lo, hi)
        skip_at = (n0 + (SPAN - 1)) // SPAN
        skip_to = n1 // SPAN
        skip = jnp.where(all_second, jnp.maximum(skip_to - skip_at, 0), 0)
        n_masked = hi - lo - skip
        n_plain = span_q - (hi - lo)
        count = 1 + n_masked + n_plain

        def masked_at(i):
            at = lo + i
            return jnp.where(at >= skip_at, at + skip, at)

        def plain_at(i):
            return jnp.where(i < lo, i, i + (hi - lo))

        def place_at(i):
            at = jnp.where(i < n_plain, plain_at(i), masked_at(i - n_plain))
            return jnp.where(i == count - 1, span_q, at)

        q = q_s[c]
        grads = do_s[c]

        def scores_of(at):
            tile = meta[32 + at]
            scores = lax.dot_general(tile_of(k_s, tile), q, NT_DIMS, preferred_element_type=F32)
            return scores * EXP_SCALE

        def seen_at(at):
            lane = lax.broadcasted_iota(jnp.int32, (1, C), 1)
            query_pos = first + core * R + xl * HR + (lane // QR) * (2 * R) + lane % HR
            key_pos = at * SPAN + lax.broadcasted_iota(jnp.int32, (SPAN, 1), 0)
            low = jnp.where(query_pos >= n1, n0, n1)
            return (key_pos <= query_pos) & ((key_pos < low) | (key_pos >= n1))

        def add_up(weights):
            return jnp.sum(weights.reshape(SPAN // 8, 8, C), axis=0)

        def weigh(at, masked):
            top = m_run[...]
            scores = scores_of(at)
            if masked:
                scores = jnp.where(seen_at(at), scores, HIDDEN)
            weights = jnp.exp2(scores - top)
            l_run[...] += add_up(weights)
            m_blk[at] = top
            stash[at] = weights

        def weigh_diagonal():
            scores = jnp.where(seen_at(span_q), scores_of(span_q), HIDDEN)
            top = jnp.max(scores, axis=0, keepdims=True)
            weights = jnp.exp2(scores - top)
            l_run[...] = add_up(weights)
            m_run[...] = top
            m_blk[span_q] = top
            stash[span_q] = weights

        def masked_step(i, carry):
            weigh(masked_at(i), True)
            return carry

        def plain_pair(i, carry):
            weigh(plain_at(2 * i), False)
            weigh(plain_at(2 * i + 1), False)
            return carry

        weigh_diagonal()
        lax.fori_loop(0, n_masked, masked_step, 0)
        lax.fori_loop(0, n_plain // 2, plain_pair, 0)

        @pl.when(n_plain % 2 == 1)
        def _():
            weigh(plain_at(n_plain - 1), False)

        @pl.when(jnp.logical_not(jnp.max(l_run[...]) < 2.0**90))
        def _():
            m_run[...] = jnp.full_like(m_run, HIDDEN)
            l_run[...] = jnp.zeros_like(l_run)

            def careful_step(i, carry):
                at = place_at(count - 1 - i)
                scores = jnp.where(seen_at(at), scores_of(at), HIDDEN)
                old = m_run[...]
                top = jnp.maximum(old, jnp.max(scores, axis=0, keepdims=True))
                weights = jnp.exp2(scores - top)
                l_run[...] = l_run[...] * jnp.exp2(old - top) + add_up(weights)
                m_run[...] = top
                m_blk[at] = top
                stash[at] = weights
                return carry

            lax.fori_loop(0, count, careful_step, 0)

        logsum = m_run[...] + jnp.log2(jnp.sum(l_run[...], axis=0, keepdims=True))
        dots = []
        for half in range(2):
            block = d_s[2 * c + half].astype(F32)
            dots.append(block[0:1] + block[1:2])
        row_dot = jnp.concatenate(dots, axis=1)
        dq_s[...] = jnp.zeros_like(dq_s)

        def grad_tile(at):
            tile = meta[32 + at]
            weights = stash[at] * jnp.exp2(m_blk[at] - logsum)
            prob_grad = lax.dot_general(
                tile_of(v_s, tile), grads, NT_DIMS, preferred_element_type=F32
            )
            score_grad = (weights * (prob_grad - row_dot)).astype(BF16)
            add_to(dv_s, tile, jnp.dot(weights.astype(BF16), grads, preferred_element_type=F32))
            add_to(dk_s, tile, jnp.dot(score_grad, q, preferred_element_type=F32))
            return jnp.dot(kt_s[tile], score_grad, preferred_element_type=F32)

        def grad_pair(i, carry):
            first_term = grad_tile(place_at(2 * i))
            second_term = grad_tile(place_at(2 * i + 1))
            dq_s[...] += first_term + second_term
            return carry

        lax.fori_loop(0, count // 2, grad_pair, 0)

        @pl.when(count % 2 == 1)
        def _():
            dq_s[...] += grad_tile(span_q)

        dq = (dq_s[...] * SCALE).T.astype(BF16)
        dq_out[2 * c] = dq[:QR]
        dq_out[2 * c + 1] = dq[QR:]
        return unused

    lax.fori_loop(0, 8, chunk_step, 0)

    for from_core, outs in (
        (core, (mine_0, mine_p, mine_m, mine_2)),
        (1 - core, (other_0, other_p, other_m, other_2)),
    ):
        for dy, out in zip((0, 1, 3, 2), outs):
            for flip in range(2):
                slot = jnp.where(xl == flip, 0, 1) * 4 + (y + dy) % 4
                out[flip, :, :R] = (dk_s[slot, :, from_core] * SCALE).astype(BF16)
                out[flip, :, R:] = dv_s[slot, :, from_core].astype(BF16)


def last_sum_kernel(mine, got, behind, ahead, dq, keep, send, out):
    for flip, total in enumerate((keep, send)):
        parts = [ref[flip].astype(F32) for ref in (mine, got, behind, ahead)]
        total[...] = ((parts[0] + parts[1]) + (parts[2] + parts[3])).astype(total.dtype)
    for g in range(8):
        for half in range(2):
            dest = (g // 4 * 2 + half) * 4 + g % 4
            for h in range(G):
                cols = slice((g * G + h) * D, (g * G + h + 1) * D)
                out[half * HR : (half + 1) * HR, cols] = dq[dest, h * HR : (h + 1) * HR]


def unpack_kv_kernel(got, key_grad, value_grad):
    for g in range(8):
        key_grad[:, g * D : (g + 1) * D] = got[g, :R]
        value_grad[:, g * D : (g + 1) * D] = got[g, R:]


def on_vmem(kernel, outs, *args):
    return pl.pallas_call(
        kernel,
        out_shape=outs,
        compiler_params=pltpu.CompilerParams(vmem_limit_bytes=16 << 20),
    )(*args)


def exchange(array, axes):
    return lax.all_to_all(array, axes, split_axis=0, concat_axis=0, tiled=True)


def shift(array, by):
    return lax.ppermute(array, "y", [(i, (i + by) % 4) for i in range(4)])


def flip(array, axis):
    return lax.ppermute(array, axis, [(0, 1), (1, 0)])


def gather_kv(own):
    both = jnp.stack([own, flip(own, "xl")])
    behind = shift(both, 1)
    ahead = shift(both, -1)
    far_same = shift(behind[0], 1)
    far_flip = shift(ahead[1], -1)
    mine = (both, behind, ahead, far_same, far_flip)
    return mine + tuple(flip(array, "core") for array in mine)


def add(*terms):
    total = terms[0].astype(F32)
    for term in terms[1:]:
        total = total + term.astype(F32)
    return total


def reduce_kv(mine, other, dq):
    got_0, got_p, got_m, got_2 = [flip(array, "core") for array in other]
    mine_0, mine_p, mine_m, mine_2 = mine
    far = add(mine_2, got_2).astype(BF16)
    from_behind = shift(far[0], 1)
    from_ahead = shift(far[1], -1)
    to_ahead = jnp.stack([add(mine_p[0], got_p[0], from_behind), add(mine_p[1], got_p[1])])
    to_behind = jnp.stack([add(mine_m[0], got_m[0]), add(mine_m[1], got_m[1], from_ahead)])
    near_behind = shift(to_ahead.astype(BF16), 1)
    near_ahead = shift(to_behind.astype(BF16), -1)
    piece = (8, 2 * R, D)
    keep, send, query_grad = on_vmem(
        last_sum_kernel,
        [
            jax.ShapeDtypeStruct(piece, F32),
            jax.ShapeDtypeStruct(piece, BF16),
            jax.ShapeDtypeStruct((R, 8 * G * D), BF16),
        ],
        mine_0,
        got_0,
        near_behind,
        near_ahead,
        dq,
    )
    return add(keep, flip(send, "xl")).astype(BF16), query_grad


def body(queries, keys, values, attn_out, out_grad, segment, span_order):
    kv_own = exchange(
        on_vmem(pack_kv_kernel, jax.ShapeDtypeStruct((8, 2 * R, D), BF16), keys, values), HEADS
    )
    q_own = exchange(
        on_vmem(
            pack_q_kernel,
            jax.ShapeDtypeStruct((16, 2 * QR + 16, D), BF16),
            queries,
            attn_out,
            out_grad,
        ),
        SPREAD,
    )
    span_of_tile = span_order.reshape(2, 2, 4, 2).transpose(1, 2, 0, 3).reshape(NT)
    number = jnp.arange(NT, dtype=jnp.int32)
    tile_of_span = jnp.sum(
        jnp.where(span_of_tile[None, :] == number[:, None], number[None, :], 0), axis=1
    ).astype(jnp.int32)
    n0 = jnp.sum((segment == 0).astype(jnp.int32))
    n1 = jnp.sum((segment != 2).astype(jnp.int32))
    scalars = jnp.stack(
        [n0, n1, lax.axis_index("xl"), lax.axis_index("y"), lax.axis_index("core")]
    ).astype(jnp.int32)
    meta = jnp.concatenate([span_of_tile, tile_of_span, scalars])

    pieces = gather_kv(kv_own)
    group = jax.ShapeDtypeStruct((2, 8, 2 * R, D), BF16)
    outs = pl.pallas_call(
        attention_kernel,
        out_shape=[jax.ShapeDtypeStruct((16, QR, D), BF16)] + [group] * 8,
        in_specs=[pl.BlockSpec(memory_space=pltpu.SMEM)] + [pl.BlockSpec(memory_space=pl.ANY)] * 11,
        scratch_shapes=[
            pltpu.VMEM((8, C, D), BF16),
            pltpu.VMEM((8, C, D), BF16),
            pltpu.VMEM((16, 16, D), BF16),
            pltpu.VMEM((8, 8, 2, R, D), BF16),
            pltpu.VMEM((8, 8, 2, R, D), BF16),
            pltpu.VMEM((NT, D, SPAN), BF16),
            pltpu.VMEM((NT, SPAN, C), F32),
            pltpu.VMEM((NT, 1, C), F32),
            pltpu.VMEM((1, C), F32),
            pltpu.VMEM((8, C), F32),
            pltpu.VMEM((8, 8, 2, R, D), F32),
            pltpu.VMEM((8, 8, 2, R, D), F32),
            pltpu.VMEM((D, C), F32),
            pltpu.SemaphoreType.DMA,
        ],
        compiler_params=pltpu.CompilerParams(vmem_limit_bytes=48 << 20),
    )(meta, q_own, *pieces)
    dkv, query_grad = reduce_kv(outs[1:5], outs[5:9], exchange(outs[0], SPREAD))
    key_grad, value_grad = on_vmem(
        unpack_kv_kernel, [jax.ShapeDtypeStruct((R, 8 * D), BF16)] * 2, exchange(dkv, HEADS)
    )
    return query_grad, key_grad, value_grad


def solution(mesh):
    fine = Mesh(mesh.devices.reshape(4, 2, 2, 2, 4), AXES)
    rows = P(AXES, None)
    return jax.shard_map(
        body,
        mesh=fine,
        in_specs=(rows,) * 5 + (P(), P()),
        out_specs=(rows,) * 3,
        check_vma=False,
    )
```

```python
import functools
import math

import jax
import jax.numpy as jnp
from jax import lax
from jax.experimental import pallas as pl
from jax.experimental.pallas import tpu as pltpu
from jax.sharding import Mesh, PartitionSpec as P

D = 128
G = 4
R = 64
SPAN = 256
KB = 2 * SPAN
NT = 32
HR = R // 2
QR = G * HR
C = 2 * QR
SCALE = D**-0.5
LOG2E = math.log2(math.e)
EXP_SCALE = SCALE * LOG2E
HIDDEN = -1e30
F32 = jnp.float32
BF16 = jnp.bfloat16
AXES = ("z", "core", "xh", "xl", "y")
HEADS = ("xh", "z")
SPREAD = ("xh", "xl", "z")
NT_DIMS = (((1,), (1,)), ((), ()))


def pack_kv_kernel(keys, values, segment, out, counts):
    counts[0] = jnp.sum((segment[...] == 0).astype(jnp.int32))
    counts[1] = jnp.sum((segment[...] != 2).astype(jnp.int32))
    for g in range(8):
        out[g, :R] = keys[:, g * D : (g + 1) * D]
        out[g, R:] = values[:, g * D : (g + 1) * D]


def pack_q_kernel(queries, saved, grads, out):
    ones = jnp.ones((8, D), BF16)
    row = lax.broadcasted_iota(jnp.int32, (16, D), 0)
    for g in range(8):
        for half in range(2):
            dest = (g // 4 * 2 + half) * 4 + g % 4
            rows = slice(half * HR, (half + 1) * HR)
            prods = []
            for h in range(G):
                cols = slice((g * G + h) * D, (g * G + h + 1) * D)
                grad = grads[rows, cols]
                out[dest, h * HR : (h + 1) * HR] = queries[rows, cols]
                out[dest, QR + h * HR : QR + (h + 1) * HR] = grad
                prods.append(grad.astype(F32) * saved[rows, cols].astype(F32))
            prod = jnp.concatenate(prods, axis=0)
            high = prod.astype(BF16)
            low = (prod - high.astype(F32)).astype(BF16)
            dot = lax.dot_general(ones, high, NT_DIMS, preferred_element_type=F32)
            dot = dot + lax.dot_general(ones, low, NT_DIMS, preferred_element_type=F32)
            both = jnp.concatenate([dot, dot], axis=0)
            rounded = both.astype(BF16).astype(F32)
            out[dest, 2 * QR :] = jnp.where(row == 0, rounded, both - rounded).astype(BF16)


def span_id(xh, xl, y, zh):
    return ((xh * 2 + xl) * 4 + y) * 2 + zh


def attention_kernel(order, counts, qpay, *refs):
    pieces = refs[:10]
    dq_out, outs = refs[10], (refs[11:15], refs[15:19])
    (q_s, do_s, d_s, k_s, v_s, kt_s, stash, m_blk, m_run, l_run, dk_s, dv_s, dq_s, sem) = refs[19:]
    n0 = counts[0]
    n1 = counts[1]
    xl = lax.axis_index("xl")
    y = lax.axis_index("y")
    core = lax.axis_index("core")

    def place(flip, dy, j):
        return order[span_id(j // 2, xl ^ flip, y ^ dy, j % 2)]

    copies = []
    for s in range(16):
        for part, dst in ((0, q_s), (1, do_s)):
            copies.append(
                pltpu.make_async_copy(
                    qpay.at[s, pl.ds(part * QR, QR)], dst.at[s // 2, pl.ds((s % 2) * QR, QR)], sem
                )
            )
    copies.append(pltpu.make_async_copy(qpay.at[:, pl.ds(2 * QR, 16)], d_s, sem))
    for number, piece in enumerate(pieces):
        which = number % 5
        from_core = core if number < 5 else 1 - core
        dy = (0, 1, 3, 2, 2)[which]
        flips = ((0, 1), (0, 1), (0, 1), (0,), (1,))[which]
        for at, flip in enumerate(flips):
            source = piece.at[at] if len(flips) > 1 else piece
            for j in range(4):
                rank = place(flip, dy, j)
                rows = source.at[pl.ds(2 * j, 2)]
                copies.append(
                    pltpu.make_async_copy(rows.at[:, pl.ds(0, R)], k_s.at[rank, :, from_core], sem)
                )
                copies.append(
                    pltpu.make_async_copy(rows.at[:, pl.ds(R, R)], v_s.at[rank, :, from_core], sem)
                )
    for copy in copies:
        copy.start()
    dk_s[...] = jnp.zeros_like(dk_s)
    dv_s[...] = jnp.zeros_like(dv_s)
    for copy in copies:
        copy.wait()

    def block_of(ref, b):
        return ref[pl.ds(2 * b, 2)].reshape(KB, D)

    def turn(b, carry):
        kt_s[b] = block_of(k_s, b).T
        return carry

    lax.fori_loop(0, NT // 2, turn, 0)

    def chunk_step(c, unused):
        span_q = order[span_id(c // 4, c // 2 % 2, y, c % 2)]
        first = span_q * SPAN
        has_second = first + (SPAN - 1) >= n1
        all_second = first >= n1
        n_full = span_q // 2
        lo = jnp.where(has_second, n0 // KB, 0)
        hi = jnp.where(has_second, (n1 + (KB - 1)) // KB, 0)
        hi = jnp.minimum(hi, n_full)
        lo = jnp.minimum(lo, hi)
        skip_at = (n0 + (KB - 1)) // KB
        skip = jnp.where(all_second, jnp.maximum(jnp.minimum(n1 // KB, hi) - skip_at, 0), 0)
        n_masked = hi - lo - skip
        n_plain = n_full - (hi - lo)
        count = n_plain + n_masked + 1

        def masked_at(i):
            at = lo + i
            return jnp.where(at >= skip_at, at + skip, at)

        def plain_at(i):
            return jnp.where(i < lo, i, i + (hi - lo))

        def place_at(i):
            at = jnp.where(i < n_plain, plain_at(i), masked_at(i - n_plain))
            return jnp.where(i == count - 1, n_full, at)

        q = q_s[c]
        grads = do_s[c]

        def scores_of(b):
            scores = lax.dot_general(block_of(k_s, b), q, NT_DIMS, preferred_element_type=F32)
            return scores * EXP_SCALE

        def seen_at(b):
            lane = lax.broadcasted_iota(jnp.int32, (1, C), 1)
            query_pos = first + core * R + xl * HR + (lane // QR) * (2 * R) + lane % HR
            key_pos = b * KB + lax.broadcasted_iota(jnp.int32, (KB, 1), 0)
            low = jnp.where(query_pos >= n1, n0, n1)
            return (key_pos <= query_pos) & ((key_pos < low) | (key_pos >= n1))

        def add_up(weights):
            return jnp.sum(weights.reshape(KB // 8, 8, C), axis=0)

        def weigh(b, masked):
            top = m_run[...]
            scores = scores_of(b)
            if masked:
                scores = jnp.where(seen_at(b), scores, HIDDEN)
            weights = jnp.exp2(scores - top)
            l_run[...] += add_up(weights)
            m_blk[b] = top
            stash[b] = weights

        def weigh_diagonal():
            scores = jnp.where(seen_at(n_full), scores_of(n_full), HIDDEN)
            top = jnp.max(scores, axis=0, keepdims=True)
            weights = jnp.exp2(scores - top)
            l_run[...] = add_up(weights)
            m_run[...] = top
            m_blk[n_full] = top
            stash[n_full] = weights

        def masked_step(i, carry):
            weigh(masked_at(i), True)
            return carry

        def plain_pair(i, carry):
            weigh(plain_at(2 * i), False)
            weigh(plain_at(2 * i + 1), False)
            return carry

        weigh_diagonal()
        lax.fori_loop(0, n_masked, masked_step, 0)
        lax.fori_loop(0, n_plain // 2, plain_pair, 0)

        @pl.when(n_plain % 2 == 1)
        def _():
            weigh(plain_at(n_plain - 1), False)

        @pl.when(jnp.logical_not(jnp.max(l_run[...]) < 2.0**90))
        def _():
            m_run[...] = jnp.full_like(m_run, HIDDEN)
            l_run[...] = jnp.zeros_like(l_run)

            def careful_step(i, carry):
                b = place_at(count - 1 - i)
                scores = jnp.where(seen_at(b), scores_of(b), HIDDEN)
                old = m_run[...]
                top = jnp.maximum(old, jnp.max(scores, axis=0, keepdims=True))
                weights = jnp.exp2(scores - top)
                l_run[...] = l_run[...] * jnp.exp2(old - top) + add_up(weights)
                m_run[...] = top
                m_blk[b] = top
                stash[b] = weights
                return carry

            lax.fori_loop(0, count, careful_step, 0)

        logsum = m_run[...] + jnp.log2(jnp.sum(l_run[...], axis=0, keepdims=True))
        dots = []
        for half in range(2):
            block = d_s[2 * c + half].astype(F32)
            dots.append(block[0:1] + block[1:2])
        row_dot = jnp.concatenate(dots, axis=1)
        dq_s[...] = jnp.zeros_like(dq_s)

        def grad_block(b):
            weights = stash[b] * jnp.exp2(m_blk[b] - logsum)
            prob_grad = lax.dot_general(
                block_of(v_s, b), grads, NT_DIMS, preferred_element_type=F32
            )
            score_grad = (weights * (prob_grad - row_dot)).astype(BF16)
            for ref, term in (
                (dv_s, jnp.dot(weights.astype(BF16), grads, preferred_element_type=F32)),
                (dk_s, jnp.dot(score_grad, q, preferred_element_type=F32)),
            ):
                ref[pl.ds(2 * b, 2)] += term.reshape(2, 2, 2, R, D)
            return jnp.dot(kt_s[b], score_grad, preferred_element_type=F32)

        def grad_pair(i, carry):
            first_term = grad_block(place_at(2 * i))
            second_term = grad_block(place_at(2 * i + 1))
            dq_s[...] += first_term + second_term
            return carry

        lax.fori_loop(0, count // 2, grad_pair, 0)

        @pl.when(count % 2 == 1)
        def _():
            dq_s[...] += grad_block(n_full)

        dq = (dq_s[...] * SCALE).T.astype(BF16)
        dq_out[2 * c] = dq[:QR]
        dq_out[2 * c + 1] = dq[QR:]
        return unused

    lax.fori_loop(0, 8, chunk_step, 0)

    for from_core, group in ((core, outs[0]), (1 - core, outs[1])):
        for dy, out in zip((0, 1, 3, 2), group):
            for flip in range(2):
                for j in range(4):
                    rank = place(flip, dy, j)
                    rows = slice(2 * j, 2 * j + 2)
                    out[flip, rows, :R] = (dk_s[rank, :, from_core] * SCALE).astype(BF16)
                    out[flip, rows, R:] = dv_s[rank, :, from_core].astype(BF16)


def last_sum_kernel(mine, got, near_1, near_3, dq, keep, send, out):
    for flip, total in enumerate((keep, send)):
        parts = [ref[flip].astype(F32) for ref in (mine, got, near_1, near_3)]
        total[...] = ((parts[0] + parts[1]) + (parts[2] + parts[3])).astype(total.dtype)
    for g in range(8):
        for half in range(2):
            dest = (g // 4 * 2 + half) * 4 + g % 4
            for h in range(G):
                cols = slice((g * G + h) * D, (g * G + h + 1) * D)
                out[half * HR : (half + 1) * HR, cols] = dq[dest, h * HR : (h + 1) * HR]


def unpack_kv_kernel(got, key_grad, value_grad):
    for g in range(8):
        key_grad[:, g * D : (g + 1) * D] = got[g, :R]
        value_grad[:, g * D : (g + 1) * D] = got[g, R:]


def on_vmem(kernel, outs, *args):
    return pl.pallas_call(
        kernel,
        out_shape=outs,
        compiler_params=pltpu.CompilerParams(vmem_limit_bytes=16 << 20),
    )(*args)


def exchange(array, axes):
    return lax.all_to_all(array, axes, split_axis=0, concat_axis=0, tiled=True)


def flip(array, axis):
    return lax.ppermute(array, axis, [(0, 1), (1, 0)])


def swap(array, distance):
    return lax.ppermute(array, "y", [(i, i ^ distance) for i in range(4)])


def gather_kv(own):
    both = jnp.stack([own, flip(own, "xl")])
    near_1 = swap(both, 1)
    near_3 = swap(both, 3)
    far_same = swap(near_3[0], 1)
    far_flip = swap(near_1[1], 3)
    mine = (both, near_1, near_3, far_same, far_flip)
    return mine + tuple(flip(array, "core") for array in mine)


def add(*terms):
    total = terms[0].astype(F32)
    for term in terms[1:]:
        total = total + term.astype(F32)
    return total


def reduce_kv(mine, other, dq):
    got_0, got_1, got_3, got_2 = [flip(array, "core") for array in other]
    mine_0, mine_1, mine_3, mine_2 = mine
    far = add(mine_2, got_2).astype(BF16)
    from_1 = swap(far[0], 1)
    from_3 = swap(far[1], 3)
    to_3 = jnp.stack([add(mine_3[0], got_3[0], from_1), add(mine_3[1], got_3[1])])
    to_1 = jnp.stack([add(mine_1[0], got_1[0]), add(mine_1[1], got_1[1], from_3)])
    near_3 = swap(to_3.astype(BF16), 3)
    near_1 = swap(to_1.astype(BF16), 1)
    piece = (8, 2 * R, D)
    keep, send, query_grad = on_vmem(
        last_sum_kernel,
        [
            jax.ShapeDtypeStruct(piece, F32),
            jax.ShapeDtypeStruct(piece, BF16),
            jax.ShapeDtypeStruct((R, 8 * G * D), BF16),
        ],
        mine_0,
        got_0,
        near_1,
        near_3,
        dq,
    )
    return add(keep, flip(send, "xl")).astype(BF16), query_grad


def body(queries, keys, values, attn_out, out_grad, segment, span_order):
    kv_packed, counts = pl.pallas_call(
        pack_kv_kernel,
        out_shape=[jax.ShapeDtypeStruct((8, 2 * R, D), BF16), jax.ShapeDtypeStruct((2,), jnp.int32)],
        out_specs=[pl.BlockSpec(memory_space=pltpu.VMEM), pl.BlockSpec(memory_space=pltpu.SMEM)],
        compiler_params=pltpu.CompilerParams(vmem_limit_bytes=16 << 20),
    )(keys, values, segment.reshape(64, 128))
    kv_own = exchange(kv_packed, HEADS)
    q_own = exchange(
        on_vmem(
            pack_q_kernel,
            jax.ShapeDtypeStruct((16, 2 * QR + 16, D), BF16),
            queries,
            attn_out,
            out_grad,
        ),
        SPREAD,
    )
    pieces = gather_kv(kv_own)
    group = jax.ShapeDtypeStruct((2, 8, 2 * R, D), BF16)
    outs = pl.pallas_call(
        attention_kernel,
        out_shape=[jax.ShapeDtypeStruct((16, QR, D), BF16)] + [group] * 8,
        in_specs=[pl.BlockSpec(memory_space=pltpu.SMEM)] * 2
        + [pl.BlockSpec(memory_space=pl.ANY)] * 11,
        scratch_shapes=[
            pltpu.VMEM((8, C, D), BF16),
            pltpu.VMEM((8, C, D), BF16),
            pltpu.VMEM((16, 16, D), BF16),
            pltpu.VMEM((NT, 2, 2, R, D), BF16),
            pltpu.VMEM((NT, 2, 2, R, D), BF16),
            pltpu.VMEM((NT // 2, D, KB), BF16),
            pltpu.VMEM((NT // 2, KB, C), F32),
            pltpu.VMEM((NT // 2, 1, C), F32),
            pltpu.VMEM((1, C), F32),
            pltpu.VMEM((8, C), F32),
            pltpu.VMEM((NT, 2, 2, R, D), F32),
            pltpu.VMEM((NT, 2, 2, R, D), F32),
            pltpu.VMEM((D, C), F32),
            pltpu.SemaphoreType.DMA,
        ],
        compiler_params=pltpu.CompilerParams(vmem_limit_bytes=48 << 20),
    )(span_order, counts, q_own, *pieces)
    dkv, query_grad = reduce_kv(outs[1:5], outs[5:9], exchange(outs[0], SPREAD))
    key_grad, value_grad = on_vmem(
        unpack_kv_kernel, [jax.ShapeDtypeStruct((R, 8 * D), BF16)] * 2, exchange(dkv, HEADS)
    )
    return query_grad, key_grad, value_grad


def solution(mesh):
    fine = Mesh(mesh.devices.reshape(4, 2, 2, 2, 4), AXES)
    rows = P(AXES, None)
    return jax.shard_map(
        body,
        mesh=fine,
        in_specs=(rows,) * 5 + (P(), P()),
        out_specs=(rows,) * 3,
        check_vma=False,
    )
```

```python
import functools
import math

import jax
import jax.numpy as jnp
from jax import lax
from jax.experimental import pallas as pl
from jax.experimental.pallas import tpu as pltpu
from jax.sharding import Mesh, PartitionSpec as P

D = 128
G = 4
R = 64
HR = R // 2
SPAN = 256
KB = 2 * SPAN
QR = G * HR
C = 2 * QR
NC = 8
SCALE = D**-0.5
EXP_SCALE = SCALE * math.log2(math.e)
HIDDEN = -1e30
LARGE = 2.0**90
F32 = jnp.float32
BF16 = jnp.bfloat16
AXES = ("z", "core", "xh", "xl", "y")
SPREAD = ("xh", "xl", "z")
NT_DIMS = (((1,), (1,)), ((), ()))

OWN, NEAR, FAR = (0,), (1, 3), (2,)


def spread_to(g, xl):
    return (g // 4 * 2 + xl) * 4 + g % 4


def head_columns(g, h):
    return slice((g * G + h) * D, (g * G + h + 1) * D)


def pack_kv_kernel(keys, values, segment, out, counts):
    counts[0] = jnp.sum((segment[...] == 0).astype(jnp.int32))
    counts[1] = jnp.sum((segment[...] != 2).astype(jnp.int32))
    for g in range(8):
        for xl in range(2):
            out[spread_to(g, xl), :R] = keys[:, g * D : (g + 1) * D]
            out[spread_to(g, xl), R:] = values[:, g * D : (g + 1) * D]


def pack_q_kernel(queries, saved, grads, out):
    ones = jnp.ones((8, D), BF16)
    row = lax.broadcasted_iota(jnp.int32, (16, D), 0)
    for g in range(8):
        for half in range(2):
            dest = spread_to(g, half)
            rows = slice(half * HR, (half + 1) * HR)
            prods = []
            for h in range(G):
                cols = head_columns(g, h)
                grad = grads[rows, cols]
                out[dest, h * HR : (h + 1) * HR] = queries[rows, cols]
                out[dest, QR + h * HR : QR + (h + 1) * HR] = grad
                prods.append(grad.astype(F32) * saved[rows, cols].astype(F32))
            prod = jnp.concatenate(prods, axis=0)
            high = prod.astype(BF16)
            low = (prod - high.astype(F32)).astype(BF16)
            dot = lax.dot_general(ones, high, NT_DIMS, preferred_element_type=F32)
            dot = dot + lax.dot_general(ones, low, NT_DIMS, preferred_element_type=F32)
            both = jnp.concatenate([dot, dot], axis=0)
            rounded = both.astype(BF16).astype(F32)
            out[dest, 2 * QR :] = jnp.where(row == 0, rounded, both - rounded).astype(BF16)


def span_id(xh, xl, y, zh):
    return ((xh * 2 + xl) * 4 + y) * 2 + zh


class Group:
    def __init__(self, distances, order, counts, table):
        self.order, self.table = order, table
        self.n0, self.n1 = counts[0], counts[1]
        self.xl = lax.axis_index("xl")
        self.y = lax.axis_index("y")
        self.core = lax.axis_index("core")
        self.own = 0 in distances
        self.entries = [(dy, xh, xl, zh) for dy in distances for xh in (0, 1) for xl in (0, 1) for zh in (0, 1)]
        spans = [order[span_id(xh, xl, self.y ^ dy, zh)] for dy, xh, xl, zh in self.entries]
        self.ranks = []
        for mine in spans:
            rank = jnp.int32(0)
            for other in spans:
                if other is not mine:
                    rank = rank + (other < mine).astype(jnp.int32)
            self.ranks.append(rank)
            table[rank] = mine
        n0, n1 = self.n0, self.n1
        self.lo = self.below(n0 // SPAN)
        self.hi = self.below((n1 + (SPAN - 1)) // SPAN)
        self.skip_at = (self.below((n0 + (SPAN - 1)) // SPAN) + 1) // 2
        self.skip_to = self.below(n1 // SPAN) // 2

    def below(self, position):
        total = jnp.int32(0)
        for i in range(len(self.entries)):
            total = total + (self.table[i] < position).astype(jnp.int32)
        return total

    def copies(self, pieces, parts, sem):
        made = []
        for (dy, xh, xl, zh), rank in zip(self.entries, self.ranks):
            for from_core, arrays in zip((self.core, 1 - self.core), pieces[dy]):
                if len(arrays) == 2:
                    rows = arrays[xh].at[pl.ds((xl * 2 + zh) * 2, 2)]
                else:
                    rows = arrays[0].at[pl.ds(((xh * 2 + xl) * 2 + zh) * 2, 2)]
                for part, dst in enumerate(parts):
                    made.append(
                        pltpu.make_async_copy(
                            rows.at[:, pl.ds(part * R, R)], dst.at[rank, :, from_core], sem
                        )
                    )
        return made

    def chunk(self, c):
        return Chunk(self, c)


class Chunk:
    def __init__(self, group, c):
        n0, n1 = group.n0, group.n1
        self.group = group
        self.span = group.order[span_id(c // 4, c // 2 % 2, group.y, c % 2)]
        self.first = self.span * SPAN
        has_second = self.first + (SPAN - 1) >= n1
        all_second = self.first >= n1
        before = group.below(self.span)
        n_full = before // 2
        hi = jnp.minimum(jnp.where(has_second, (group.hi + 1) // 2, 0), n_full)
        lo = jnp.minimum(jnp.where(has_second, group.lo // 2, 0), hi)
        skip_to = jnp.minimum(group.skip_to, hi)
        self.skip = jnp.where(all_second, jnp.maximum(skip_to - group.skip_at, 0), 0)
        self.lo, self.hi, self.n_full = lo, hi, n_full
        self.n_masked = hi - lo - self.skip
        self.n_plain = n_full - (hi - lo)
        self.n_tail = jnp.int32(1) if group.own else before % 2

    def masked_at(self, i):
        at = self.lo + i
        at = jnp.where(at >= self.group.skip_at, at + self.skip, at)
        return jnp.where(i == self.n_masked, self.n_full, at)

    def plain_at(self, i):
        return jnp.where(i < self.lo, i, i + (self.hi - self.lo))

    def seen(self, b):
        group = self.group
        lane = lax.broadcasted_iota(jnp.int32, (1, C), 1)
        query_pos = self.first + group.core * R + group.xl * HR + (lane // QR) * (2 * R) + lane % HR
        row = lax.broadcasted_iota(jnp.int32, (KB, 1), 0)
        key_span = jnp.where(row < SPAN, group.table[2 * b], group.table[2 * b + 1])
        key_pos = key_span * SPAN + row % SPAN
        low = jnp.where(query_pos >= group.n1, group.n0, group.n1)
        return (key_pos <= query_pos) & ((key_pos < low) | (key_pos >= group.n1))


def block_of(ref, b):
    return ref[pl.ds(2 * b, 2)].reshape(KB, D)


def add_up(weights):
    return jnp.sum(weights.reshape(KB // 8, 8, C), axis=0)


def scores_of(chunk, b, k_s, q, masked):
    scores = lax.dot_general(block_of(k_s, b), q, NT_DIMS, preferred_element_type=F32) * EXP_SCALE
    return jnp.where(chunk.seen(b), scores, HIDDEN) if masked else scores


def stats_pass(group, first, q_s, k_s, m_in, l_in, m_out, l_out):
    def chunk_step(c, unused):
        chunk = group.chunk(c)
        q = q_s[c]

        def careful_step(i, carry):
            is_tail = i < chunk.n_tail
            number = i - chunk.n_tail
            b = jnp.where(
                number < chunk.n_masked,
                chunk.masked_at(number),
                chunk.plain_at(number - chunk.n_masked),
            )
            b = jnp.where(is_tail, chunk.n_full, b)
            scores = scores_of(chunk, b, k_s, q, True)
            old = m_out[c]
            top = jnp.maximum(old, jnp.max(scores, axis=0, keepdims=True))
            l_out[c] = l_out[c] * jnp.exp2(old - top) + add_up(jnp.exp2(scores - top))
            m_out[c] = top
            return carry

        def weigh(b, masked):
            scores = scores_of(chunk, b, k_s, q, masked)
            l_out[c] += add_up(jnp.exp2(scores - m_out[c]))

        def masked_step(i, carry):
            weigh(chunk.masked_at(i), True)
            return carry

        def plain_step(i, carry):
            weigh(chunk.plain_at(i), False)
            return carry

        if first:
            scores = scores_of(chunk, chunk.n_full, k_s, q, True)
            top = jnp.max(scores, axis=0, keepdims=True)
            m_out[c] = top
            l_out[c] = add_up(jnp.exp2(scores - top))
            lax.fori_loop(0, chunk.n_masked, masked_step, 0)
        else:
            m_out[c] = m_in[c]
            l_out[c] = l_in[c]
            lax.fori_loop(0, chunk.n_masked + chunk.n_tail, masked_step, 0)
        lax.fori_loop(0, chunk.n_plain, plain_step, 0)

        @pl.when(jnp.logical_not(jnp.max(l_out[c]) < LARGE))
        def _():
            if first:
                m_out[c] = jnp.full_like(m_out[c], HIDDEN)
                l_out[c] = jnp.zeros_like(l_out[c])
            else:
                m_out[c] = m_in[c]
                l_out[c] = l_in[c]
            lax.fori_loop(0, chunk.n_tail + chunk.n_masked + chunk.n_plain, careful_step, 0)

        return unused

    lax.fori_loop(0, NC, chunk_step, 0)


def grad_pass(group, q_s, do_s, d_s, k_s, v_s, kt_s, logsum_ref, dk_s, dv_s, dq_in, dq_out):
    def turn(b, carry):
        kt_s[b] = block_of(k_s, b).T
        return carry

    lax.fori_loop(0, len(group.entries) // 2, turn, 0)

    def chunk_step(c, unused):
        chunk = group.chunk(c)
        q = q_s[c]
        grads = do_s[c]
        logsum = logsum_ref[c]
        dots = []
        for half in range(2):
            block = d_s[2 * c + half].astype(F32)
            dots.append(block[0:1] + block[1:2])
        row_dot = jnp.concatenate(dots, axis=1)
        dq_out[c] = jnp.zeros((D, C), F32) if dq_in is None else dq_in[c]

        def grad_block(b, masked):
            weights = jnp.exp2(scores_of(chunk, b, k_s, q, masked) - logsum)
            prob_grad = lax.dot_general(
                block_of(v_s, b), grads, NT_DIMS, preferred_element_type=F32
            )
            score_grad = (weights * (prob_grad - row_dot)).astype(BF16)
            for ref, term in (
                (dv_s, jnp.dot(weights.astype(BF16), grads, preferred_element_type=F32)),
                (dk_s, jnp.dot(score_grad, q, preferred_element_type=F32)),
            ):
                ref[pl.ds(2 * b, 2)] += term.reshape(2, 2, 2, R, D)
            dq_out[c] += jnp.dot(kt_s[b], score_grad, preferred_element_type=F32)

        def masked_step(i, carry):
            grad_block(chunk.masked_at(i), True)
            return carry

        def plain_step(i, carry):
            grad_block(chunk.plain_at(i), False)
            return carry

        lax.fori_loop(0, chunk.n_masked + chunk.n_tail, masked_step, 0)
        lax.fori_loop(0, chunk.n_plain, plain_step, 0)
        return unused

    lax.fori_loop(0, NC, chunk_step, 0)


def put_sums(group, dy, xh, array, from_core, at_xh, dk_s, dv_s):
    for (entry_dy, entry_xh, xl, zh), rank in zip(group.entries, group.ranks):
        if entry_dy == dy and entry_xh == xh:
            row = (((xh * 2 if at_xh else 0) + xl) * 2 + zh) * 2
            array[row : row + 2, :R] = (dk_s[rank, :, from_core] * SCALE).astype(BF16)
            array[row : row + 2, R:] = dv_s[rank, :, from_core].astype(BF16)


def query_copies(qpay, q_s, sem, do_s=None, d_s=None):
    copies = []
    for s in range(2 * NC):
        for part, dst in ((0, q_s), (1, do_s)):
            if dst is not None:
                copies.append(
                    pltpu.make_async_copy(
                        qpay.at[s, pl.ds(part * QR, QR)],
                        dst.at[s // 2, pl.ds((s % 2) * QR, QR)],
                        sem,
                    )
                )
    if d_s is not None:
        copies.append(pltpu.make_async_copy(qpay.at[:, pl.ds(2 * QR, 16)], d_s, sem))
    return copies


def run_all(copies, between=()):
    for copy in copies:
        copy.start()
    for ref in between:
        ref[...] = jnp.zeros_like(ref)
    for copy in copies:
        copy.wait()


def stats_own_kernel(order, counts, qpay, mine, other, m_out, l_out, table, q_s, k_s, sem):
    group = Group(OWN, order, counts, table)
    pieces = {0: ([mine], [other])}
    run_all(query_copies(qpay, q_s, sem) + group.copies(pieces, (k_s,), sem))
    stats_pass(group, True, q_s, k_s, None, None, m_out, l_out)


def stats_near_kernel(
    order, counts, qpay, m_in, l_in, mine_1, other_1, mine_3, other_3, m_out, l_out, table, q_s, k_s, sem
):
    group = Group(NEAR, order, counts, table)
    pieces = {1: ([mine_1], [other_1]), 3: ([mine_3], [other_3])}
    run_all(query_copies(qpay, q_s, sem) + group.copies(pieces, (k_s,), sem))
    stats_pass(group, False, q_s, k_s, m_in, l_in, m_out, l_out)


def far_kernel(
    order, counts, qpay, m_in, l_in, mine_a, mine_b, other_a, other_b,
    logsum, dq_out, sum_a, sum_b, give,
    table, q_s, do_s, d_s, k_s, v_s, kt_s, dk_s, dv_s, m_s, l_s, sem,
):
    group = Group(FAR, order, counts, table)
    pieces = {2: ([mine_a, mine_b], [other_a, other_b])}
    copies = query_copies(qpay, q_s, sem, do_s, d_s) + group.copies(pieces, (k_s, v_s), sem)
    run_all(copies, (dk_s, dv_s))
    stats_pass(group, False, q_s, k_s, m_in, l_in, m_s, l_s)
    logsum[...] = m_s[...] + jnp.log2(jnp.sum(l_s[...], axis=1, keepdims=True))
    grad_pass(group, q_s, do_s, d_s, k_s, v_s, kt_s, logsum, dk_s, dv_s, None, dq_out)
    put_sums(group, 2, 0, sum_a, group.core, False, dk_s, dv_s)
    put_sums(group, 2, 1, sum_b, group.core, False, dk_s, dv_s)
    for xh in range(2):
        put_sums(group, 2, xh, give, 1 - group.core, True, dk_s, dv_s)


def near_kernel(
    order, counts, qpay, logsum, dq_in, mine_1, other_1, mine_3, other_3,
    dq_out, sum_1, sum_3, give_1, give_3,
    table, q_s, do_s, d_s, k_s, v_s, kt_s, dk_s, dv_s, sem,
):
    group = Group(NEAR, order, counts, table)
    pieces = {1: ([mine_1], [other_1]), 3: ([mine_3], [other_3])}
    copies = query_copies(qpay, q_s, sem, do_s, d_s) + group.copies(pieces, (k_s, v_s), sem)
    run_all(copies, (dk_s, dv_s))
    grad_pass(group, q_s, do_s, d_s, k_s, v_s, kt_s, logsum, dk_s, dv_s, dq_in, dq_out)
    for xh in range(2):
        for dy, keep, give in ((1, sum_1, give_1), (3, sum_3, give_3)):
            put_sums(group, dy, xh, keep, group.core, True, dk_s, dv_s)
            put_sums(group, dy, xh, give, 1 - group.core, True, dk_s, dv_s)


def own_kernel(
    order, counts, qpay, logsum, dq_in, mine, other,
    dq_out, keep, give,
    table, q_s, do_s, d_s, k_s, v_s, kt_s, dk_s, dv_s, dq_s, sem,
):
    group = Group(OWN, order, counts, table)
    pieces = {0: ([mine], [other])}
    copies = query_copies(qpay, q_s, sem, do_s, d_s) + group.copies(pieces, (k_s, v_s), sem)
    run_all(copies, (dk_s, dv_s))
    grad_pass(group, q_s, do_s, d_s, k_s, v_s, kt_s, logsum, dk_s, dv_s, dq_in, dq_s)
    for xh in range(2):
        put_sums(group, 0, xh, keep, group.core, True, dk_s, dv_s)
        put_sums(group, 0, xh, give, 1 - group.core, True, dk_s, dv_s)

    def finish(c, unused):
        dq = (dq_s[c] * SCALE).T.astype(BF16)
        dq_out[2 * c] = dq[:QR]
        dq_out[2 * c + 1] = dq[QR:]
        return unused

    lax.fori_loop(0, NC, finish, 0)


def far_sum_kernel(sum_a, sum_b, got, out_a, out_b):
    out_a[...] = (sum_a[...].astype(F32) + got[:8].astype(F32)).astype(BF16)
    out_b[...] = (sum_b[...].astype(F32) + got[8:].astype(F32)).astype(BF16)


def near_sum_kernel(sum_1, got_1, sum_3, got_3, from_1, from_3, out_1, out_3):
    for rows, with_from in ((slice(0, 8), 3), (slice(8, 16), 1)):
        for number, keep, got, came, out in (
            (1, sum_1, got_1, from_3, out_1),
            (3, sum_3, got_3, from_1, out_3),
        ):
            total = keep[rows].astype(F32) + got[rows].astype(F32)
            if number == with_from:
                total = total + came[...].astype(F32)
            out[rows] = total.astype(BF16)


def last_sum_kernel(keep, got, near_1, near_3, dq, out):
    total = keep[...].astype(F32) + got[...].astype(F32)
    total = total + (near_1[...].astype(F32) + near_3[...].astype(F32))
    out[:, QR:] = total.astype(BF16)
    out[:, :QR] = dq[...]


def unpack_kernel(got, query_grad, key_grad, value_grad):
    for g in range(8):
        for half in range(2):
            for h in range(G):
                rows = slice(half * HR, (half + 1) * HR)
                query_grad[rows, head_columns(g, h)] = got[spread_to(g, half), h * HR : (h + 1) * HR]
        for start, out in ((QR, key_grad), (QR + R, value_grad)):
            total = got[spread_to(g, 0), start : start + R].astype(F32)
            total = total + got[spread_to(g, 1), start : start + R].astype(F32)
            out[:, g * D : (g + 1) * D] = total.astype(BF16)


def bf16(*shape):
    return jax.ShapeDtypeStruct(shape, BF16)


def f32(*shape):
    return jax.ShapeDtypeStruct(shape, F32)


def on_vmem(kernel, outs, *args):
    return pl.pallas_call(
        kernel,
        out_shape=outs,
        compiler_params=pltpu.CompilerParams(vmem_limit_bytes=16 << 20),
    )(*args)


IN_SMEM = pl.BlockSpec(memory_space=pltpu.SMEM)
IN_VMEM = pl.BlockSpec(memory_space=pltpu.VMEM)
ANYWHERE = pl.BlockSpec(memory_space=pl.ANY)


def on_group(kernel, outs, spans, grads, extra, tables, qpay, held, pieces, products):
    query = [pltpu.VMEM((NC, C, D), BF16)]
    keys = [pltpu.VMEM((spans, 2, 2, R, D), BF16)]
    scratch = query + keys
    if grads:
        scratch = query * 2 + [pltpu.VMEM((2 * NC, 16, D), BF16)] + keys * 2
        scratch += [pltpu.VMEM((spans // 2, D, KB), BF16)]
        scratch += [pltpu.VMEM((spans, 2, 2, R, D), F32)] * 2
    work = products * NC * C * spans * SPAN * D * 2 // 3
    return pl.pallas_call(
        kernel,
        out_shape=outs,
        in_specs=[IN_SMEM] * 2 + [ANYWHERE] + [IN_VMEM] * len(held) + [ANYWHERE] * len(pieces),
        scratch_shapes=[pltpu.SMEM((spans,), jnp.int32)] + scratch + extra + [pltpu.SemaphoreType.DMA],
        compiler_params=pltpu.CompilerParams(vmem_limit_bytes=40 << 20),
        cost_estimate=pl.CostEstimate(
            flops=work, bytes_accessed=4 << 20, transcendentals=NC * C * spans * SPAN // 3
        ),
    )(*tables, qpay, *held, *pieces)


def exchange(array):
    return lax.all_to_all(array, SPREAD, split_axis=0, concat_axis=0, tiled=True)


def flip(array):
    return lax.ppermute(array, "core", [(0, 1), (1, 0)])


def swap(array, distance):
    return lax.ppermute(array, "y", [(i, i ^ distance) for i in range(4)])


def body(queries, keys, values, attn_out, out_grad, segment, span_order):
    kv_packed, counts = pl.pallas_call(
        pack_kv_kernel,
        out_shape=[bf16(16, 2 * R, D), jax.ShapeDtypeStruct((2,), jnp.int32)],
        out_specs=[IN_VMEM, IN_SMEM],
        compiler_params=pltpu.CompilerParams(vmem_limit_bytes=16 << 20),
    )(keys, values, segment.reshape(64, 128))
    own = exchange(kv_packed)
    qpay = exchange(on_vmem(pack_q_kernel, bf16(16, 2 * QR + 16, D), queries, attn_out, out_grad))
    tables = (span_order, counts)

    near_1 = swap(own, 1)
    near_3 = swap(own, 3)
    far_a = swap(near_3[:8], 1)
    far_b = swap(near_1[8:], 3)
    own_pieces = (own, flip(own))
    near_pieces = (near_1, flip(near_1), near_3, flip(near_3))
    far_pieces = (far_a, far_b, flip(far_a), flip(far_b))

    state = [f32(NC, 1, C), f32(NC, 8, C)]
    top, total = on_group(stats_own_kernel, state, 8, False, [], tables, qpay, (), own_pieces, 1)
    top, total = on_group(
        stats_near_kernel, state, 16, False, [], tables, qpay, (top, total), near_pieces, 1
    )
    logsum, dq, far_sum_a, far_sum_b, far_give = on_group(
        far_kernel,
        [f32(NC, 1, C), f32(NC, D, C), bf16(8, 2 * R, D), bf16(8, 2 * R, D), bf16(16, 2 * R, D)],
        8,
        True,
        [pltpu.VMEM((NC, 1, C), F32), pltpu.VMEM((NC, 8, C), F32)],
        tables,
        qpay,
        (top, total),
        far_pieces,
        6,
    )
    far_sums = on_vmem(far_sum_kernel, [bf16(8, 2 * R, D)] * 2, far_sum_a, far_sum_b, flip(far_give))
    from_1 = swap(far_sums[0], 1)
    from_3 = swap(far_sums[1], 3)

    dq, sum_1, sum_3, give_1, give_3 = on_group(
        near_kernel,
        [f32(NC, D, C)] + [bf16(16, 2 * R, D)] * 4,
        16,
        True,
        [],
        tables,
        qpay,
        (logsum, dq),
        near_pieces,
        5,
    )
    to_1, to_3 = on_vmem(
        near_sum_kernel,
        [bf16(16, 2 * R, D)] * 2,
        sum_1,
        flip(give_1),
        sum_3,
        flip(give_3),
        from_1,
        from_3,
    )
    at_1 = swap(to_1, 1)
    at_3 = swap(to_3, 3)

    dq, keep, give = on_group(
        own_kernel,
        [bf16(16, QR, D), bf16(16, 2 * R, D), bf16(16, 2 * R, D)],
        8,
        True,
        [pltpu.VMEM((NC, D, C), F32)],
        tables,
        qpay,
        (logsum, dq),
        own_pieces,
        5,
    )
    sums = on_vmem(last_sum_kernel, bf16(16, QR + 2 * R, D), keep, flip(give), at_1, at_3, dq)
    return tuple(
        on_vmem(unpack_kernel, [bf16(R, 8 * G * D), bf16(R, 8 * D), bf16(R, 8 * D)], exchange(sums))
    )


def solution(mesh):
    fine = Mesh(mesh.devices.reshape(4, 2, 2, 2, 4), AXES)
    rows = P(AXES, None)
    return jax.shard_map(
        body,
        mesh=fine,
        in_specs=(rows,) * 5 + (P(), P()),
        out_specs=(rows,) * 3,
        check_vma=False,
    )
```

```python
import functools
import math

import jax
import jax.numpy as jnp
from jax import lax
from jax.experimental import pallas as pl
from jax.experimental.pallas import tpu as pltpu
from jax.sharding import Mesh, PartitionSpec as P

D = 128
G = 4
R = 64
SPAN = 256
KB = 2 * SPAN
NT = 32
HR = R // 2
QR = G * HR
C = 2 * QR
SCALE = D**-0.5
LOG2E = math.log2(math.e)
EXP_SCALE = SCALE * LOG2E
HIDDEN = -1e30
F32 = jnp.float32
BF16 = jnp.bfloat16
AXES = ("z", "core", "xh", "xl", "y")
HEADS = ("xh", "z")
SPREAD = ("xh", "xl", "z")
NT_DIMS = (((1,), (1,)), ((), ()))


def pack_kv_kernel(keys, values, segment, out, counts):
    counts[0] = jnp.sum((segment[...] == 0).astype(jnp.int32))
    counts[1] = jnp.sum((segment[...] != 2).astype(jnp.int32))
    for g in range(8):
        out[g, :R] = keys[:, g * D : (g + 1) * D]
        out[g, R:] = values[:, g * D : (g + 1) * D]


def pack_q_kernel(queries, saved, grads, out):
    ones = jnp.ones((8, D), BF16)
    row = lax.broadcasted_iota(jnp.int32, (16, D), 0)
    for g in range(8):
        for half in range(2):
            dest = (g // 4 * 2 + half) * 4 + g % 4
            rows = slice(half * HR, (half + 1) * HR)
            prods = []
            for h in range(G):
                cols = slice((g * G + h) * D, (g * G + h + 1) * D)
                grad = grads[rows, cols]
                out[dest, h * HR : (h + 1) * HR] = queries[rows, cols]
                out[dest, QR + h * HR : QR + (h + 1) * HR] = grad
                prods.append(grad.astype(F32) * saved[rows, cols].astype(F32))
            prod = jnp.concatenate(prods, axis=0)
            high = prod.astype(BF16)
            low = (prod - high.astype(F32)).astype(BF16)
            dot = lax.dot_general(ones, high, NT_DIMS, preferred_element_type=F32)
            dot = dot + lax.dot_general(ones, low, NT_DIMS, preferred_element_type=F32)
            both = jnp.concatenate([dot, dot], axis=0)
            rounded = both.astype(BF16).astype(F32)
            out[dest, 2 * QR :] = jnp.where(row == 0, rounded, both - rounded).astype(BF16)


def span_id(xh, xl, y, zh):
    return ((xh * 2 + xl) * 4 + y) * 2 + zh


def attention_kernel(order, counts, qpay, *refs):
    pieces = refs[:10]
    dq_out, outs = refs[10], (refs[11:15], refs[15:19])
    (q_s, do_s, d_s, k_s, v_s, kt_s, qa_s, ga_s, stash, m_blk, m_run, l_run, dk_s, dv_s, dq_s, sem) = (
        refs[19:]
    )
    n0 = counts[0]
    n1 = counts[1]
    xl = lax.axis_index("xl")
    y = lax.axis_index("y")
    core = lax.axis_index("core")

    def place(flip, dy, j):
        return order[span_id(j // 2, xl ^ flip, y ^ dy, j % 2)]

    copies = []
    for s in range(16):
        for part, dst in ((0, q_s), (1, do_s)):
            copies.append(
                pltpu.make_async_copy(
                    qpay.at[s, pl.ds(part * QR, QR)], dst.at[s // 2, pl.ds((s % 2) * QR, QR)], sem
                )
            )
    copies.append(pltpu.make_async_copy(qpay.at[:, pl.ds(2 * QR, 16)], d_s, sem))
    for number, piece in enumerate(pieces):
        which = number % 5
        from_core = core if number < 5 else 1 - core
        dy = (0, 1, 3, 2, 2)[which]
        flips = ((0, 1), (0, 1), (0, 1), (0,), (1,))[which]
        for at, flip in enumerate(flips):
            source = piece.at[at] if len(flips) > 1 else piece
            for j in range(4):
                rank = place(flip, dy, j)
                rows = source.at[pl.ds(2 * j, 2)]
                copies.append(
                    pltpu.make_async_copy(rows.at[:, pl.ds(0, R)], k_s.at[rank, :, from_core, :, pl.ds(0, D)], sem)
                )
                copies.append(
                    pltpu.make_async_copy(rows.at[:, pl.ds(R, R)], v_s.at[rank, :, from_core, :, pl.ds(0, D)], sem)
                )
    for copy in copies:
        copy.start()
    dk_s[...] = jnp.zeros_like(dk_s)
    dv_s[...] = jnp.zeros_like(dv_s)
    beside = lax.broadcasted_iota(jnp.int32, (1, 1, 1, 1, D), 4) < 2
    beside = jnp.broadcast_to(beside.astype(F32), (1, 2, 2, R, D)).astype(BF16)

    def put_beside(i, carry):
        k_s[pl.ds(i, 1), :, :, :, D:] = beside
        v_s[pl.ds(i, 1), :, :, :, D:] = beside
        return carry

    lax.fori_loop(0, NT, put_beside, 0)
    for copy in copies:
        copy.wait()

    def block_of(ref, b):
        return ref[pl.ds(2 * b, 2)].reshape(KB, 2 * D)

    def keys_of(b):
        return k_s[pl.ds(2 * b, 2), :, :, :, :D].reshape(KB, D)

    def turn(b, carry):
        kt_s[b] = keys_of(b).T
        return carry

    lax.fori_loop(0, NT // 2, turn, 0)

    def chunk_step(c, unused):
        span_q = order[span_id(c // 4, c // 2 % 2, y, c % 2)]
        first = span_q * SPAN
        has_second = first + (SPAN - 1) >= n1
        all_second = first >= n1
        n_full = span_q // 2
        lo = jnp.where(has_second, n0 // KB, 0)
        hi = jnp.where(has_second, (n1 + (KB - 1)) // KB, 0)
        hi = jnp.minimum(hi, n_full)
        lo = jnp.minimum(lo, hi)
        skip_at = (n0 + (KB - 1)) // KB
        skip = jnp.where(all_second, jnp.maximum(jnp.minimum(n1 // KB, hi) - skip_at, 0), 0)
        n_masked = hi - lo - skip
        n_plain = n_full - (hi - lo)
        count = n_plain + n_masked + 1

        def masked_at(i):
            at = lo + i
            return jnp.where(at >= skip_at, at + skip, at)

        def plain_at(i):
            return jnp.where(i < lo, i, i + (hi - lo))

        def place_at(i):
            at = jnp.where(i < n_plain, plain_at(i), masked_at(i - n_plain))
            return jnp.where(i == count - 1, n_full, at)

        q = q_s[c]
        grads = do_s[c]

        def put_under(ref, *rows):
            number = lax.broadcasted_iota(jnp.int32, (D, C), 0)
            block = jnp.zeros((D, C), F32)
            for i, values in enumerate(rows):
                block = jnp.where(number == i, values, block)
            ref[D:] = block.astype(BF16)

        def raw_scores(b):
            return jnp.dot(keys_of(b), qa_s[:D], preferred_element_type=F32)

        qa_s[:D] = q.T
        ga_s[:D] = grads.T
        halves = [d_s[2 * c + half].astype(F32) for half in range(2)]
        put_under(
            ga_s,
            -jnp.concatenate([half[0:1] for half in halves], axis=1),
            -jnp.concatenate([half[1:2] for half in halves], axis=1),
        )

        def seen_at(b):
            lane = lax.broadcasted_iota(jnp.int32, (1, C), 1)
            query_pos = first + core * R + xl * HR + (lane // QR) * (2 * R) + lane % HR
            key_pos = b * KB + lax.broadcasted_iota(jnp.int32, (KB, 1), 0)
            low = jnp.where(query_pos >= n1, n0, n1)
            return (key_pos <= query_pos) & ((key_pos < low) | (key_pos >= n1))

        def add_up(weights):
            return jnp.sum(weights.reshape(KB // 8, 8, C), axis=0)

        def weigh(b, masked):
            scores = jnp.dot(block_of(k_s, b), qa_s[...], preferred_element_type=F32)
            if masked:
                scores = jnp.where(seen_at(b), scores, HIDDEN)
            weights = jnp.exp2(scores * EXP_SCALE)
            l_run[...] += add_up(weights)
            m_blk[b] = m_run[...]
            stash[b] = weights

        def weigh_diagonal():
            scores = jnp.where(seen_at(n_full), raw_scores(n_full), HIDDEN)
            top = jnp.max(scores, axis=0, keepdims=True).astype(BF16).astype(F32)
            put_under(qa_s, -top)
            weights = jnp.exp2((scores - top) * EXP_SCALE)
            l_run[...] = add_up(weights)
            m_run[...] = top * EXP_SCALE
            m_blk[n_full] = top * EXP_SCALE
            stash[n_full] = weights

        def masked_step(i, carry):
            weigh(masked_at(i), True)
            return carry

        def plain_pair(i, carry):
            weigh(plain_at(2 * i), False)
            weigh(plain_at(2 * i + 1), False)
            return carry

        weigh_diagonal()
        lax.fori_loop(0, n_masked, masked_step, 0)
        lax.fori_loop(0, n_plain // 2, plain_pair, 0)

        @pl.when(n_plain % 2 == 1)
        def _():
            weigh(plain_at(n_plain - 1), False)

        @pl.when(jnp.logical_not(jnp.max(l_run[...]) < 2.0**90))
        def _():
            m_run[...] = jnp.full_like(m_run, HIDDEN)
            l_run[...] = jnp.zeros_like(l_run)

            def careful_step(i, carry):
                b = place_at(count - 1 - i)
                scores = jnp.where(seen_at(b), raw_scores(b) * EXP_SCALE, HIDDEN)
                old = m_run[...]
                top = jnp.maximum(old, jnp.max(scores, axis=0, keepdims=True))
                weights = jnp.exp2(scores - top)
                l_run[...] = l_run[...] * jnp.exp2(old - top) + add_up(weights)
                m_run[...] = top
                m_blk[b] = top
                stash[b] = weights
                return carry

            lax.fori_loop(0, count, careful_step, 0)

        logsum = m_run[...] + jnp.log2(jnp.sum(l_run[...], axis=0, keepdims=True))
        dq_s[...] = jnp.zeros_like(dq_s)

        def grad_block(b):
            weights = stash[b] * jnp.exp2(m_blk[b] - logsum)
            above = jnp.dot(block_of(v_s, b), ga_s[...], preferred_element_type=F32)
            score_grad = (weights * above).astype(BF16)
            for ref, term in (
                (dv_s, jnp.dot(weights.astype(BF16), grads, preferred_element_type=F32)),
                (dk_s, jnp.dot(score_grad, q, preferred_element_type=F32)),
            ):
                ref[pl.ds(2 * b, 2)] += term.reshape(2, 2, 2, R, D)
            return jnp.dot(kt_s[b], score_grad, preferred_element_type=F32)

        def grad_pair(i, carry):
            first_term = grad_block(place_at(2 * i))
            second_term = grad_block(place_at(2 * i + 1))
            dq_s[...] += first_term + second_term
            return carry

        lax.fori_loop(0, count // 2, grad_pair, 0)

        @pl.when(count % 2 == 1)
        def _():
            dq_s[...] += grad_block(n_full)

        dq = (dq_s[...] * SCALE).T.astype(BF16)
        dq_out[2 * c] = dq[:QR]
        dq_out[2 * c + 1] = dq[QR:]
        return unused

    lax.fori_loop(0, 8, chunk_step, 0)

    for from_core, group in ((core, outs[0]), (1 - core, outs[1])):
        for dy, out in zip((0, 1, 3, 2), group):
            for flip in range(2):
                for j in range(4):
                    rank = place(flip, dy, j)
                    rows = slice(2 * j, 2 * j + 2)
                    out[flip, rows, :R] = (dk_s[rank, :, from_core] * SCALE).astype(BF16)
                    out[flip, rows, R:] = dv_s[rank, :, from_core].astype(BF16)


def last_sum_kernel(mine, got, near_1, near_3, dq, sums, out):
    for flip in range(2):
        for xh in range(2):
            rows = slice(xh * 4, xh * 4 + 4)
            parts = [ref[flip, rows].astype(F32) for ref in (mine, got, near_1, near_3)]
            total = (parts[0] + parts[1]) + (parts[2] + parts[3])
            sums[xh, lax.axis_index("xl") ^ flip] = total.astype(BF16)
    for g in range(8):
        for half in range(2):
            dest = (g // 4 * 2 + half) * 4 + g % 4
            for h in range(G):
                cols = slice((g * G + h) * D, (g * G + h + 1) * D)
                out[half * HR : (half + 1) * HR, cols] = dq[dest, h * HR : (h + 1) * HR]


def unpack_kv_kernel(got, key_grad, value_grad):
    for g in range(8):
        pair = [(g // 4 * 2 + xl) * 4 + g % 4 for xl in range(2)]
        for start, out in ((0, key_grad), (R, value_grad)):
            rows = slice(start, start + R)
            total = got[pair[0], rows].astype(F32) + got[pair[1], rows].astype(F32)
            out[:, g * D : (g + 1) * D] = total.astype(BF16)


def on_vmem(kernel, outs, *args):
    return pl.pallas_call(
        kernel,
        out_shape=outs,
        compiler_params=pltpu.CompilerParams(vmem_limit_bytes=16 << 20),
    )(*args)


def exchange(array, axes):
    return lax.all_to_all(array, axes, split_axis=0, concat_axis=0, tiled=True)


def flip(array, axis):
    return lax.ppermute(array, axis, [(0, 1), (1, 0)])


def swap(array, distance):
    return lax.ppermute(array, "y", [(i, i ^ distance) for i in range(4)])


def gather_kv(own):
    both = jnp.stack([own, flip(own, "xl")])
    near_1 = swap(both, 1)
    near_3 = swap(both, 3)
    far_same = swap(near_3[0], 1)
    far_flip = swap(near_1[1], 3)
    mine = (both, near_1, near_3, far_same, far_flip)
    return mine + tuple(flip(array, "core") for array in mine)


def add(*terms):
    total = terms[0].astype(F32)
    for term in terms[1:]:
        total = total + term.astype(F32)
    return total


def reduce_kv(mine, other, dq):
    got_0, got_1, got_3, got_2 = [flip(array, "core") for array in other]
    mine_0, mine_1, mine_3, mine_2 = mine
    far = add(mine_2, got_2).astype(BF16)
    from_1 = swap(far[0], 1)
    from_3 = swap(far[1], 3)
    to_3 = jnp.stack([add(mine_3[0], got_3[0], from_1), add(mine_3[1], got_3[1])])
    to_1 = jnp.stack([add(mine_1[0], got_1[0]), add(mine_1[1], got_1[1], from_3)])
    near_3 = swap(to_3.astype(BF16), 3)
    near_1 = swap(to_1.astype(BF16), 1)
    pair = (2, 2, 4, 2 * R, D)
    sums, query_grad = on_vmem(
        last_sum_kernel,
        [jax.ShapeDtypeStruct(pair, BF16), jax.ShapeDtypeStruct((R, 8 * G * D), BF16)],
        mine_0,
        got_0,
        near_1,
        near_3,
        dq,
    )
    return sums.reshape(16, 2 * R, D), query_grad


def body(queries, keys, values, attn_out, out_grad, segment, span_order):
    kv_packed, counts = pl.pallas_call(
        pack_kv_kernel,
        out_shape=[jax.ShapeDtypeStruct((8, 2 * R, D), BF16), jax.ShapeDtypeStruct((2,), jnp.int32)],
        out_specs=[pl.BlockSpec(memory_space=pltpu.VMEM), pl.BlockSpec(memory_space=pltpu.SMEM)],
        compiler_params=pltpu.CompilerParams(vmem_limit_bytes=16 << 20),
    )(keys, values, segment.reshape(64, 128))
    kv_own = exchange(kv_packed, HEADS)
    q_own = exchange(
        on_vmem(
            pack_q_kernel,
            jax.ShapeDtypeStruct((16, 2 * QR + 16, D), BF16),
            queries,
            attn_out,
            out_grad,
        ),
        SPREAD,
    )
    pieces = gather_kv(kv_own)
    group = jax.ShapeDtypeStruct((2, 8, 2 * R, D), BF16)
    outs = pl.pallas_call(
        attention_kernel,
        out_shape=[jax.ShapeDtypeStruct((16, QR, D), BF16)] + [group] * 8,
        in_specs=[pl.BlockSpec(memory_space=pltpu.SMEM)] * 2
        + [pl.BlockSpec(memory_space=pl.ANY)] * 11,
        scratch_shapes=[
            pltpu.VMEM((8, C, D), BF16),
            pltpu.VMEM((8, C, D), BF16),
            pltpu.VMEM((16, 16, D), BF16),
            pltpu.VMEM((NT, 2, 2, R, 2 * D), BF16),
            pltpu.VMEM((NT, 2, 2, R, 2 * D), BF16),
            pltpu.VMEM((NT // 2, D, KB), BF16),
            pltpu.VMEM((2 * D, C), BF16),
            pltpu.VMEM((2 * D, C), BF16),
            pltpu.VMEM((NT // 2, KB, C), F32),
            pltpu.VMEM((NT // 2, 1, C), F32),
            pltpu.VMEM((1, C), F32),
            pltpu.VMEM((8, C), F32),
            pltpu.VMEM((NT, 2, 2, R, D), F32),
            pltpu.VMEM((NT, 2, 2, R, D), F32),
            pltpu.VMEM((D, C), F32),
            pltpu.SemaphoreType.DMA,
        ],
        compiler_params=pltpu.CompilerParams(vmem_limit_bytes=48 << 20),
    )(span_order, counts, q_own, *pieces)
    dkv, query_grad = reduce_kv(outs[1:5], outs[5:9], exchange(outs[0], SPREAD))
    key_grad, value_grad = on_vmem(
        unpack_kv_kernel, [jax.ShapeDtypeStruct((R, 8 * D), BF16)] * 2, exchange(dkv, SPREAD)
    )
    return query_grad, key_grad, value_grad


def solution(mesh):
    fine = Mesh(mesh.devices.reshape(4, 2, 2, 2, 4), AXES)
    rows = P(AXES, None)
    return jax.shard_map(
        body,
        mesh=fine,
        in_specs=(rows,) * 5 + (P(), P()),
        out_specs=(rows,) * 3,
        check_vma=False,
    )
```

```python
import functools
import math

import jax
import jax.numpy as jnp
from jax import lax
from jax.experimental import pallas as pl
from jax.experimental.pallas import tpu as pltpu
from jax.sharding import Mesh, PartitionSpec as P

D = 128
G = 4
R = 64
SPAN = 256
KB = 2 * SPAN
NT = 32
HR = R // 2
QR = G * HR
C = 2 * QR
NC = 8
W = 4
SCALE = D**-0.5
LOG2E = math.log2(math.e)
EXP_SCALE = SCALE * LOG2E
HIDDEN = -1e30
LARGE = 2.0**90
F32 = jnp.float32
BF16 = jnp.bfloat16
AXES = ("z", "core", "xh", "xl", "y")
HEADS = ("xh", "z")
SPREAD = ("xh", "xl", "z")
NT_DIMS = (((1,), (1,)), ((), ()))


def pack_kv_kernel(keys, values, segment, out, counts):
    counts[0] = jnp.sum((segment[...] == 0).astype(jnp.int32))
    counts[1] = jnp.sum((segment[...] != 2).astype(jnp.int32))
    for g in range(8):
        out[g, :R] = keys[:, g * D : (g + 1) * D]
        out[g, R:] = values[:, g * D : (g + 1) * D]


def pack_q_kernel(queries, saved, grads, out):
    ones = jnp.ones((8, D), BF16)
    row = lax.broadcasted_iota(jnp.int32, (16, D), 0)
    for g in range(8):
        for half in range(2):
            dest = (g // 4 * 2 + half) * 4 + g % 4
            rows = slice(half * HR, (half + 1) * HR)
            prods = []
            for h in range(G):
                cols = slice((g * G + h) * D, (g * G + h + 1) * D)
                grad = grads[rows, cols]
                out[dest, h * HR : (h + 1) * HR] = queries[rows, cols]
                out[dest, QR + h * HR : QR + (h + 1) * HR] = grad
                prods.append(grad.astype(F32) * saved[rows, cols].astype(F32))
            prod = jnp.concatenate(prods, axis=0)
            high = prod.astype(BF16)
            low = (prod - high.astype(F32)).astype(BF16)
            dot = lax.dot_general(ones, high, NT_DIMS, preferred_element_type=F32)
            dot = dot + lax.dot_general(ones, low, NT_DIMS, preferred_element_type=F32)
            both = jnp.concatenate([dot, dot], axis=0)
            rounded = both.astype(BF16).astype(F32)
            out[dest, 2 * QR :] = jnp.where(row == 0, rounded, both - rounded).astype(BF16)


def span_id(xh, xl, y, zh):
    return ((xh * 2 + xl) * 4 + y) * 2 + zh


def attention_kernel(order, counts, qpay, *refs):
    pieces = refs[:10]
    dq_out, outs = refs[10], (refs[11:15], refs[15:19])
    (plain_c, plain_b, masked_c, masked_b, q_s, do_s, d_s, k_s, v_s, kt_s, qa_s, ga_s) = refs[19:31]
    m_s, l_s, dk_s, dv_s, dq_s, sem, value_sem = refs[31:]
    n0 = counts[0]
    n1 = counts[1]
    xl = lax.axis_index("xl")
    y = lax.axis_index("y")
    core = lax.axis_index("core")

    def place(flip, dy, j):
        return order[span_id(j // 2, xl ^ flip, y ^ dy, j % 2)]

    copies = []
    value_copies = []
    for s in range(16):
        for part, dst in ((0, q_s), (1, do_s)):
            copies.append(
                pltpu.make_async_copy(
                    qpay.at[s, pl.ds(part * QR, QR)], dst.at[s // 2, pl.ds((s % 2) * QR, QR)], sem
                )
            )
    copies.append(pltpu.make_async_copy(qpay.at[:, pl.ds(2 * QR, 16)], d_s, sem))
    for number, piece in enumerate(pieces):
        which = number % 5
        from_core = core if number < 5 else 1 - core
        dy = (0, 1, 3, 2, 2)[which]
        flips = ((0, 1), (0, 1), (0, 1), (0,), (1,))[which]
        for at, flip in enumerate(flips):
            source = piece.at[at] if len(flips) > 1 else piece
            for j in range(4):
                rank = place(flip, dy, j)
                rows = source.at[pl.ds(2 * j, 2)]
                copies.append(
                    pltpu.make_async_copy(
                        rows.at[:, pl.ds(0, R)], k_s.at[rank, :, from_core, :, pl.ds(0, D)], sem
                    )
                )
                value_copies.append(
                    pltpu.make_async_copy(
                        rows.at[:, pl.ds(R, R)],
                        v_s.at[rank, :, from_core, :, pl.ds(0, D)],
                        value_sem,
                    )
                )
    for copy in copies + value_copies:
        copy.start()

    beside = lax.broadcasted_iota(jnp.int32, (1, 1, 1, 1, D), 4) < 3
    beside = jnp.broadcast_to(beside.astype(F32), (1, 2, 2, R, D)).astype(BF16)

    def put_beside(i, carry):
        k_s[pl.ds(i, 1), :, :, :, D:] = beside
        v_s[pl.ds(i, 1), :, :, :, D:] = beside
        return carry

    lax.fori_loop(0, NT, put_beside, 0)
    dk_s[...] = jnp.zeros_like(dk_s)
    dv_s[...] = jnp.zeros_like(dv_s)
    dq_s[...] = jnp.zeros_like(dq_s)

    def span_of(c):
        return order[span_id(c // 4, c // 2 % 2, y, c % 2)]

    def list_chunk(c, sizes):
        n_plain, n_masked = sizes
        span_q = span_of(c)
        first = span_q * SPAN
        has_second = first + (SPAN - 1) >= n1
        all_second = first >= n1
        n_full = span_q // 2
        hi = jnp.minimum(jnp.where(has_second, (n1 + (KB - 1)) // KB, 0), n_full)
        lo = jnp.minimum(jnp.where(has_second, n0 // KB, 0), hi)
        skip_at = jnp.where(all_second, (n0 + (KB - 1)) // KB, hi)
        skip_to = jnp.where(all_second, n1 // KB, 0)
        masked_c[c] = c
        masked_b[c] = n_full

        def put_plain(b, n):
            plain_c[n] = c
            plain_b[n] = b
            return n + 1

        def put_masked(b, n):
            hidden = (b >= skip_at) & (b < skip_to)
            masked_c[n] = c
            masked_b[n] = b
            return jnp.where(hidden, n, n + 1)

        n_plain = lax.fori_loop(0, lo, put_plain, n_plain)
        n_plain = lax.fori_loop(hi, n_full, put_plain, n_plain)
        return n_plain, lax.fori_loop(lo, hi, put_masked, n_masked)

    n_plain, n_masked = lax.fori_loop(0, NC, list_chunk, (jnp.int32(0), jnp.int32(NC)))
    for i in range(W - 1):
        plain_c[n_plain + i] = NC
        plain_b[n_plain + i] = 0
        masked_c[n_masked + i] = NC
        masked_b[n_masked + i] = 0

    for copy in copies:
        copy.wait()

    def block_of(ref, b):
        return ref[pl.ds(2 * b, 2)].reshape(KB, 2 * D)

    def keys_of(b):
        return k_s[pl.ds(2 * b, 2), :, :, :, :D].reshape(KB, D)

    def turn_keys(b, carry):
        kt_s[b] = keys_of(b).T
        return carry

    lax.fori_loop(0, NT // 2, turn_keys, 0)

    def put_under(ref, c, *rows):
        number = lax.broadcasted_iota(jnp.int32, (D, C), 0)
        block = jnp.zeros((D, C), F32)
        for i, values in enumerate(rows):
            block = jnp.where(number == i, values, block)
        ref[c, D:] = block.astype(BF16)

    def turn_rows(c, carry):
        qa_s[c, :D] = q_s[c].T
        ga_s[c, :D] = do_s[c].T
        halves = [d_s[2 * c + half].astype(F32) for half in range(2)]
        put_under(
            ga_s,
            c,
            -jnp.concatenate([half[0:1] for half in halves], axis=1),
            -jnp.concatenate([half[1:2] for half in halves], axis=1),
        )
        return carry

    lax.fori_loop(0, NC, turn_rows, 0)
    qa_s[NC, :D] = jnp.zeros((D, C), BF16)
    put_under(qa_s, NC, jnp.full((1, C), HIDDEN, F32))
    ga_s[NC] = jnp.zeros((2 * D, C), BF16)
    q_s[NC] = jnp.zeros((C, D), BF16)
    do_s[NC] = jnp.zeros((C, D), BF16)
    l_s[NC] = jnp.zeros((8, C), F32)

    def seen(c, b):
        lane = lax.broadcasted_iota(jnp.int32, (1, C), 1)
        row = span_of(jnp.minimum(c, NC - 1)) * SPAN + core * R + xl * HR
        query_pos = row + (lane // QR) * (2 * R) + lane % HR
        key_pos = b * KB + lax.broadcasted_iota(jnp.int32, (KB, 1), 0)
        low = jnp.where(query_pos >= n1, n0, n1)
        return (key_pos <= query_pos) & ((key_pos < low) | (key_pos >= n1))

    def add_up(weights):
        return jnp.sum(weights.reshape(KB // 8, 8, C), axis=0)

    def raw_scores(c, b):
        return jnp.dot(keys_of(b), qa_s[c, :D], preferred_element_type=F32)

    def weights_of(c, b, masked):
        scores = jnp.dot(block_of(k_s, b), qa_s[c], preferred_element_type=F32)
        if masked:
            scores = jnp.where(seen(c, b), scores, HIDDEN)
        return jnp.exp2(scores * EXP_SCALE)

    def diagonal_step(i, carry):
        for c in [2 * i + k for k in range(2)]:
            b = masked_b[c]
            scores = jnp.where(seen(c, b), raw_scores(c, b), HIDDEN)
            top = jnp.max(scores, axis=0, keepdims=True).astype(BF16).astype(F32)
            put_under(qa_s, c, -top)
            m_s[c] = top * EXP_SCALE
            l_s[c] = add_up(jnp.exp2((scores - top) * EXP_SCALE))
        return carry

    lax.fori_loop(0, NC // 2, diagonal_step, 0)

    def add_weights(items, masked):
        parts = [add_up(weights_of(c, b, masked)) for c, b in items]
        for (c, b), part in zip(items, parts):
            l_s[c] += part

    def masked_stats(i, carry):
        at = [NC + 2 * i + k for k in range(2)]
        add_weights([(masked_c[n], masked_b[n]) for n in at], True)
        return carry

    def plain_stats(i, carry):
        at = [W * i + k for k in range(W)]
        add_weights([(plain_c[n], plain_b[n]) for n in at], False)
        return carry

    lax.fori_loop(0, (n_masked - NC + 1) // 2, masked_stats, 0)
    lax.fori_loop(0, (n_plain + W - 1) // W, plain_stats, 0)

    @pl.when(jnp.logical_not(jnp.max(l_s[...]) < LARGE))
    def _():
        def careful(c, b):
            scores = jnp.where(seen(c, b), raw_scores(c, b) * EXP_SCALE, HIDDEN)
            old = m_s[c]
            top = jnp.maximum(old, jnp.max(scores, axis=0, keepdims=True))
            l_s[c] = l_s[c] * jnp.exp2(old - top) + add_up(jnp.exp2(scores - top))
            m_s[c] = top

        def careful_masked(n, carry):
            c = masked_c[n]

            @pl.when(n < NC)
            def _():
                m_s[c] = jnp.full((1, C), HIDDEN, F32)
                l_s[c] = jnp.zeros((8, C), F32)

            careful(c, masked_b[n])
            return carry

        def careful_plain(n, carry):
            careful(plain_c[n], plain_b[n])
            return carry

        lax.fori_loop(0, n_masked, careful_masked, 0)
        lax.fori_loop(0, n_plain, careful_plain, 0)

    def put_logsum(c, carry):
        logsum = m_s[c] + jnp.log2(jnp.sum(l_s[c], axis=0, keepdims=True))
        rest = logsum * (1.0 / EXP_SCALE)
        rows = []
        for _ in range(3):
            part = rest.astype(BF16).astype(F32)
            rows.append(-part)
            rest = rest - part
        put_under(qa_s, c, *rows)
        return carry

    lax.fori_loop(0, NC, put_logsum, 0)
    for copy in value_copies:
        copy.wait()

    def grad_step(items, masked):
        weights = [weights_of(c, b, masked) for c, b in items]
        above = [
            jnp.dot(block_of(v_s, b), ga_s[c], preferred_element_type=F32) for c, b in items
        ]
        score_grads = [(w * p).astype(BF16) for w, p in zip(weights, above)]
        for (c, b), w, score_grad in zip(items, weights, score_grads):
            for ref, term in (
                (dv_s, jnp.dot(w.astype(BF16), do_s[c], preferred_element_type=F32)),
                (dk_s, jnp.dot(score_grad, q_s[c], preferred_element_type=F32)),
            ):
                ref[pl.ds(2 * b, 2)] += term.reshape(2, 2, 2, R, D)
            dq_s[c] += jnp.dot(kt_s[b], score_grad, preferred_element_type=F32)

    def masked_grads(i, carry):
        at = [2 * i + k for k in range(2)]
        grad_step([(masked_c[n], masked_b[n]) for n in at], True)
        return carry

    def plain_grads(i, carry):
        at = [W * i + k for k in range(W)]
        grad_step([(plain_c[n], plain_b[n]) for n in at], False)
        return carry

    lax.fori_loop(0, (n_masked + 1) // 2, masked_grads, 0)
    lax.fori_loop(0, (n_plain + W - 1) // W, plain_grads, 0)

    def finish(c, carry):
        dq = (dq_s[c] * SCALE).T.astype(BF16)
        dq_out[2 * c] = dq[:QR]
        dq_out[2 * c + 1] = dq[QR:]
        return carry

    lax.fori_loop(0, NC, finish, 0)

    for from_core, group in ((core, outs[0]), (1 - core, outs[1])):
        for dy, out in zip((0, 1, 3, 2), group):
            for flip in range(2):
                for j in range(4):
                    rank = place(flip, dy, j)
                    rows = slice(2 * j, 2 * j + 2)
                    out[flip, rows, :R] = (dk_s[rank, :, from_core] * SCALE).astype(BF16)
                    out[flip, rows, R:] = dv_s[rank, :, from_core].astype(BF16)


def last_sum_kernel(mine, got, near_1, near_3, dq, sums, out):
    for flip in range(2):
        for xh in range(2):
            rows = slice(xh * 4, xh * 4 + 4)
            parts = [ref[flip, rows].astype(F32) for ref in (mine, got, near_1, near_3)]
            total = (parts[0] + parts[1]) + (parts[2] + parts[3])
            sums[xh, lax.axis_index("xl") ^ flip] = total.astype(BF16)
    for g in range(8):
        for half in range(2):
            dest = (g // 4 * 2 + half) * 4 + g % 4
            for h in range(G):
                cols = slice((g * G + h) * D, (g * G + h + 1) * D)
                out[half * HR : (half + 1) * HR, cols] = dq[dest, h * HR : (h + 1) * HR]


def unpack_kv_kernel(got, key_grad, value_grad):
    for g in range(8):
        pair = [(g // 4 * 2 + xl) * 4 + g % 4 for xl in range(2)]
        for start, out in ((0, key_grad), (R, value_grad)):
            rows = slice(start, start + R)
            total = got[pair[0], rows].astype(F32) + got[pair[1], rows].astype(F32)
            out[:, g * D : (g + 1) * D] = total.astype(BF16)


def on_vmem(kernel, outs, *args):
    return pl.pallas_call(
        kernel,
        out_shape=outs,
        compiler_params=pltpu.CompilerParams(vmem_limit_bytes=16 << 20),
    )(*args)


def exchange(array, axes):
    return lax.all_to_all(array, axes, split_axis=0, concat_axis=0, tiled=True)


def flip(array, axis):
    return lax.ppermute(array, axis, [(0, 1), (1, 0)])


def swap(array, distance):
    return lax.ppermute(array, "y", [(i, i ^ distance) for i in range(4)])


def gather_kv(own):
    both = jnp.stack([own, flip(own, "xl")])
    near_1 = swap(both, 1)
    near_3 = swap(both, 3)
    far_same = swap(near_3[0], 1)
    far_flip = swap(near_1[1], 3)
    mine = (both, near_1, near_3, far_same, far_flip)
    return mine + tuple(flip(array, "core") for array in mine)


def add(*terms):
    total = terms[0].astype(F32)
    for term in terms[1:]:
        total = total + term.astype(F32)
    return total


def reduce_kv(mine, other, dq):
    got_0, got_1, got_3, got_2 = [flip(array, "core") for array in other]
    mine_0, mine_1, mine_3, mine_2 = mine
    far = add(mine_2, got_2).astype(BF16)
    from_1 = swap(far[0], 1)
    from_3 = swap(far[1], 3)
    to_3 = jnp.stack([add(mine_3[0], got_3[0], from_1), add(mine_3[1], got_3[1])])
    to_1 = jnp.stack([add(mine_1[0], got_1[0]), add(mine_1[1], got_1[1], from_3)])
    near_3 = swap(to_3.astype(BF16), 3)
    near_1 = swap(to_1.astype(BF16), 1)
    pair = (2, 2, 4, 2 * R, D)
    sums, query_grad = on_vmem(
        last_sum_kernel,
        [jax.ShapeDtypeStruct(pair, BF16), jax.ShapeDtypeStruct((R, 8 * G * D), BF16)],
        mine_0,
        got_0,
        near_1,
        near_3,
        dq,
    )
    return sums.reshape(16, 2 * R, D), query_grad


def body(queries, keys, values, attn_out, out_grad, segment, span_order):
    kv_packed, counts = pl.pallas_call(
        pack_kv_kernel,
        out_shape=[jax.ShapeDtypeStruct((8, 2 * R, D), BF16), jax.ShapeDtypeStruct((2,), jnp.int32)],
        out_specs=[pl.BlockSpec(memory_space=pltpu.VMEM), pl.BlockSpec(memory_space=pltpu.SMEM)],
        compiler_params=pltpu.CompilerParams(vmem_limit_bytes=16 << 20),
    )(keys, values, segment.reshape(64, 128))
    kv_own = exchange(kv_packed, HEADS)
    q_own = exchange(
        on_vmem(
            pack_q_kernel,
            jax.ShapeDtypeStruct((16, 2 * QR + 16, D), BF16),
            queries,
            attn_out,
            out_grad,
        ),
        SPREAD,
    )
    pieces = gather_kv(kv_own)
    group = jax.ShapeDtypeStruct((2, 8, 2 * R, D), BF16)
    outs = pl.pallas_call(
        attention_kernel,
        out_shape=[jax.ShapeDtypeStruct((16, QR, D), BF16)] + [group] * 8,
        in_specs=[pl.BlockSpec(memory_space=pltpu.SMEM)] * 2
        + [pl.BlockSpec(memory_space=pl.ANY)] * 11,
        scratch_shapes=[
            pltpu.SMEM((NC * NT // 2 + W,), jnp.int32),
            pltpu.SMEM((NC * NT // 2 + W,), jnp.int32),
            pltpu.SMEM((NC * NT // 2 + NC + W,), jnp.int32),
            pltpu.SMEM((NC * NT // 2 + NC + W,), jnp.int32),
            pltpu.VMEM((NC + 1, C, D), BF16),
            pltpu.VMEM((NC + 1, C, D), BF16),
            pltpu.VMEM((16, 16, D), BF16),
            pltpu.VMEM((NT, 2, 2, R, 2 * D), BF16),
            pltpu.VMEM((NT, 2, 2, R, 2 * D), BF16),
            pltpu.VMEM((NT // 2, D, KB), BF16),
            pltpu.VMEM((NC + 1, 2 * D, C), BF16),
            pltpu.VMEM((NC + 1, 2 * D, C), BF16),
            pltpu.VMEM((NC, 1, C), F32),
            pltpu.VMEM((NC + 1, 8, C), F32),
            pltpu.VMEM((NT, 2, 2, R, D), F32),
            pltpu.VMEM((NT, 2, 2, R, D), F32),
            pltpu.VMEM((NC + 1, D, C), F32),
            pltpu.SemaphoreType.DMA,
            pltpu.SemaphoreType.DMA,
        ],
        compiler_params=pltpu.CompilerParams(vmem_limit_bytes=48 << 20),
    )(span_order, counts, q_own, *pieces)
    dkv, query_grad = reduce_kv(outs[1:5], outs[5:9], exchange(outs[0], SPREAD))
    key_grad, value_grad = on_vmem(
        unpack_kv_kernel, [jax.ShapeDtypeStruct((R, 8 * D), BF16)] * 2, exchange(dkv, SPREAD)
    )
    return query_grad, key_grad, value_grad


def solution(mesh):
    fine = Mesh(mesh.devices.reshape(4, 2, 2, 2, 4), AXES)
    rows = P(AXES, None)
    return jax.shard_map(
        body,
        mesh=fine,
        in_specs=(rows,) * 5 + (P(), P()),
        out_specs=(rows,) * 3,
        check_vma=False,
    )
```

```python
import math

import jax
import jax.numpy as jnp
from jax import lax
from jax.experimental import pallas as pl
from jax.experimental.pallas import tpu as pltpu
from jax.sharding import Mesh, PartitionSpec as P

D = 128
G = 4
R = 64
HR = R // 2
SPAN = 256
SPANS = 32
KB = 2 * SPAN
QR = G * HR
C = 2 * QR
NC = 8
W = 4
WM = 2
SCALE = D**-0.5
EXP_SCALE = SCALE * math.log2(math.e)
HIDDEN = -1e30
LARGE = 2.0**90
F32 = jnp.float32
BF16 = jnp.bfloat16
AXES = ("z", "core", "xh", "xl", "y")
SPREAD = ("xh", "xl", "z")
NT_DIMS = (((1,), (1,)), ((), ()))

OWN, NEAR, FAR = (0,), (1, 3), (2,)


def spread_to(g, xl):
    return (g // 4 * 2 + xl) * 4 + g % 4


def head_columns(g, h):
    return slice((g * G + h) * D, (g * G + h + 1) * D)


def pack_kv_kernel(keys, values, segment, out, counts):
    counts[0] = jnp.sum((segment[...] == 0).astype(jnp.int32))
    counts[1] = jnp.sum((segment[...] != 2).astype(jnp.int32))
    for g in range(8):
        for xl in range(2):
            out[spread_to(g, xl), :R] = keys[:, g * D : (g + 1) * D]
            out[spread_to(g, xl), R:] = values[:, g * D : (g + 1) * D]


def pack_q_kernel(queries, saved, grads, after, out):
    del after
    ones = jnp.ones((8, D), BF16)
    row = lax.broadcasted_iota(jnp.int32, (16, D), 0)
    for g in range(8):
        for half in range(2):
            dest = spread_to(g, half)
            rows = slice(half * HR, (half + 1) * HR)
            prods = []
            for h in range(G):
                cols = head_columns(g, h)
                grad = grads[rows, cols]
                out[dest, h * HR : (h + 1) * HR] = queries[rows, cols]
                out[dest, QR + h * HR : QR + (h + 1) * HR] = grad
                prods.append(grad.astype(F32) * saved[rows, cols].astype(F32))
            prod = jnp.concatenate(prods, axis=0)
            high = prod.astype(BF16)
            low = (prod - high.astype(F32)).astype(BF16)
            dot = lax.dot_general(ones, high, NT_DIMS, preferred_element_type=F32)
            dot = dot + lax.dot_general(ones, low, NT_DIMS, preferred_element_type=F32)
            both = jnp.concatenate([dot, dot], axis=0)
            rounded = both.astype(BF16).astype(F32)
            out[dest, 2 * QR :] = jnp.where(row == 0, rounded, both - rounded).astype(BF16)


def span_id(xh, xl, y, zh):
    return ((xh * 2 + xl) * 4 + y) * 2 + zh


class Place:
    def __init__(self, order, counts):
        self.order = order
        self.n0, self.n1 = counts[0], counts[1]
        self.xl = lax.axis_index("xl")
        self.y = lax.axis_index("y")
        self.core = lax.axis_index("core")

    def span_of(self, c):
        return self.order[span_id(c // 4, c // 2 % 2, self.y, c % 2)]


class Group:
    def __init__(self, place, distances, base, table, below):
        self.place, self.base, self.table, self.below = place, base, table, below
        self.own = 0 in distances
        self.entries = [
            (dy, xh, xl, zh)
            for dy in distances
            for xh in range(2)
            for xl in range(2)
            for zh in range(2)
        ]

        def clear(i, carry):
            below[i] = 0
            return carry

        lax.fori_loop(0, SPANS + 1, clear, 0)
        spans = []
        for dy, xh, xl, zh in self.entries:
            span = place.order[span_id(xh, xl, place.y ^ dy, zh)]
            below[span] = 1
            spans.append(span)

        def count(i, total):
            here = below[i]
            below[i] = total

            @pl.when(here == 1)
            def _():
                table[base + total] = i

            return total + here

        lax.fori_loop(0, SPANS + 1, count, jnp.int32(0))
        self.slots = [base + below[span] for span in spans]

    def copies(self, pieces, part, dst, sem):
        made = []
        for (dy, xh, xl, zh), slot in zip(self.entries, self.slots):
            for from_core, arrays in zip((self.place.core, 1 - self.place.core), pieces[dy]):
                row = (xl * 2 + zh) * 2
                if len(arrays) == 2:
                    rows = arrays[xh].at[pl.ds(row, 2)]
                else:
                    rows = arrays[0].at[pl.ds(xh * 8 + row, 2)]
                made.append(
                    pltpu.make_async_copy(
                        rows.at[:, pl.ds(part * R, R)],
                        dst.at[slot, :, from_core, :, pl.ds(0, D)],
                        sem,
                    )
                )
        return made

    def put_sums(self, dy, xh, array, from_core, at_xh, dk_s, dv_s):
        for (entry_dy, entry_xh, xl, zh), slot in zip(self.entries, self.slots):
            if entry_dy == dy and entry_xh == xh:
                row = (((xh * 2 if at_xh else 0) + xl) * 2 + zh) * 2
                array[row : row + 2, :R] = (dk_s[slot, :, from_core] * SCALE).astype(BF16)
                array[row : row + 2, R:] = dv_s[slot, :, from_core].astype(BF16)


class Lists:
    def __init__(self, place, table, refs):
        self.place, self.table = place, table
        self.plain_c, self.plain_b, self.masked_c, self.masked_b = refs
        self.n_plain = self.n_masked = jnp.int32(0)

    def add(self, group):
        place, base = self.place, group.base // 2
        n0, n1 = place.n0, place.n1
        if group.own:
            self.n_masked = jnp.int32(NC)

        def chunk(c, sizes):
            n_plain, n_masked = sizes
            span_q = place.span_of(c)
            first = span_q * SPAN
            has_second = first + (SPAN - 1) >= n1
            all_second = first >= n1
            before = group.below[span_q]
            n_full = before // 2
            hi = (group.below[(n1 + (SPAN - 1)) // SPAN] + 1) // 2
            hi = jnp.minimum(jnp.where(has_second, hi, 0), n_full)
            lo = jnp.minimum(jnp.where(has_second, group.below[n0 // SPAN] // 2, 0), hi)
            skip_at = (group.below[(n0 + (SPAN - 1)) // SPAN] + 1) // 2
            skip_at = jnp.where(all_second, skip_at, hi)
            skip_to = jnp.where(all_second, group.below[n1 // SPAN] // 2, 0)

            def put_plain(b, n):
                self.plain_c[n] = c
                self.plain_b[n] = base + b
                return n + 1

            def put_masked(b, n):
                hidden = (b >= skip_at) & (b < skip_to)
                self.masked_c[n] = c
                self.masked_b[n] = base + b
                return jnp.where(hidden, n, n + 1)

            n_plain = lax.fori_loop(0, lo, put_plain, n_plain)
            n_plain = lax.fori_loop(hi, n_full, put_plain, n_plain)
            n_masked = lax.fori_loop(lo, hi, put_masked, n_masked)
            if group.own:
                self.masked_c[c] = c
                self.masked_b[c] = base + n_full
            else:
                self.masked_c[n_masked] = c
                self.masked_b[n_masked] = base + n_full
                n_masked = n_masked + before % 2
            return n_plain, n_masked

        self.n_plain, self.n_masked = lax.fori_loop(0, NC, chunk, (self.n_plain, self.n_masked))
        for i in range(W - 1):
            self.plain_c[self.n_plain + i] = NC
            self.plain_b[self.n_plain + i] = 0
        for i in range(WM - 1):
            self.masked_c[self.n_masked + i] = NC
            self.masked_b[self.n_masked + i] = 0
        self.n_plain = (self.n_plain + (W - 1)) // W * W
        self.n_masked = (self.n_masked + (WM - 1)) // WM * WM

    def each(self, step, first_masked=0):
        def masked(i, carry):
            at = [WM * i + k for k in range(WM)]
            step([(self.masked_c[n], self.masked_b[n]) for n in at], True)
            return carry

        def plain(i, carry):
            at = [W * i + k for k in range(W)]
            step([(self.plain_c[n], self.plain_b[n]) for n in at], False)
            return carry

        lax.fori_loop(first_masked // WM, self.n_masked // WM, masked, 0)
        lax.fori_loop(0, self.n_plain // W, plain, 0)

    def one_by_one(self, step):
        def masked(n, carry):
            @pl.when(self.masked_c[n] < NC)
            def _():
                step(self.masked_c[n], self.masked_b[n])

            return carry

        def plain(n, carry):
            @pl.when(self.plain_c[n] < NC)
            def _():
                step(self.plain_c[n], self.plain_b[n])

            return carry

        lax.fori_loop(0, self.n_masked, masked, 0)
        lax.fori_loop(0, self.n_plain, plain, 0)

    def seen(self, c, b):
        place = self.place
        lane = lax.broadcasted_iota(jnp.int32, (1, C), 1)
        start = place.span_of(jnp.minimum(c, NC - 1)) * SPAN + place.core * R + place.xl * HR
        query_pos = start + (lane // QR) * (2 * R) + lane % HR
        row = lax.broadcasted_iota(jnp.int32, (KB, 1), 0)
        start = jnp.where(row < SPAN, self.table[2 * b], self.table[2 * b + 1] - 1)
        key_pos = start * SPAN + row
        low = jnp.where(query_pos >= place.n1, place.n0, place.n1)
        return (key_pos <= query_pos) & ((key_pos < low) | (key_pos >= place.n1))


def block_of(ref, b):
    return ref[pl.ds(2 * b, 2)].reshape(KB, 2 * D)


def keys_of(k_s, b):
    return k_s[pl.ds(2 * b, 2), :, :, :, :D].reshape(KB, D)


def add_up(weights):
    return jnp.sum(weights.reshape(KB // 8, 8, C), axis=0)


def put_under(ref, c, *rows):
    number = lax.broadcasted_iota(jnp.int32, (D, C), 0)
    block = jnp.zeros((D, C), F32)
    for i, values in enumerate(rows):
        block = jnp.where(number == i, values, block)
    ref[c, D:] = block.astype(BF16)


def put_beside(*refs):
    beside = lax.broadcasted_iota(jnp.int32, (1, 1, 1, 1, D), 4) < 3
    beside = jnp.broadcast_to(beside.astype(F32), (1, 2, 2, R, D)).astype(BF16)

    def step(i, carry):
        for ref in refs:
            ref[pl.ds(i, 1), :, :, :, D:] = beside
        return carry

    lax.fori_loop(0, refs[0].shape[0], step, 0)


def put_empty_chunk(qa_s):
    qa_s[NC, :D] = jnp.zeros((D, C), BF16)
    put_under(qa_s, NC, jnp.full((1, C), HIDDEN, F32))


def weights_of(lists, c, b, masked, k_s, qa_s):
    scores = jnp.dot(block_of(k_s, b), qa_s[c], preferred_element_type=F32)
    if masked:
        scores = jnp.where(lists.seen(c, b), scores, HIDDEN)
    return jnp.exp2(scores * EXP_SCALE)


def add_stats(lists, k_s, qa_s, l_s, first_masked=0):
    def step(items, masked):
        parts = [add_up(weights_of(lists, c, b, masked, k_s, qa_s)) for c, b in items]
        for (c, b), part in zip(items, parts):
            l_s[c] += part

    lists.each(step, first_masked)


def careful_stats(lists, k_s, qa_s, m_s, l_s):
    def step(c, b):
        scores = jnp.dot(keys_of(k_s, b), qa_s[c, :D], preferred_element_type=F32) * EXP_SCALE
        scores = jnp.where(lists.seen(c, b), scores, HIDDEN)
        old = m_s[c]
        top = jnp.maximum(old, jnp.max(scores, axis=0, keepdims=True))
        l_s[c] = l_s[c] * jnp.exp2(old - top) + add_up(jnp.exp2(scores - top))
        m_s[c] = top

    lists.one_by_one(step)


def stats_kernel(
    order, counts, qpay, own, own_o, near_1, near_1o, near_3, near_3o,
    m_out, l_out, qt_out, g_out, ga_out,
    table, below_0, below_1, plain_c, plain_b, masked_c, masked_b,
    q_s, d_s, k_s, qa_s, l_s, sem, grad_sem,
):
    place = Place(order, counts)
    copies = []
    grad_copies = []
    for s in range(2 * NC):
        rows = pl.ds((s % 2) * QR, QR)
        copies.append(
            pltpu.make_async_copy(qpay.at[s, pl.ds(0, QR)], q_s.at[s // 2, rows], sem)
        )
        grad_copies.append(
            pltpu.make_async_copy(qpay.at[s, pl.ds(QR, QR)], g_out.at[s // 2, rows], grad_sem)
        )
    grad_copies.append(pltpu.make_async_copy(qpay.at[:, pl.ds(2 * QR, 16)], d_s, grad_sem))
    for copy in copies:
        copy.start()
    pieces = {0: ([own], [own_o]), 1: ([near_1], [near_1o]), 3: ([near_3], [near_3o])}
    groups = [Group(place, OWN, 0, table, below_0), Group(place, NEAR, 8, table, below_1)]
    for group in groups:
        key_copies = group.copies(pieces, 0, k_s, sem)
        for copy in key_copies:
            copy.start()
        copies += key_copies
    for copy in grad_copies:
        copy.start()
    put_beside(k_s)
    put_empty_chunk(qa_s)
    l_s[NC] = jnp.zeros((8, C), F32)
    lists = Lists(place, table, (plain_c, plain_b, masked_c, masked_b))
    for group in groups:
        lists.add(group)
    for copy in copies:
        copy.wait()

    def turn(c, carry):
        turned = q_s[c].T
        qa_s[c, :D] = turned
        qt_out[c] = turned
        return carry

    lax.fori_loop(0, NC, turn, 0)

    def diagonal_step(i, carry):
        for c in [2 * i + k for k in range(2)]:
            b = masked_b[c]
            scores = jnp.dot(keys_of(k_s, b), qa_s[c, :D], preferred_element_type=F32)
            scores = jnp.where(lists.seen(c, b), scores, HIDDEN)
            top = jnp.max(scores, axis=0, keepdims=True).astype(BF16).astype(F32)
            put_under(qa_s, c, -top)
            m_out[c] = top * EXP_SCALE
            l_s[c] = add_up(jnp.exp2((scores - top) * EXP_SCALE))
        return carry

    lax.fori_loop(0, NC // 2, diagonal_step, 0)
    add_stats(lists, k_s, qa_s, l_s, NC)

    @pl.when(jnp.logical_not(jnp.max(l_s[...]) < LARGE))
    def _():
        for c in range(NC):
            m_out[c] = jnp.full((1, C), HIDDEN, F32)
            l_s[c] = jnp.zeros((8, C), F32)
        careful_stats(lists, k_s, qa_s, m_out, l_s)

    for c in range(NC):
        l_out[c] = l_s[c]

    for copy in grad_copies:
        copy.wait()

    def turn_grads(c, carry):
        ga_out[c, :D] = g_out[c].T
        halves = [d_s[2 * c + half].astype(F32) for half in range(2)]
        put_under(
            ga_out,
            c,
            -jnp.concatenate([half[0:1] for half in halves], axis=1),
            -jnp.concatenate([half[1:2] for half in halves], axis=1),
        )
        return carry

    lax.fori_loop(0, NC, turn_grads, 0)


def query_copies(qpay, qt, q_s, qa_s, sem):
    made = [pltpu.make_async_copy(qt, qa_s.at[pl.ds(0, NC), pl.ds(0, D)], sem)]
    for s in range(2 * NC):
        rows = pl.ds((s % 2) * QR, QR)
        made.append(pltpu.make_async_copy(qpay.at[s, pl.ds(0, QR)], q_s.at[s // 2, rows], sem))
    return made


def grad_pass(lists, logsum, q_s, g_in, ga_in, k_s, v_s, kt_s, qa_s, dk_s, dv_s, dq_s):
    def turn(b, carry):
        kt_s[b] = keys_of(k_s, b).T
        return carry

    lax.fori_loop(0, kt_s.shape[0], turn, 0)

    def put_logsum(c, carry):
        rest = logsum[c] * (1.0 / EXP_SCALE)
        rows = []
        for _ in range(3):
            part = rest.astype(BF16).astype(F32)
            rows.append(-part)
            rest = rest - part
        put_under(qa_s, c, *rows)
        return carry

    lax.fori_loop(0, NC, put_logsum, 0)

    def step(items, masked):
        weights = [weights_of(lists, c, b, masked, k_s, qa_s) for c, b in items]
        of = [jnp.minimum(c, NC - 1) for c, b in items]
        above = [
            jnp.dot(block_of(v_s, b), ga_in[c], preferred_element_type=F32)
            for c, (_, b) in zip(of, items)
        ]
        score_grads = [(w * p).astype(BF16) for w, p in zip(weights, above)]
        for c, (_, b), w, score_grad in zip(of, items, weights, score_grads):
            for ref, term in (
                (dv_s, jnp.dot(w.astype(BF16), g_in[c], preferred_element_type=F32)),
                (dk_s, jnp.dot(score_grad, q_s[c], preferred_element_type=F32)),
            ):
                ref[pl.ds(2 * b, 2)] += term.reshape(2, 2, 2, R, D)
            dq_s[c] += jnp.dot(kt_s[b], score_grad, preferred_element_type=F32)

    lists.each(step)


def far_near_kernel(
    order, counts, m_in, l_in, g_in, ga_in,
    qpay, qt, far_a, far_b, far_ao, far_bo, near_1, near_1o, near_3, near_3o,
    logsum, dq, far_give, give_1, give_3, sum_a, sum_b, sum_1, sum_3,
    table, below_0, below_1, plain_c, plain_b, masked_c, masked_b,
    q_s, k_s, v_s, kt_s, qa_s, dk_s, dv_s, m_s, l_s, sem, value_sem,
):
    place = Place(order, counts)
    copies = query_copies(qpay, qt, q_s, qa_s, sem)
    for copy in copies:
        copy.start()
    pieces = {
        2: ([far_a, far_b], [far_ao, far_bo]),
        1: ([near_1], [near_1o]),
        3: ([near_3], [near_3o]),
    }
    groups = [Group(place, FAR, 0, table, below_0), Group(place, NEAR, 8, table, below_1)]
    value_copies = []
    for group in groups:
        key_copies = group.copies(pieces, 0, k_s, sem)
        for copy in key_copies:
            copy.start()
        copies += key_copies
    for group in groups:
        value_copies += group.copies(pieces, 1, v_s, value_sem)
    for copy in value_copies:
        copy.start()
    put_beside(k_s, v_s)
    put_empty_chunk(qa_s)
    for ref in (dk_s, dv_s, dq):
        ref[...] = jnp.zeros_like(ref)

    def take(c, carry):
        top = (m_in[c] * (1.0 / EXP_SCALE)).astype(BF16).astype(F32)
        put_under(qa_s, c, -top)
        m_s[c] = top * EXP_SCALE
        l_s[c] = l_in[c] * jnp.exp2(m_in[c] - top * EXP_SCALE)
        return carry

    lax.fori_loop(0, NC, take, 0)
    l_s[NC] = jnp.zeros((8, C), F32)
    lists = Lists(place, table, (plain_c, plain_b, masked_c, masked_b))
    lists.add(groups[0])
    for copy in copies:
        copy.wait()
    add_stats(lists, k_s, qa_s, l_s)

    @pl.when(jnp.logical_not(jnp.max(l_s[...]) < LARGE))
    def _():
        for c in range(NC):
            m_s[c] = m_in[c]
            l_s[c] = l_in[c]
        careful_stats(lists, k_s, qa_s, m_s, l_s)

    for c in range(NC):
        logsum[c] = m_s[c] + jnp.log2(jnp.sum(l_s[c], axis=0, keepdims=True))
    lists.add(groups[1])
    for copy in value_copies:
        copy.wait()
    grad_pass(lists, logsum, q_s, g_in, ga_in, k_s, v_s, kt_s, qa_s, dk_s, dv_s, dq)
    far, near = groups
    far.put_sums(2, 0, sum_a, place.core, False, dk_s, dv_s)
    far.put_sums(2, 1, sum_b, place.core, False, dk_s, dv_s)
    for xh in range(2):
        far.put_sums(2, xh, far_give, 1 - place.core, True, dk_s, dv_s)
        for dy, keep, give in ((1, sum_1, give_1), (3, sum_3, give_3)):
            near.put_sums(dy, xh, keep, place.core, True, dk_s, dv_s)
            near.put_sums(dy, xh, give, 1 - place.core, True, dk_s, dv_s)


def own_kernel(
    order, counts, logsum, dq_in, g_in, ga_in, after, qpay, qt, own, own_o,
    dq_out, keep, give,
    table, below_0, plain_c, plain_b, masked_c, masked_b,
    q_s, k_s, v_s, kt_s, qa_s, dk_s, dv_s, dq_s, sem,
):
    del after
    place = Place(order, counts)
    copies = query_copies(qpay, qt, q_s, qa_s, sem)
    group = Group(place, OWN, 0, table, below_0)
    pieces = {0: ([own], [own_o])}
    copies += group.copies(pieces, 0, k_s, sem) + group.copies(pieces, 1, v_s, sem)
    for copy in copies:
        copy.start()
    put_beside(k_s, v_s)
    put_empty_chunk(qa_s)
    for ref in (dk_s, dv_s):
        ref[...] = jnp.zeros_like(ref)
    dq_s[...] = dq_in[...]
    lists = Lists(place, table, (plain_c, plain_b, masked_c, masked_b))
    lists.add(group)
    for copy in copies:
        copy.wait()
    grad_pass(lists, logsum, q_s, g_in, ga_in, k_s, v_s, kt_s, qa_s, dk_s, dv_s, dq_s)
    for xh in range(2):
        group.put_sums(0, xh, keep, place.core, True, dk_s, dv_s)
        group.put_sums(0, xh, give, 1 - place.core, True, dk_s, dv_s)

    def finish(c, carry):
        dq = (dq_s[c] * SCALE).T.astype(BF16)
        dq_out[2 * c] = dq[:QR]
        dq_out[2 * c + 1] = dq[QR:]
        return carry

    lax.fori_loop(0, NC, finish, 0)


def far_sum_kernel(sum_a, sum_b, got, out_a, out_b, after):
    out_a[...] = (sum_a[...].astype(F32) + got[:8].astype(F32)).astype(BF16)
    out_b[...] = (sum_b[...].astype(F32) + got[8:].astype(F32)).astype(BF16)
    after[...] = jnp.zeros_like(after)


def near_sum_kernel(sum_1, got_1, sum_3, got_3, from_1, from_3, out_1, out_3):
    for rows, with_from in ((slice(0, 8), 3), (slice(8, 16), 1)):
        for number, keep, got, came, out in (
            (1, sum_1, got_1, from_3, out_1),
            (3, sum_3, got_3, from_1, out_3),
        ):
            total = keep[rows].astype(F32) + got[rows].astype(F32)
            if number == with_from:
                total = total + came[...].astype(F32)
            out[rows] = total.astype(BF16)


def last_sum_kernel(keep, got, near_1, near_3, dq, sums, query_grad):
    total = keep[...].astype(F32) + got[...].astype(F32)
    total = total + (near_1[...].astype(F32) + near_3[...].astype(F32))
    sums[...] = total.astype(BF16)
    for g in range(8):
        for half in range(2):
            rows = slice(half * HR, (half + 1) * HR)
            for h in range(G):
                query_grad[rows, head_columns(g, h)] = dq[spread_to(g, half), h * HR : (h + 1) * HR]


def unpack_kernel(got, key_grad, value_grad):
    for g in range(8):
        for start, out in ((0, key_grad), (R, value_grad)):
            total = got[spread_to(g, 0), start : start + R].astype(F32)
            total = total + got[spread_to(g, 1), start : start + R].astype(F32)
            out[:, g * D : (g + 1) * D] = total.astype(BF16)


def bf16(*shape):
    return jax.ShapeDtypeStruct(shape, BF16)


def f32(*shape):
    return jax.ShapeDtypeStruct(shape, F32)


def on_vmem(kernel, outs, *args):
    return pl.pallas_call(
        kernel,
        out_shape=outs,
        compiler_params=pltpu.CompilerParams(vmem_limit_bytes=16 << 20),
    )(*args)


IN_SMEM = pl.BlockSpec(memory_space=pltpu.SMEM)
IN_VMEM = pl.BlockSpec(memory_space=pltpu.VMEM)
ANYWHERE = pl.BlockSpec(memory_space=pl.ANY)


def on_group(kernel, outs, spans, groups, scratch, tables, held, anywhere, products):
    smem = [pltpu.SMEM((spans,), jnp.int32)] + [pltpu.SMEM((SPANS + 1,), jnp.int32)] * groups
    smem += [pltpu.SMEM((NC * (spans // 2 + 1) + 4 * W,), jnp.int32)] * 4
    work = products * NC * C * spans * SPAN * D * 2 // 3
    return pl.pallas_call(
        kernel,
        out_shape=outs,
        in_specs=[IN_SMEM] * 2 + [IN_VMEM] * len(held) + [ANYWHERE] * len(anywhere),
        scratch_shapes=smem + scratch,
        compiler_params=pltpu.CompilerParams(vmem_limit_bytes=44 << 20),
        cost_estimate=pl.CostEstimate(
            flops=work, bytes_accessed=4 << 20, transcendentals=NC * C * spans * SPAN // 3
        ),
    )(*tables, *held, *anywhere)


def exchange(array):
    return lax.all_to_all(array, SPREAD, split_axis=0, concat_axis=0, tiled=True)


def flip(array):
    return lax.ppermute(array, "core", [(0, 1), (1, 0)])


def swap(array, distance):
    return lax.ppermute(array, "y", [(i, i ^ distance) for i in range(4)])


def body(queries, keys, values, attn_out, out_grad, segment, span_order):
    kv_packed, counts = pl.pallas_call(
        pack_kv_kernel,
        out_shape=[bf16(16, 2 * R, D), jax.ShapeDtypeStruct((2,), jnp.int32)],
        out_specs=[IN_VMEM, IN_SMEM],
        compiler_params=pltpu.CompilerParams(vmem_limit_bytes=16 << 20),
    )(keys, values, segment.reshape(64, 128))
    tables = (span_order, counts)
    own = exchange(kv_packed)
    q_packed = pl.pallas_call(
        pack_q_kernel,
        out_shape=bf16(16, 2 * QR + 16, D),
        in_specs=[IN_VMEM] * 3 + [ANYWHERE],
        compiler_params=pltpu.CompilerParams(vmem_limit_bytes=16 << 20),
    )(queries, attn_out, out_grad, own)
    qpay = exchange(q_packed)

    near_1 = swap(own, 1)
    near_3 = swap(own, 3)
    far_a = swap(near_3[:8], 1)
    far_b = swap(near_1[8:], 3)
    own_pieces = (own, flip(own))
    near_pieces = (near_1, flip(near_1), near_3, flip(near_3))
    far_pieces = (far_a, far_b, flip(far_a), flip(far_b))

    def keys_scratch(spans):
        return pltpu.VMEM((spans, 2, 2, R, 2 * D), BF16)

    def sums_scratch(spans):
        return pltpu.VMEM((spans, 2, 2, R, D), F32)

    queries_scratch = pltpu.VMEM((NC, C, D), BF16)
    turned_scratch = pltpu.VMEM((NC + 1, 2 * D, C), BF16)
    total_scratch = pltpu.VMEM((NC + 1, 8, C), F32)
    dma = pltpu.SemaphoreType.DMA

    top, total, turned, grads, grads_turned = on_group(
        stats_kernel,
        [f32(NC, 1, C), f32(NC, 8, C), bf16(NC, D, C), bf16(NC, C, D), bf16(NC, 2 * D, C)],
        24,
        2,
        [queries_scratch, pltpu.VMEM((16, 16, D), BF16), keys_scratch(24)]
        + [turned_scratch, total_scratch, dma, dma],
        tables,
        (),
        (qpay,) + own_pieces + near_pieces,
        1,
    )
    group = bf16(16, 2 * R, D)
    half = bf16(8, 2 * R, D)
    logsum, dq, far_give, give_1, give_3, sum_a, sum_b, sum_1, sum_3 = on_group(
        far_near_kernel,
        [f32(NC, 1, C), f32(NC, D, C)] + [group] * 3 + [half] * 2 + [group] * 2,
        24,
        2,
        [queries_scratch, keys_scratch(24), keys_scratch(24), pltpu.VMEM((12, D, KB), BF16)]
        + [turned_scratch, sums_scratch(24), sums_scratch(24)]
        + [pltpu.VMEM((NC, 1, C), F32), total_scratch, dma, dma],
        tables,
        (top, total, grads, grads_turned),
        (qpay, turned) + far_pieces + near_pieces,
        6,
    )
    far_sum_a, far_sum_b, after = on_vmem(
        far_sum_kernel, [half, half, f32(8, D)], sum_a, sum_b, flip(far_give)
    )
    from_1 = swap(far_sum_a, 1)
    from_3 = swap(far_sum_b, 3)
    dq, keep, give = on_group(
        own_kernel,
        [bf16(16, QR, D), group, group],
        8,
        1,
        [queries_scratch, keys_scratch(8), keys_scratch(8), pltpu.VMEM((4, D, KB), BF16)]
        + [turned_scratch, sums_scratch(8), sums_scratch(8), pltpu.VMEM((NC, D, C), F32), dma],
        tables,
        (logsum, dq, grads, grads_turned, after),
        (qpay, turned) + own_pieces,
        5,
    )
    to_1, to_3 = on_vmem(
        near_sum_kernel, [group] * 2, sum_1, flip(give_1), sum_3, flip(give_3), from_1, from_3
    )
    sums, query_grad = on_vmem(
        last_sum_kernel,
        [group, bf16(R, 8 * G * D)],
        keep,
        flip(give),
        swap(to_1, 1),
        swap(to_3, 3),
        exchange(dq),
    )
    key_grad, value_grad = on_vmem(unpack_kernel, [bf16(R, 8 * D)] * 2, exchange(sums))
    return query_grad, key_grad, value_grad


def solution(mesh):
    fine = Mesh(mesh.devices.reshape(4, 2, 2, 2, 4), AXES)
    rows = P(AXES, None)
    return jax.shard_map(
        body,
        mesh=fine,
        in_specs=(rows,) * 5 + (P(), P()),
        out_specs=(rows,) * 3,
        check_vma=False,
    )
```

```python
import jax
import jax.numpy as jnp
from jax import lax
from jax.experimental import pallas as pl
from jax.experimental.pallas import tpu as pltpu
from jax.sharding import Mesh, PartitionSpec as P

D = 128
G = 4
R = 64
HR = R // 2
SPAN = 256
NT = 32
KB = 2 * SPAN
QR = G * HR
C = 2 * QR
NC = 8
W = 4
SCALE = D**-0.5
HIDDEN = -1e30
LARGE = 2.0**90
F32 = jnp.float32
BF16 = jnp.bfloat16
AXES = ("z", "core", "xh", "xl", "y")
SPREAD = ("xh", "xl", "z")
NT_DIMS = (((1,), (1,)), ((), ()))


def spread_to(g, xl):
    return (g // 4 * 2 + xl) * 4 + g % 4


def head_columns(g, h):
    return slice((g * G + h) * D, (g * G + h + 1) * D)


def pack_kv_kernel(keys, values, segment, out, counts):
    counts[0] = jnp.sum((segment[...] == 0).astype(jnp.int32))
    counts[1] = jnp.sum((segment[...] != 2).astype(jnp.int32))
    for g in range(8):
        for xl in range(2):
            out[spread_to(g, xl), :R] = keys[:, g * D : (g + 1) * D]
            out[spread_to(g, xl), R:] = values[:, g * D : (g + 1) * D]


def pack_q_kernel(queries, saved, grads, after, out):
    del after
    ones = jnp.ones((8, D), BF16)
    row = lax.broadcasted_iota(jnp.int32, (16, D), 0)
    for g in range(8):
        for half in range(2):
            dest = spread_to(g, half)
            rows = slice(half * HR, (half + 1) * HR)
            prods = []
            for h in range(G):
                cols = head_columns(g, h)
                grad = grads[rows, cols]
                out[dest, h * HR : (h + 1) * HR] = queries[rows, cols]
                out[dest, QR + h * HR : QR + (h + 1) * HR] = grad
                prods.append(grad.astype(F32) * saved[rows, cols].astype(F32))
            prod = jnp.concatenate(prods, axis=0)
            high = prod.astype(BF16)
            low = (prod - high.astype(F32)).astype(BF16)
            dot = lax.dot_general(ones, high, NT_DIMS, preferred_element_type=F32)
            dot = dot + lax.dot_general(ones, low, NT_DIMS, preferred_element_type=F32)
            both = jnp.concatenate([dot, dot], axis=0)
            rounded = both.astype(BF16).astype(F32)
            out[dest, 2 * QR :] = jnp.where(row == 0, rounded, both - rounded).astype(BF16)


def span_id(xh, xl, y, zh):
    return ((xh * 2 + xl) * 4 + y) * 2 + zh


def attention_kernel(order, counts, qpay, *refs):
    pieces = refs[:10]
    dq_out, keep_0, keep_1, keep_3, sum_a, sum_b, give_0, give_1, give_3, far_give = refs[10:20]
    (plain_c, plain_b, masked_c, masked_b, q_s, do_s, d_s, k_s, v_s, kt_s, qa_s, ga_s) = refs[20:32]
    m_s, l_s, dk_s, dv_s, dq_s, sem, value_sem = refs[32:]
    n0 = counts[0]
    n1 = counts[1]
    xl = lax.axis_index("xl")
    y = lax.axis_index("y")
    core = lax.axis_index("core")

    def place(dy, xh, xl, zh):
        return order[span_id(xh, xl, y ^ dy, zh)]

    copies = []
    value_copies = []
    for s in range(16):
        for part, dst in ((0, q_s), (1, do_s)):
            copies.append(
                pltpu.make_async_copy(
                    qpay.at[s, pl.ds(part * QR, QR)], dst.at[s // 2, pl.ds((s % 2) * QR, QR)], sem
                )
            )
    copies.append(pltpu.make_async_copy(qpay.at[:, pl.ds(2 * QR, 16)], d_s, sem))
    for number, piece in enumerate(pieces):
        from_core = core if number < 5 else 1 - core
        dy = (0, 1, 3, 2, 2)[number % 5]
        halves = ((0, 1), (0, 1), (0, 1), (0,), (1,))[number % 5]
        for at in range(4 * len(halves)):
            rank = place(dy, halves[at // 4], at // 2 % 2, at % 2)
            rows = piece.at[pl.ds(2 * at, 2)]
            copies.append(
                pltpu.make_async_copy(
                    rows.at[:, pl.ds(0, R)], k_s.at[rank, :, from_core, :, pl.ds(0, D)], sem
                )
            )
            value_copies.append(
                pltpu.make_async_copy(
                    rows.at[:, pl.ds(R, R)], v_s.at[rank, :, from_core, :, pl.ds(0, D)], value_sem
                )
            )
    for copy in copies + value_copies:
        copy.start()

    beside = lax.broadcasted_iota(jnp.int32, (1, 1, 1, 1, D), 4) < 3
    beside = jnp.broadcast_to(beside.astype(F32), (1, 2, 2, R, D)).astype(BF16)

    def put_beside(i, carry):
        k_s[pl.ds(i, 1), :, :, :, D:] = beside
        v_s[pl.ds(i, 1), :, :, :, D:] = beside
        return carry

    lax.fori_loop(0, NT, put_beside, 0)
    dk_s[...] = jnp.zeros_like(dk_s)
    dv_s[...] = jnp.zeros_like(dv_s)
    dq_s[...] = jnp.zeros_like(dq_s)

    def span_of(c):
        return order[span_id(c // 4, c // 2 % 2, y, c % 2)]

    def list_chunk(c, sizes):
        n_plain, n_masked = sizes
        span_q = span_of(c)
        first = span_q * SPAN
        has_second = first + (SPAN - 1) >= n1
        all_second = first >= n1
        n_full = span_q // 2
        hi = jnp.minimum(jnp.where(has_second, (n1 + (KB - 1)) // KB, 0), n_full)
        lo = jnp.minimum(jnp.where(has_second, n0 // KB, 0), hi)
        skip_at = jnp.where(all_second, (n0 + (KB - 1)) // KB, hi)
        skip_to = jnp.where(all_second, n1 // KB, 0)
        masked_c[c] = c
        masked_b[c] = n_full

        def put_plain(b, n):
            plain_c[n] = c
            plain_b[n] = b
            return n + 1

        def put_masked(b, n):
            hidden = (b >= skip_at) & (b < skip_to)
            masked_c[n] = c
            masked_b[n] = b
            return jnp.where(hidden, n, n + 1)

        n_plain = lax.fori_loop(0, lo, put_plain, n_plain)
        n_plain = lax.fori_loop(hi, n_full, put_plain, n_plain)
        return n_plain, lax.fori_loop(lo, hi, put_masked, n_masked)

    n_plain, n_masked = lax.fori_loop(0, NC, list_chunk, (jnp.int32(0), jnp.int32(NC)))
    for i in range(W - 1):
        plain_c[n_plain + i] = NC
        plain_b[n_plain + i] = 0
        masked_c[n_masked + i] = NC
        masked_b[n_masked + i] = 0

    for copy in copies:
        copy.wait()

    def block_of(ref, b):
        return ref[pl.ds(2 * b, 2)].reshape(KB, 2 * D)

    def keys_of(b):
        return k_s[pl.ds(2 * b, 2), :, :, :, :D].reshape(KB, D)

    def turn_keys(b, carry):
        kt_s[b] = keys_of(b).T
        return carry

    lax.fori_loop(0, NT // 2, turn_keys, 0)

    def put_under(ref, c, *rows):
        number = lax.broadcasted_iota(jnp.int32, (D, C), 0)
        block = jnp.zeros((D, C), F32)
        for i, values in enumerate(rows):
            block = jnp.where(number == i, values, block)
        ref[c, D:] = block.astype(BF16)

    def turn_rows(c, carry):
        qa_s[c, :D] = q_s[c].T
        ga_s[c, :D] = do_s[c].T
        halves = [d_s[2 * c + half].astype(F32) for half in range(2)]
        put_under(
            ga_s,
            c,
            -jnp.concatenate([half[0:1] for half in halves], axis=1),
            -jnp.concatenate([half[1:2] for half in halves], axis=1),
        )
        return carry

    lax.fori_loop(0, NC, turn_rows, 0)
    qa_s[NC, :D] = jnp.zeros((D, C), BF16)
    put_under(qa_s, NC, jnp.full((1, C), HIDDEN, F32))
    ga_s[NC] = jnp.zeros((2 * D, C), BF16)
    q_s[NC] = jnp.zeros((C, D), BF16)
    do_s[NC] = jnp.zeros((C, D), BF16)
    l_s[NC] = jnp.zeros((8, C), F32)

    def seen(c, b):
        lane = lax.broadcasted_iota(jnp.int32, (1, C), 1)
        row = span_of(jnp.minimum(c, NC - 1)) * SPAN + core * R + xl * HR
        query_pos = row + (lane // QR) * (2 * R) + lane % HR
        key_pos = b * KB + lax.broadcasted_iota(jnp.int32, (KB, 1), 0)
        low = jnp.where(query_pos >= n1, n0, n1)
        return (key_pos <= query_pos) & ((key_pos < low) | (key_pos >= n1))

    def add_up(weights):
        return jnp.sum(weights.reshape(KB // 8, 8, C), axis=0)

    def raw_scores(c, b):
        return jnp.dot(keys_of(b), qa_s[c, :D], preferred_element_type=F32)

    def weights_of(c, b, masked):
        scores = jnp.dot(block_of(k_s, b), qa_s[c], preferred_element_type=F32)
        if masked:
            scores = jnp.where(seen(c, b), scores, HIDDEN)
        return jnp.exp(scores * SCALE)

    def diagonal_step(i, carry):
        for c in [2 * i + k for k in range(2)]:
            b = masked_b[c]
            scores = jnp.where(seen(c, b), raw_scores(c, b), HIDDEN)
            top = jnp.max(scores, axis=0, keepdims=True).astype(BF16).astype(F32)
            put_under(qa_s, c, -top)
            m_s[c] = top * SCALE
            l_s[c] = add_up(jnp.exp((scores - top) * SCALE))
        return carry

    lax.fori_loop(0, NC // 2, diagonal_step, 0)

    def add_weights(items, masked):
        parts = [add_up(weights_of(c, b, masked)) for c, b in items]
        for (c, b), part in zip(items, parts):
            l_s[c] += part

    def masked_stats(i, carry):
        at = [NC + 2 * i + k for k in range(2)]
        add_weights([(masked_c[n], masked_b[n]) for n in at], True)
        return carry

    def plain_stats(i, carry):
        at = [W * i + k for k in range(W)]
        add_weights([(plain_c[n], plain_b[n]) for n in at], False)
        return carry

    lax.fori_loop(0, (n_masked - NC + 1) // 2, masked_stats, 0)
    lax.fori_loop(0, (n_plain + W - 1) // W, plain_stats, 0)

    @pl.when(jnp.logical_not(jnp.max(l_s[...]) < LARGE))
    def _():
        def careful(c, b):
            scores = jnp.where(seen(c, b), raw_scores(c, b) * SCALE, HIDDEN)
            old = m_s[c]
            top = jnp.maximum(old, jnp.max(scores, axis=0, keepdims=True))
            l_s[c] = l_s[c] * jnp.exp(old - top) + add_up(jnp.exp(scores - top))
            m_s[c] = top

        def careful_masked(n, carry):
            c = masked_c[n]

            @pl.when(n < NC)
            def _():
                m_s[c] = jnp.full((1, C), HIDDEN, F32)
                l_s[c] = jnp.zeros((8, C), F32)

            careful(c, masked_b[n])
            return carry

        def careful_plain(n, carry):
            careful(plain_c[n], plain_b[n])
            return carry

        lax.fori_loop(0, n_masked, careful_masked, 0)
        lax.fori_loop(0, n_plain, careful_plain, 0)

    def put_logsum(c, carry):
        logsum = m_s[c] + jnp.log(jnp.sum(l_s[c], axis=0, keepdims=True))
        rest = logsum * (1.0 / SCALE)
        rows = []
        for _ in range(3):
            part = rest.astype(BF16).astype(F32)
            rows.append(-part)
            rest = rest - part
        put_under(qa_s, c, *rows)
        return carry

    lax.fori_loop(0, NC, put_logsum, 0)
    for copy in value_copies:
        copy.wait()

    def grad_step(items, masked):
        weights = [weights_of(c, b, masked) for c, b in items]
        above = [
            jnp.dot(block_of(v_s, b), ga_s[c], preferred_element_type=F32) for c, b in items
        ]
        score_grads = [(w * p).astype(BF16) for w, p in zip(weights, above)]
        for (c, b), w, score_grad in zip(items, weights, score_grads):
            for ref, term in (
                (dv_s, jnp.dot(w.astype(BF16), do_s[c], preferred_element_type=F32)),
                (dk_s, jnp.dot(score_grad, q_s[c], preferred_element_type=F32)),
            ):
                ref[pl.ds(2 * b, 2)] += term.reshape(2, 2, 2, R, D)
            dq_s[c] += jnp.dot(kt_s[b], score_grad, preferred_element_type=F32)

    def masked_grads(i, carry):
        at = [2 * i + k for k in range(2)]
        grad_step([(masked_c[n], masked_b[n]) for n in at], True)
        return carry

    def plain_grads(i, carry):
        at = [W * i + k for k in range(W)]
        grad_step([(plain_c[n], plain_b[n]) for n in at], False)
        return carry

    lax.fori_loop(0, (n_masked + 1) // 2, masked_grads, 0)
    lax.fori_loop(0, (n_plain + W - 1) // W, plain_grads, 0)

    def finish(c, carry):
        dq = (dq_s[c] * SCALE).T.astype(BF16)
        dq_out[2 * c] = dq[:QR]
        dq_out[2 * c + 1] = dq[QR:]
        return carry

    lax.fori_loop(0, NC, finish, 0)

    for from_core, group in (
        (core, ((0, keep_0, 0), (1, keep_1, 0), (3, keep_3, 0), (2, sum_a, 0), (2, sum_b, 1))),
        (1 - core, ((0, give_0, 0), (1, give_1, 0), (3, give_3, 0), (2, far_give, 0))),
    ):
        for dy, out, first_xh in group:
            for at in range(out.shape[0] // 2):
                rank = place(dy, first_xh + at // 4, at // 2 % 2, at % 2)
                rows = slice(2 * at, 2 * at + 2)
                out[rows, :R] = (dk_s[rank, :, from_core] * SCALE).astype(BF16)
                out[rows, R:] = dv_s[rank, :, from_core].astype(BF16)


def far_sum_kernel(sum_a, sum_b, got, out_a, out_b):
    out_a[...] = (sum_a[...].astype(F32) + got[:8].astype(F32)).astype(BF16)
    out_b[...] = (sum_b[...].astype(F32) + got[8:].astype(F32)).astype(BF16)


def near_sum_kernel(sum_1, got_1, sum_3, got_3, from_1, from_3, out_1, out_3):
    for rows, with_from in ((slice(0, 8), 3), (slice(8, 16), 1)):
        for number, keep, got, came, out in (
            (1, sum_1, got_1, from_3, out_1),
            (3, sum_3, got_3, from_1, out_3),
        ):
            total = keep[rows].astype(F32) + got[rows].astype(F32)
            if number == with_from:
                total = total + came[...].astype(F32)
            out[rows] = total.astype(BF16)


def last_sum_kernel(keep, got, near_1, near_3, dq, sums, query_grad):
    total = keep[...].astype(F32) + got[...].astype(F32)
    total = total + (near_1[...].astype(F32) + near_3[...].astype(F32))
    sums[...] = total.astype(BF16)
    for g in range(8):
        for half in range(2):
            rows = slice(half * HR, (half + 1) * HR)
            for h in range(G):
                query_grad[rows, head_columns(g, h)] = dq[spread_to(g, half), h * HR : (h + 1) * HR]


def unpack_kernel(got, key_grad, value_grad):
    for g in range(8):
        for start, out in ((0, key_grad), (R, value_grad)):
            total = got[spread_to(g, 0), start : start + R].astype(F32)
            total = total + got[spread_to(g, 1), start : start + R].astype(F32)
            out[:, g * D : (g + 1) * D] = total.astype(BF16)


def bf16(*shape):
    return jax.ShapeDtypeStruct(shape, BF16)


def on_vmem(kernel, outs, *args):
    return pl.pallas_call(
        kernel,
        out_shape=outs,
        compiler_params=pltpu.CompilerParams(vmem_limit_bytes=16 << 20),
    )(*args)


IN_SMEM = pl.BlockSpec(memory_space=pltpu.SMEM)
IN_VMEM = pl.BlockSpec(memory_space=pltpu.VMEM)
ANYWHERE = pl.BlockSpec(memory_space=pl.ANY)


def exchange(array):
    return lax.all_to_all(array, SPREAD, split_axis=0, concat_axis=0, tiled=True)


def flip(array):
    return lax.ppermute(array, "core", [(0, 1), (1, 0)])


def swap(array, distance):
    return lax.ppermute(array, "y", [(i, i ^ distance) for i in range(4)])


def body(queries, keys, values, attn_out, out_grad, segment, span_order):
    kv_packed, counts = pl.pallas_call(
        pack_kv_kernel,
        out_shape=[bf16(16, 2 * R, D), jax.ShapeDtypeStruct((2,), jnp.int32)],
        out_specs=[IN_VMEM, IN_SMEM],
        compiler_params=pltpu.CompilerParams(vmem_limit_bytes=16 << 20),
    )(keys, values, segment.reshape(64, 128))
    own = exchange(kv_packed)
    q_packed = pl.pallas_call(
        pack_q_kernel,
        out_shape=bf16(16, 2 * QR + 16, D),
        in_specs=[IN_VMEM] * 3 + [ANYWHERE],
        compiler_params=pltpu.CompilerParams(vmem_limit_bytes=16 << 20),
    )(queries, attn_out, out_grad, own)
    qpay = exchange(q_packed)

    near_1 = swap(own, 1)
    near_3 = swap(own, 3)
    far_a = swap(near_3[:8], 1)
    far_b = swap(near_1[8:], 3)
    mine = (own, near_1, near_3, far_a, far_b)
    group = bf16(16, 2 * R, D)
    half = bf16(8, 2 * R, D)
    dq, keep_0, keep_1, keep_3, sum_a, sum_b, give_0, give_1, give_3, far_give = pl.pallas_call(
        attention_kernel,
        out_shape=[bf16(16, QR, D)] + [group] * 3 + [half] * 2 + [group] * 4,
        in_specs=[IN_SMEM] * 2 + [ANYWHERE] * 11,
        scratch_shapes=[
            pltpu.SMEM((NC * NT // 2 + W,), jnp.int32),
            pltpu.SMEM((NC * NT // 2 + W,), jnp.int32),
            pltpu.SMEM((NC * NT // 2 + NC + W,), jnp.int32),
            pltpu.SMEM((NC * NT // 2 + NC + W,), jnp.int32),
            pltpu.VMEM((NC + 1, C, D), BF16),
            pltpu.VMEM((NC + 1, C, D), BF16),
            pltpu.VMEM((16, 16, D), BF16),
            pltpu.VMEM((NT, 2, 2, R, 2 * D), BF16),
            pltpu.VMEM((NT, 2, 2, R, 2 * D), BF16),
            pltpu.VMEM((NT // 2, D, KB), BF16),
            pltpu.VMEM((NC + 1, 2 * D, C), BF16),
            pltpu.VMEM((NC + 1, 2 * D, C), BF16),
            pltpu.VMEM((NC, 1, C), F32),
            pltpu.VMEM((NC + 1, 8, C), F32),
            pltpu.VMEM((NT, 2, 2, R, D), F32),
            pltpu.VMEM((NT, 2, 2, R, D), F32),
            pltpu.VMEM((NC + 1, D, C), F32),
            pltpu.SemaphoreType.DMA,
            pltpu.SemaphoreType.DMA,
        ],
        compiler_params=pltpu.CompilerParams(vmem_limit_bytes=48 << 20),
    )(span_order, counts, qpay, *mine, *[flip(array) for array in mine])
    far_sum_a, far_sum_b = on_vmem(far_sum_kernel, [half, half], sum_a, sum_b, flip(far_give))
    from_1 = swap(far_sum_a, 1)
    from_3 = swap(far_sum_b, 3)
    to_1, to_3 = on_vmem(
        near_sum_kernel, [group] * 2, keep_1, flip(give_1), keep_3, flip(give_3), from_1, from_3
    )
    sums, query_grad = on_vmem(
        last_sum_kernel,
        [group, bf16(R, 8 * G * D)],
        keep_0,
        flip(give_0),
        swap(to_1, 1),
        swap(to_3, 3),
        exchange(dq),
    )
    key_grad, value_grad = on_vmem(unpack_kernel, [bf16(R, 8 * D)] * 2, exchange(sums))
    return query_grad, key_grad, value_grad


def solution(mesh):
    fine = Mesh(mesh.devices.reshape(4, 2, 2, 2, 4), AXES)
    rows = P(AXES, None)
    return jax.shard_map(
        body,
        mesh=fine,
        in_specs=(rows,) * 5 + (P(), P()),
        out_specs=(rows,) * 3,
        check_vma=False,
    )
```

```python
import jax
import jax.numpy as jnp
from jax import lax
from jax.experimental import pallas as pl
from jax.experimental.pallas import tpu as pltpu
from jax.sharding import Mesh, PartitionSpec as P

D = 128
G = 4
R = 64
HR = R // 2
SPAN = 256
NT = 32
KB = 2 * SPAN
QR = G * HR
C = 2 * QR
NC = 8
HC = 4
W = 4
WM = 2
SCALE = D**-0.5
HIDDEN = -1e30
LARGE = 2.0**90
F32 = jnp.float32
BF16 = jnp.bfloat16
AXES = ("z", "core", "xh", "xl", "y")
SPREAD = ("xh", "xl", "z")
NT_DIMS = (((1,), (1,)), ((), ()))


def spread_to(g, xl):
    return (g // 4 * 2 + xl) * 4 + g % 4


def head_columns(g, h):
    return slice((g * G + h) * D, (g * G + h + 1) * D)


def pack_kv_kernel(keys, values, segment, out, counts):
    counts[0] = jnp.sum((segment[...] == 0).astype(jnp.int32))
    counts[1] = jnp.sum((segment[...] != 2).astype(jnp.int32))
    for g in range(8):
        for xl in range(2):
            out[spread_to(g, xl), :R] = keys[:, g * D : (g + 1) * D]
            out[spread_to(g, xl), R:] = values[:, g * D : (g + 1) * D]


def pack_q_kernel(queries, saved, grads, after, out):
    del after
    ones = jnp.ones((8, D), BF16)
    row = lax.broadcasted_iota(jnp.int32, (16, D), 0)
    for g in range(8):
        for half in range(2):
            dest = spread_to(g, half)
            rows = slice(half * HR, (half + 1) * HR)
            prods = []
            for h in range(G):
                cols = head_columns(g, h)
                grad = grads[rows, cols]
                out[dest, h * HR : (h + 1) * HR] = queries[rows, cols]
                out[dest, QR + h * HR : QR + (h + 1) * HR] = grad
                prods.append(grad.astype(F32) * saved[rows, cols].astype(F32))
            prod = jnp.concatenate(prods, axis=0)
            high = prod.astype(BF16)
            low = (prod - high.astype(F32)).astype(BF16)
            dot = lax.dot_general(ones, high, NT_DIMS, preferred_element_type=F32)
            dot = dot + lax.dot_general(ones, low, NT_DIMS, preferred_element_type=F32)
            both = jnp.concatenate([dot, dot], axis=0)
            rounded = both.astype(BF16).astype(F32)
            out[dest, 2 * QR :] = jnp.where(row == 0, rounded, both - rounded).astype(BF16)


def span_id(xh, xl, y, zh):
    return ((xh * 2 + xl) * 4 + y) * 2 + zh


def attention_kernel(order, counts, qpay, *refs):
    pieces = refs[:10]
    dq_out, keep_0, keep_1, keep_3, sum_a, sum_b, give_0, give_1, give_3, far_give = refs[10:20]
    (plain_c, plain_b, masked_c, masked_b, q_s, do_s, d_s, k_s, v_s, kt_s, qa_s, ga_s) = refs[20:32]
    stash, m_s, l_s, dk_s, dv_s, dq_s, sem, value_sem = refs[32:]
    n0 = counts[0]
    n1 = counts[1]
    xl = lax.axis_index("xl")
    y = lax.axis_index("y")
    core = lax.axis_index("core")

    def place(dy, xh, xl, zh):
        return order[span_id(xh, xl, y ^ dy, zh)]

    copies = []
    value_copies = []
    for s in range(16):
        for part, dst in ((0, q_s), (1, do_s)):
            copies.append(
                pltpu.make_async_copy(
                    qpay.at[s, pl.ds(part * QR, QR)], dst.at[s // 2, pl.ds((s % 2) * QR, QR)], sem
                )
            )
    copies.append(pltpu.make_async_copy(qpay.at[:, pl.ds(2 * QR, 16)], d_s, sem))
    for number, piece in enumerate(pieces):
        from_core = core if number < 5 else 1 - core
        dy = (0, 1, 3, 2, 2)[number % 5]
        halves = ((0, 1), (0, 1), (0, 1), (0,), (1,))[number % 5]
        for at in range(4 * len(halves)):
            rank = place(dy, halves[at // 4], at // 2 % 2, at % 2)
            rows = piece.at[pl.ds(2 * at, 2)]
            copies.append(
                pltpu.make_async_copy(
                    rows.at[:, pl.ds(0, R)], k_s.at[rank, :, from_core, :, pl.ds(0, D)], sem
                )
            )
            value_copies.append(
                pltpu.make_async_copy(
                    rows.at[:, pl.ds(R, R)], v_s.at[rank, :, from_core, :, pl.ds(0, D)], value_sem
                )
            )
    for copy in copies + value_copies:
        copy.start()

    beside = lax.broadcasted_iota(jnp.int32, (1, 1, 1, 1, D), 4) < 3
    beside = jnp.broadcast_to(beside.astype(F32), (1, 2, 2, R, D)).astype(BF16)

    def put_beside(i, carry):
        k_s[pl.ds(i, 1), :, :, :, D:] = beside
        v_s[pl.ds(i, 1), :, :, :, D:] = beside
        return carry

    lax.fori_loop(0, NT, put_beside, 0)
    dk_s[...] = jnp.zeros_like(dk_s)
    dv_s[...] = jnp.zeros_like(dv_s)
    dq_s[...] = jnp.zeros_like(dq_s)

    def span_of(c):
        return order[span_id(c // 4, c // 2 % 2, y, c % 2)]

    def list_chunk(c, sizes):
        n_plain, n_masked = sizes
        span_q = span_of(c)
        first = span_q * SPAN
        has_second = first + (SPAN - 1) >= n1
        all_second = first >= n1
        n_full = span_q // 2
        hi = jnp.minimum(jnp.where(has_second, (n1 + (KB - 1)) // KB, 0), n_full)
        lo = jnp.minimum(jnp.where(has_second, n0 // KB, 0), hi)
        skip_at = jnp.where(all_second, (n0 + (KB - 1)) // KB, hi)
        skip_to = jnp.where(all_second, n1 // KB, 0)
        masked_c[c % HC] = c
        masked_b[c % HC] = n_full

        def put_plain(b, n):
            plain_c[n] = c
            plain_b[n] = b
            return n + 1

        def put_masked(b, n):
            hidden = (b >= skip_at) & (b < skip_to)
            masked_c[n] = c
            masked_b[n] = b
            return jnp.where(hidden, n, n + 1)

        n_plain = lax.fori_loop(0, lo, put_plain, n_plain)
        n_plain = lax.fori_loop(hi, n_full, put_plain, n_plain)
        return n_plain, lax.fori_loop(lo, hi, put_masked, n_masked)

    for copy in copies:
        copy.wait()

    def block_of(ref, b):
        return ref[pl.ds(2 * b, 2)].reshape(KB, 2 * D)

    def keys_of(b):
        return k_s[pl.ds(2 * b, 2), :, :, :, :D].reshape(KB, D)

    def turn_keys(b, carry):
        kt_s[b] = keys_of(b).T
        return carry

    lax.fori_loop(0, NT // 2, turn_keys, 0)

    def put_under(ref, c, *rows):
        number = lax.broadcasted_iota(jnp.int32, (D, C), 0)
        block = jnp.zeros((D, C), F32)
        for i, values in enumerate(rows):
            block = jnp.where(number == i, values, block)
        ref[c, D:] = block.astype(BF16)

    def turn_rows(c, carry):
        qa_s[c, :D] = q_s[c].T
        ga_s[c, :D] = do_s[c].T
        halves = [d_s[2 * c + half].astype(F32) for half in range(2)]
        put_under(
            ga_s,
            c,
            -jnp.concatenate([half[0:1] for half in halves], axis=1),
            -jnp.concatenate([half[1:2] for half in halves], axis=1),
        )
        return carry

    lax.fori_loop(0, NC, turn_rows, 0)
    qa_s[NC, :D] = jnp.zeros((D, C), BF16)
    put_under(qa_s, NC, jnp.full((1, C), HIDDEN, F32))
    ga_s[NC] = jnp.zeros((2 * D, C), BF16)
    l_s[...] = jnp.zeros_like(l_s)

    def seen(c, b):
        lane = lax.broadcasted_iota(jnp.int32, (1, C), 1)
        row = span_of(jnp.minimum(c, NC - 1)) * SPAN + core * R + xl * HR
        query_pos = row + (lane // QR) * (2 * R) + lane % HR
        key_pos = b * KB + lax.broadcasted_iota(jnp.int32, (KB, 1), 0)
        low = jnp.where(query_pos >= n1, n0, n1)
        return (key_pos <= query_pos) & ((key_pos < low) | (key_pos >= n1))

    def add_up(weights):
        parts = jnp.sum(weights.reshape(8, KB // 8, C), axis=0)
        return jnp.sum(parts.reshape(KB // 64, 8, C), axis=0)

    def raw_scores(c, b):
        return jnp.dot(keys_of(b), qa_s[c, :D], preferred_element_type=F32)

    def weights_of(c, b, masked):
        scores = jnp.dot(block_of(k_s, b), qa_s[c], preferred_element_type=F32)
        if masked:
            scores = jnp.where(seen(c, b), scores, HIDDEN)
        return jnp.exp(scores * SCALE)

    for copy in value_copies:
        copy.wait()

    def half_step(half, unused):
        n_plain, n_masked = lax.fori_loop(
            half * HC, half * HC + HC, list_chunk, (jnp.int32(0), jnp.int32(HC))
        )
        for i in range(W - 1):
            plain_c[n_plain + i] = NC
            plain_b[n_plain + i] = 0
        for i in range(WM - 1):
            masked_c[n_masked + i] = NC
            masked_b[n_masked + i] = 0
        n_plain = (n_plain + (W - 1)) // W * W
        n_masked = (n_masked + (WM - 1)) // WM * WM

        def masked_items(i):
            at = [WM * i + k for k in range(WM)]
            return [(n, masked_c[n], masked_b[n]) for n in at]

        def plain_items(i):
            at = [W * i + k for k in range(W)]
            return [(n_masked + n, plain_c[n], plain_b[n]) for n in at]

        def diagonal_step(i, carry):
            for n, c, b in masked_items(i):
                scores = jnp.where(seen(c, b), raw_scores(c, b), HIDDEN)
                top = jnp.max(scores, axis=0, keepdims=True).astype(BF16).astype(F32)
                put_under(qa_s, c, -top)
                m_s[c] = top * SCALE
                weights = jnp.exp((scores - top) * SCALE)
                stash[n] = weights.astype(BF16)
                l_s[c] = add_up(weights)
            return carry

        def weigh(items, masked):
            for n, c, b in items:
                weights = weights_of(c, b, masked)
                stash[n] = weights.astype(BF16)
                l_s[c] += add_up(weights)

        def masked_stats(i, carry):
            weigh(masked_items(i), True)
            return carry

        def plain_stats(i, carry):
            weigh(plain_items(i), False)
            return carry

        lax.fori_loop(0, HC // WM, diagonal_step, 0)
        lax.fori_loop(HC // WM, n_masked // WM, masked_stats, 0)
        lax.fori_loop(0, n_plain // W, plain_stats, 0)

        @pl.when(jnp.logical_not(jnp.max(l_s[...]) < LARGE))
        def _():
            def careful(c, b):
                scores = jnp.where(seen(c, b), raw_scores(c, b) * SCALE, HIDDEN)
                old = m_s[c]
                top = jnp.maximum(old, jnp.max(scores, axis=0, keepdims=True))
                l_s[c] = l_s[c] * jnp.exp(old - top) + add_up(jnp.exp(scores - top))
                m_s[c] = top

            def each(step):
                def masked(n, carry):
                    @pl.when(masked_c[n] < NC)
                    def _():
                        step(n, masked_c[n], masked_b[n])

                    return carry

                def plain(n, carry):
                    @pl.when(plain_c[n] < NC)
                    def _():
                        step(n_masked + n, plain_c[n], plain_b[n])

                    return carry

                lax.fori_loop(0, n_masked, masked, 0)
                lax.fori_loop(0, n_plain, plain, 0)

            def keep(n, c, b):
                scores = jnp.where(seen(c, b), raw_scores(c, b) * SCALE, HIDDEN)
                stash[n] = jnp.exp(scores - m_s[c]).astype(BF16)

            def start(c, carry):
                m_s[c] = jnp.full((1, C), HIDDEN, F32)
                l_s[c] = jnp.zeros((8, C), F32)
                return carry

            lax.fori_loop(half * HC, half * HC + HC, start, 0)
            each(lambda n, c, b: careful(c, b))
            each(keep)

        def divide(c, carry):
            share = 1.0 / jnp.sum(l_s[c], axis=0, keepdims=True)
            m_s[c] = share
            column = jnp.broadcast_to(share, (8, C)).T[:, :1]
            q_s[c] = (q_s[c].astype(F32) * column).astype(BF16)
            do_s[c] = (do_s[c].astype(F32) * column).astype(BF16)
            return carry

        lax.fori_loop(half * HC, half * HC + HC, divide, 0)

        def grad_step(items):
            for n, c, b in items:
                c = jnp.minimum(c, NC - 1)
                weights = stash[n]
                above = jnp.dot(block_of(v_s, b), ga_s[c], preferred_element_type=F32)
                score_grad = (weights.astype(F32) * above).astype(BF16)
                for ref, term in (
                    (dv_s, jnp.dot(weights, do_s[c], preferred_element_type=F32)),
                    (dk_s, jnp.dot(score_grad, q_s[c], preferred_element_type=F32)),
                ):
                    ref[pl.ds(2 * b, 2)] += term.reshape(2, 2, 2, R, D)
                dq_s[c] += jnp.dot(kt_s[b], score_grad, preferred_element_type=F32)

        def masked_grads(i, carry):
            grad_step(masked_items(i))
            return carry

        def plain_grads(i, carry):
            grad_step(plain_items(i))
            return carry

        lax.fori_loop(0, n_masked // WM, masked_grads, 0)
        lax.fori_loop(0, n_plain // W, plain_grads, 0)
        return unused

    lax.fori_loop(0, NC // HC, half_step, 0)

    def finish(c, carry):
        dq = (dq_s[c] * (m_s[c] * SCALE)).T.astype(BF16)
        dq_out[2 * c] = dq[:QR]
        dq_out[2 * c + 1] = dq[QR:]
        return carry

    lax.fori_loop(0, NC, finish, 0)

    for from_core, group in (
        (core, ((0, keep_0, 0), (1, keep_1, 0), (3, keep_3, 0), (2, sum_a, 0), (2, sum_b, 1))),
        (1 - core, ((0, give_0, 0), (1, give_1, 0), (3, give_3, 0), (2, far_give, 0))),
    ):
        for dy, out, first_xh in group:
            for at in range(out.shape[0] // 2):
                rank = place(dy, first_xh + at // 4, at // 2 % 2, at % 2)
                rows = slice(2 * at, 2 * at + 2)
                out[rows, :R] = (dk_s[rank, :, from_core] * SCALE).astype(BF16)
                out[rows, R:] = dv_s[rank, :, from_core].astype(BF16)


def far_sum_kernel(sum_a, sum_b, got, out_a, out_b):
    out_a[...] = (sum_a[...].astype(F32) + got[:8].astype(F32)).astype(BF16)
    out_b[...] = (sum_b[...].astype(F32) + got[8:].astype(F32)).astype(BF16)


def near_sum_kernel(sum_1, got_1, sum_3, got_3, from_1, from_3, out_1, out_3):
    for rows, with_from in ((slice(0, 8), 3), (slice(8, 16), 1)):
        for number, keep, got, came, out in (
            (1, sum_1, got_1, from_3, out_1),
            (3, sum_3, got_3, from_1, out_3),
        ):
            total = keep[rows].astype(F32) + got[rows].astype(F32)
            if number == with_from:
                total = total + came[...].astype(F32)
            out[rows] = total.astype(BF16)


def last_sum_kernel(keep, got, near_1, near_3, dq, sums, query_grad):
    total = keep[...].astype(F32) + got[...].astype(F32)
    total = total + (near_1[...].astype(F32) + near_3[...].astype(F32))
    sums[...] = total.astype(BF16)
    for g in range(8):
        for half in range(2):
            rows = slice(half * HR, (half + 1) * HR)
            for h in range(G):
                query_grad[rows, head_columns(g, h)] = dq[spread_to(g, half), h * HR : (h + 1) * HR]


def unpack_kernel(got, key_grad, value_grad):
    for g in range(8):
        for start, out in ((0, key_grad), (R, value_grad)):
            total = got[spread_to(g, 0), start : start + R].astype(F32)
            total = total + got[spread_to(g, 1), start : start + R].astype(F32)
            out[:, g * D : (g + 1) * D] = total.astype(BF16)


def bf16(*shape):
    return jax.ShapeDtypeStruct(shape, BF16)


def on_vmem(kernel, outs, *args):
    return pl.pallas_call(
        kernel,
        out_shape=outs,
        compiler_params=pltpu.CompilerParams(vmem_limit_bytes=16 << 20),
    )(*args)


IN_SMEM = pl.BlockSpec(memory_space=pltpu.SMEM)
IN_VMEM = pl.BlockSpec(memory_space=pltpu.VMEM)
ANYWHERE = pl.BlockSpec(memory_space=pl.ANY)


def exchange(array):
    return lax.all_to_all(array, SPREAD, split_axis=0, concat_axis=0, tiled=True)


def flip(array):
    return lax.ppermute(array, "core", [(0, 1), (1, 0)])


def swap(array, distance):
    return lax.ppermute(array, "y", [(i, i ^ distance) for i in range(4)])


def body(queries, keys, values, attn_out, out_grad, segment, span_order):
    kv_packed, counts = pl.pallas_call(
        pack_kv_kernel,
        out_shape=[bf16(16, 2 * R, D), jax.ShapeDtypeStruct((2,), jnp.int32)],
        out_specs=[IN_VMEM, IN_SMEM],
        compiler_params=pltpu.CompilerParams(vmem_limit_bytes=16 << 20),
    )(keys, values, segment.reshape(64, 128))
    own = exchange(kv_packed)
    q_packed = pl.pallas_call(
        pack_q_kernel,
        out_shape=bf16(16, 2 * QR + 16, D),
        in_specs=[IN_VMEM] * 3 + [ANYWHERE],
        compiler_params=pltpu.CompilerParams(vmem_limit_bytes=16 << 20),
    )(queries, attn_out, out_grad, own)
    qpay = exchange(q_packed)

    near_1 = swap(own, 1)
    near_3 = swap(own, 3)
    far_a = swap(near_3[:8], 1)
    far_b = swap(near_1[8:], 3)
    mine = (own, near_1, near_3, far_a, far_b)
    group = bf16(16, 2 * R, D)
    half = bf16(8, 2 * R, D)
    dq, keep_0, keep_1, keep_3, sum_a, sum_b, give_0, give_1, give_3, far_give = pl.pallas_call(
        attention_kernel,
        out_shape=[bf16(16, QR, D)] + [group] * 3 + [half] * 2 + [group] * 4,
        in_specs=[IN_SMEM] * 2 + [ANYWHERE] * 11,
        scratch_shapes=[
            pltpu.SMEM((HC * NT // 2 + W,), jnp.int32),
            pltpu.SMEM((HC * NT // 2 + W,), jnp.int32),
            pltpu.SMEM((HC * NT // 2 + HC + W,), jnp.int32),
            pltpu.SMEM((HC * NT // 2 + HC + W,), jnp.int32),
            pltpu.VMEM((NC, C, D), BF16),
            pltpu.VMEM((NC, C, D), BF16),
            pltpu.VMEM((16, 16, D), BF16),
            pltpu.VMEM((NT, 2, 2, R, 2 * D), BF16),
            pltpu.VMEM((NT, 2, 2, R, 2 * D), BF16),
            pltpu.VMEM((NT // 2, D, KB), BF16),
            pltpu.VMEM((NC + 1, 2 * D, C), BF16),
            pltpu.VMEM((NC + 1, 2 * D, C), BF16),
            pltpu.VMEM((HC * NT // 2 + W + WM, KB, C), BF16),
            pltpu.VMEM((NC, 1, C), F32),
            pltpu.VMEM((NC + 1, 8, C), F32),
            pltpu.VMEM((NT, 2, 2, R, D), F32),
            pltpu.VMEM((NT, 2, 2, R, D), F32),
            pltpu.VMEM((NC, D, C), F32),
            pltpu.SemaphoreType.DMA,
            pltpu.SemaphoreType.DMA,
        ],
        compiler_params=pltpu.CompilerParams(vmem_limit_bytes=56 << 20),
    )(span_order, counts, qpay, *mine, *[flip(array) for array in mine])
    far_sum_a, far_sum_b = on_vmem(far_sum_kernel, [half, half], sum_a, sum_b, flip(far_give))
    from_1 = swap(far_sum_a, 1)
    from_3 = swap(far_sum_b, 3)
    to_1, to_3 = on_vmem(
        near_sum_kernel, [group] * 2, keep_1, flip(give_1), keep_3, flip(give_3), from_1, from_3
    )
    sums, query_grad = on_vmem(
        last_sum_kernel,
        [group, bf16(R, 8 * G * D)],
        keep_0,
        flip(give_0),
        swap(to_1, 1),
        swap(to_3, 3),
        exchange(dq),
    )
    key_grad, value_grad = on_vmem(unpack_kernel, [bf16(R, 8 * D)] * 2, exchange(sums))
    return query_grad, key_grad, value_grad


def solution(mesh):
    fine = Mesh(mesh.devices.reshape(4, 2, 2, 2, 4), AXES)
    rows = P(AXES, None)
    return jax.shard_map(
        body,
        mesh=fine,
        in_specs=(rows,) * 5 + (P(), P()),
        out_specs=(rows,) * 3,
        check_vma=False,
    )
```

```python
import jax
import jax.numpy as jnp
from jax import lax
from jax.experimental import pallas as pl
from jax.experimental.pallas import tpu as pltpu
from jax.sharding import Mesh, PartitionSpec as P

D = 128
G = 4
R = 64
HR = R // 2
SPAN = 256
NT = 32
KB = 2 * SPAN
KS = 2 * KB
QR = G * HR
C = 2 * QR
NC = 8
SCALE = D**-0.5
HIDDEN = -1e30
LARGE = 2.0**90
F32 = jnp.float32
BF16 = jnp.bfloat16
AXES = ("z", "core", "xh", "xl", "y")
SPREAD = ("xh", "xl", "z")
NT_DIMS = (((1,), (1,)), ((), ()))


def spread_to(g, xl):
    return (g // 4 * 2 + xl) * 4 + g % 4


def head_columns(g, h):
    return slice((g * G + h) * D, (g * G + h + 1) * D)


def pack_kv_kernel(keys, values, segment, out, counts):
    counts[0] = jnp.sum((segment[...] == 0).astype(jnp.int32))
    counts[1] = jnp.sum((segment[...] != 2).astype(jnp.int32))
    for g in range(8):
        for xl in range(2):
            out[spread_to(g, xl), :R] = keys[:, g * D : (g + 1) * D]
            out[spread_to(g, xl), R:] = values[:, g * D : (g + 1) * D]


def pack_q_kernel(queries, saved, grads, after, out):
    del after
    ones = jnp.ones((8, D), BF16)
    row = lax.broadcasted_iota(jnp.int32, (16, D), 0)
    for g in range(8):
        for half in range(2):
            dest = spread_to(g, half)
            rows = slice(half * HR, (half + 1) * HR)
            prods = []
            for h in range(G):
                cols = head_columns(g, h)
                grad = grads[rows, cols]
                out[dest, h * HR : (h + 1) * HR] = queries[rows, cols]
                out[dest, QR + h * HR : QR + (h + 1) * HR] = grad
                prods.append(grad.astype(F32) * saved[rows, cols].astype(F32))
            prod = jnp.concatenate(prods, axis=0)
            high = prod.astype(BF16)
            low = (prod - high.astype(F32)).astype(BF16)
            dot = lax.dot_general(ones, high, NT_DIMS, preferred_element_type=F32)
            dot = dot + lax.dot_general(ones, low, NT_DIMS, preferred_element_type=F32)
            both = jnp.concatenate([dot, dot], axis=0)
            rounded = both.astype(BF16).astype(F32)
            out[dest, 2 * QR :] = jnp.where(row == 0, rounded, both - rounded).astype(BF16)


def span_id(xh, xl, y, zh):
    return ((xh * 2 + xl) * 4 + y) * 2 + zh


def attention_kernel(order, counts, qpay, *refs):
    pieces = refs[:10]
    dq_out, keep_0, keep_1, keep_3, sum_a, sum_b, give_0, give_1, give_3, far_give = refs[10:20]
    (todo, plain_c, plain_0, plain_1, masked_c, masked_0, masked_1) = refs[20:27]
    qg_s, kv_s, kt_s, ones_s, qa_s, ga_s, m_s, l_s, dk_s, dv_s, dq_s, sem = refs[27:]
    n0 = counts[0]
    n1 = counts[1]
    xl = lax.axis_index("xl")
    y = lax.axis_index("y")
    core = lax.axis_index("core")

    def place(dy, xh, xl, zh):
        return order[span_id(xh, xl, y ^ dy, zh)]

    copies = [pltpu.make_async_copy(qpay, qg_s, sem)]
    for number, piece in enumerate(pieces):
        from_core = core if number < 5 else 1 - core
        dy = (0, 1, 3, 2, 2)[number % 5]
        halves = ((0, 1), (0, 1), (0, 1), (0,), (1,))[number % 5]
        for at in range(4 * len(halves)):
            rank = place(dy, halves[at // 4], at // 2 % 2, at % 2)
            copies.append(
                pltpu.make_async_copy(
                    piece.at[pl.ds(2 * at, 2)], kv_s.at[rank, :, from_core], sem
                )
            )
    for copy in copies:
        copy.start()

    ones_s[...] = (lax.broadcasted_iota(jnp.int32, (KS, D), 1) < 3).astype(F32).astype(BF16)
    dk_s[...] = jnp.zeros_like(dk_s)
    dv_s[...] = jnp.zeros_like(dv_s)
    dq_s[...] = jnp.zeros_like(dq_s)
    kv_s[NT:] = jnp.zeros((2, 2, 2, 2 * R, D), BF16)
    kt_s[NT // 2] = jnp.zeros((D, KB), BF16)

    def span_of(c):
        return order[span_id(c // 4, c // 2 % 2, y, c % 2)]

    def list_chunk(c, sizes):
        n_plain, n_masked = sizes
        span_q = span_of(c)
        first = span_q * SPAN
        has_second = first + (SPAN - 1) >= n1
        all_second = first >= n1
        n_full = span_q // 2
        hi = jnp.minimum(jnp.where(has_second, (n1 + (KB - 1)) // KB, 0), n_full)
        lo = jnp.minimum(jnp.where(has_second, n0 // KB, 0), hi)
        skip_at = jnp.where(all_second, (n0 + (KB - 1)) // KB, hi)
        skip_to = jnp.where(all_second, n1 // KB, 0)
        all_plain = lo + n_full - hi

        def plain_at(i):
            return jnp.where(i < lo, i, i + (hi - lo))

        def put_plain(i, n):
            plain_c[n] = c
            plain_0[n] = plain_at(2 * i)
            plain_1[n] = plain_at(2 * i + 1)
            return n + 1

        def put_todo(b, n):
            hidden = (b >= skip_at) & (b < skip_to)
            todo[n] = b
            return jnp.where(hidden, n, n + 1)

        n_plain = lax.fori_loop(0, all_plain // 2, put_plain, n_plain)
        todo[0] = n_full
        n_todo = lax.fori_loop(lo, hi, put_todo, jnp.int32(1))
        todo[n_todo] = plain_at(all_plain - 1)
        n_todo = n_todo + all_plain % 2
        todo[n_todo] = NT // 2
        masked_c[c] = c
        masked_0[c] = todo[0]
        masked_1[c] = todo[1]

        def put_masked(i, n):
            masked_c[n] = c
            masked_0[n] = todo[2 * i]
            masked_1[n] = todo[2 * i + 1]
            return n + 1

        return n_plain, lax.fori_loop(1, (n_todo + 1) // 2, put_masked, n_masked)

    n_plain, n_masked = lax.fori_loop(0, NC, list_chunk, (jnp.int32(0), jnp.int32(NC)))
    plain_c[n_plain] = NC
    plain_0[n_plain] = 0
    plain_1[n_plain] = 0

    def plain_item(n):
        return plain_c[n], plain_0[n], plain_1[n]

    def masked_item(n):
        return masked_c[n], masked_0[n], masked_1[n]

    for copy in copies:
        copy.wait()

    def block_of(b, part):
        return kv_s[pl.ds(2 * b, 2), :, :, part * R : (part + 1) * R].reshape(KB, D)

    def rows_of(item, part):
        _, b0, b1 = item
        return jnp.concatenate([block_of(b0, part), block_of(b1, part)], axis=0)

    def with_ones(rows):
        return jnp.concatenate([rows, ones_s[...]], axis=1)

    def query_rows(c, part):
        rows = slice(part * QR, (part + 1) * QR)
        return jnp.concatenate([qg_s[2 * c, rows], qg_s[2 * c + 1, rows]], axis=0)

    def turn_keys(b, carry):
        kt_s[b] = block_of(b, 0).T
        return carry

    lax.fori_loop(0, NT // 2, turn_keys, 0)

    def put_under(ref, c, *rows):
        number = lax.broadcasted_iota(jnp.int32, (D, C), 0)
        block = jnp.zeros((D, C), F32)
        for i, values in enumerate(rows):
            block = jnp.where(number == i, values, block)
        ref[c, D:] = block.astype(BF16)

    def turn_rows(c, carry):
        qa_s[c, :D] = query_rows(c, 0).T
        ga_s[c, :D] = query_rows(c, 1).T
        halves = [qg_s[2 * c + half, 2 * QR :].astype(F32) for half in range(2)]
        put_under(
            ga_s,
            c,
            -jnp.concatenate([half[0:1] for half in halves], axis=1),
            -jnp.concatenate([half[1:2] for half in halves], axis=1),
        )
        return carry

    lax.fori_loop(0, NC, turn_rows, 0)
    qa_s[NC, :D] = jnp.zeros((D, C), BF16)
    put_under(qa_s, NC, jnp.full((1, C), HIDDEN, F32))
    l_s[NC] = jnp.zeros((8, C), F32)

    def seen(item):
        c, b0, b1 = item
        lane = lax.broadcasted_iota(jnp.int32, (1, C), 1)
        start = span_of(c) * SPAN + core * R + xl * HR
        query_pos = start + (lane // QR) * (2 * R) + lane % HR
        row = lax.broadcasted_iota(jnp.int32, (KS, 1), 0)
        key_pos = jnp.where(row < KB, b0 * KB, b1 * KB - KB) + row
        low = jnp.where(query_pos >= n1, n0, n1)
        return (key_pos <= query_pos) & ((key_pos < low) | (key_pos >= n1))

    def add_up(weights):
        parts = jnp.sum(weights.reshape(16, KS // 16, C), axis=0)
        return jnp.sum(parts.reshape(KS // 128, 8, C), axis=0)

    def raw_scores(item):
        scores = jnp.dot(rows_of(item, 0), qa_s[item[0], :D], preferred_element_type=F32)
        return jnp.where(seen(item), scores, HIDDEN)

    def weights_of(item, masked):
        scores = jnp.dot(with_ones(rows_of(item, 0)), qa_s[item[0]], preferred_element_type=F32)
        if masked:
            scores = jnp.where(seen(item), scores, HIDDEN)
        return jnp.exp(scores * SCALE)

    def diagonal_step(i, carry):
        items = [masked_item(2 * i + k) for k in range(2)]
        found = []
        for item in items:
            scores = raw_scores(item)
            top = jnp.max(scores, axis=0, keepdims=True).astype(BF16).astype(F32)
            found.append((top, add_up(jnp.exp((scores - top) * SCALE))))
        for (c, _, _), (top, total) in zip(items, found):
            put_under(qa_s, c, -top)
            m_s[c] = top * SCALE
            l_s[c] = total
        return carry

    lax.fori_loop(0, NC // 2, diagonal_step, 0)

    def add_weights(items, masked):
        parts = [add_up(weights_of(item, masked)) for item in items]
        for (c, _, _), part in zip(items, parts):
            l_s[c] += part

    def masked_stats(n, carry):
        add_weights([masked_item(n)], True)
        return carry

    def plain_stats(i, carry):
        add_weights([plain_item(2 * i), plain_item(2 * i + 1)], False)
        return carry

    lax.fori_loop(NC, n_masked, masked_stats, 0)
    lax.fori_loop(0, (n_plain + 1) // 2, plain_stats, 0)

    @pl.when(jnp.logical_not(jnp.max(l_s[...]) < LARGE))
    def _():
        def careful(item):
            c = item[0]
            scores = raw_scores(item) * SCALE
            old = m_s[c]
            top = jnp.maximum(old, jnp.max(scores, axis=0, keepdims=True))
            l_s[c] = l_s[c] * jnp.exp(old - top) + add_up(jnp.exp(scores - top))
            m_s[c] = top

        def careful_masked(n, carry):
            c = masked_c[n]

            @pl.when(n < NC)
            def _():
                m_s[c] = jnp.full((1, C), HIDDEN, F32)
                l_s[c] = jnp.zeros((8, C), F32)

            careful(masked_item(n))
            return carry

        def careful_plain(n, carry):
            careful(plain_item(n))
            return carry

        lax.fori_loop(0, n_masked, careful_masked, 0)
        lax.fori_loop(0, n_plain, careful_plain, 0)

    def put_logsum(c, carry):
        logsum = m_s[c] + jnp.log(jnp.sum(l_s[c], axis=0, keepdims=True))
        rest = logsum * (1.0 / SCALE)
        rows = []
        for _ in range(3):
            part = rest.astype(BF16).astype(F32)
            rows.append(-part)
            rest = rest - part
        put_under(qa_s, c, *rows)
        return carry

    lax.fori_loop(0, NC, put_logsum, 0)

    def grad_step(item, masked):
        c, b0, b1 = item
        above = jnp.dot(with_ones(rows_of(item, 1)), ga_s[c], preferred_element_type=F32)
        weights = weights_of(item, masked)
        score_grad = (weights * above).astype(BF16)
        value_term = jnp.dot(weights.astype(BF16), query_rows(c, 1), preferred_element_type=F32)
        key_term = jnp.dot(score_grad, query_rows(c, 0), preferred_element_type=F32)
        keys_turned = jnp.concatenate([kt_s[b0], kt_s[b1]], axis=1)
        query_term = jnp.dot(keys_turned, score_grad, preferred_element_type=F32)
        sums = []
        for ref, term in ((dv_s, value_term), (dk_s, key_term)):
            for b, part in ((b0, term[:KB]), (b1, term[KB:])):
                at = pl.ds(2 * b, 2)
                sums.append((ref, at, ref[at] + part.reshape(2, 2, 2, R, D)))
        query_sum = dq_s[c] + query_term
        for ref, at, value in sums:
            ref[at] = value
        dq_s[c] = query_sum

    def masked_grads(n, carry):
        grad_step(masked_item(n), True)
        return carry

    def plain_grads(n, carry):
        grad_step(plain_item(n), False)
        return carry

    lax.fori_loop(0, n_masked, masked_grads, 0)
    lax.fori_loop(0, n_plain, plain_grads, 0)

    def finish(c, carry):
        dq = (dq_s[c] * SCALE).T.astype(BF16)
        dq_out[2 * c] = dq[:QR]
        dq_out[2 * c + 1] = dq[QR:]
        return carry

    lax.fori_loop(0, NC, finish, 0)

    for from_core, group in (
        (core, ((0, keep_0, 0), (1, keep_1, 0), (3, keep_3, 0), (2, sum_a, 0), (2, sum_b, 1))),
        (1 - core, ((0, give_0, 0), (1, give_1, 0), (3, give_3, 0), (2, far_give, 0))),
    ):
        for dy, out, first_xh in group:
            for at in range(out.shape[0] // 2):
                rank = place(dy, first_xh + at // 4, at // 2 % 2, at % 2)
                rows = slice(2 * at, 2 * at + 2)
                out[rows, :R] = (dk_s[rank, :, from_core] * SCALE).astype(BF16)
                out[rows, R:] = dv_s[rank, :, from_core].astype(BF16)


def far_sum_kernel(sum_a, sum_b, got, out_a, out_b):
    out_a[...] = (sum_a[...].astype(F32) + got[:8].astype(F32)).astype(BF16)
    out_b[...] = (sum_b[...].astype(F32) + got[8:].astype(F32)).astype(BF16)


def near_sum_kernel(sum_1, got_1, sum_3, got_3, from_1, from_3, out_1, out_3):
    for rows, with_from in ((slice(0, 8), 3), (slice(8, 16), 1)):
        for number, keep, got, came, out in (
            (1, sum_1, got_1, from_3, out_1),
            (3, sum_3, got_3, from_1, out_3),
        ):
            total = keep[rows].astype(F32) + got[rows].astype(F32)
            if number == with_from:
                total = total + came[...].astype(F32)
            out[rows] = total.astype(BF16)


def last_sum_kernel(keep, got, near_1, near_3, dq, sums, query_grad):
    total = keep[...].astype(F32) + got[...].astype(F32)
    total = total + (near_1[...].astype(F32) + near_3[...].astype(F32))
    sums[...] = total.astype(BF16)
    for g in range(8):
        for half in range(2):
            rows = slice(half * HR, (half + 1) * HR)
            for h in range(G):
                query_grad[rows, head_columns(g, h)] = dq[spread_to(g, half), h * HR : (h + 1) * HR]


def unpack_kernel(got, key_grad, value_grad):
    for g in range(8):
        for start, out in ((0, key_grad), (R, value_grad)):
            total = got[spread_to(g, 0), start : start + R].astype(F32)
            total = total + got[spread_to(g, 1), start : start + R].astype(F32)
            out[:, g * D : (g + 1) * D] = total.astype(BF16)


def bf16(*shape):
    return jax.ShapeDtypeStruct(shape, BF16)


def on_vmem(kernel, outs, *args):
    return pl.pallas_call(
        kernel,
        out_shape=outs,
        compiler_params=pltpu.CompilerParams(vmem_limit_bytes=16 << 20),
    )(*args)


IN_SMEM = pl.BlockSpec(memory_space=pltpu.SMEM)
IN_VMEM = pl.BlockSpec(memory_space=pltpu.VMEM)
ANYWHERE = pl.BlockSpec(memory_space=pl.ANY)


def exchange(array):
    return lax.all_to_all(array, SPREAD, split_axis=0, concat_axis=0, tiled=True)


def flip(array):
    return lax.ppermute(array, "core", [(0, 1), (1, 0)])


def swap(array, distance):
    return lax.ppermute(array, "y", [(i, i ^ distance) for i in range(4)])


def body(queries, keys, values, attn_out, out_grad, segment, span_order):
    kv_packed, counts = pl.pallas_call(
        pack_kv_kernel,
        out_shape=[bf16(16, 2 * R, D), jax.ShapeDtypeStruct((2,), jnp.int32)],
        out_specs=[IN_VMEM, IN_SMEM],
        compiler_params=pltpu.CompilerParams(vmem_limit_bytes=16 << 20),
    )(keys, values, segment.reshape(64, 128))
    own = exchange(kv_packed)
    q_packed = pl.pallas_call(
        pack_q_kernel,
        out_shape=bf16(16, 2 * QR + 16, D),
        in_specs=[IN_VMEM] * 3 + [ANYWHERE],
        compiler_params=pltpu.CompilerParams(vmem_limit_bytes=16 << 20),
    )(queries, attn_out, out_grad, own)
    qpay = exchange(q_packed)

    near_1 = swap(own, 1)
    near_3 = swap(own, 3)
    far_a = swap(near_3[:8], 1)
    far_b = swap(near_1[8:], 3)
    mine = (own, near_1, near_3, far_a, far_b)
    group = bf16(16, 2 * R, D)
    half = bf16(8, 2 * R, D)
    dq, keep_0, keep_1, keep_3, sum_a, sum_b, give_0, give_1, give_3, far_give = pl.pallas_call(
        attention_kernel,
        out_shape=[bf16(16, QR, D)] + [group] * 3 + [half] * 2 + [group] * 4,
        in_specs=[IN_SMEM] * 2 + [ANYWHERE] * 11,
        scratch_shapes=[
            pltpu.SMEM((NT // 2 + 3,), jnp.int32),
            *[pltpu.SMEM((NC * NT // 4 + 1,), jnp.int32)] * 3,
            *[pltpu.SMEM((NC * NT // 4 + NC,), jnp.int32)] * 3,
            pltpu.VMEM((16, 2 * QR + 16, D), BF16),
            pltpu.VMEM((NT + 2, 2, 2, 2 * R, D), BF16),
            pltpu.VMEM((NT // 2 + 1, D, KB), BF16),
            pltpu.VMEM((KS, D), BF16),
            pltpu.VMEM((NC + 1, 2 * D, C), BF16),
            pltpu.VMEM((NC, 2 * D, C), BF16),
            pltpu.VMEM((NC, 1, C), F32),
            pltpu.VMEM((NC + 1, 8, C), F32),
            pltpu.VMEM((NT + 2, 2, 2, R, D), F32),
            pltpu.VMEM((NT + 2, 2, 2, R, D), F32),
            pltpu.VMEM((NC, D, C), F32),
            pltpu.SemaphoreType.DMA,
        ],
        compiler_params=pltpu.CompilerParams(vmem_limit_bytes=48 << 20),
    )(span_order, counts, qpay, *mine, *[flip(array) for array in mine])
    far_sum_a, far_sum_b = on_vmem(far_sum_kernel, [half, half], sum_a, sum_b, flip(far_give))
    from_1 = swap(far_sum_a, 1)
    from_3 = swap(far_sum_b, 3)
    to_1, to_3 = on_vmem(
        near_sum_kernel, [group] * 2, keep_1, flip(give_1), keep_3, flip(give_3), from_1, from_3
    )
    sums, query_grad = on_vmem(
        last_sum_kernel,
        [group, bf16(R, 8 * G * D)],
        keep_0,
        flip(give_0),
        swap(to_1, 1),
        swap(to_3, 3),
        exchange(dq),
    )
    key_grad, value_grad = on_vmem(unpack_kernel, [bf16(R, 8 * D)] * 2, exchange(sums))
    return query_grad, key_grad, value_grad


def solution(mesh):
    fine = Mesh(mesh.devices.reshape(4, 2, 2, 2, 4), AXES)
    rows = P(AXES, None)
    return jax.shard_map(
        body,
        mesh=fine,
        in_specs=(rows,) * 5 + (P(), P()),
        out_specs=(rows,) * 3,
        check_vma=False,
    )
```

```python
import math

import jax
import jax.numpy as jnp
from jax import lax
from jax.experimental import pallas as pl
from jax.experimental.pallas import tpu as pltpu
from jax.sharding import Mesh, PartitionSpec as P

D = 128
G = 4
R = 64
HR = R // 2
SPAN = 256
NT = 32
KB = 2 * SPAN
KS = 2 * KB
QR = G * HR
C = 2 * QR
NC = 8
SCALE = D**-0.5
EXP_SCALE = SCALE * math.log2(math.e)
HIDDEN = -1e30
LARGE = 2.0**90
F32 = jnp.float32
BF16 = jnp.bfloat16
AXES = ("z", "core", "xh", "xl", "y")
HEADS = ("xh", "z")
SPREAD = ("xh", "xl", "z")
NT_DIMS = (((1,), (1,)), ((), ()))


def spread_to(g, xl):
    return (g // 4 * 2 + xl) * 4 + g % 4


def head_columns(g, h):
    return slice((g * G + h) * D, (g * G + h + 1) * D)


def pack_kv_kernel(keys, values, out, keys_s, values_s, sems):
    copies = [
        pltpu.make_async_copy(keys, keys_s, sems.at[0]),
        pltpu.make_async_copy(values, values_s, sems.at[1]),
    ]
    for copy in copies:
        copy.start()
    for copy, held, start in zip(copies, (keys_s, values_s), (0, R)):
        copy.wait()
        for g in range(8):
            out[g, start : start + R] = held[:, g * D : (g + 1) * D]


def pack_q_kernel(queries, saved, grads, segment, after, out, counts):
    del after
    counts[0] = jnp.sum((segment[...] == 0).astype(jnp.int32))
    counts[1] = jnp.sum((segment[...] != 2).astype(jnp.int32))
    ones = jnp.ones((8, D), BF16)
    row = lax.broadcasted_iota(jnp.int32, (16, D), 0)
    for g in range(8):
        for half in range(2):
            dest = spread_to(g, half)
            rows = slice(half * HR, (half + 1) * HR)
            prods = []
            for h in range(G):
                cols = head_columns(g, h)
                grad = grads[rows, cols]
                out[dest, h * HR : (h + 1) * HR] = queries[rows, cols]
                out[dest, QR + h * HR : QR + (h + 1) * HR] = grad
                prods.append(grad.astype(F32) * saved[rows, cols].astype(F32))
            prod = jnp.concatenate(prods, axis=0)
            high = prod.astype(BF16)
            low = (prod - high.astype(F32)).astype(BF16)
            dot = lax.dot_general(ones, high, NT_DIMS, preferred_element_type=F32)
            dot = dot + lax.dot_general(ones, low, NT_DIMS, preferred_element_type=F32)
            both = jnp.concatenate([dot, dot], axis=0)
            rounded = both.astype(BF16).astype(F32)
            out[dest, 2 * QR :] = jnp.where(row == 0, rounded, both - rounded).astype(BF16)


def span_id(xh, xl, y, zh):
    return ((xh * 2 + xl) * 4 + y) * 2 + zh


def attention_kernel(order, counts, qpay, *refs):
    pieces = refs[:16]
    dq_out, keep_0, far_a, far_b, near_1a, near_3b, near_1b, near_3a = refs[16:24]
    give_0, give_far, give_early, give_late = refs[24:28]
    (todo, plain_c, plain_0, plain_1, masked_c, masked_0, masked_1) = refs[28:35]
    qg_s, kv_s, kt_s, ones_s, qa_s, ga_s, m_s, l_s, dk_s, dv_s, dq_s, sem = refs[35:]
    n0 = counts[0]
    n1 = counts[1]
    xl = lax.axis_index("xl")
    y = lax.axis_index("y")
    core = lax.axis_index("core")

    def place(dy, xh, xl, zh):
        return order[span_id(xh, xl, y ^ dy, zh)]

    copies = [pltpu.make_async_copy(qpay, qg_s, sem)]
    for number, piece in enumerate(pieces):
        from_core = core if number < 8 else 1 - core
        from_xl = xl if number % 8 < 4 else 1 - xl
        for at in range(4):
            rank = place((0, 1, 3, 2)[number % 4], at // 2, from_xl, at % 2)
            copies.append(
                pltpu.make_async_copy(
                    piece.at[pl.ds(2 * at, 2)], kv_s.at[rank, :, from_core], sem
                )
            )
    for copy in copies:
        copy.start()

    ones_s[...] = (lax.broadcasted_iota(jnp.int32, (KS, D), 1) < 3).astype(F32).astype(BF16)
    dk_s[...] = jnp.zeros_like(dk_s)
    dv_s[...] = jnp.zeros_like(dv_s)
    dq_s[...] = jnp.zeros_like(dq_s)
    kv_s[NT:] = jnp.zeros((2, 2, 2, 2 * R, D), BF16)
    kt_s[NT // 2] = jnp.zeros((D, KB), BF16)

    def span_of(c):
        return order[span_id(c // 4, c // 2 % 2, y, c % 2)]

    def list_chunk(c, sizes):
        n_plain, n_masked = sizes
        span_q = span_of(c)
        first = span_q * SPAN
        has_second = first + (SPAN - 1) >= n1
        all_second = first >= n1
        n_full = span_q // 2
        hi = jnp.minimum(jnp.where(has_second, (n1 + (KB - 1)) // KB, 0), n_full)
        lo = jnp.minimum(jnp.where(has_second, n0 // KB, 0), hi)
        skip_at = jnp.where(all_second, (n0 + (KB - 1)) // KB, hi)
        skip_to = jnp.where(all_second, n1 // KB, 0)
        all_plain = lo + n_full - hi

        def plain_at(i):
            return jnp.where(i < lo, i, i + (hi - lo))

        def put_plain(i, n):
            plain_c[n] = c
            plain_0[n] = plain_at(2 * i)
            plain_1[n] = plain_at(2 * i + 1)
            return n + 1

        def put_todo(b, n):
            hidden = (b >= skip_at) & (b < skip_to)
            todo[n] = b
            return jnp.where(hidden, n, n + 1)

        n_plain = lax.fori_loop(0, all_plain // 2, put_plain, n_plain)
        todo[0] = n_full
        n_todo = lax.fori_loop(lo, hi, put_todo, jnp.int32(1))
        todo[n_todo] = plain_at(all_plain - 1)
        n_todo = n_todo + all_plain % 2
        todo[n_todo] = NT // 2
        masked_c[c] = c
        masked_0[c] = todo[0]
        masked_1[c] = todo[1]

        def put_masked(i, n):
            masked_c[n] = c
            masked_0[n] = todo[2 * i]
            masked_1[n] = todo[2 * i + 1]
            return n + 1

        return n_plain, lax.fori_loop(1, (n_todo + 1) // 2, put_masked, n_masked)

    n_plain, n_masked = lax.fori_loop(0, NC, list_chunk, (jnp.int32(0), jnp.int32(NC)))
    plain_c[n_plain] = NC
    plain_0[n_plain] = 0
    plain_1[n_plain] = 0

    def plain_item(n):
        return plain_c[n], plain_0[n], plain_1[n]

    def masked_item(n):
        return masked_c[n], masked_0[n], masked_1[n]

    for copy in copies:
        copy.wait()

    def block_of(b, part):
        return kv_s[pl.ds(2 * b, 2), :, :, part * R : (part + 1) * R].reshape(KB, D)

    def rows_of(item, part):
        _, b0, b1 = item
        return jnp.concatenate([block_of(b0, part), block_of(b1, part)], axis=0)

    def with_ones(rows):
        return jnp.concatenate([rows, ones_s[...]], axis=1)

    def query_rows(c, part):
        rows = slice(part * QR, (part + 1) * QR)
        return jnp.concatenate([qg_s[2 * c, rows], qg_s[2 * c + 1, rows]], axis=0)

    def turn_keys(b, carry):
        kt_s[b] = block_of(b, 0).T
        return carry

    lax.fori_loop(0, NT // 2, turn_keys, 0)

    def put_under(ref, c, *rows):
        number = lax.broadcasted_iota(jnp.int32, (D, C), 0)
        block = jnp.zeros((D, C), F32)
        for i, values in enumerate(rows):
            block = jnp.where(number == i, values, block)
        ref[c, D:] = block.astype(BF16)

    def turn_rows(c, carry):
        qa_s[c, :D] = query_rows(c, 0).T
        ga_s[c, :D] = query_rows(c, 1).T
        halves = [qg_s[2 * c + half, 2 * QR :].astype(F32) for half in range(2)]
        put_under(
            ga_s,
            c,
            -jnp.concatenate([half[0:1] for half in halves], axis=1),
            -jnp.concatenate([half[1:2] for half in halves], axis=1),
        )
        return carry

    lax.fori_loop(0, NC, turn_rows, 0)
    qa_s[NC, :D] = jnp.zeros((D, C), BF16)
    put_under(qa_s, NC, jnp.full((1, C), HIDDEN, F32))
    l_s[NC] = jnp.zeros((8, C), F32)

    def seen(item):
        c, b0, b1 = item
        lane = lax.broadcasted_iota(jnp.int32, (1, C), 1)
        start = span_of(c) * SPAN + core * R + xl * HR
        query_pos = start + (lane // QR) * (2 * R) + lane % HR
        row = lax.broadcasted_iota(jnp.int32, (KS, 1), 0)
        key_pos = jnp.where(row < KB, b0 * KB, b1 * KB - KB) + row
        low = jnp.where(query_pos >= n1, n0, n1)
        return (key_pos <= query_pos) & ((key_pos < low) | (key_pos >= n1))

    def add_up(weights):
        parts = jnp.sum(weights.reshape(16, KS // 16, C), axis=0)
        return jnp.sum(parts.reshape(KS // 128, 8, C), axis=0)

    def raw_scores(item):
        scores = jnp.dot(rows_of(item, 0), qa_s[item[0], :D], preferred_element_type=F32)
        return jnp.where(seen(item), scores, HIDDEN)

    def weights_of(item, masked):
        scores = jnp.dot(with_ones(rows_of(item, 0)), qa_s[item[0]], preferred_element_type=F32)
        if masked:
            scores = jnp.where(seen(item), scores, HIDDEN)
        return jnp.exp2(scores * EXP_SCALE)

    def diagonal_step(i, carry):
        items = [masked_item(2 * i + k) for k in range(2)]
        found = []
        for item in items:
            scores = raw_scores(item)
            top = jnp.max(scores, axis=0, keepdims=True).astype(BF16).astype(F32)
            found.append((top, add_up(jnp.exp2((scores - top) * EXP_SCALE))))
        for (c, _, _), (top, total) in zip(items, found):
            put_under(qa_s, c, -top)
            m_s[c] = top * EXP_SCALE
            l_s[c] = total
        return carry

    lax.fori_loop(0, NC // 2, diagonal_step, 0)

    def add_weights(items, masked):
        parts = [add_up(weights_of(item, masked)) for item in items]
        for (c, _, _), part in zip(items, parts):
            l_s[c] += part

    def masked_stats(n, carry):
        add_weights([masked_item(n)], True)
        return carry

    def plain_stats(i, carry):
        add_weights([plain_item(2 * i), plain_item(2 * i + 1)], False)
        return carry

    lax.fori_loop(NC, n_masked, masked_stats, 0)
    lax.fori_loop(0, (n_plain + 1) // 2, plain_stats, 0)

    @pl.when(jnp.logical_not(jnp.max(l_s[...]) < LARGE))
    def _():
        def careful(item):
            c = item[0]
            scores = raw_scores(item) * EXP_SCALE
            old = m_s[c]
            top = jnp.maximum(old, jnp.max(scores, axis=0, keepdims=True))
            l_s[c] = l_s[c] * jnp.exp2(old - top) + add_up(jnp.exp2(scores - top))
            m_s[c] = top

        def careful_masked(n, carry):
            c = masked_c[n]

            @pl.when(n < NC)
            def _():
                m_s[c] = jnp.full((1, C), HIDDEN, F32)
                l_s[c] = jnp.zeros((8, C), F32)

            careful(masked_item(n))
            return carry

        def careful_plain(n, carry):
            careful(plain_item(n))
            return carry

        lax.fori_loop(0, n_masked, careful_masked, 0)
        lax.fori_loop(0, n_plain, careful_plain, 0)

    def put_logsum(c, carry):
        logsum = m_s[c] + jnp.log2(jnp.sum(l_s[c], axis=0, keepdims=True))
        rest = logsum * (1.0 / EXP_SCALE)
        rows = []
        for _ in range(3):
            part = rest.astype(BF16).astype(F32)
            rows.append(-part)
            rest = rest - part
        put_under(qa_s, c, *rows)
        return carry

    lax.fori_loop(0, NC, put_logsum, 0)

    def grad_step(item, masked):
        c, b0, b1 = item
        above = jnp.dot(with_ones(rows_of(item, 1)), ga_s[c], preferred_element_type=F32)
        weights = weights_of(item, masked)
        score_grad = (weights * above).astype(BF16)
        value_term = jnp.dot(weights.astype(BF16), query_rows(c, 1), preferred_element_type=F32)
        key_term = jnp.dot(score_grad, query_rows(c, 0), preferred_element_type=F32)
        keys_turned = jnp.concatenate([kt_s[b0], kt_s[b1]], axis=1)
        query_term = jnp.dot(keys_turned, score_grad, preferred_element_type=F32)
        sums = []
        for ref, term in ((dv_s, value_term), (dk_s, key_term)):
            for b, part in ((b0, term[:KB]), (b1, term[KB:])):
                at = pl.ds(2 * b, 2)
                sums.append((ref, at, ref[at] + part.reshape(2, 2, 2, R, D)))
        query_sum = dq_s[c] + query_term
        for ref, at, value in sums:
            ref[at] = value
        dq_s[c] = query_sum

    def masked_grads(n, carry):
        grad_step(masked_item(n), True)
        return carry

    def plain_grads(n, carry):
        grad_step(plain_item(n), False)
        return carry

    lax.fori_loop(0, n_masked, masked_grads, 0)
    lax.fori_loop(0, n_plain, plain_grads, 0)

    def finish(c, carry):
        dq = (dq_s[c] * SCALE).T.astype(BF16)
        dq_out[2 * c] = dq[:QR]
        dq_out[2 * c + 1] = dq[QR:]
        return carry

    lax.fori_loop(0, NC, finish, 0)

    for from_core, group in (
        (core, (((2, 0), far_a), ((2, 1), far_b), ((1, 0), near_1a), ((3, 1), near_3b))),
        (1 - core, (((2, 0), (2, 1), give_far), ((1, 0), (3, 1), give_early))),
        (core, (((1, 1), near_1b), ((3, 0), near_3a), ((0, 0), (0, 1), keep_0))),
        (1 - core, (((1, 1), (3, 0), give_late), ((0, 0), (0, 1), give_0))),
    ):
        for *parts, out in group:
            for number, (dy, xh) in enumerate(parts):
                for at in range(4):
                    rank = place(dy, xh, at // 2, at % 2)
                    rows = slice(number * 8 + 2 * at, number * 8 + 2 * at + 2)
                    out[rows, :R] = (dk_s[rank, :, from_core] * SCALE).astype(BF16)
                    out[rows, R:] = dv_s[rank, :, from_core].astype(BF16)


def add(*terms):
    total = terms[0].astype(F32)
    for term in terms[1:]:
        total = total + term.astype(F32)
    return total.astype(BF16)


def first_sum_kernel(far_a, far_b, near_1a, near_3b, got_far, got_early, *outs):
    outs[0][...] = add(far_a[...], got_far[:8])
    outs[1][...] = add(far_b[...], got_far[8:])
    outs[2][...] = add(near_1a[...], got_early[:8])
    outs[3][...] = add(near_3b[...], got_early[8:])


def second_sum_kernel(near_1b, near_3a, got_late, from_1, from_3, *outs):
    outs[0][...] = add(near_1b[...], got_late[:8], from_3[...])
    outs[1][...] = add(near_3a[...], got_late[8:], from_1[...])


def last_sum_kernel(keep, got, at_1a, at_3a, at_1b, at_3b, dq, sums, query_grad):
    sums[:8] = add(keep[:8], got[:8], at_1a[...], at_3a[...])
    sums[8:] = add(keep[8:], got[8:], at_1b[...], at_3b[...])
    for g in range(8):
        for half in range(2):
            rows = slice(half * HR, (half + 1) * HR)
            for h in range(G):
                query_grad[rows, head_columns(g, h)] = dq[spread_to(g, half), h * HR : (h + 1) * HR]


def unpack_kernel(got, key_grad, value_grad):
    for g in range(8):
        for start, out in ((0, key_grad), (R, value_grad)):
            total = got[spread_to(g, 0), start : start + R].astype(F32)
            total = total + got[spread_to(g, 1), start : start + R].astype(F32)
            out[:, g * D : (g + 1) * D] = total.astype(BF16)


def bf16(*shape):
    return jax.ShapeDtypeStruct(shape, BF16)


def on_vmem(kernel, outs, *args):
    return pl.pallas_call(
        kernel,
        out_shape=outs,
        compiler_params=pltpu.CompilerParams(vmem_limit_bytes=16 << 20),
    )(*args)


IN_SMEM = pl.BlockSpec(memory_space=pltpu.SMEM)
IN_VMEM = pl.BlockSpec(memory_space=pltpu.VMEM)
ANYWHERE = pl.BlockSpec(memory_space=pl.ANY)


def exchange(array, axes=SPREAD):
    return lax.all_to_all(array, axes, split_axis=0, concat_axis=0, tiled=True)


def flip(array, axis="core"):
    return lax.ppermute(array, axis, [(0, 1), (1, 0)])


def swap(array, distance):
    return lax.ppermute(array, "y", [(i, i ^ distance) for i in range(4)])


def come_after(array, other):
    def nothing(*refs):
        del refs

    return pl.pallas_call(
        nothing,
        out_shape=jax.ShapeDtypeStruct(array.shape, array.dtype),
        in_specs=[ANYWHERE] * 2,
        out_specs=ANYWHERE,
        input_output_aliases={0: 0},
    )(array, other)


def body(queries, keys, values, attn_out, out_grad, segment, span_order):
    half = bf16(8, 2 * R, D)
    kv_packed = pl.pallas_call(
        pack_kv_kernel,
        out_shape=half,
        in_specs=[ANYWHERE] * 2,
        scratch_shapes=[pltpu.VMEM((R, 8 * D), BF16)] * 2 + [pltpu.SemaphoreType.DMA((2,))],
        compiler_params=pltpu.CompilerParams(vmem_limit_bytes=16 << 20),
    )(keys, values)
    q_packed, counts = pl.pallas_call(
        pack_q_kernel,
        out_shape=[bf16(16, 2 * QR + 16, D), jax.ShapeDtypeStruct((2,), jnp.int32)],
        in_specs=[IN_VMEM] * 4 + [ANYWHERE],
        out_specs=[IN_VMEM, IN_SMEM],
        compiler_params=pltpu.CompilerParams(vmem_limit_bytes=16 << 20),
    )(queries, attn_out, out_grad, segment.reshape(64, 128), kv_packed)
    own = exchange(kv_packed, HEADS)
    qpay = exchange(come_after(q_packed, own))

    def round_y(array, way):
        near_1, near_3 = swap(array, 1), swap(array, 3)
        far = swap(near_3, 1) if way == 1 else swap(near_1, 3)
        return [array, near_1, near_3, far]

    mine = round_y(own, 1) + round_y(flip(own, "xl"), 3)
    group = bf16(16, 2 * R, D)
    (
        dq, keep_0, far_a, far_b, near_1a, near_3b, near_1b, near_3a,
        give_0, give_far, give_early, give_late,
    ) = pl.pallas_call(
        attention_kernel,
        out_shape=[bf16(16, QR, D), group] + [half] * 6 + [group] * 4,
        in_specs=[IN_SMEM] * 2 + [ANYWHERE] * 17,
        scratch_shapes=[
            pltpu.SMEM((NT // 2 + 3,), jnp.int32),
            *[pltpu.SMEM((NC * NT // 4 + 1,), jnp.int32)] * 3,
            *[pltpu.SMEM((NC * NT // 4 + NC,), jnp.int32)] * 3,
            pltpu.VMEM((16, 2 * QR + 16, D), BF16),
            pltpu.VMEM((NT + 2, 2, 2, 2 * R, D), BF16),
            pltpu.VMEM((NT // 2 + 1, D, KB), BF16),
            pltpu.VMEM((KS, D), BF16),
            pltpu.VMEM((NC + 1, 2 * D, C), BF16),
            pltpu.VMEM((NC, 2 * D, C), BF16),
            pltpu.VMEM((NC, 1, C), F32),
            pltpu.VMEM((NC + 1, 8, C), F32),
            pltpu.VMEM((NT + 2, 2, 2, R, D), F32),
            pltpu.VMEM((NT + 2, 2, 2, R, D), F32),
            pltpu.VMEM((NC, D, C), F32),
            pltpu.SemaphoreType.DMA,
        ],
        compiler_params=pltpu.CompilerParams(vmem_limit_bytes=48 << 20),
    )(span_order, counts, qpay, *mine, *[flip(array) for array in mine])
    far_a, far_b, near_1a, near_3b = on_vmem(
        first_sum_kernel, [half] * 4, far_a, far_b, near_1a, near_3b, flip(give_far), flip(give_early)
    )
    from_1 = swap(far_a, 1)
    from_3 = swap(far_b, 3)
    at_1a, at_3b = swap(near_1a, 1), swap(near_3b, 3)
    near_1b, near_3a = on_vmem(
        second_sum_kernel, [half] * 2, near_1b, near_3a, flip(give_late), from_1, from_3
    )
    at_1b, at_3a = swap(near_1b, 1), swap(near_3a, 3)
    sums, query_grad = on_vmem(
        last_sum_kernel,
        [group, bf16(R, 8 * G * D)],
        keep_0,
        flip(give_0),
        at_1a,
        at_3a,
        at_1b,
        at_3b,
        exchange(dq),
    )
    key_grad, value_grad = on_vmem(unpack_kernel, [bf16(R, 8 * D)] * 2, exchange(sums))
    return query_grad, key_grad, value_grad


def solution(mesh):
    fine = Mesh(mesh.devices.reshape(4, 2, 2, 2, 4), AXES)
    rows = P(AXES, None)
    return jax.shard_map(
        body,
        mesh=fine,
        in_specs=(rows,) * 5 + (P(), P()),
        out_specs=(rows,) * 3,
        check_vma=False,
    )
```

```python
import math

import jax
import jax.numpy as jnp
from jax import lax
from jax.experimental import pallas as pl
from jax.experimental.pallas import tpu as pltpu
from jax.sharding import Mesh, PartitionSpec as P

D = 128
G = 4
R = 64
HR = R // 2
SPAN = 256
NT = 32
KB = 2 * SPAN
QR = G * HR
C = 2 * QR
NC = 8
W = 4
WM = 2
SCALE = D**-0.5
EXP_SCALE = SCALE * math.log2(math.e)
HIDDEN = -1e30
LARGE = 2.0**90
F32 = jnp.float32
BF16 = jnp.bfloat16
AXES = ("z", "core", "xh", "xl", "y")
SPREAD = ("xh", "xl", "z")
NT_DIMS = (((1,), (1,)), ((), ()))
TN_DIMS = (((0,), (0,)), ((), ()))


def spread_to(g, xl):
    return (g // 4 * 2 + xl) * 4 + g % 4


def head_columns(g, h):
    return slice((g * G + h) * D, (g * G + h + 1) * D)


def pack_kv_kernel(keys, values, segment, out, counts):
    counts[0] = jnp.sum((segment[...] == 0).astype(jnp.int32))
    counts[1] = jnp.sum((segment[...] != 2).astype(jnp.int32))
    for g in range(8):
        for xl in range(2):
            out[spread_to(g, xl), :R] = keys[:, g * D : (g + 1) * D]
            out[spread_to(g, xl), R:] = values[:, g * D : (g + 1) * D]


def pack_q_kernel(queries, saved, grads, after, out):
    del after
    ones = jnp.ones((8, D), BF16)
    row = lax.broadcasted_iota(jnp.int32, (16, D), 0)
    for g in range(8):
        for half in range(2):
            dest = spread_to(g, half)
            rows = slice(half * HR, (half + 1) * HR)
            prods = []
            for h in range(G):
                cols = head_columns(g, h)
                grad = grads[rows, cols]
                out[dest, h * HR : (h + 1) * HR] = queries[rows, cols]
                out[dest, QR + h * HR : QR + (h + 1) * HR] = grad
                prods.append(grad.astype(F32) * saved[rows, cols].astype(F32))
            prod = jnp.concatenate(prods, axis=0)
            high = prod.astype(BF16)
            low = (prod - high.astype(F32)).astype(BF16)
            dot = lax.dot_general(ones, high, NT_DIMS, preferred_element_type=F32)
            dot = dot + lax.dot_general(ones, low, NT_DIMS, preferred_element_type=F32)
            both = jnp.concatenate([dot, dot], axis=0)
            rounded = both.astype(BF16).astype(F32)
            out[dest, 2 * QR :] = jnp.where(row == 0, rounded, both - rounded).astype(BF16)


def span_id(xh, xl, y, zh):
    return ((xh * 2 + xl) * 4 + y) * 2 + zh


def attention_kernel(order, counts, qpay, *refs):
    pieces = refs[:10]
    dq_out, keep_0, keep_1, keep_3, sum_a, sum_b, give_0, give_1, give_3, far_give = refs[10:20]
    plain_c, plain_b, masked_c, masked_b = refs[20:24]
    qg_s, kv_s, ones_s, qa_s, ga_s, m_s, l_s, dk_s, dv_s, dq_s, sem = refs[24:]
    n0 = counts[0]
    n1 = counts[1]
    xl = lax.axis_index("xl")
    y = lax.axis_index("y")
    core = lax.axis_index("core")

    def place(dy, xh, xl, zh):
        return order[span_id(xh, xl, y ^ dy, zh)]

    copies = [pltpu.make_async_copy(qpay, qg_s, sem)]
    for number, piece in enumerate(pieces):
        from_core = core if number < 5 else 1 - core
        dy = (0, 1, 3, 2, 2)[number % 5]
        halves = ((0, 1), (0, 1), (0, 1), (0,), (1,))[number % 5]
        for at in range(4 * len(halves)):
            rank = place(dy, halves[at // 4], at // 2 % 2, at % 2)
            copies.append(
                pltpu.make_async_copy(
                    piece.at[pl.ds(2 * at, 2)], kv_s.at[rank, :, from_core], sem
                )
            )
    for copy in copies:
        copy.start()

    ones_s[...] = (lax.broadcasted_iota(jnp.int32, (KB, D), 1) < 3).astype(F32).astype(BF16)
    dk_s[...] = jnp.zeros_like(dk_s)
    dv_s[...] = jnp.zeros_like(dv_s)
    dq_s[...] = jnp.zeros_like(dq_s)

    def span_of(c):
        return order[span_id(c // 4, c // 2 % 2, y, c % 2)]

    def list_chunk(c, sizes):
        n_plain, n_masked = sizes
        span_q = span_of(c)
        first = span_q * SPAN
        has_second = first + (SPAN - 1) >= n1
        all_second = first >= n1
        n_full = span_q // 2
        hi = jnp.minimum(jnp.where(has_second, (n1 + (KB - 1)) // KB, 0), n_full)
        lo = jnp.minimum(jnp.where(has_second, n0 // KB, 0), hi)
        skip_at = jnp.where(all_second, (n0 + (KB - 1)) // KB, hi)
        skip_to = jnp.where(all_second, n1 // KB, 0)
        masked_c[c] = c
        masked_b[c] = n_full

        def put_plain(b, n):
            plain_c[n] = c
            plain_b[n] = b
            return n + 1

        def put_masked(b, n):
            hidden = (b >= skip_at) & (b < skip_to)
            masked_c[n] = c
            masked_b[n] = b
            return jnp.where(hidden, n, n + 1)

        n_plain = lax.fori_loop(0, lo, put_plain, n_plain)
        n_plain = lax.fori_loop(hi, n_full, put_plain, n_plain)
        return n_plain, lax.fori_loop(lo, hi, put_masked, n_masked)

    n_plain, n_masked = lax.fori_loop(0, NC, list_chunk, (jnp.int32(0), jnp.int32(NC)))
    for i in range(W - 1):
        plain_c[n_plain + i] = NC
        plain_b[n_plain + i] = 0
    for i in range(WM - 1):
        masked_c[n_masked + i] = NC
        masked_b[n_masked + i] = 0

    def plain_item(n):
        return plain_c[n], plain_b[n]

    def masked_item(n):
        return masked_c[n], masked_b[n]

    def each_step(step, first_masked):
        def masked(i, carry):
            step([masked_item(WM * i + k) for k in range(WM)], True)
            return carry

        def plain(i, carry):
            step([plain_item(W * i + k) for k in range(W)], False)
            return carry

        lax.fori_loop(first_masked // WM, (n_masked + (WM - 1)) // WM, masked, 0)
        lax.fori_loop(0, (n_plain + (W - 1)) // W, plain, 0)

    for copy in copies:
        copy.wait()

    def block_of(b, part):
        return kv_s[pl.ds(2 * b, 2), :, :, part * R : (part + 1) * R].reshape(KB, D)

    def with_ones(rows):
        return jnp.concatenate([rows, ones_s[...]], axis=1)

    def query_rows(c, part):
        rows = slice(part * QR, (part + 1) * QR)
        return jnp.concatenate([qg_s[2 * c, rows], qg_s[2 * c + 1, rows]], axis=0)

    def put_under(ref, c, *rows):
        number = lax.broadcasted_iota(jnp.int32, (D, C), 0)
        block = jnp.zeros((D, C), F32)
        for i, values in enumerate(rows):
            block = jnp.where(number == i, values, block)
        ref[c, D:] = block.astype(BF16)

    def turn_rows(c, carry):
        qa_s[c, :D] = query_rows(c, 0).T
        ga_s[c, :D] = query_rows(c, 1).T
        halves = [qg_s[2 * c + half, 2 * QR :].astype(F32) for half in range(2)]
        put_under(
            ga_s,
            c,
            -jnp.concatenate([half[0:1] for half in halves], axis=1),
            -jnp.concatenate([half[1:2] for half in halves], axis=1),
        )
        return carry

    lax.fori_loop(0, NC, turn_rows, 0)
    qa_s[NC, :D] = jnp.zeros((D, C), BF16)
    put_under(qa_s, NC, jnp.full((1, C), HIDDEN, F32))
    l_s[NC] = jnp.zeros((8, C), F32)

    def seen(item):
        c, b = item
        lane = lax.broadcasted_iota(jnp.int32, (1, C), 1)
        start = span_of(jnp.minimum(c, NC - 1)) * SPAN + core * R + xl * HR
        query_pos = start + (lane // QR) * (2 * R) + lane % HR
        key_pos = b * KB + lax.broadcasted_iota(jnp.int32, (KB, 1), 0)
        low = jnp.where(query_pos >= n1, n0, n1)
        return (key_pos <= query_pos) & ((key_pos < low) | (key_pos >= n1))

    def add_up(weights):
        parts = jnp.sum(weights.reshape(8, KB // 8, C), axis=0)
        return jnp.sum(parts.reshape(KB // 64, 8, C), axis=0)

    def raw_scores(item):
        scores = jnp.dot(block_of(item[1], 0), qa_s[item[0], :D], preferred_element_type=F32)
        return jnp.where(seen(item), scores, HIDDEN)

    def weights_of(item, masked):
        scores = jnp.dot(with_ones(block_of(item[1], 0)), qa_s[item[0]], preferred_element_type=F32)
        if masked:
            scores = jnp.where(seen(item), scores, HIDDEN)
        return jnp.exp2(scores * EXP_SCALE)

    def diagonal_step(i, carry):
        items = [masked_item(2 * i + k) for k in range(2)]
        found = []
        for item in items:
            scores = raw_scores(item)
            top = jnp.max(scores, axis=0, keepdims=True).astype(BF16).astype(F32)
            found.append((top, add_up(jnp.exp2((scores - top) * EXP_SCALE))))
        for (c, _), (top, total) in zip(items, found):
            put_under(qa_s, c, -top)
            m_s[c] = top * EXP_SCALE
            l_s[c] = total
        return carry

    lax.fori_loop(0, NC // 2, diagonal_step, 0)

    def add_weights(items, masked):
        parts = [add_up(weights_of(item, masked)) for item in items]
        for (c, _), part in zip(items, parts):
            l_s[c] += part

    each_step(add_weights, NC)

    @pl.when(jnp.logical_not(jnp.max(l_s[...]) < LARGE))
    def _():
        def careful(item):
            c = item[0]
            scores = raw_scores(item) * EXP_SCALE
            old = m_s[c]
            top = jnp.maximum(old, jnp.max(scores, axis=0, keepdims=True))
            l_s[c] = l_s[c] * jnp.exp2(old - top) + add_up(jnp.exp2(scores - top))
            m_s[c] = top

        def careful_masked(n, carry):
            c = masked_c[n]

            @pl.when(n < NC)
            def _():
                m_s[c] = jnp.full((1, C), HIDDEN, F32)
                l_s[c] = jnp.zeros((8, C), F32)

            careful(masked_item(n))
            return carry

        def careful_plain(n, carry):
            careful(plain_item(n))
            return carry

        lax.fori_loop(0, n_masked, careful_masked, 0)
        lax.fori_loop(0, n_plain, careful_plain, 0)

    def put_logsum(c, carry):
        logsum = m_s[c] + jnp.log2(jnp.sum(l_s[c], axis=0, keepdims=True))
        rest = logsum * (1.0 / EXP_SCALE)
        rows = []
        for _ in range(3):
            part = rest.astype(BF16).astype(F32)
            rows.append(-part)
            rest = rest - part
        put_under(qa_s, c, *rows)
        return carry

    lax.fori_loop(0, NC, put_logsum, 0)

    def grad_step(items, masked):
        weights = [weights_of(item, masked) for item in items]
        of = [jnp.minimum(c, NC - 1) for c, _ in items]
        above = [
            jnp.dot(with_ones(block_of(b, 1)), ga_s[c], preferred_element_type=F32)
            for c, (_, b) in zip(of, items)
        ]
        score_grads = [(w * p).astype(BF16) for w, p in zip(weights, above)]
        for c, (_, b), w, score_grad in zip(of, items, weights, score_grads):
            for ref, term in (
                (dv_s, jnp.dot(w.astype(BF16), query_rows(c, 1), preferred_element_type=F32)),
                (dk_s, jnp.dot(score_grad, query_rows(c, 0), preferred_element_type=F32)),
            ):
                ref[pl.ds(2 * b, 2)] += term.reshape(2, 2, 2, R, D)
            dq_s[c] += lax.dot_general(
                score_grad, block_of(b, 0), TN_DIMS, preferred_element_type=F32
            )

    each_step(grad_step, 0)

    def finish(c, carry):
        dq = (dq_s[c] * SCALE).astype(BF16)
        dq_out[2 * c] = dq[:QR]
        dq_out[2 * c + 1] = dq[QR:]
        return carry

    lax.fori_loop(0, NC, finish, 0)

    for from_core, group in (
        (core, ((0, keep_0, 0), (1, keep_1, 0), (3, keep_3, 0), (2, sum_a, 0), (2, sum_b, 1))),
        (1 - core, ((0, give_0, 0), (1, give_1, 0), (3, give_3, 0), (2, far_give, 0))),
    ):
        for dy, out, first_xh in group:
            for at in range(out.shape[0] // 2):
                rank = place(dy, first_xh + at // 4, at // 2 % 2, at % 2)
                rows = slice(2 * at, 2 * at + 2)
                out[rows, :R] = (dk_s[rank, :, from_core] * SCALE).astype(BF16)
                out[rows, R:] = dv_s[rank, :, from_core].astype(BF16)


def far_sum_kernel(sum_a, sum_b, got, out_a, out_b):
    out_a[...] = (sum_a[...].astype(F32) + got[:8].astype(F32)).astype(BF16)
    out_b[...] = (sum_b[...].astype(F32) + got[8:].astype(F32)).astype(BF16)


def near_sum_kernel(sum_1, got_1, sum_3, got_3, from_1, from_3, out_1, out_3):
    for rows, with_from in ((slice(0, 8), 3), (slice(8, 16), 1)):
        for number, keep, got, came, out in (
            (1, sum_1, got_1, from_3, out_1),
            (3, sum_3, got_3, from_1, out_3),
        ):
            total = keep[rows].astype(F32) + got[rows].astype(F32)
            if number == with_from:
                total = total + came[...].astype(F32)
            out[rows] = total.astype(BF16)


def last_sum_kernel(keep, got, near_1, near_3, dq, sums, query_grad):
    total = keep[...].astype(F32) + got[...].astype(F32)
    total = total + (near_1[...].astype(F32) + near_3[...].astype(F32))
    sums[...] = total.astype(BF16)
    for g in range(8):
        for half in range(2):
            rows = slice(half * HR, (half + 1) * HR)
            for h in range(G):
                query_grad[rows, head_columns(g, h)] = dq[spread_to(g, half), h * HR : (h + 1) * HR]


def unpack_kernel(got, key_grad, value_grad):
    for g in range(8):
        for start, out in ((0, key_grad), (R, value_grad)):
            total = got[spread_to(g, 0), start : start + R].astype(F32)
            total = total + got[spread_to(g, 1), start : start + R].astype(F32)
            out[:, g * D : (g + 1) * D] = total.astype(BF16)


def bf16(*shape):
    return jax.ShapeDtypeStruct(shape, BF16)


def on_vmem(kernel, outs, *args):
    return pl.pallas_call(
        kernel,
        out_shape=outs,
        compiler_params=pltpu.CompilerParams(vmem_limit_bytes=16 << 20),
    )(*args)


IN_SMEM = pl.BlockSpec(memory_space=pltpu.SMEM)
IN_VMEM = pl.BlockSpec(memory_space=pltpu.VMEM)
ANYWHERE = pl.BlockSpec(memory_space=pl.ANY)


def exchange(array):
    return lax.all_to_all(array, SPREAD, split_axis=0, concat_axis=0, tiled=True)


def flip(array):
    return lax.ppermute(array, "core", [(0, 1), (1, 0)])


def swap(array, distance):
    return lax.ppermute(array, "y", [(i, i ^ distance) for i in range(4)])


def body(queries, keys, values, attn_out, out_grad, segment, span_order):
    kv_packed, counts = pl.pallas_call(
        pack_kv_kernel,
        out_shape=[bf16(16, 2 * R, D), jax.ShapeDtypeStruct((2,), jnp.int32)],
        out_specs=[IN_VMEM, IN_SMEM],
        compiler_params=pltpu.CompilerParams(vmem_limit_bytes=16 << 20),
    )(keys, values, segment.reshape(64, 128))
    own = exchange(kv_packed)
    q_packed = pl.pallas_call(
        pack_q_kernel,
        out_shape=bf16(16, 2 * QR + 16, D),
        in_specs=[IN_VMEM] * 3 + [ANYWHERE],
        compiler_params=pltpu.CompilerParams(vmem_limit_bytes=16 << 20),
    )(queries, attn_out, out_grad, own)
    qpay = exchange(q_packed)

    near_1 = swap(own, 1)
    near_3 = swap(own, 3)
    far_a = swap(near_3[:8], 1)
    far_b = swap(near_1[8:], 3)
    mine = (own, near_1, near_3, far_a, far_b)
    group = bf16(16, 2 * R, D)
    half = bf16(8, 2 * R, D)
    dq, keep_0, keep_1, keep_3, sum_a, sum_b, give_0, give_1, give_3, far_give = pl.pallas_call(
        attention_kernel,
        out_shape=[bf16(16, QR, D)] + [group] * 3 + [half] * 2 + [group] * 4,
        in_specs=[IN_SMEM] * 2 + [ANYWHERE] * 11,
        scratch_shapes=[
            *[pltpu.SMEM((NC * NT // 2 + W,), jnp.int32)] * 2,
            *[pltpu.SMEM((NC * NT // 2 + NC + W,), jnp.int32)] * 2,
            pltpu.VMEM((16, 2 * QR + 16, D), BF16),
            pltpu.VMEM((NT, 2, 2, 2 * R, D), BF16),
            pltpu.VMEM((KB, D), BF16),
            pltpu.VMEM((NC + 1, 2 * D, C), BF16),
            pltpu.VMEM((NC, 2 * D, C), BF16),
            pltpu.VMEM((NC, 1, C), F32),
            pltpu.VMEM((NC + 1, 8, C), F32),
            pltpu.VMEM((NT, 2, 2, R, D), F32),
            pltpu.VMEM((NT, 2, 2, R, D), F32),
            pltpu.VMEM((NC, C, D), F32),
            pltpu.SemaphoreType.DMA,
        ],
        compiler_params=pltpu.CompilerParams(vmem_limit_bytes=48 << 20),
    )(span_order, counts, qpay, *mine, *[flip(array) for array in mine])
    far_sum_a, far_sum_b = on_vmem(far_sum_kernel, [half, half], sum_a, sum_b, flip(far_give))
    from_1 = swap(far_sum_a, 1)
    from_3 = swap(far_sum_b, 3)
    to_1, to_3 = on_vmem(
        near_sum_kernel, [group] * 2, keep_1, flip(give_1), keep_3, flip(give_3), from_1, from_3
    )
    sums, query_grad = on_vmem(
        last_sum_kernel,
        [group, bf16(R, 8 * G * D)],
        keep_0,
        flip(give_0),
        swap(to_1, 1),
        swap(to_3, 3),
        exchange(dq),
    )
    key_grad, value_grad = on_vmem(unpack_kernel, [bf16(R, 8 * D)] * 2, exchange(sums))
    return query_grad, key_grad, value_grad


def solution(mesh):
    fine = Mesh(mesh.devices.reshape(4, 2, 2, 2, 4), AXES)
    rows = P(AXES, None)
    return jax.shard_map(
        body,
        mesh=fine,
        in_specs=(rows,) * 5 + (P(), P()),
        out_specs=(rows,) * 3,
        check_vma=False,
    )
```

```python
import math

import jax
import jax.numpy as jnp
from jax import lax
from jax.experimental import pallas as pl
from jax.experimental.pallas import tpu as pltpu
from jax.sharding import Mesh, PartitionSpec as P

D = 128
G = 4
R = 64
HR = R // 2
SPAN = 256
NT = 32
KB = 2 * SPAN
QR = G * HR
C = 2 * QR
NC = 8
W = 4
SCALE = D**-0.5
EXP_SCALE = SCALE * math.log2(math.e)
HIDDEN = -1e30
LARGE = 2.0**90
F32 = jnp.float32
BF16 = jnp.bfloat16
AXES = ("z", "core", "xh", "xl", "y")
SPREAD = ("xh", "xl", "z")
NT_DIMS = (((1,), (1,)), ((), ()))


def spread_to(g, xl):
    return (g // 4 * 2 + xl) * 4 + g % 4


def head_columns(g, h):
    return slice((g * G + h) * D, (g * G + h + 1) * D)


def pack_kv_kernel(keys, values, out):
    for g in range(8):
        for xl in range(2):
            out[spread_to(g, xl), :R] = keys[:, g * D : (g + 1) * D]
            out[spread_to(g, xl), R:] = values[:, g * D : (g + 1) * D]


def pack_q_kernel(queries, saved, grads, segment, after, out, counts):
    del after
    counts[0] = jnp.sum((segment[...] == 0).astype(jnp.int32))
    counts[1] = jnp.sum((segment[...] != 2).astype(jnp.int32))
    ones = jnp.ones((8, D), BF16)
    row = lax.broadcasted_iota(jnp.int32, (16, D), 0)
    for g in range(8):
        for half in range(2):
            dest = spread_to(g, half)
            rows = slice(half * HR, (half + 1) * HR)
            prods = []
            for h in range(G):
                cols = head_columns(g, h)
                grad = grads[rows, cols]
                out[dest, h * HR : (h + 1) * HR] = queries[rows, cols]
                out[dest, QR + h * HR : QR + (h + 1) * HR] = grad
                prods.append(grad.astype(F32) * saved[rows, cols].astype(F32))
            prod = jnp.concatenate(prods, axis=0)
            high = prod.astype(BF16)
            low = (prod - high.astype(F32)).astype(BF16)
            dot = lax.dot_general(ones, high, NT_DIMS, preferred_element_type=F32)
            dot = dot + lax.dot_general(ones, low, NT_DIMS, preferred_element_type=F32)
            both = jnp.concatenate([dot, dot], axis=0)
            rounded = both.astype(BF16).astype(F32)
            out[dest, 2 * QR :] = jnp.where(row == 0, rounded, both - rounded).astype(BF16)


def span_id(xh, xl, y, zh):
    return ((xh * 2 + xl) * 4 + y) * 2 + zh


def attention_kernel(order, counts, qpay, *refs):
    pieces = refs[:10]
    dq_out, keep_0, keep_1, keep_3, sum_a, sum_b, give_0, give_1, give_3, far_give = refs[10:20]
    plain_c, plain_b, q_s, do_s, d_s, k_s, v_s, kt_s, qa_s, ga_s = refs[20:30]
    m_s, l_s, dk_s, dv_s, dq_s, sem, value_sem = refs[30:]
    n0 = counts[0]
    n1 = counts[1]
    xl = lax.axis_index("xl")
    y = lax.axis_index("y")
    core = lax.axis_index("core")

    def place(dy, xh, xl, zh):
        return order[span_id(xh, xl, y ^ dy, zh)]

    copies = []
    value_copies = []
    for s in range(16):
        for part, dst in ((0, q_s), (1, do_s)):
            copies.append(
                pltpu.make_async_copy(
                    qpay.at[s, pl.ds(part * QR, QR)], dst.at[s // 2, pl.ds((s % 2) * QR, QR)], sem
                )
            )
    copies.append(pltpu.make_async_copy(qpay.at[:, pl.ds(2 * QR, 16)], d_s, sem))
    for number, piece in enumerate(pieces):
        from_core = core if number < 5 else 1 - core
        dy = (0, 1, 3, 2, 2)[number % 5]
        halves = ((0, 1), (0, 1), (0, 1), (0,), (1,))[number % 5]
        for at in range(4 * len(halves)):
            rank = place(dy, halves[at // 4], at // 2 % 2, at % 2)
            rows = piece.at[pl.ds(2 * at, 2)]
            copies.append(
                pltpu.make_async_copy(
                    rows.at[:, pl.ds(0, R)], k_s.at[rank, :, from_core, :, pl.ds(0, D)], sem
                )
            )
            value_copies.append(
                pltpu.make_async_copy(
                    rows.at[:, pl.ds(R, R)], v_s.at[rank, :, from_core, :, pl.ds(0, D)], value_sem
                )
            )
    for copy in copies + value_copies:
        copy.start()

    column = lax.broadcasted_iota(jnp.int32, (SPAN, D), 1)
    row = lax.broadcasted_iota(jnp.int32, (SPAN, D), 0)

    def put_beside(i, carry):
        chosen = (i * SPAN + row >= n0) & (i * SPAN + row < n1)
        beside = jnp.where((column < 3) | ((column == 3) & chosen), 1.0, 0.0).astype(BF16)
        beside = beside.reshape(1, 2, 2, R, D)
        k_s[pl.ds(i, 1), :, :, :, D:] = beside
        v_s[pl.ds(i, 1), :, :, :, D:] = beside
        return carry

    lax.fori_loop(0, NT, put_beside, 0)
    dk_s[...] = jnp.zeros_like(dk_s)
    dv_s[...] = jnp.zeros_like(dv_s)
    dq_s[...] = jnp.zeros_like(dq_s)

    def span_of(c):
        return order[span_id(c // 4, c // 2 % 2, y, c % 2)]

    def full_blocks(c):
        return span_of(c) // 2

    def list_chunk(c, size):
        all_second = span_of(c) * SPAN >= n1
        skip_at = (n0 + (KB - 1)) // KB
        skip_to = jnp.where(all_second, n1 // KB, 0)

        def put(b, n):
            hidden = (b >= skip_at) & (b < skip_to)
            plain_c[n] = c
            plain_b[n] = b
            return jnp.where(hidden, n, n + 1)

        return lax.fori_loop(0, full_blocks(c), put, size)

    n_plain = lax.fori_loop(0, NC, list_chunk, jnp.int32(0))
    for i in range(W - 1):
        plain_c[n_plain + i] = NC
        plain_b[n_plain + i] = 0

    for copy in copies:
        copy.wait()

    def block_of(ref, b):
        return ref[pl.ds(2 * b, 2)].reshape(KB, 2 * D)

    def keys_of(b):
        return k_s[pl.ds(2 * b, 2), :, :, :, :D].reshape(KB, D)

    def turn_keys(b, carry):
        kt_s[b] = keys_of(b).T
        return carry

    lax.fori_loop(0, NT // 2, turn_keys, 0)

    def put_under(ref, c, *rows):
        number = lax.broadcasted_iota(jnp.int32, (D, C), 0)
        block = jnp.zeros((D, C), F32)
        for i, values in enumerate(rows):
            block = jnp.where(number == i, values, block)
        ref[c, D:] = block.astype(BF16)

    def turn_rows(c, carry):
        qa_s[c, :D] = q_s[c].T
        ga_s[c, :D] = do_s[c].T
        halves = [d_s[2 * c + half].astype(F32) for half in range(2)]
        put_under(
            ga_s,
            c,
            -jnp.concatenate([half[0:1] for half in halves], axis=1),
            -jnp.concatenate([half[1:2] for half in halves], axis=1),
        )
        return carry

    lax.fori_loop(0, NC, turn_rows, 0)
    qa_s[NC, :D] = jnp.zeros((D, C), BF16)
    put_under(qa_s, NC, jnp.full((1, C), HIDDEN, F32))
    ga_s[NC] = jnp.zeros((2 * D, C), BF16)
    q_s[NC] = jnp.zeros((C, D), BF16)
    do_s[NC] = jnp.zeros((C, D), BF16)
    l_s[NC] = jnp.zeros((8, C), F32)

    def query_positions(c):
        lane = lax.broadcasted_iota(jnp.int32, (1, C), 1)
        start = span_of(c) * SPAN + core * R + xl * HR
        return start + (lane // QR) * (2 * R) + lane % HR

    def key_positions(b):
        return b * KB + lax.broadcasted_iota(jnp.int32, (KB, 1), 0)

    def seen(c, b):
        query_pos, key_pos = query_positions(c), key_positions(b)
        low = jnp.where(query_pos >= n1, n0, n1)
        return (key_pos <= query_pos) & ((key_pos < low) | (key_pos >= n1))

    def add_up(weights):
        return jnp.sum(weights.reshape(KB // 8, 8, C), axis=0)

    def raw_scores(c, b):
        return jnp.dot(keys_of(b), qa_s[c, :D], preferred_element_type=F32)

    def put_shift(c, *rows):
        rows = (rows + (jnp.zeros((1, C), F32),) * 3)[:3]
        hide = jnp.where(query_positions(c) >= n1, HIDDEN, 0.0)
        put_under(qa_s, c, *rows, hide)

    def weights_of(c, b, masked):
        scores = jnp.dot(block_of(k_s, b), qa_s[c], preferred_element_type=F32)
        if masked:
            scores = jnp.where(key_positions(b) <= query_positions(c), scores, HIDDEN)
        return jnp.exp2(scores * EXP_SCALE)

    def diagonal_step(i, carry):
        for c in [2 * i + k for k in range(2)]:
            b = full_blocks(c)
            scores = jnp.where(seen(c, b), raw_scores(c, b), HIDDEN)
            top = jnp.max(scores, axis=0, keepdims=True).astype(BF16).astype(F32)
            put_shift(c, -top)
            m_s[c] = top * EXP_SCALE
            l_s[c] = add_up(jnp.exp2((scores - top) * EXP_SCALE))
        return carry

    lax.fori_loop(0, NC // 2, diagonal_step, 0)

    def add_weights(items, masked):
        parts = [add_up(weights_of(c, b, masked)) for c, b in items]
        for (c, b), part in zip(items, parts):
            l_s[c] += part

    def plain_items(i):
        return [(plain_c[n], plain_b[n]) for n in [W * i + k for k in range(W)]]

    def plain_stats(i, carry):
        add_weights(plain_items(i), False)
        return carry

    lax.fori_loop(0, (n_plain + W - 1) // W, plain_stats, 0)

    @pl.when(jnp.logical_not(jnp.max(l_s[...]) < LARGE))
    def _():
        def careful(c, b):
            scores = jnp.where(seen(c, b), raw_scores(c, b) * EXP_SCALE, HIDDEN)
            old = m_s[c]
            top = jnp.maximum(old, jnp.max(scores, axis=0, keepdims=True))
            l_s[c] = l_s[c] * jnp.exp2(old - top) + add_up(jnp.exp2(scores - top))
            m_s[c] = top

        def careful_diagonal(c, carry):
            m_s[c] = jnp.full((1, C), HIDDEN, F32)
            l_s[c] = jnp.zeros((8, C), F32)
            careful(c, full_blocks(c))
            return carry

        def careful_plain(n, carry):
            careful(plain_c[n], plain_b[n])
            return carry

        lax.fori_loop(0, NC, careful_diagonal, 0)
        lax.fori_loop(0, n_plain, careful_plain, 0)

    def put_logsum(c, carry):
        logsum = m_s[c] + jnp.log2(jnp.sum(l_s[c], axis=0, keepdims=True))
        rest = logsum * (1.0 / EXP_SCALE)
        rows = []
        for _ in range(3):
            part = rest.astype(BF16).astype(F32)
            rows.append(-part)
            rest = rest - part
        put_shift(c, *rows)
        return carry

    lax.fori_loop(0, NC, put_logsum, 0)
    for copy in value_copies:
        copy.wait()

    def grad_step(items, masked):
        weights = [weights_of(c, b, masked) for c, b in items]
        above = [
            jnp.dot(block_of(v_s, b), ga_s[c], preferred_element_type=F32) for c, b in items
        ]
        score_grads = [(w * p).astype(BF16) for w, p in zip(weights, above)]
        for (c, b), w, score_grad in zip(items, weights, score_grads):
            for ref, term in (
                (dv_s, jnp.dot(w.astype(BF16), do_s[c], preferred_element_type=F32)),
                (dk_s, jnp.dot(score_grad, q_s[c], preferred_element_type=F32)),
            ):
                ref[pl.ds(2 * b, 2)] += term.reshape(2, 2, 2, R, D)
            dq_s[c] += jnp.dot(kt_s[b], score_grad, preferred_element_type=F32)

    def diagonal_grads(i, carry):
        grad_step([(c, full_blocks(c)) for c in [2 * i + k for k in range(2)]], True)
        return carry

    def plain_grads(i, carry):
        grad_step(plain_items(i), False)
        return carry

    lax.fori_loop(0, NC // 2, diagonal_grads, 0)
    lax.fori_loop(0, (n_plain + W - 1) // W, plain_grads, 0)

    def finish(c, carry):
        dq = (dq_s[c] * SCALE).T.astype(BF16)
        dq_out[2 * c] = dq[:QR]
        dq_out[2 * c + 1] = dq[QR:]
        return carry

    lax.fori_loop(0, NC, finish, 0)

    for from_core, group in (
        (core, ((0, keep_0, 0), (1, keep_1, 0), (3, keep_3, 0), (2, sum_a, 0), (2, sum_b, 1))),
        (1 - core, ((0, give_0, 0), (1, give_1, 0), (3, give_3, 0), (2, far_give, 0))),
    ):
        for dy, out, first_xh in group:
            for at in range(out.shape[0] // 2):
                rank = place(dy, first_xh + at // 4, at // 2 % 2, at % 2)
                rows = slice(2 * at, 2 * at + 2)
                out[rows, :R] = (dk_s[rank, :, from_core] * SCALE).astype(BF16)
                out[rows, R:] = dv_s[rank, :, from_core].astype(BF16)


def far_sum_kernel(sum_a, sum_b, got, out_a, out_b):
    out_a[...] = (sum_a[...].astype(F32) + got[:8].astype(F32)).astype(BF16)
    out_b[...] = (sum_b[...].astype(F32) + got[8:].astype(F32)).astype(BF16)


def near_sum_kernel(sum_1, got_1, sum_3, got_3, from_1, from_3, out_1, out_3):
    for rows, with_from in ((slice(0, 8), 3), (slice(8, 16), 1)):
        for number, keep, got, came, out in (
            (1, sum_1, got_1, from_3, out_1),
            (3, sum_3, got_3, from_1, out_3),
        ):
            total = keep[rows].astype(F32) + got[rows].astype(F32)
            if number == with_from:
                total = total + came[...].astype(F32)
            out[rows] = total.astype(BF16)


def last_sum_kernel(keep, got, near_1, near_3, dq, sums, query_grad):
    total = keep[...].astype(F32) + got[...].astype(F32)
    total = total + (near_1[...].astype(F32) + near_3[...].astype(F32))
    sums[...] = total.astype(BF16)
    for g in range(8):
        for half in range(2):
            rows = slice(half * HR, (half + 1) * HR)
            for h in range(G):
                query_grad[rows, head_columns(g, h)] = dq[spread_to(g, half), h * HR : (h + 1) * HR]


def unpack_kernel(got, key_grad, value_grad):
    for g in range(8):
        for start, out in ((0, key_grad), (R, value_grad)):
            total = got[spread_to(g, 0), start : start + R].astype(F32)
            total = total + got[spread_to(g, 1), start : start + R].astype(F32)
            out[:, g * D : (g + 1) * D] = total.astype(BF16)


def bf16(*shape):
    return jax.ShapeDtypeStruct(shape, BF16)


def on_vmem(kernel, outs, *args):
    return pl.pallas_call(
        kernel,
        out_shape=outs,
        compiler_params=pltpu.CompilerParams(vmem_limit_bytes=16 << 20),
    )(*args)


IN_SMEM = pl.BlockSpec(memory_space=pltpu.SMEM)
IN_VMEM = pl.BlockSpec(memory_space=pltpu.VMEM)
ANYWHERE = pl.BlockSpec(memory_space=pl.ANY)


def exchange(array):
    return lax.all_to_all(array, SPREAD, split_axis=0, concat_axis=0, tiled=True)


def flip(array):
    return lax.ppermute(array, "core", [(0, 1), (1, 0)])


def swap(array, distance):
    return lax.ppermute(array, "y", [(i, i ^ distance) for i in range(4)])


def body(queries, keys, values, attn_out, out_grad, segment, span_order):
    own = exchange(on_vmem(pack_kv_kernel, bf16(16, 2 * R, D), keys, values))
    q_packed, counts = pl.pallas_call(
        pack_q_kernel,
        out_shape=[bf16(16, 2 * QR + 16, D), jax.ShapeDtypeStruct((2,), jnp.int32)],
        in_specs=[IN_VMEM] * 4 + [ANYWHERE],
        out_specs=[IN_VMEM, IN_SMEM],
        compiler_params=pltpu.CompilerParams(vmem_limit_bytes=16 << 20),
    )(queries, attn_out, out_grad, segment.reshape(64, 128), own)
    qpay = exchange(q_packed)

    near_1 = swap(own, 1)
    near_3 = swap(own, 3)
    far_a = swap(near_3[:8], 1)
    far_b = swap(near_1[8:], 3)
    mine = (own, near_1, near_3, far_a, far_b)
    group = bf16(16, 2 * R, D)
    half = bf16(8, 2 * R, D)
    dq, keep_0, keep_1, keep_3, sum_a, sum_b, give_0, give_1, give_3, far_give = pl.pallas_call(
        attention_kernel,
        out_shape=[bf16(16, QR, D)] + [group] * 3 + [half] * 2 + [group] * 4,
        in_specs=[IN_SMEM] * 2 + [ANYWHERE] * 11,
        scratch_shapes=[
            pltpu.SMEM((NC * NT // 2 + W,), jnp.int32),
            pltpu.SMEM((NC * NT // 2 + W,), jnp.int32),
            pltpu.VMEM((NC + 1, C, D), BF16),
            pltpu.VMEM((NC + 1, C, D), BF16),
            pltpu.VMEM((16, 16, D), BF16),
            pltpu.VMEM((NT, 2, 2, R, 2 * D), BF16),
            pltpu.VMEM((NT, 2, 2, R, 2 * D), BF16),
            pltpu.VMEM((NT // 2, D, KB), BF16),
            pltpu.VMEM((NC + 1, 2 * D, C), BF16),
            pltpu.VMEM((NC + 1, 2 * D, C), BF16),
            pltpu.VMEM((NC, 1, C), F32),
            pltpu.VMEM((NC + 1, 8, C), F32),
            pltpu.VMEM((NT, 2, 2, R, D), F32),
            pltpu.VMEM((NT, 2, 2, R, D), F32),
            pltpu.VMEM((NC + 1, D, C), F32),
            pltpu.SemaphoreType.DMA,
            pltpu.SemaphoreType.DMA,
        ],
        compiler_params=pltpu.CompilerParams(vmem_limit_bytes=48 << 20),
    )(span_order, counts, qpay, *mine, *[flip(array) for array in mine])
    far_sum_a, far_sum_b = on_vmem(far_sum_kernel, [half, half], sum_a, sum_b, flip(far_give))
    from_1 = swap(far_sum_a, 1)
    from_3 = swap(far_sum_b, 3)
    to_1, to_3 = on_vmem(
        near_sum_kernel, [group] * 2, keep_1, flip(give_1), keep_3, flip(give_3), from_1, from_3
    )
    sums, query_grad = on_vmem(
        last_sum_kernel,
        [group, bf16(R, 8 * G * D)],
        keep_0,
        flip(give_0),
        swap(to_1, 1),
        swap(to_3, 3),
        exchange(dq),
    )
    key_grad, value_grad = on_vmem(unpack_kernel, [bf16(R, 8 * D)] * 2, exchange(sums))
    return query_grad, key_grad, value_grad


def solution(mesh):
    fine = Mesh(mesh.devices.reshape(4, 2, 2, 2, 4), AXES)
    rows = P(AXES, None)
    return jax.shard_map(
        body,
        mesh=fine,
        in_specs=(rows,) * 5 + (P(), P()),
        out_specs=(rows,) * 3,
        check_vma=False,
    )
```

```python
import math

import jax
import jax.numpy as jnp
from jax import lax
from jax.experimental import pallas as pl
from jax.experimental.pallas import tpu as pltpu
from jax.sharding import Mesh, PartitionSpec as P

D = 128
G = 4
R = 64
HR = R // 2
SPAN = 256
NT = 32
KB = 2 * SPAN
QR = G * HR
C = 2 * QR
NC = 8
W = 4
SCALE = D**-0.5
EXP_SCALE = SCALE * math.log2(math.e)
HIDDEN = -1e30
LARGE = 2.0**90
F32 = jnp.float32
BF16 = jnp.bfloat16
AXES = ("z", "core", "xh", "xl", "y")
SPREAD = ("xh", "xl", "z")
NT_DIMS = (((1,), (1,)), ((), ()))


def spread_to(g, xl):
    return (g // 4 * 2 + xl) * 4 + g % 4


def head_columns(g, h):
    return slice((g * G + h) * D, (g * G + h + 1) * D)


def pack_kv_kernel(keys, values, out, sem):
    copies = []
    for g in range(8):
        for xl in range(2):
            for part, array in enumerate((keys, values)):
                copies.append(
                    pltpu.make_async_copy(
                        array.at[:, pl.ds(g * D, D)],
                        out.at[spread_to(g, xl), pl.ds(part * R, R)],
                        sem,
                    )
                )
    for copy in copies:
        copy.start()
    for copy in copies:
        copy.wait()


def pack_q_kernel(queries, saved, grads, segment, after, out, counts):
    del after
    counts[0] = jnp.sum((segment[...] == 0).astype(jnp.int32))
    counts[1] = jnp.sum((segment[...] != 2).astype(jnp.int32))
    ones = jnp.ones((8, D), BF16)
    row = lax.broadcasted_iota(jnp.int32, (16, D), 0)
    for g in range(8):
        for half in range(2):
            dest = spread_to(g, half)
            rows = slice(half * HR, (half + 1) * HR)
            prods = []
            for h in range(G):
                cols = head_columns(g, h)
                grad = grads[rows, cols]
                out[dest, h * HR : (h + 1) * HR] = queries[rows, cols]
                out[dest, QR + h * HR : QR + (h + 1) * HR] = grad
                prods.append(grad.astype(F32) * saved[rows, cols].astype(F32))
            prod = jnp.concatenate(prods, axis=0)
            high = prod.astype(BF16)
            low = (prod - high.astype(F32)).astype(BF16)
            dot = lax.dot_general(ones, high, NT_DIMS, preferred_element_type=F32)
            dot = dot + lax.dot_general(ones, low, NT_DIMS, preferred_element_type=F32)
            both = jnp.concatenate([dot, dot], axis=0)
            rounded = both.astype(BF16).astype(F32)
            out[dest, 2 * QR :] = jnp.where(row == 0, rounded, both - rounded).astype(BF16)


def span_id(xh, xl, y, zh):
    return ((xh * 2 + xl) * 4 + y) * 2 + zh


def attention_kernel(order, counts, qpay, *refs):
    pieces = refs[:10]
    dq_out, keep_0, keep_1, keep_3, sum_a, sum_b, give_0, give_1, give_3, far_give = refs[10:20]
    plain_c, plain_b, q_s, do_s, d_s, k_s, v_s, kt_s, qa_s, ga_s = refs[20:30]
    m_s, l_s, dk_s, dv_s, dq_s, sem, value_sem = refs[30:]
    n0 = counts[0]
    n1 = counts[1]
    xl = lax.axis_index("xl")
    y = lax.axis_index("y")
    core = lax.axis_index("core")

    def place(dy, xh, xl, zh):
        return order[span_id(xh, xl, y ^ dy, zh)]

    copies = []
    value_copies = []
    for s in range(16):
        for part, dst in ((0, q_s), (1, do_s)):
            copies.append(
                pltpu.make_async_copy(
                    qpay.at[s, pl.ds(part * QR, QR)], dst.at[s // 2, pl.ds((s % 2) * QR, QR)], sem
                )
            )
    copies.append(pltpu.make_async_copy(qpay.at[:, pl.ds(2 * QR, 16)], d_s, sem))
    for number, piece in enumerate(pieces):
        from_core = core if number < 5 else 1 - core
        dy = (0, 1, 3, 2, 2)[number % 5]
        halves = ((0, 1), (0, 1), (0, 1), (0,), (1,))[number % 5]
        for at in range(4 * len(halves)):
            rank = place(dy, halves[at // 4], at // 2 % 2, at % 2)
            rows = piece.at[pl.ds(2 * at, 2)]
            copies.append(
                pltpu.make_async_copy(
                    rows.at[:, pl.ds(0, R)], k_s.at[rank, :, from_core, :, pl.ds(0, D)], sem
                )
            )
            value_copies.append(
                pltpu.make_async_copy(
                    rows.at[:, pl.ds(R, R)], v_s.at[rank, :, from_core, :, pl.ds(0, D)], value_sem
                )
            )
    for copy in copies + value_copies:
        copy.start()

    column = lax.broadcasted_iota(jnp.int32, (SPAN, D), 1)
    row = lax.broadcasted_iota(jnp.int32, (SPAN, D), 0)

    def put_beside(i, carry):
        chosen = (i * SPAN + row >= n0) & (i * SPAN + row < n1)
        beside = jnp.where((column < 3) | ((column == 3) & chosen), 1.0, 0.0).astype(BF16)
        beside = beside.reshape(1, 2, 2, R, D)
        k_s[pl.ds(i, 1), :, :, :, D:] = beside
        v_s[pl.ds(i, 1), :, :, :, D:] = beside
        return carry

    lax.fori_loop(0, NT, put_beside, 0, unroll=4)
    dk_s[...] = jnp.zeros_like(dk_s)
    dv_s[...] = jnp.zeros_like(dv_s)
    dq_s[...] = jnp.zeros_like(dq_s)

    def span_of(c):
        return order[span_id(c // 4, c // 2 % 2, y, c % 2)]

    def full_blocks(c):
        return span_of(c) // 2

    def list_chunk(c, size):
        all_second = span_of(c) * SPAN >= n1
        skip_at = (n0 + (KB - 1)) // KB
        skip_to = jnp.where(all_second, n1 // KB, 0)

        def put(b, n):
            hidden = (b >= skip_at) & (b < skip_to)
            plain_c[n] = c
            plain_b[n] = b
            return jnp.where(hidden, n, n + 1)

        return lax.fori_loop(0, full_blocks(c), put, size)

    n_plain = lax.fori_loop(0, NC, list_chunk, jnp.int32(0))
    for i in range(W - 1):
        plain_c[n_plain + i] = NC
        plain_b[n_plain + i] = 0

    for copy in copies:
        copy.wait()

    def block_of(ref, b):
        return ref[pl.ds(2 * b, 2)].reshape(KB, 2 * D)

    def keys_of(b):
        return k_s[pl.ds(2 * b, 2), :, :, :, :D].reshape(KB, D)

    def turn_keys(b, carry):
        kt_s[b] = keys_of(b).T
        return carry

    lax.fori_loop(0, NT // 2, turn_keys, 0, unroll=4)

    def put_under(ref, c, *rows):
        number = lax.broadcasted_iota(jnp.int32, (D, C), 0)
        block = jnp.zeros((D, C), F32)
        for i, values in enumerate(rows):
            block = jnp.where(number == i, values, block)
        ref[c, D:] = block.astype(BF16)

    def turn_rows(c, carry):
        qa_s[c, :D] = q_s[c].T
        ga_s[c, :D] = do_s[c].T
        halves = [d_s[2 * c + half].astype(F32) for half in range(2)]
        put_under(
            ga_s,
            c,
            -jnp.concatenate([half[0:1] for half in halves], axis=1),
            -jnp.concatenate([half[1:2] for half in halves], axis=1),
        )
        return carry

    lax.fori_loop(0, NC, turn_rows, 0, unroll=4)
    qa_s[NC, :D] = jnp.zeros((D, C), BF16)
    put_under(qa_s, NC, jnp.full((1, C), HIDDEN, F32))
    ga_s[NC] = jnp.zeros((2 * D, C), BF16)
    q_s[NC] = jnp.zeros((C, D), BF16)
    do_s[NC] = jnp.zeros((C, D), BF16)
    l_s[NC] = jnp.zeros((8, C), F32)

    def query_positions(c):
        lane = lax.broadcasted_iota(jnp.int32, (1, C), 1)
        start = span_of(c) * SPAN + core * R + xl * HR
        return start + (lane // QR) * (2 * R) + lane % HR

    def key_positions(b):
        return b * KB + lax.broadcasted_iota(jnp.int32, (KB, 1), 0)

    def seen(c, b):
        query_pos, key_pos = query_positions(c), key_positions(b)
        low = jnp.where(query_pos >= n1, n0, n1)
        return (key_pos <= query_pos) & ((key_pos < low) | (key_pos >= n1))

    def add_up(weights):
        return jnp.sum(weights.reshape(KB // 8, 8, C), axis=0)

    def raw_scores(c, b):
        return jnp.dot(keys_of(b), qa_s[c, :D], preferred_element_type=F32)

    def put_shift(c, *rows):
        rows = (rows + (jnp.zeros((1, C), F32),) * 3)[:3]
        hide = jnp.where(query_positions(c) >= n1, HIDDEN, 0.0)
        put_under(qa_s, c, *rows, hide)

    def weights_of(c, b, masked):
        scores = jnp.dot(block_of(k_s, b), qa_s[c], preferred_element_type=F32)
        if masked:
            scores = jnp.where(key_positions(b) <= query_positions(c), scores, HIDDEN)
        return jnp.exp2(scores * EXP_SCALE)

    def diagonal_step(i, carry):
        chunks = [W * i + k for k in range(W)]
        found = []
        for c in chunks:
            b = full_blocks(c)
            scores = jnp.where(seen(c, b), raw_scores(c, b), HIDDEN)
            top = jnp.max(scores, axis=0, keepdims=True).astype(BF16).astype(F32)
            found.append((top, add_up(jnp.exp2((scores - top) * EXP_SCALE))))
        for c, (top, total) in zip(chunks, found):
            put_shift(c, -top)
            m_s[c] = top * EXP_SCALE
            l_s[c] = total
        return carry

    lax.fori_loop(0, NC // W, diagonal_step, 0)

    def add_weights(items, masked):
        parts = [add_up(weights_of(c, b, masked)) for c, b in items]
        for (c, b), part in zip(items, parts):
            l_s[c] += part

    def plain_items(i):
        return [(plain_c[n], plain_b[n]) for n in [W * i + k for k in range(W)]]

    def plain_stats(i, carry):
        add_weights(plain_items(i), False)
        return carry

    lax.fori_loop(0, (n_plain + W - 1) // W, plain_stats, 0)

    @pl.when(jnp.logical_not(jnp.max(l_s[...]) < LARGE))
    def _():
        def careful(c, b):
            scores = jnp.where(seen(c, b), raw_scores(c, b) * EXP_SCALE, HIDDEN)
            old = m_s[c]
            top = jnp.maximum(old, jnp.max(scores, axis=0, keepdims=True))
            l_s[c] = l_s[c] * jnp.exp2(old - top) + add_up(jnp.exp2(scores - top))
            m_s[c] = top

        def careful_diagonal(c, carry):
            m_s[c] = jnp.full((1, C), HIDDEN, F32)
            l_s[c] = jnp.zeros((8, C), F32)
            careful(c, full_blocks(c))
            return carry

        def careful_plain(n, carry):
            careful(plain_c[n], plain_b[n])
            return carry

        lax.fori_loop(0, NC, careful_diagonal, 0)
        lax.fori_loop(0, n_plain, careful_plain, 0)

    def put_logsum(c, carry):
        logsum = m_s[c] + jnp.log2(jnp.sum(l_s[c], axis=0, keepdims=True))
        rest = logsum * (1.0 / EXP_SCALE)
        rows = []
        for _ in range(3):
            part = rest.astype(BF16).astype(F32)
            rows.append(-part)
            rest = rest - part
        put_shift(c, *rows)
        return carry

    lax.fori_loop(0, NC, put_logsum, 0, unroll=4)
    for copy in value_copies:
        copy.wait()

    def grad_step(items, masked):
        made = []
        for c, b in items:
            weights = weights_of(c, b, masked)
            above = jnp.dot(block_of(v_s, b), ga_s[c], preferred_element_type=F32)
            made.append((weights.astype(BF16), (weights * above).astype(BF16)))
        for (c, b), (weights, score_grad) in zip(items, made):
            for ref, term in (
                (dv_s, jnp.dot(weights, do_s[c], preferred_element_type=F32)),
                (dk_s, jnp.dot(score_grad, q_s[c], preferred_element_type=F32)),
            ):
                ref[pl.ds(2 * b, 2)] += term.reshape(2, 2, 2, R, D)
            dq_s[c] += jnp.dot(kt_s[b], score_grad, preferred_element_type=F32)

    def diagonal_grads(i, carry):
        grad_step([(c, full_blocks(c)) for c in [W * i + k for k in range(W)]], True)
        return carry

    def plain_grads(i, carry):
        grad_step(plain_items(i), False)
        return carry

    lax.fori_loop(0, NC // W, diagonal_grads, 0)
    lax.fori_loop(0, (n_plain + W - 1) // W, plain_grads, 0)

    def finish(c, carry):
        dq = (dq_s[c] * SCALE).T.astype(BF16)
        dq_out[2 * c] = dq[:QR]
        dq_out[2 * c + 1] = dq[QR:]
        return carry

    lax.fori_loop(0, NC, finish, 0, unroll=4)

    for from_core, group in (
        (core, ((0, keep_0, 0), (1, keep_1, 0), (3, keep_3, 0), (2, sum_a, 0), (2, sum_b, 1))),
        (1 - core, ((0, give_0, 0), (1, give_1, 0), (3, give_3, 0), (2, far_give, 0))),
    ):
        for dy, out, first_xh in group:
            for at in range(out.shape[0] // 2):
                rank = place(dy, first_xh + at // 4, at // 2 % 2, at % 2)
                rows = slice(2 * at, 2 * at + 2)
                out[rows, :R] = (dk_s[rank, :, from_core] * SCALE).astype(BF16)
                out[rows, R:] = dv_s[rank, :, from_core].astype(BF16)


def far_sum_kernel(sum_a, sum_b, got, out_a, out_b):
    out_a[...] = (sum_a[...].astype(F32) + got[:8].astype(F32)).astype(BF16)
    out_b[...] = (sum_b[...].astype(F32) + got[8:].astype(F32)).astype(BF16)


def near_sum_kernel(sum_1, got_1, sum_3, got_3, from_1, from_3, out_1, out_3):
    for rows, with_from in ((slice(0, 8), 3), (slice(8, 16), 1)):
        for number, keep, got, came, out in (
            (1, sum_1, got_1, from_3, out_1),
            (3, sum_3, got_3, from_1, out_3),
        ):
            total = keep[rows].astype(F32) + got[rows].astype(F32)
            if number == with_from:
                total = total + came[...].astype(F32)
            out[rows] = total.astype(BF16)


def last_sum_kernel(keep, got, near_1, near_3, dq, sums, query_grad):
    total = keep[...].astype(F32) + got[...].astype(F32)
    total = total + (near_1[...].astype(F32) + near_3[...].astype(F32))
    sums[...] = total.astype(BF16)
    for g in range(8):
        for half in range(2):
            rows = slice(half * HR, (half + 1) * HR)
            for h in range(G):
                query_grad[rows, head_columns(g, h)] = dq[spread_to(g, half), h * HR : (h + 1) * HR]


def unpack_kernel(got, key_grad, value_grad):
    for g in range(8):
        for start, out in ((0, key_grad), (R, value_grad)):
            total = got[spread_to(g, 0), start : start + R].astype(F32)
            total = total + got[spread_to(g, 1), start : start + R].astype(F32)
            out[:, g * D : (g + 1) * D] = total.astype(BF16)


def bf16(*shape):
    return jax.ShapeDtypeStruct(shape, BF16)


def on_vmem(kernel, outs, *args):
    return pl.pallas_call(
        kernel,
        out_shape=outs,
        compiler_params=pltpu.CompilerParams(vmem_limit_bytes=16 << 20),
    )(*args)


IN_SMEM = pl.BlockSpec(memory_space=pltpu.SMEM)
IN_VMEM = pl.BlockSpec(memory_space=pltpu.VMEM)
ANYWHERE = pl.BlockSpec(memory_space=pl.ANY)


def exchange(array):
    return lax.all_to_all(array, SPREAD, split_axis=0, concat_axis=0, tiled=True)


def flip(array):
    return lax.ppermute(array, "core", [(0, 1), (1, 0)])


def swap(array, distance):
    return lax.ppermute(array, "y", [(i, i ^ distance) for i in range(4)])


def body(queries, keys, values, attn_out, out_grad, segment, span_order):
    kv_packed = pl.pallas_call(
        pack_kv_kernel,
        out_shape=bf16(16, 2 * R, D),
        in_specs=[pl.BlockSpec(memory_space=pltpu.HBM)] * 2,
        scratch_shapes=[pltpu.SemaphoreType.DMA],
        compiler_params=pltpu.CompilerParams(vmem_limit_bytes=16 << 20),
    )(keys, values)
    own = exchange(kv_packed)
    q_packed, counts = pl.pallas_call(
        pack_q_kernel,
        out_shape=[bf16(16, 2 * QR + 16, D), jax.ShapeDtypeStruct((2,), jnp.int32)],
        in_specs=[IN_VMEM] * 4 + [ANYWHERE],
        out_specs=[IN_VMEM, IN_SMEM],
        compiler_params=pltpu.CompilerParams(vmem_limit_bytes=16 << 20),
    )(queries, attn_out, out_grad, segment.reshape(64, 128), own)
    qpay = exchange(q_packed)

    near_1 = swap(own, 1)
    near_3 = swap(own, 3)
    far_a = swap(near_3[:8], 1)
    far_b = swap(near_1[8:], 3)
    mine = (own, near_1, near_3, far_a, far_b)
    group = bf16(16, 2 * R, D)
    half = bf16(8, 2 * R, D)
    dq, keep_0, keep_1, keep_3, sum_a, sum_b, give_0, give_1, give_3, far_give = pl.pallas_call(
        attention_kernel,
        out_shape=[bf16(16, QR, D)] + [group] * 3 + [half] * 2 + [group] * 4,
        in_specs=[IN_SMEM] * 2 + [ANYWHERE] * 11,
        scratch_shapes=[
            pltpu.SMEM((NC * NT // 2 + W,), jnp.int32),
            pltpu.SMEM((NC * NT // 2 + W,), jnp.int32),
            pltpu.VMEM((NC + 1, C, D), BF16),
            pltpu.VMEM((NC + 1, C, D), BF16),
            pltpu.VMEM((16, 16, D), BF16),
            pltpu.VMEM((NT, 2, 2, R, 2 * D), BF16),
            pltpu.VMEM((NT, 2, 2, R, 2 * D), BF16),
            pltpu.VMEM((NT // 2, D, KB), BF16),
            pltpu.VMEM((NC + 1, 2 * D, C), BF16),
            pltpu.VMEM((NC + 1, 2 * D, C), BF16),
            pltpu.VMEM((NC, 1, C), F32),
            pltpu.VMEM((NC + 1, 8, C), F32),
            pltpu.VMEM((NT, 2, 2, R, D), F32),
            pltpu.VMEM((NT, 2, 2, R, D), F32),
            pltpu.VMEM((NC + 1, D, C), F32),
            pltpu.SemaphoreType.DMA,
            pltpu.SemaphoreType.DMA,
        ],
        compiler_params=pltpu.CompilerParams(vmem_limit_bytes=48 << 20),
    )(span_order, counts, qpay, *mine, *[flip(array) for array in mine])
    far_sum_a, far_sum_b = on_vmem(far_sum_kernel, [half, half], sum_a, sum_b, flip(far_give))
    from_1 = swap(far_sum_a, 1)
    from_3 = swap(far_sum_b, 3)
    to_1, to_3 = on_vmem(
        near_sum_kernel, [group] * 2, keep_1, flip(give_1), keep_3, flip(give_3), from_1, from_3
    )
    sums, query_grad = on_vmem(
        last_sum_kernel,
        [group, bf16(R, 8 * G * D)],
        keep_0,
        flip(give_0),
        swap(to_1, 1),
        swap(to_3, 3),
        exchange(dq),
    )
    key_grad, value_grad = on_vmem(unpack_kernel, [bf16(R, 8 * D)] * 2, exchange(sums))
    return query_grad, key_grad, value_grad


def solution(mesh):
    fine = Mesh(mesh.devices.reshape(4, 2, 2, 2, 4), AXES)
    rows = P(AXES, None)
    return jax.shard_map(
        body,
        mesh=fine,
        in_specs=(rows,) * 5 + (P(), P()),
        out_specs=(rows,) * 3,
        check_vma=False,
    )
```

```python
import math

import jax
import jax.numpy as jnp
from jax import lax
from jax.experimental import pallas as pl
from jax.experimental.pallas import tpu as pltpu
from jax.sharding import Mesh, PartitionSpec as P

D = 128
G = 4
R = 64
HR = R // 2
SPAN = 256
NT = 32
KB = 2 * SPAN
QR = G * HR
C = 2 * QR
NC = 8
W = 4
WG = 2
SCALE = D**-0.5
EXP_SCALE = SCALE * math.log2(math.e)
HIDDEN = -1e30
LARGE = 2.0**90
F32 = jnp.float32
BF16 = jnp.bfloat16
AXES = ("z", "core", "xh", "xl", "y")
SPREAD = ("xh", "xl", "z")
NT_DIMS = (((1,), (1,)), ((), ()))


def spread_to(g, xl):
    return (g // 4 * 2 + xl) * 4 + g % 4


def head_columns(g, h):
    return slice((g * G + h) * D, (g * G + h + 1) * D)


def pack_kv_kernel(keys, values, out, sem):
    copies = []
    for g in range(8):
        for xl in range(2):
            for part, array in enumerate((keys, values)):
                copies.append(
                    pltpu.make_async_copy(
                        array.at[:, pl.ds(g * D, D)],
                        out.at[spread_to(g, xl), pl.ds(part * R, R)],
                        sem,
                    )
                )
    for copy in copies:
        copy.start()
    for copy in copies:
        copy.wait()


def pack_q_kernel(queries, saved, grads, segment, after, out, counts):
    del after
    counts[0] = jnp.sum((segment[...] == 0).astype(jnp.int32))
    counts[1] = jnp.sum((segment[...] != 2).astype(jnp.int32))
    ones = jnp.ones((8, D), BF16)
    row = lax.broadcasted_iota(jnp.int32, (16, D), 0)
    for g in range(8):
        for half in range(2):
            dest = spread_to(g, half)
            rows = slice(half * HR, (half + 1) * HR)
            prods = []
            for h in range(G):
                cols = head_columns(g, h)
                grad = grads[rows, cols]
                out[dest, h * HR : (h + 1) * HR] = queries[rows, cols]
                out[dest, QR + h * HR : QR + (h + 1) * HR] = grad
                prods.append(grad.astype(F32) * saved[rows, cols].astype(F32))
            prod = jnp.concatenate(prods, axis=0)
            high = prod.astype(BF16)
            low = (prod - high.astype(F32)).astype(BF16)
            dot = lax.dot_general(ones, high, NT_DIMS, preferred_element_type=F32)
            dot = dot + lax.dot_general(ones, low, NT_DIMS, preferred_element_type=F32)
            both = jnp.concatenate([dot, dot], axis=0)
            rounded = both.astype(BF16).astype(F32)
            out[dest, 2 * QR :] = jnp.where(row == 0, rounded, both - rounded).astype(BF16)


def span_id(xh, xl, y, zh):
    return ((xh * 2 + xl) * 4 + y) * 2 + zh


def attention_kernel(order, counts, qpay, *refs):
    pieces = refs[:10]
    dq_out, keep_0, keep_1, keep_3, sum_a, sum_b, give_0, give_1, give_3, far_give = refs[10:20]
    plain_c, plain_b, q_s, do_s, d_s, k_s, v_s, kt_s, qa_s, ga_s = refs[20:30]
    m_s, l_s, dk_s, dv_s, dq_s, sem, value_sem = refs[30:]
    n0 = counts[0]
    n1 = counts[1]
    xl = lax.axis_index("xl")
    y = lax.axis_index("y")
    core = lax.axis_index("core")

    def place(dy, xh, xl, zh):
        return order[span_id(xh, xl, y ^ dy, zh)]

    copies = []
    value_copies = []
    for s in range(16):
        for part, dst in ((0, q_s), (1, do_s)):
            copies.append(
                pltpu.make_async_copy(
                    qpay.at[s, pl.ds(part * QR, QR)], dst.at[s // 2, pl.ds((s % 2) * QR, QR)], sem
                )
            )
    copies.append(pltpu.make_async_copy(qpay.at[:, pl.ds(2 * QR, 16)], d_s, sem))
    for number, piece in enumerate(pieces):
        from_core = core if number < 5 else 1 - core
        dy = (0, 1, 3, 2, 2)[number % 5]
        halves = ((0, 1), (0, 1), (0, 1), (0,), (1,))[number % 5]
        for at in range(4 * len(halves)):
            rank = place(dy, halves[at // 4], at // 2 % 2, at % 2)
            rows = piece.at[pl.ds(2 * at, 2)]
            copies.append(
                pltpu.make_async_copy(
                    rows.at[:, pl.ds(0, R)], k_s.at[rank, :, from_core, :, pl.ds(0, D)], sem
                )
            )
            value_copies.append(
                pltpu.make_async_copy(
                    rows.at[:, pl.ds(R, R)], v_s.at[rank, :, from_core, :, pl.ds(0, D)], value_sem
                )
            )
    for copy in copies + value_copies:
        copy.start()

    column = lax.broadcasted_iota(jnp.int32, (SPAN, D), 1)
    row = lax.broadcasted_iota(jnp.int32, (SPAN, D), 0)

    def put_beside(i, carry):
        chosen = (i * SPAN + row >= n0) & (i * SPAN + row < n1)
        beside = jnp.where((column < 3) | ((column == 3) & chosen), 1.0, 0.0).astype(BF16)
        beside = beside.reshape(1, 2, 2, R, D)
        k_s[pl.ds(i, 1), :, :, :, D:] = beside
        v_s[pl.ds(i, 1), :, :, :, D:] = beside
        return carry

    lax.fori_loop(0, NT, put_beside, 0, unroll=4)
    dk_s[...] = jnp.zeros_like(dk_s)
    dv_s[...] = jnp.zeros_like(dv_s)
    dq_s[...] = jnp.zeros_like(dq_s)

    def span_of(c):
        return order[span_id(c // 4, c // 2 % 2, y, c % 2)]

    def full_blocks(c):
        return span_of(c) // 2

    def list_chunk(c, size):
        all_second = span_of(c) * SPAN >= n1
        skip_at = (n0 + (KB - 1)) // KB
        skip_to = jnp.where(all_second, n1 // KB, 0)

        def put(b, n):
            hidden = (b >= skip_at) & (b < skip_to)
            plain_c[n] = c
            plain_b[n] = b
            return jnp.where(hidden, n, n + 1)

        return lax.fori_loop(0, full_blocks(c), put, size)

    n_plain = lax.fori_loop(0, NC, list_chunk, jnp.int32(0))
    for i in range(W - 1):
        plain_c[n_plain + i] = NC
        plain_b[n_plain + i] = 0

    for copy in copies:
        copy.wait()

    def block_of(ref, b):
        return ref[pl.ds(2 * b, 2)].reshape(KB, 2 * D)

    def keys_of(b):
        return k_s[pl.ds(2 * b, 2), :, :, :, :D].reshape(KB, D)

    def turn_keys(b, carry):
        kt_s[b] = keys_of(b).T
        return carry

    lax.fori_loop(0, NT // 2, turn_keys, 0, unroll=4)

    def put_under(ref, c, *rows):
        number = lax.broadcasted_iota(jnp.int32, (D, C), 0)
        block = jnp.zeros((D, C), F32)
        for i, values in enumerate(rows):
            block = jnp.where(number == i, values, block)
        ref[c, D:] = block.astype(BF16)

    def turn_rows(c, carry):
        qa_s[c, :D] = q_s[c].T
        ga_s[c, :D] = do_s[c].T
        halves = [d_s[2 * c + half].astype(F32) for half in range(2)]
        put_under(
            ga_s,
            c,
            -jnp.concatenate([half[0:1] for half in halves], axis=1),
            -jnp.concatenate([half[1:2] for half in halves], axis=1),
        )
        return carry

    lax.fori_loop(0, NC, turn_rows, 0, unroll=4)
    qa_s[NC, :D] = jnp.zeros((D, C), BF16)
    put_under(qa_s, NC, jnp.full((1, C), HIDDEN, F32))
    ga_s[NC] = jnp.zeros((2 * D, C), BF16)
    q_s[NC] = jnp.zeros((C, D), BF16)
    do_s[NC] = jnp.zeros((C, D), BF16)
    l_s[NC] = jnp.zeros((8, C), F32)

    def query_positions(c):
        lane = lax.broadcasted_iota(jnp.int32, (1, C), 1)
        start = span_of(c) * SPAN + core * R + xl * HR
        return start + (lane // QR) * (2 * R) + lane % HR

    def key_positions(b):
        return b * KB + lax.broadcasted_iota(jnp.int32, (KB, 1), 0)

    def seen(c, b):
        query_pos, key_pos = query_positions(c), key_positions(b)
        low = jnp.where(query_pos >= n1, n0, n1)
        return (key_pos <= query_pos) & ((key_pos < low) | (key_pos >= n1))

    def add_up(weights):
        return jnp.sum(weights.reshape(KB // 8, 8, C), axis=0)

    def raw_scores(c, b):
        return jnp.dot(keys_of(b), qa_s[c, :D], preferred_element_type=F32)

    def put_shift(c, *rows):
        rows = (rows + (jnp.zeros((1, C), F32),) * 3)[:3]
        hide = jnp.where(query_positions(c) >= n1, HIDDEN, 0.0)
        put_under(qa_s, c, *rows, hide)

    def weights_of(c, b, masked):
        scores = jnp.dot(block_of(k_s, b), qa_s[c], preferred_element_type=F32)
        if masked:
            scores = jnp.where(key_positions(b) <= query_positions(c), scores, HIDDEN)
        return jnp.exp2(scores * EXP_SCALE)

    def diagonal_step(i, carry):
        chunks = [W * i + k for k in range(W)]
        found = []
        for c in chunks:
            b = full_blocks(c)
            scores = jnp.where(seen(c, b), raw_scores(c, b), HIDDEN)
            top = jnp.max(scores, axis=0, keepdims=True).astype(BF16).astype(F32)
            found.append((top, add_up(jnp.exp2((scores - top) * EXP_SCALE))))
        for c, (top, total) in zip(chunks, found):
            put_shift(c, -top)
            m_s[c] = top * EXP_SCALE
            l_s[c] = total
        return carry

    lax.fori_loop(0, NC // W, diagonal_step, 0)

    def add_weights(items, masked):
        parts = [add_up(weights_of(c, b, masked)) for c, b in items]
        for (c, b), part in zip(items, parts):
            l_s[c] += part

    def plain_items(i, width):
        return [(plain_c[n], plain_b[n]) for n in [width * i + k for k in range(width)]]

    def plain_stats(i, carry):
        add_weights(plain_items(i, W), False)
        return carry

    lax.fori_loop(0, (n_plain + W - 1) // W, plain_stats, 0)

    @pl.when(jnp.logical_not(jnp.max(l_s[...]) < LARGE))
    def _():
        def careful(c, b):
            scores = jnp.where(seen(c, b), raw_scores(c, b) * EXP_SCALE, HIDDEN)
            old = m_s[c]
            top = jnp.maximum(old, jnp.max(scores, axis=0, keepdims=True))
            l_s[c] = l_s[c] * jnp.exp2(old - top) + add_up(jnp.exp2(scores - top))
            m_s[c] = top

        def careful_diagonal(c, carry):
            m_s[c] = jnp.full((1, C), HIDDEN, F32)
            l_s[c] = jnp.zeros((8, C), F32)
            careful(c, full_blocks(c))
            return carry

        def careful_plain(n, carry):
            careful(plain_c[n], plain_b[n])
            return carry

        lax.fori_loop(0, NC, careful_diagonal, 0)
        lax.fori_loop(0, n_plain, careful_plain, 0)

    def put_logsum(c, carry):
        logsum = m_s[c] + jnp.log2(jnp.sum(l_s[c], axis=0, keepdims=True))
        rest = logsum * (1.0 / EXP_SCALE)
        rows = []
        for _ in range(3):
            part = rest.astype(BF16).astype(F32)
            rows.append(-part)
            rest = rest - part
        put_shift(c, *rows)
        return carry

    lax.fori_loop(0, NC, put_logsum, 0, unroll=4)
    for copy in value_copies:
        copy.wait()

    def grad_step(items, masked):
        made = []
        for c, b in items:
            weights = weights_of(c, b, masked)
            above = jnp.dot(block_of(v_s, b), ga_s[c], preferred_element_type=F32)
            made.append((weights.astype(BF16), (weights * above).astype(BF16)))
        for (c, b), (weights, score_grad) in zip(items, made):
            for ref, term in (
                (dv_s, jnp.dot(weights, do_s[c], preferred_element_type=F32)),
                (dk_s, jnp.dot(score_grad, q_s[c], preferred_element_type=F32)),
            ):
                ref[pl.ds(2 * b, 2)] += term.reshape(2, 2, 2, R, D)
            dq_s[c] += jnp.dot(kt_s[b], score_grad, preferred_element_type=F32)

    def diagonal_grads(i, carry):
        grad_step([(c, full_blocks(c)) for c in [WG * i + k for k in range(WG)]], True)
        return carry

    def plain_grads(i, carry):
        grad_step(plain_items(i, WG), False)
        return carry

    lax.fori_loop(0, NC // WG, diagonal_grads, 0)
    lax.fori_loop(0, (n_plain + WG - 1) // WG, plain_grads, 0)

    def finish(c, carry):
        dq = (dq_s[c] * SCALE).T.astype(BF16)
        dq_out[2 * c] = dq[:QR]
        dq_out[2 * c + 1] = dq[QR:]
        return carry

    lax.fori_loop(0, NC, finish, 0, unroll=4)

    for from_core, group in (
        (core, ((0, keep_0, 0), (1, keep_1, 0), (3, keep_3, 0), (2, sum_a, 0), (2, sum_b, 1))),
        (1 - core, ((0, give_0, 0), (1, give_1, 0), (3, give_3, 0), (2, far_give, 0))),
    ):
        for dy, out, first_xh in group:
            for at in range(out.shape[0] // 2):
                rank = place(dy, first_xh + at // 4, at // 2 % 2, at % 2)
                rows = slice(2 * at, 2 * at + 2)
                out[rows, :R] = (dk_s[rank, :, from_core] * SCALE).astype(BF16)
                out[rows, R:] = dv_s[rank, :, from_core].astype(BF16)


def far_sum_kernel(sum_a, sum_b, got, out_a, out_b):
    out_a[...] = (sum_a[...].astype(F32) + got[:8].astype(F32)).astype(BF16)
    out_b[...] = (sum_b[...].astype(F32) + got[8:].astype(F32)).astype(BF16)


def near_sum_kernel(sum_1, got_1, sum_3, got_3, from_1, from_3, out_1, out_3):
    for rows, with_from in ((slice(0, 8), 3), (slice(8, 16), 1)):
        for number, keep, got, came, out in (
            (1, sum_1, got_1, from_3, out_1),
            (3, sum_3, got_3, from_1, out_3),
        ):
            total = keep[rows].astype(F32) + got[rows].astype(F32)
            if number == with_from:
                total = total + came[...].astype(F32)
            out[rows] = total.astype(BF16)


def last_sum_kernel(keep, got, near_1, near_3, dq, sums, query_grad):
    total = keep[...].astype(F32) + got[...].astype(F32)
    total = total + (near_1[...].astype(F32) + near_3[...].astype(F32))
    sums[...] = total.astype(BF16)
    for g in range(8):
        for half in range(2):
            rows = slice(half * HR, (half + 1) * HR)
            for h in range(G):
                query_grad[rows, head_columns(g, h)] = dq[spread_to(g, half), h * HR : (h + 1) * HR]


def unpack_kernel(got, key_grad, value_grad):
    for g in range(8):
        for start, out in ((0, key_grad), (R, value_grad)):
            total = got[spread_to(g, 0), start : start + R].astype(F32)
            total = total + got[spread_to(g, 1), start : start + R].astype(F32)
            out[:, g * D : (g + 1) * D] = total.astype(BF16)


def bf16(*shape):
    return jax.ShapeDtypeStruct(shape, BF16)


def on_vmem(kernel, outs, *args):
    return pl.pallas_call(
        kernel,
        out_shape=outs,
        compiler_params=pltpu.CompilerParams(vmem_limit_bytes=16 << 20),
    )(*args)


IN_SMEM = pl.BlockSpec(memory_space=pltpu.SMEM)
IN_VMEM = pl.BlockSpec(memory_space=pltpu.VMEM)
ANYWHERE = pl.BlockSpec(memory_space=pl.ANY)


def exchange(array):
    return lax.all_to_all(array, SPREAD, split_axis=0, concat_axis=0, tiled=True)


def flip(array):
    return lax.ppermute(array, "core", [(0, 1), (1, 0)])


def swap(array, distance):
    return lax.ppermute(array, "y", [(i, i ^ distance) for i in range(4)])


def body(queries, keys, values, attn_out, out_grad, segment, span_order):
    kv_packed = pl.pallas_call(
        pack_kv_kernel,
        out_shape=bf16(16, 2 * R, D),
        in_specs=[pl.BlockSpec(memory_space=pltpu.HBM)] * 2,
        scratch_shapes=[pltpu.SemaphoreType.DMA],
        compiler_params=pltpu.CompilerParams(vmem_limit_bytes=60 << 20),
    )(keys, values)
    own = exchange(kv_packed)
    q_packed, counts = pl.pallas_call(
        pack_q_kernel,
        out_shape=[bf16(16, 2 * QR + 16, D), jax.ShapeDtypeStruct((2,), jnp.int32)],
        in_specs=[IN_VMEM] * 4 + [ANYWHERE],
        out_specs=[IN_VMEM, IN_SMEM],
        compiler_params=pltpu.CompilerParams(vmem_limit_bytes=16 << 20),
    )(queries, attn_out, out_grad, segment.reshape(64, 128), own)
    qpay = exchange(q_packed)

    near_1 = swap(own, 1)
    near_3 = swap(own, 3)
    far_a = swap(near_3[:8], 1)
    far_b = swap(near_1[8:], 3)
    mine = (own, near_1, near_3, far_a, far_b)
    group = bf16(16, 2 * R, D)
    half = bf16(8, 2 * R, D)
    dq, keep_0, keep_1, keep_3, sum_a, sum_b, give_0, give_1, give_3, far_give = pl.pallas_call(
        attention_kernel,
        out_shape=[bf16(16, QR, D)] + [group] * 3 + [half] * 2 + [group] * 4,
        in_specs=[IN_SMEM] * 2 + [ANYWHERE] * 11,
        scratch_shapes=[
            pltpu.SMEM((NC * NT // 2 + W,), jnp.int32),
            pltpu.SMEM((NC * NT // 2 + W,), jnp.int32),
            pltpu.VMEM((NC + 1, C, D), BF16),
            pltpu.VMEM((NC + 1, C, D), BF16),
            pltpu.VMEM((16, 16, D), BF16),
            pltpu.VMEM((NT, 2, 2, R, 2 * D), BF16),
            pltpu.VMEM((NT, 2, 2, R, 2 * D), BF16),
            pltpu.VMEM((NT // 2, D, KB), BF16),
            pltpu.VMEM((NC + 1, 2 * D, C), BF16),
            pltpu.VMEM((NC + 1, 2 * D, C), BF16),
            pltpu.VMEM((NC, 1, C), F32),
            pltpu.VMEM((NC + 1, 8, C), F32),
            pltpu.VMEM((NT, 2, 2, R, D), F32),
            pltpu.VMEM((NT, 2, 2, R, D), F32),
            pltpu.VMEM((NC + 1, D, C), F32),
            pltpu.SemaphoreType.DMA,
            pltpu.SemaphoreType.DMA,
        ],
        compiler_params=pltpu.CompilerParams(vmem_limit_bytes=34 << 20),
    )(span_order, counts, qpay, *mine, *[flip(array) for array in mine])
    far_sum_a, far_sum_b = on_vmem(far_sum_kernel, [half, half], sum_a, sum_b, flip(far_give))
    from_1 = swap(far_sum_a, 1)
    from_3 = swap(far_sum_b, 3)
    to_1, to_3 = on_vmem(
        near_sum_kernel, [group] * 2, keep_1, flip(give_1), keep_3, flip(give_3), from_1, from_3
    )
    sums, query_grad = on_vmem(
        last_sum_kernel,
        [group, bf16(R, 8 * G * D)],
        keep_0,
        flip(give_0),
        swap(to_1, 1),
        swap(to_3, 3),
        exchange(dq),
    )
    key_grad, value_grad = on_vmem(unpack_kernel, [bf16(R, 8 * D)] * 2, exchange(sums))
    return query_grad, key_grad, value_grad


def solution(mesh):
    fine = Mesh(mesh.devices.reshape(4, 2, 2, 2, 4), AXES)
    rows = P(AXES, None)
    return jax.shard_map(
        body,
        mesh=fine,
        in_specs=(rows,) * 5 + (P(), P()),
        out_specs=(rows,) * 3,
        check_vma=False,
    )
```

```python
import math

import jax
import jax.numpy as jnp
from jax import lax
from jax.experimental import pallas as pl
from jax.experimental.pallas import tpu as pltpu
from jax.sharding import Mesh, PartitionSpec as P

D = 128
G = 4
R = 64
HR = R // 2
SPAN = 256
NT = 32
KB = 2 * SPAN
QR = G * HR
C = 2 * QR
NC = 8
W = 8
REST = 2
SCALE = D**-0.5
EXP_SCALE = SCALE * math.log2(math.e)
HIDDEN = -1e30
LARGE = 2.0**90
F32 = jnp.float32
BF16 = jnp.bfloat16
AXES = ("z", "core", "xh", "xl", "y")
SPREAD = ("xh", "xl", "z")
NT_DIMS = (((1,), (1,)), ((), ()))


def spread_to(g, xl):
    return (g // 4 * 2 + xl) * 4 + g % 4


def head_columns(g, h):
    return slice((g * G + h) * D, (g * G + h + 1) * D)


def pack_kv_kernel(keys, values, out, sem):
    copies = []
    for g in range(8):
        for xl in range(2):
            for part, array in enumerate((keys, values)):
                copies.append(
                    pltpu.make_async_copy(
                        array.at[:, pl.ds(g * D, D)],
                        out.at[spread_to(g, xl), pl.ds(part * R, R)],
                        sem,
                    )
                )
    for copy in copies:
        copy.start()
    for copy in copies:
        copy.wait()


def pack_q_kernel(queries, saved, grads, segment, after, out, counts):
    del after
    counts[0] = jnp.sum((segment[...] == 0).astype(jnp.int32))
    counts[1] = jnp.sum((segment[...] != 2).astype(jnp.int32))
    ones = jnp.ones((8, D), BF16)
    row = lax.broadcasted_iota(jnp.int32, (16, D), 0)
    for g in range(8):
        for half in range(2):
            dest = spread_to(g, half)
            rows = slice(half * HR, (half + 1) * HR)
            prods = []
            for h in range(G):
                cols = head_columns(g, h)
                grad = grads[rows, cols]
                out[dest, h * HR : (h + 1) * HR] = queries[rows, cols]
                out[dest, QR + h * HR : QR + (h + 1) * HR] = grad
                prods.append(grad.astype(F32) * saved[rows, cols].astype(F32))
            prod = jnp.concatenate(prods, axis=0)
            high = prod.astype(BF16)
            low = (prod - high.astype(F32)).astype(BF16)
            dot = lax.dot_general(ones, high, NT_DIMS, preferred_element_type=F32)
            dot = dot + lax.dot_general(ones, low, NT_DIMS, preferred_element_type=F32)
            both = jnp.concatenate([dot, dot], axis=0)
            rounded = both.astype(BF16).astype(F32)
            out[dest, 2 * QR :] = jnp.where(row == 0, rounded, both - rounded).astype(BF16)


def span_id(xh, xl, y, zh):
    return ((xh * 2 + xl) * 4 + y) * 2 + zh


def attention_kernel(order, counts, qpay, *refs):
    pieces = refs[:10]
    dq_out, keep_0, keep_1, keep_3, sum_a, sum_b, give_0, give_1, give_3, far_give = refs[10:20]
    plain_c, plain_b, q_s, do_s, d_s, k_s, v_s, kt_s, qa_s, ga_s = refs[20:30]
    m_s, l_s, dk_s, dv_s, dq_s, sem, value_sem = refs[30:]
    n0 = counts[0]
    n1 = counts[1]
    xl = lax.axis_index("xl")
    y = lax.axis_index("y")
    core = lax.axis_index("core")

    def place(dy, xh, xl, zh):
        return order[span_id(xh, xl, y ^ dy, zh)]

    copies = []
    value_copies = []
    for s in range(16):
        for part, dst in ((0, q_s), (1, do_s)):
            copies.append(
                pltpu.make_async_copy(
                    qpay.at[s, pl.ds(part * QR, QR)], dst.at[s // 2, pl.ds((s % 2) * QR, QR)], sem
                )
            )
    copies.append(pltpu.make_async_copy(qpay.at[:, pl.ds(2 * QR, 16)], d_s, sem))
    for number, piece in enumerate(pieces):
        from_core = core if number < 5 else 1 - core
        dy = (0, 1, 3, 2, 2)[number % 5]
        halves = ((0, 1), (0, 1), (0, 1), (0,), (1,))[number % 5]
        for at in range(4 * len(halves)):
            rank = place(dy, halves[at // 4], at // 2 % 2, at % 2)
            rows = piece.at[pl.ds(2 * at, 2)]
            copies.append(
                pltpu.make_async_copy(
                    rows.at[:, pl.ds(0, R)], k_s.at[rank, :, from_core, :, pl.ds(0, D)], sem
                )
            )
            value_copies.append(
                pltpu.make_async_copy(
                    rows.at[:, pl.ds(R, R)], v_s.at[rank, :, from_core, :, pl.ds(0, D)], value_sem
                )
            )
    for copy in copies + value_copies:
        copy.start()

    column = lax.broadcasted_iota(jnp.int32, (SPAN, D), 1)
    row = lax.broadcasted_iota(jnp.int32, (SPAN, D), 0)

    def put_beside(i, carry):
        chosen = (i * SPAN + row >= n0) & (i * SPAN + row < n1)
        beside = jnp.where((column < 3) | ((column == 3) & chosen), 1.0, 0.0).astype(BF16)
        beside = beside.reshape(1, 2, 2, R, D)
        k_s[pl.ds(i, 1), :, :, :, D:] = beside
        v_s[pl.ds(i, 1), :, :, :, D:] = beside
        return carry

    lax.fori_loop(0, NT, put_beside, 0, unroll=4)
    dk_s[...] = jnp.zeros_like(dk_s)
    dv_s[...] = jnp.zeros_like(dv_s)
    dq_s[...] = jnp.zeros_like(dq_s)

    def span_of(c):
        return order[span_id(c // 4, c // 2 % 2, y, c % 2)]

    def full_blocks(c):
        return span_of(c) // 2

    def list_chunk(c, size):
        all_second = span_of(c) * SPAN >= n1
        skip_at = (n0 + (KB - 1)) // KB
        skip_to = jnp.where(all_second, n1 // KB, 0)

        def put(b, n):
            hidden = (b >= skip_at) & (b < skip_to)
            plain_c[n] = c
            plain_b[n] = b
            return jnp.where(hidden, n, n + 1)

        return lax.fori_loop(0, full_blocks(c), put, size)

    n_plain = lax.fori_loop(0, NC, list_chunk, jnp.int32(0))
    for i in range(REST - 1):
        plain_c[n_plain + i] = NC
        plain_b[n_plain + i] = 0

    for copy in copies:
        copy.wait()

    def block_of(ref, b):
        return ref[pl.ds(2 * b, 2)].reshape(KB, 2 * D)

    def keys_of(b):
        return k_s[pl.ds(2 * b, 2), :, :, :, :D].reshape(KB, D)

    def turn_keys(b, carry):
        kt_s[b] = keys_of(b).T
        return carry

    lax.fori_loop(0, NT // 2, turn_keys, 0, unroll=4)

    def put_under(ref, c, *rows):
        number = lax.broadcasted_iota(jnp.int32, (D, C), 0)
        block = jnp.zeros((D, C), F32)
        for i, values in enumerate(rows):
            block = jnp.where(number == i, values, block)
        ref[c, D:] = block.astype(BF16)

    def turn_rows(c, carry):
        qa_s[c, :D] = q_s[c].T
        ga_s[c, :D] = do_s[c].T
        halves = [d_s[2 * c + half].astype(F32) for half in range(2)]
        put_under(
            ga_s,
            c,
            -jnp.concatenate([half[0:1] for half in halves], axis=1),
            -jnp.concatenate([half[1:2] for half in halves], axis=1),
        )
        return carry

    lax.fori_loop(0, NC, turn_rows, 0, unroll=4)
    qa_s[NC, :D] = jnp.zeros((D, C), BF16)
    put_under(qa_s, NC, jnp.full((1, C), HIDDEN, F32))
    ga_s[NC] = jnp.zeros((2 * D, C), BF16)
    q_s[NC] = jnp.zeros((C, D), BF16)
    do_s[NC] = jnp.zeros((C, D), BF16)
    l_s[NC] = jnp.zeros((8, C), F32)

    def query_positions(c):
        lane = lax.broadcasted_iota(jnp.int32, (1, C), 1)
        start = span_of(c) * SPAN + core * R + xl * HR
        return start + (lane // QR) * (2 * R) + lane % HR

    def key_positions(b):
        return b * KB + lax.broadcasted_iota(jnp.int32, (KB, 1), 0)

    def seen(c, b):
        query_pos, key_pos = query_positions(c), key_positions(b)
        low = jnp.where(query_pos >= n1, n0, n1)
        return (key_pos <= query_pos) & ((key_pos < low) | (key_pos >= n1))

    def add_up(weights):
        return jnp.sum(weights.reshape(KB // 8, 8, C), axis=0)

    def raw_scores(c, b):
        return jnp.dot(keys_of(b), qa_s[c, :D], preferred_element_type=F32)

    def put_shift(c, *rows):
        rows = (rows + (jnp.zeros((1, C), F32),) * 3)[:3]
        hide = jnp.where(query_positions(c) >= n1, HIDDEN, 0.0)
        put_under(qa_s, c, *rows, hide)

    def weights_of(c, b, masked):
        scores = jnp.dot(block_of(k_s, b), qa_s[c], preferred_element_type=F32)
        if masked:
            scores = jnp.where(key_positions(b) <= query_positions(c), scores, HIDDEN)
        return jnp.exp2(scores * EXP_SCALE)

    def diagonal_step(i, carry):
        chunks = [4 * i + k for k in range(4)]
        found = []
        for c in chunks:
            b = full_blocks(c)
            scores = jnp.where(seen(c, b), raw_scores(c, b), HIDDEN)
            top = jnp.max(scores, axis=0, keepdims=True).astype(BF16).astype(F32)
            found.append((top, add_up(jnp.exp2((scores - top) * EXP_SCALE))))
        for c, (top, total) in zip(chunks, found):
            put_shift(c, -top)
            m_s[c] = top * EXP_SCALE
            l_s[c] = total
        return carry

    lax.fori_loop(0, NC // 4, diagonal_step, 0)

    def add_weights(items, masked):
        parts = [add_up(weights_of(c, b, masked)) for c, b in items]
        for (c, b), part in zip(items, parts):
            l_s[c] += part

    def each_plain(step):
        def wide(i, carry):
            step([(plain_c[n], plain_b[n]) for n in [W * i + k for k in range(W)]], False)
            return carry

        def narrow(i, carry):
            step([(plain_c[n], plain_b[n]) for n in [REST * i + k for k in range(REST)]], False)
            return carry

        n_wide = n_plain // W
        lax.fori_loop(0, n_wide, wide, 0)
        lax.fori_loop(n_wide * (W // REST), (n_plain + (REST - 1)) // REST, narrow, 0)

    each_plain(add_weights)

    @pl.when(jnp.logical_not(jnp.max(l_s[...]) < LARGE))
    def _():
        def careful(c, b):
            scores = jnp.where(seen(c, b), raw_scores(c, b) * EXP_SCALE, HIDDEN)
            old = m_s[c]
            top = jnp.maximum(old, jnp.max(scores, axis=0, keepdims=True))
            l_s[c] = l_s[c] * jnp.exp2(old - top) + add_up(jnp.exp2(scores - top))
            m_s[c] = top

        def careful_diagonal(c, carry):
            m_s[c] = jnp.full((1, C), HIDDEN, F32)
            l_s[c] = jnp.zeros((8, C), F32)
            careful(c, full_blocks(c))
            return carry

        def careful_plain(n, carry):
            careful(plain_c[n], plain_b[n])
            return carry

        lax.fori_loop(0, NC, careful_diagonal, 0)
        lax.fori_loop(0, n_plain, careful_plain, 0)

    def put_logsum(c, carry):
        logsum = m_s[c] + jnp.log2(jnp.sum(l_s[c], axis=0, keepdims=True))
        rest = logsum * (1.0 / EXP_SCALE)
        rows = []
        for _ in range(3):
            part = rest.astype(BF16).astype(F32)
            rows.append(-part)
            rest = rest - part
        put_shift(c, *rows)
        return carry

    lax.fori_loop(0, NC, put_logsum, 0, unroll=4)
    for copy in value_copies:
        copy.wait()

    def grad_step(items, masked):
        made = []
        for c, b in items:
            weights = weights_of(c, b, masked)
            above = jnp.dot(block_of(v_s, b), ga_s[c], preferred_element_type=F32)
            made.append((weights.astype(BF16), (weights * above).astype(BF16)))
        for (c, b), (weights, score_grad) in zip(items, made):
            for ref, term in (
                (dv_s, jnp.dot(weights, do_s[c], preferred_element_type=F32)),
                (dk_s, jnp.dot(score_grad, q_s[c], preferred_element_type=F32)),
            ):
                ref[pl.ds(2 * b, 2)] += term.reshape(2, 2, 2, R, D)
            dq_s[c] += jnp.dot(kt_s[b], score_grad, preferred_element_type=F32)

    def diagonal_grads(i, carry):
        grad_step([(c, full_blocks(c)) for c in [4 * i + k for k in range(4)]], True)
        return carry

    lax.fori_loop(0, NC // 4, diagonal_grads, 0)
    each_plain(grad_step)

    def finish(c, carry):
        dq = (dq_s[c] * SCALE).T.astype(BF16)
        dq_out[2 * c] = dq[:QR]
        dq_out[2 * c + 1] = dq[QR:]
        return carry

    lax.fori_loop(0, NC, finish, 0, unroll=4)

    for from_core, group in (
        (core, ((0, keep_0, 0), (1, keep_1, 0), (3, keep_3, 0), (2, sum_a, 0), (2, sum_b, 1))),
        (1 - core, ((0, give_0, 0), (1, give_1, 0), (3, give_3, 0), (2, far_give, 0))),
    ):
        for dy, out, first_xh in group:
            for at in range(out.shape[0] // 2):
                rank = place(dy, first_xh + at // 4, at // 2 % 2, at % 2)
                rows = slice(2 * at, 2 * at + 2)
                out[rows, :R] = (dk_s[rank, :, from_core] * SCALE).astype(BF16)
                out[rows, R:] = dv_s[rank, :, from_core].astype(BF16)


def far_sum_kernel(sum_a, sum_b, got, out_a, out_b):
    out_a[...] = (sum_a[...].astype(F32) + got[:8].astype(F32)).astype(BF16)
    out_b[...] = (sum_b[...].astype(F32) + got[8:].astype(F32)).astype(BF16)


def near_sum_kernel(sum_1, got_1, sum_3, got_3, from_1, from_3, out_1, out_3):
    for rows, with_from in ((slice(0, 8), 3), (slice(8, 16), 1)):
        for number, keep, got, came, out in (
            (1, sum_1, got_1, from_3, out_1),
            (3, sum_3, got_3, from_1, out_3),
        ):
            total = keep[rows].astype(F32) + got[rows].astype(F32)
            if number == with_from:
                total = total + came[...].astype(F32)
            out[rows] = total.astype(BF16)


def last_sum_kernel(keep, got, near_1, near_3, dq, sums, query_grad):
    total = keep[...].astype(F32) + got[...].astype(F32)
    total = total + (near_1[...].astype(F32) + near_3[...].astype(F32))
    sums[...] = total.astype(BF16)
    for g in range(8):
        for half in range(2):
            rows = slice(half * HR, (half + 1) * HR)
            for h in range(G):
                query_grad[rows, head_columns(g, h)] = dq[spread_to(g, half), h * HR : (h + 1) * HR]


def unpack_kernel(got, key_grad, value_grad):
    for g in range(8):
        for start, out in ((0, key_grad), (R, value_grad)):
            total = got[spread_to(g, 0), start : start + R].astype(F32)
            total = total + got[spread_to(g, 1), start : start + R].astype(F32)
            out[:, g * D : (g + 1) * D] = total.astype(BF16)


def bf16(*shape):
    return jax.ShapeDtypeStruct(shape, BF16)


def on_vmem(kernel, outs, *args):
    return pl.pallas_call(
        kernel,
        out_shape=outs,
        compiler_params=pltpu.CompilerParams(vmem_limit_bytes=16 << 20),
    )(*args)


IN_SMEM = pl.BlockSpec(memory_space=pltpu.SMEM)
IN_VMEM = pl.BlockSpec(memory_space=pltpu.VMEM)
ANYWHERE = pl.BlockSpec(memory_space=pl.ANY)


def exchange(array):
    return lax.all_to_all(array, SPREAD, split_axis=0, concat_axis=0, tiled=True)


def flip(array):
    return lax.ppermute(array, "core", [(0, 1), (1, 0)])


def swap(array, distance):
    return lax.ppermute(array, "y", [(i, i ^ distance) for i in range(4)])


def body(queries, keys, values, attn_out, out_grad, segment, span_order):
    kv_packed = pl.pallas_call(
        pack_kv_kernel,
        out_shape=bf16(16, 2 * R, D),
        in_specs=[pl.BlockSpec(memory_space=pltpu.HBM)] * 2,
        scratch_shapes=[pltpu.SemaphoreType.DMA],
        compiler_params=pltpu.CompilerParams(vmem_limit_bytes=60 << 20),
    )(keys, values)
    own = exchange(kv_packed)
    q_packed, counts = pl.pallas_call(
        pack_q_kernel,
        out_shape=[bf16(16, 2 * QR + 16, D), jax.ShapeDtypeStruct((2,), jnp.int32)],
        in_specs=[IN_VMEM] * 4 + [ANYWHERE],
        out_specs=[IN_VMEM, IN_SMEM],
        compiler_params=pltpu.CompilerParams(vmem_limit_bytes=16 << 20),
    )(queries, attn_out, out_grad, segment.reshape(64, 128), own)
    qpay = exchange(q_packed)

    near_1 = swap(own, 1)
    near_3 = swap(own, 3)
    far_a = swap(near_3[:8], 1)
    far_b = swap(near_1[8:], 3)
    mine = (own, near_1, near_3, far_a, far_b)
    group = bf16(16, 2 * R, D)
    half = bf16(8, 2 * R, D)
    dq, keep_0, keep_1, keep_3, sum_a, sum_b, give_0, give_1, give_3, far_give = pl.pallas_call(
        attention_kernel,
        out_shape=[bf16(16, QR, D)] + [group] * 3 + [half] * 2 + [group] * 4,
        in_specs=[IN_SMEM] * 2 + [ANYWHERE] * 11,
        scratch_shapes=[
            pltpu.SMEM((NC * NT // 2 + W,), jnp.int32),
            pltpu.SMEM((NC * NT // 2 + W,), jnp.int32),
            pltpu.VMEM((NC + 1, C, D), BF16),
            pltpu.VMEM((NC + 1, C, D), BF16),
            pltpu.VMEM((16, 16, D), BF16),
            pltpu.VMEM((NT, 2, 2, R, 2 * D), BF16),
            pltpu.VMEM((NT, 2, 2, R, 2 * D), BF16),
            pltpu.VMEM((NT // 2, D, KB), BF16),
            pltpu.VMEM((NC + 1, 2 * D, C), BF16),
            pltpu.VMEM((NC + 1, 2 * D, C), BF16),
            pltpu.VMEM((NC, 1, C), F32),
            pltpu.VMEM((NC + 1, 8, C), F32),
            pltpu.VMEM((NT, 2, 2, R, D), F32),
            pltpu.VMEM((NT, 2, 2, R, D), F32),
            pltpu.VMEM((NC + 1, D, C), F32),
            pltpu.SemaphoreType.DMA,
            pltpu.SemaphoreType.DMA,
        ],
        compiler_params=pltpu.CompilerParams(vmem_limit_bytes=34 << 20),
    )(span_order, counts, qpay, *mine, *[flip(array) for array in mine])
    far_sum_a, far_sum_b = on_vmem(far_sum_kernel, [half, half], sum_a, sum_b, flip(far_give))
    from_1 = swap(far_sum_a, 1)
    from_3 = swap(far_sum_b, 3)
    to_1, to_3 = on_vmem(
        near_sum_kernel, [group] * 2, keep_1, flip(give_1), keep_3, flip(give_3), from_1, from_3
    )
    sums, query_grad = on_vmem(
        last_sum_kernel,
        [group, bf16(R, 8 * G * D)],
        keep_0,
        flip(give_0),
        swap(to_1, 1),
        swap(to_3, 3),
        exchange(dq),
    )
    key_grad, value_grad = on_vmem(unpack_kernel, [bf16(R, 8 * D)] * 2, exchange(sums))
    return query_grad, key_grad, value_grad


def solution(mesh):
    fine = Mesh(mesh.devices.reshape(4, 2, 2, 2, 4), AXES)
    rows = P(AXES, None)
    return jax.shard_map(
        body,
        mesh=fine,
        in_specs=(rows,) * 5 + (P(), P()),
        out_specs=(rows,) * 3,
        check_vma=False,
    )
```

```python
import math

import jax
import jax.numpy as jnp
from jax import lax
from jax.experimental import pallas as pl
from jax.experimental.pallas import tpu as pltpu
from jax.sharding import Mesh, PartitionSpec as P

D = 128
G = 4
R = 64
HR = R // 2
SPAN = 256
NT = 32
KB = 2 * SPAN
QR = G * HR
C = 2 * QR
NC = 8
WIDTHS = (8, 2)
REST = WIDTHS[-1]
SCALE = D**-0.5
EXP_SCALE = SCALE * math.log2(math.e)
HIDDEN = -1e30
LARGE = 2.0**90
F32 = jnp.float32
BF16 = jnp.bfloat16
AXES = ("z", "core", "xh", "xl", "y")
SPREAD = ("xh", "xl", "z")
NT_DIMS = (((1,), (1,)), ((), ()))


def spread_to(g, xl):
    return (g // 4 * 2 + xl) * 4 + g % 4


def head_columns(g, h):
    return slice((g * G + h) * D, (g * G + h + 1) * D)


def pack_kv_kernel(keys, values, out, sem):
    copies = []
    for g in range(8):
        for xl in range(2):
            for part, array in enumerate((keys, values)):
                copies.append(
                    pltpu.make_async_copy(
                        array.at[:, pl.ds(g * D, D)],
                        out.at[spread_to(g, xl), pl.ds(part * R, R)],
                        sem,
                    )
                )
    for copy in copies:
        copy.start()
    for copy in copies:
        copy.wait()


def pack_q_kernel(queries, saved, grads, segment, after, out, counts):
    del after
    counts[0] = jnp.sum((segment[...] == 0).astype(jnp.int32))
    counts[1] = jnp.sum((segment[...] != 2).astype(jnp.int32))
    ones = jnp.ones((8, D), BF16)
    row = lax.broadcasted_iota(jnp.int32, (16, D), 0)
    for g in range(8):
        for half in range(2):
            dest = spread_to(g, half)
            rows = slice(half * HR, (half + 1) * HR)
            prods = []
            for h in range(G):
                cols = head_columns(g, h)
                grad = grads[rows, cols]
                out[dest, h * HR : (h + 1) * HR] = queries[rows, cols]
                out[dest, QR + h * HR : QR + (h + 1) * HR] = grad
                prods.append(grad.astype(F32) * saved[rows, cols].astype(F32))
            prod = jnp.concatenate(prods, axis=0)
            high = prod.astype(BF16)
            low = (prod - high.astype(F32)).astype(BF16)
            dot = lax.dot_general(ones, high, NT_DIMS, preferred_element_type=F32)
            dot = dot + lax.dot_general(ones, low, NT_DIMS, preferred_element_type=F32)
            both = jnp.concatenate([dot, dot], axis=0)
            rounded = both.astype(BF16).astype(F32)
            out[dest, 2 * QR :] = jnp.where(row == 0, rounded, both - rounded).astype(BF16)


def span_id(xh, xl, y, zh):
    return ((xh * 2 + xl) * 4 + y) * 2 + zh


def attention_kernel(order, counts, qpay, *refs):
    pieces = refs[:10]
    dq_out, keep_0, keep_1, keep_3, sum_a, sum_b, give_0, give_1, give_3, far_give = refs[10:20]
    plain_c, plain_b, q_s, do_s, d_s, k_s, v_s, kt_s, qa_s, ga_s = refs[20:30]
    m_s, l_s, dk_s, dv_s, dq_s, sem, value_sem = refs[30:]
    n0 = counts[0]
    n1 = counts[1]
    xl = lax.axis_index("xl")
    y = lax.axis_index("y")
    core = lax.axis_index("core")

    def place(dy, xh, xl, zh):
        return order[span_id(xh, xl, y ^ dy, zh)]

    copies = []
    value_copies = []
    for s in range(16):
        for part, dst in ((0, q_s), (1, do_s)):
            copies.append(
                pltpu.make_async_copy(
                    qpay.at[s, pl.ds(part * QR, QR)], dst.at[s // 2, pl.ds((s % 2) * QR, QR)], sem
                )
            )
    copies.append(pltpu.make_async_copy(qpay.at[:, pl.ds(2 * QR, 16)], d_s, sem))
    for number, piece in enumerate(pieces):
        from_core = core if number < 5 else 1 - core
        dy = (0, 1, 3, 2, 2)[number % 5]
        halves = ((0, 1), (0, 1), (0, 1), (0,), (1,))[number % 5]
        for at in range(4 * len(halves)):
            rank = place(dy, halves[at // 4], at // 2 % 2, at % 2)
            rows = piece.at[pl.ds(2 * at, 2)]
            copies.append(
                pltpu.make_async_copy(
                    rows.at[:, pl.ds(0, R)], k_s.at[rank, :, from_core, :, pl.ds(0, D)], sem
                )
            )
            value_copies.append(
                pltpu.make_async_copy(
                    rows.at[:, pl.ds(R, R)], v_s.at[rank, :, from_core, :, pl.ds(0, D)], value_sem
                )
            )
    for copy in copies + value_copies:
        copy.start()

    column = lax.broadcasted_iota(jnp.int32, (SPAN, D), 1)
    row = lax.broadcasted_iota(jnp.int32, (SPAN, D), 0)

    def put_beside(i, carry):
        chosen = (i * SPAN + row >= n0) & (i * SPAN + row < n1)
        beside = jnp.where((column < 3) | ((column == 3) & chosen), 1.0, 0.0).astype(BF16)
        beside = beside.reshape(1, 2, 2, R, D)
        k_s[pl.ds(i, 1), :, :, :, D:] = beside
        v_s[pl.ds(i, 1), :, :, :, D:] = beside
        return carry

    lax.fori_loop(0, NT, put_beside, 0, unroll=4)
    dk_s[...] = jnp.zeros_like(dk_s)
    dv_s[...] = jnp.zeros_like(dv_s)
    dq_s[...] = jnp.zeros_like(dq_s)

    def span_of(c):
        return order[span_id(c // 4, c // 2 % 2, y, c % 2)]

    def full_blocks(c):
        return span_of(c) // 2

    def list_chunk(c, size):
        all_second = span_of(c) * SPAN >= n1
        skip_at = (n0 + (KB - 1)) // KB
        skip_to = jnp.where(all_second, n1 // KB, 0)

        def put(b, n):
            hidden = (b >= skip_at) & (b < skip_to)
            plain_c[n] = c
            plain_b[n] = b
            return jnp.where(hidden, n, n + 1)

        return lax.fori_loop(0, full_blocks(c), put, size)

    n_plain = lax.fori_loop(0, NC, list_chunk, jnp.int32(0))
    for i in range(REST - 1):
        plain_c[n_plain + i] = NC
        plain_b[n_plain + i] = 0

    for copy in copies:
        copy.wait()

    def block_of(ref, b):
        return ref[pl.ds(2 * b, 2)].reshape(KB, 2 * D)

    def keys_of(b):
        return k_s[pl.ds(2 * b, 2), :, :, :, :D].reshape(KB, D)

    def turn_keys(b, carry):
        kt_s[b] = keys_of(b).T
        return carry

    lax.fori_loop(0, NT // 2, turn_keys, 0, unroll=4)

    def put_under(ref, c, *rows):
        number = lax.broadcasted_iota(jnp.int32, (D, C), 0)
        block = jnp.zeros((D, C), F32)
        for i, values in enumerate(rows):
            block = jnp.where(number == i, values, block)
        ref[c, D:] = block.astype(BF16)

    def turn_rows(c, carry):
        qa_s[c, :D] = q_s[c].T
        ga_s[c, :D] = do_s[c].T
        halves = [d_s[2 * c + half].astype(F32) for half in range(2)]
        put_under(
            ga_s,
            c,
            -jnp.concatenate([half[0:1] for half in halves], axis=1),
            -jnp.concatenate([half[1:2] for half in halves], axis=1),
        )
        return carry

    lax.fori_loop(0, NC, turn_rows, 0, unroll=4)
    qa_s[NC, :D] = jnp.zeros((D, C), BF16)
    put_under(qa_s, NC, jnp.full((1, C), HIDDEN, F32))
    ga_s[NC] = jnp.zeros((2 * D, C), BF16)
    q_s[NC] = jnp.zeros((C, D), BF16)
    do_s[NC] = jnp.zeros((C, D), BF16)
    l_s[NC] = jnp.zeros((8, C), F32)

    def query_positions(c):
        lane = lax.broadcasted_iota(jnp.int32, (1, C), 1)
        start = span_of(c) * SPAN + core * R + xl * HR
        return start + (lane // QR) * (2 * R) + lane % HR

    def key_positions(b):
        return b * KB + lax.broadcasted_iota(jnp.int32, (KB, 1), 0)

    def seen(c, b):
        query_pos, key_pos = query_positions(c), key_positions(b)
        low = jnp.where(query_pos >= n1, n0, n1)
        return (key_pos <= query_pos) & ((key_pos < low) | (key_pos >= n1))

    def add_up(weights):
        return jnp.sum(weights.reshape(KB // 8, 8, C), axis=0)

    def raw_scores(c, b):
        return jnp.dot(keys_of(b), qa_s[c, :D], preferred_element_type=F32)

    def put_shift(c, *rows):
        rows = (rows + (jnp.zeros((1, C), F32),) * 3)[:3]
        hide = jnp.where(query_positions(c) >= n1, HIDDEN, 0.0)
        put_under(qa_s, c, *rows, hide)

    def weights_of(c, b, masked):
        scores = jnp.dot(block_of(k_s, b), qa_s[c], preferred_element_type=F32)
        if masked:
            scores = jnp.where(key_positions(b) <= query_positions(c), scores, HIDDEN)
        return jnp.exp2(scores * EXP_SCALE)

    found = []
    for c in range(NC):
        b = full_blocks(c)
        scores = jnp.where(seen(c, b), raw_scores(c, b), HIDDEN)
        top = jnp.max(scores, axis=0, keepdims=True).astype(BF16).astype(F32)
        found.append((top, add_up(jnp.exp2((scores - top) * EXP_SCALE))))
    for c, (top, total) in enumerate(found):
        put_shift(c, -top)
        m_s[c] = top * EXP_SCALE
        l_s[c] = total

    def add_weights(items, masked):
        parts = [add_up(weights_of(c, b, masked)) for c, b in items]
        for (c, b), part in zip(items, parts):
            l_s[c] += part

    def each_plain(step):
        done = jnp.int32(0)
        for width in WIDTHS:

            def some(i, carry, width=width, done=done):
                at = [done + width * i + k for k in range(width)]
                step([(plain_c[n], plain_b[n]) for n in at], False)
                return carry

            left = n_plain - done
            count = (left + (REST - 1)) // width if width == REST else left // width
            lax.fori_loop(0, count, some, 0)
            done = done + count * width

    each_plain(add_weights)

    @pl.when(jnp.logical_not(jnp.max(l_s[...]) < LARGE))
    def _():
        def careful(c, b):
            scores = jnp.where(seen(c, b), raw_scores(c, b) * EXP_SCALE, HIDDEN)
            old = m_s[c]
            top = jnp.maximum(old, jnp.max(scores, axis=0, keepdims=True))
            l_s[c] = l_s[c] * jnp.exp2(old - top) + add_up(jnp.exp2(scores - top))
            m_s[c] = top

        def careful_diagonal(c, carry):
            m_s[c] = jnp.full((1, C), HIDDEN, F32)
            l_s[c] = jnp.zeros((8, C), F32)
            careful(c, full_blocks(c))
            return carry

        def careful_plain(n, carry):
            careful(plain_c[n], plain_b[n])
            return carry

        lax.fori_loop(0, NC, careful_diagonal, 0)
        lax.fori_loop(0, n_plain, careful_plain, 0)

    def put_logsum(c, carry):
        logsum = m_s[c] + jnp.log2(jnp.sum(l_s[c], axis=0, keepdims=True))
        rest = logsum * (1.0 / EXP_SCALE)
        rows = []
        for _ in range(3):
            part = rest.astype(BF16).astype(F32)
            rows.append(-part)
            rest = rest - part
        put_shift(c, *rows)
        return carry

    lax.fori_loop(0, NC, put_logsum, 0, unroll=4)
    for copy in value_copies:
        copy.wait()

    def grad_step(items, masked):
        made = []
        for c, b in items:
            weights = weights_of(c, b, masked)
            above = jnp.dot(block_of(v_s, b), ga_s[c], preferred_element_type=F32)
            made.append((weights.astype(BF16), (weights * above).astype(BF16)))
        for (c, b), (weights, score_grad) in zip(items, made):
            for ref, term in (
                (dv_s, jnp.dot(weights, do_s[c], preferred_element_type=F32)),
                (dk_s, jnp.dot(score_grad, q_s[c], preferred_element_type=F32)),
            ):
                ref[pl.ds(2 * b, 2)] += term.reshape(2, 2, 2, R, D)
            dq_s[c] += jnp.dot(kt_s[b], score_grad, preferred_element_type=F32)

    grad_step([(c, full_blocks(c)) for c in range(NC)], True)
    each_plain(grad_step)

    def finish(c, carry):
        dq = (dq_s[c] * SCALE).T.astype(BF16)
        dq_out[2 * c] = dq[:QR]
        dq_out[2 * c + 1] = dq[QR:]
        return carry

    lax.fori_loop(0, NC, finish, 0, unroll=4)

    for from_core, group in (
        (core, ((0, keep_0, 0), (1, keep_1, 0), (3, keep_3, 0), (2, sum_a, 0), (2, sum_b, 1))),
        (1 - core, ((0, give_0, 0), (1, give_1, 0), (3, give_3, 0), (2, far_give, 0))),
    ):
        for dy, out, first_xh in group:
            for at in range(out.shape[0] // 2):
                rank = place(dy, first_xh + at // 4, at // 2 % 2, at % 2)
                rows = slice(2 * at, 2 * at + 2)
                out[rows, :R] = (dk_s[rank, :, from_core] * SCALE).astype(BF16)
                out[rows, R:] = dv_s[rank, :, from_core].astype(BF16)


def far_sum_kernel(sum_a, sum_b, got, out_a, out_b):
    out_a[...] = (sum_a[...].astype(F32) + got[:8].astype(F32)).astype(BF16)
    out_b[...] = (sum_b[...].astype(F32) + got[8:].astype(F32)).astype(BF16)


def near_sum_kernel(sum_1, got_1, sum_3, got_3, from_1, from_3, out_1, out_3):
    for rows, with_from in ((slice(0, 8), 3), (slice(8, 16), 1)):
        for number, keep, got, came, out in (
            (1, sum_1, got_1, from_3, out_1),
            (3, sum_3, got_3, from_1, out_3),
        ):
            total = keep[rows].astype(F32) + got[rows].astype(F32)
            if number == with_from:
                total = total + came[...].astype(F32)
            out[rows] = total.astype(BF16)


def last_sum_kernel(keep, got, near_1, near_3, dq, sums, query_grad):
    total = keep[...].astype(F32) + got[...].astype(F32)
    total = total + (near_1[...].astype(F32) + near_3[...].astype(F32))
    sums[...] = total.astype(BF16)
    for g in range(8):
        for half in range(2):
            rows = slice(half * HR, (half + 1) * HR)
            for h in range(G):
                query_grad[rows, head_columns(g, h)] = dq[spread_to(g, half), h * HR : (h + 1) * HR]


def unpack_kernel(got, key_grad, value_grad):
    for g in range(8):
        for start, out in ((0, key_grad), (R, value_grad)):
            total = got[spread_to(g, 0), start : start + R].astype(F32)
            total = total + got[spread_to(g, 1), start : start + R].astype(F32)
            out[:, g * D : (g + 1) * D] = total.astype(BF16)


def bf16(*shape):
    return jax.ShapeDtypeStruct(shape, BF16)


def on_vmem(kernel, outs, *args):
    return pl.pallas_call(
        kernel,
        out_shape=outs,
        compiler_params=pltpu.CompilerParams(vmem_limit_bytes=16 << 20),
    )(*args)


IN_SMEM = pl.BlockSpec(memory_space=pltpu.SMEM)
IN_VMEM = pl.BlockSpec(memory_space=pltpu.VMEM)
ANYWHERE = pl.BlockSpec(memory_space=pl.ANY)


def exchange(array):
    return lax.all_to_all(array, SPREAD, split_axis=0, concat_axis=0, tiled=True)


def flip(array):
    return lax.ppermute(array, "core", [(0, 1), (1, 0)])


def swap(array, distance):
    return lax.ppermute(array, "y", [(i, i ^ distance) for i in range(4)])


def body(queries, keys, values, attn_out, out_grad, segment, span_order):
    kv_packed = pl.pallas_call(
        pack_kv_kernel,
        out_shape=bf16(16, 2 * R, D),
        in_specs=[pl.BlockSpec(memory_space=pltpu.HBM)] * 2,
        scratch_shapes=[pltpu.SemaphoreType.DMA],
        compiler_params=pltpu.CompilerParams(vmem_limit_bytes=60 << 20),
    )(keys, values)
    own = exchange(kv_packed)
    q_packed, counts = pl.pallas_call(
        pack_q_kernel,
        out_shape=[bf16(16, 2 * QR + 16, D), jax.ShapeDtypeStruct((2,), jnp.int32)],
        in_specs=[IN_VMEM] * 4 + [ANYWHERE],
        out_specs=[IN_VMEM, IN_SMEM],
        compiler_params=pltpu.CompilerParams(vmem_limit_bytes=16 << 20),
    )(queries, attn_out, out_grad, segment.reshape(64, 128), own)
    qpay = exchange(q_packed)

    near_1 = swap(own, 1)
    near_3 = swap(own, 3)
    far_a = swap(near_3[:8], 1)
    far_b = swap(near_1[8:], 3)
    mine = (own, near_1, near_3, far_a, far_b)
    group = bf16(16, 2 * R, D)
    half = bf16(8, 2 * R, D)
    dq, keep_0, keep_1, keep_3, sum_a, sum_b, give_0, give_1, give_3, far_give = pl.pallas_call(
        attention_kernel,
        out_shape=[bf16(16, QR, D)] + [group] * 3 + [half] * 2 + [group] * 4,
        in_specs=[IN_SMEM] * 2 + [ANYWHERE] * 11,
        scratch_shapes=[
            pltpu.SMEM((NC * NT // 2 + REST,), jnp.int32),
            pltpu.SMEM((NC * NT // 2 + REST,), jnp.int32),
            pltpu.VMEM((NC + 1, C, D), BF16),
            pltpu.VMEM((NC + 1, C, D), BF16),
            pltpu.VMEM((16, 16, D), BF16),
            pltpu.VMEM((NT, 2, 2, R, 2 * D), BF16),
            pltpu.VMEM((NT, 2, 2, R, 2 * D), BF16),
            pltpu.VMEM((NT // 2, D, KB), BF16),
            pltpu.VMEM((NC + 1, 2 * D, C), BF16),
            pltpu.VMEM((NC + 1, 2 * D, C), BF16),
            pltpu.VMEM((NC, 1, C), F32),
            pltpu.VMEM((NC + 1, 8, C), F32),
            pltpu.VMEM((NT, 2, 2, R, D), F32),
            pltpu.VMEM((NT, 2, 2, R, D), F32),
            pltpu.VMEM((NC + 1, D, C), F32),
            pltpu.SemaphoreType.DMA,
            pltpu.SemaphoreType.DMA,
        ],
        compiler_params=pltpu.CompilerParams(vmem_limit_bytes=40 << 20),
    )(span_order, counts, qpay, *mine, *[flip(array) for array in mine])
    far_sum_a, far_sum_b = on_vmem(far_sum_kernel, [half, half], sum_a, sum_b, flip(far_give))
    from_1 = swap(far_sum_a, 1)
    from_3 = swap(far_sum_b, 3)
    to_1, to_3 = on_vmem(
        near_sum_kernel, [group] * 2, keep_1, flip(give_1), keep_3, flip(give_3), from_1, from_3
    )
    sums, query_grad = on_vmem(
        last_sum_kernel,
        [group, bf16(R, 8 * G * D)],
        keep_0,
        flip(give_0),
        swap(to_1, 1),
        swap(to_3, 3),
        exchange(dq),
    )
    key_grad, value_grad = on_vmem(unpack_kernel, [bf16(R, 8 * D)] * 2, exchange(sums))
    return query_grad, key_grad, value_grad


def solution(mesh):
    fine = Mesh(mesh.devices.reshape(4, 2, 2, 2, 4), AXES)
    rows = P(AXES, None)
    return jax.shard_map(
        body,
        mesh=fine,
        in_specs=(rows,) * 5 + (P(), P()),
        out_specs=(rows,) * 3,
        check_vma=False,
    )
```

```python
import math

import jax
import jax.numpy as jnp
from jax import lax
from jax.experimental import pallas as pl
from jax.experimental.pallas import tpu as pltpu
from jax.sharding import Mesh, PartitionSpec as P

D = 128
G = 4
R = 64
HR = R // 2
SPAN = 256
NT = 32
KB = 2 * SPAN
QR = G * HR
C = 2 * QR
NC = 8
REST = 2
STATS_WIDTHS = (16, 4, REST)
GRAD_WIDTHS = (8, 4, REST)
SCALE = D**-0.5
EXP_SCALE = SCALE * math.log2(math.e)
HIDDEN = -1e30
LARGE = 2.0**90
F32 = jnp.float32
BF16 = jnp.bfloat16
AXES = ("z", "core", "xh", "xl", "y")
SPREAD = ("xh", "xl", "z")
NT_DIMS = (((1,), (1,)), ((), ()))


def spread_to(g, xl):
    return (g // 4 * 2 + xl) * 4 + g % 4


def head_columns(g, h):
    return slice((g * G + h) * D, (g * G + h + 1) * D)


def pack_kv_kernel(keys, values, out, sem):
    copies = []
    for g in range(8):
        for xl in range(2):
            for part, array in enumerate((keys, values)):
                copies.append(
                    pltpu.make_async_copy(
                        array.at[:, pl.ds(g * D, D)],
                        out.at[spread_to(g, xl), pl.ds(part * R, R)],
                        sem,
                    )
                )
    for copy in copies:
        copy.start()
    for copy in copies:
        copy.wait()


def pack_q_kernel(queries, saved, grads, segment, after, packed, counts, out, sem):
    del after
    counts[0] = jnp.sum((segment[...] == 0).astype(jnp.int32))
    counts[1] = jnp.sum((segment[...] != 2).astype(jnp.int32))
    copies = []
    ones = jnp.ones((8, D), BF16)
    row = lax.broadcasted_iota(jnp.int32, (16, D), 0)
    for g in range(8):
        for half in range(2):
            dest = spread_to(g, half)
            rows = slice(half * HR, (half + 1) * HR)
            prods = []
            for h in range(G):
                cols = head_columns(g, h)
                grad = grads[rows, cols]
                out[dest, h * HR : (h + 1) * HR] = queries[rows, cols]
                out[dest, QR + h * HR : QR + (h + 1) * HR] = grad
                prods.append(grad.astype(F32) * saved[rows, cols].astype(F32))
            prod = jnp.concatenate(prods, axis=0)
            high = prod.astype(BF16)
            low = (prod - high.astype(F32)).astype(BF16)
            dot = lax.dot_general(ones, high, NT_DIMS, preferred_element_type=F32)
            dot = dot + lax.dot_general(ones, low, NT_DIMS, preferred_element_type=F32)
            both = jnp.concatenate([dot, dot], axis=0)
            rounded = both.astype(BF16).astype(F32)
            out[dest, 2 * QR :] = jnp.where(row == 0, rounded, both - rounded).astype(BF16)
            copies.append(pltpu.make_async_copy(out.at[dest], packed.at[dest], sem))
            copies[-1].start()
    for copy in copies:
        copy.wait()


def span_id(xh, xl, y, zh):
    return ((xh * 2 + xl) * 4 + y) * 2 + zh


def attention_kernel(order, counts, qpay, *refs):
    pieces = refs[:10]
    dq_out, keep_0, keep_1, keep_3, sum_a, sum_b, give_0, give_1, give_3, far_give = refs[10:20]
    plain_c, plain_b, q_s, do_s, d_s, k_s, v_s, kt_s, qa_s, ga_s = refs[20:30]
    m_s, l_s, dk_s, dv_s, dq_s, sem, value_sem = refs[30:]
    n0 = counts[0]
    n1 = counts[1]
    xl = lax.axis_index("xl")
    y = lax.axis_index("y")
    core = lax.axis_index("core")

    def place(dy, xh, xl, zh):
        return order[span_id(xh, xl, y ^ dy, zh)]

    copies = []
    value_copies = []
    for s in range(16):
        for part, dst in ((0, q_s), (1, do_s)):
            copies.append(
                pltpu.make_async_copy(
                    qpay.at[s, pl.ds(part * QR, QR)], dst.at[s // 2, pl.ds((s % 2) * QR, QR)], sem
                )
            )
    copies.append(pltpu.make_async_copy(qpay.at[:, pl.ds(2 * QR, 16)], d_s, sem))
    for number, piece in enumerate(pieces):
        from_core = core if number < 5 else 1 - core
        dy = (0, 1, 3, 2, 2)[number % 5]
        halves = ((0, 1), (0, 1), (0, 1), (0,), (1,))[number % 5]
        for at in range(4 * len(halves)):
            rank = place(dy, halves[at // 4], at // 2 % 2, at % 2)
            rows = piece.at[pl.ds(2 * at, 2)]
            copies.append(
                pltpu.make_async_copy(
                    rows.at[:, pl.ds(0, R)], k_s.at[rank, :, from_core, :, pl.ds(0, D)], sem
                )
            )
            value_copies.append(
                pltpu.make_async_copy(
                    rows.at[:, pl.ds(R, R)], v_s.at[rank, :, from_core, :, pl.ds(0, D)], value_sem
                )
            )
    for copy in copies + value_copies:
        copy.start()

    column = lax.broadcasted_iota(jnp.int32, (SPAN, D), 1)
    row = lax.broadcasted_iota(jnp.int32, (SPAN, D), 0)

    def put_beside(i, carry):
        chosen = (i * SPAN + row >= n0) & (i * SPAN + row < n1)
        beside = jnp.where((column < 3) | ((column == 3) & chosen), 1.0, 0.0).astype(BF16)
        beside = beside.reshape(1, 2, 2, R, D)
        k_s[pl.ds(i, 1), :, :, :, D:] = beside
        v_s[pl.ds(i, 1), :, :, :, D:] = beside
        return carry

    lax.fori_loop(0, NT, put_beside, 0, unroll=4)
    dk_s[...] = jnp.zeros_like(dk_s)
    dv_s[...] = jnp.zeros_like(dv_s)
    dq_s[...] = jnp.zeros_like(dq_s)

    def span_of(c):
        return order[span_id(c // 4, c // 2 % 2, y, c % 2)]

    def full_blocks(c):
        return span_of(c) // 2

    def list_chunk(c, size):
        all_second = span_of(c) * SPAN >= n1
        skip_at = (n0 + (KB - 1)) // KB
        skip_to = jnp.where(all_second, n1 // KB, 0)

        def put(b, n):
            hidden = (b >= skip_at) & (b < skip_to)
            plain_c[n] = c
            plain_b[n] = b
            return jnp.where(hidden, n, n + 1)

        return lax.fori_loop(0, full_blocks(c), put, size)

    n_plain = lax.fori_loop(0, NC, list_chunk, jnp.int32(0))
    for i in range(REST - 1):
        plain_c[n_plain + i] = NC
        plain_b[n_plain + i] = 0

    for copy in copies:
        copy.wait()

    def block_of(ref, b):
        return ref[pl.ds(2 * b, 2)].reshape(KB, 2 * D)

    def keys_of(b):
        return k_s[pl.ds(2 * b, 2), :, :, :, :D].reshape(KB, D)

    def turn_keys(b, carry):
        kt_s[b] = keys_of(b).T
        return carry

    lax.fori_loop(0, NT // 2, turn_keys, 0, unroll=4)

    def put_under(ref, c, *rows):
        number = lax.broadcasted_iota(jnp.int32, (D, C), 0)
        block = jnp.zeros((D, C), F32)
        for i, values in enumerate(rows):
            block = jnp.where(number == i, values, block)
        ref[c, D:] = block.astype(BF16)

    def turn_rows(c, carry):
        qa_s[c, :D] = q_s[c].T
        ga_s[c, :D] = do_s[c].T
        halves = [d_s[2 * c + half].astype(F32) for half in range(2)]
        put_under(
            ga_s,
            c,
            -jnp.concatenate([half[0:1] for half in halves], axis=1),
            -jnp.concatenate([half[1:2] for half in halves], axis=1),
        )
        return carry

    lax.fori_loop(0, NC, turn_rows, 0, unroll=4)
    qa_s[NC, :D] = jnp.zeros((D, C), BF16)
    put_under(qa_s, NC, jnp.full((1, C), HIDDEN, F32))
    ga_s[NC] = jnp.zeros((2 * D, C), BF16)
    q_s[NC] = jnp.zeros((C, D), BF16)
    do_s[NC] = jnp.zeros((C, D), BF16)
    l_s[NC] = jnp.zeros((8, C), F32)

    def query_positions(c):
        lane = lax.broadcasted_iota(jnp.int32, (1, C), 1)
        start = span_of(c) * SPAN + core * R + xl * HR
        return start + (lane // QR) * (2 * R) + lane % HR

    def key_positions(b):
        return b * KB + lax.broadcasted_iota(jnp.int32, (KB, 1), 0)

    def seen(c, b):
        query_pos, key_pos = query_positions(c), key_positions(b)
        low = jnp.where(query_pos >= n1, n0, n1)
        return (key_pos <= query_pos) & ((key_pos < low) | (key_pos >= n1))

    def add_up(weights):
        return jnp.sum(weights.reshape(KB // 8, 8, C), axis=0)

    def raw_scores(c, b):
        return jnp.dot(keys_of(b), qa_s[c, :D], preferred_element_type=F32)

    def put_shift(c, *rows):
        rows = (rows + (jnp.zeros((1, C), F32),) * 3)[:3]
        hide = jnp.where(query_positions(c) >= n1, HIDDEN, 0.0)
        put_under(qa_s, c, *rows, hide)

    def weights_of(c, b, masked):
        scores = jnp.dot(block_of(k_s, b), qa_s[c], preferred_element_type=F32)
        if masked:
            scores = jnp.where(key_positions(b) <= query_positions(c), scores, HIDDEN)
        return jnp.exp2(scores * EXP_SCALE)

    found = []
    for c in range(NC):
        b = full_blocks(c)
        scores = jnp.where(seen(c, b), raw_scores(c, b), HIDDEN)
        top = jnp.max(scores, axis=0, keepdims=True).astype(BF16).astype(F32)
        found.append((top, add_up(jnp.exp2((scores - top) * EXP_SCALE))))
    for c, (top, total) in enumerate(found):
        put_shift(c, -top)
        m_s[c] = top * EXP_SCALE
        l_s[c] = total

    def add_weights(items, masked):
        parts = [add_up(weights_of(c, b, masked)) for c, b in items]
        for (c, b), part in zip(items, parts):
            l_s[c] += part

    def each_plain(step, widths):
        done = jnp.int32(0)
        for width in widths:

            def some(i, carry, width=width, done=done):
                at = [done + width * i + k for k in range(width)]
                step([(plain_c[n], plain_b[n]) for n in at], False)
                return carry

            left = n_plain - done
            count = (left + (REST - 1)) // width if width == REST else left // width
            lax.fori_loop(0, count, some, 0)
            done = done + count * width

    each_plain(add_weights, STATS_WIDTHS)

    @pl.when(jnp.logical_not(jnp.max(l_s[...]) < LARGE))
    def _():
        def careful(c, b):
            scores = jnp.where(seen(c, b), raw_scores(c, b) * EXP_SCALE, HIDDEN)
            old = m_s[c]
            top = jnp.maximum(old, jnp.max(scores, axis=0, keepdims=True))
            l_s[c] = l_s[c] * jnp.exp2(old - top) + add_up(jnp.exp2(scores - top))
            m_s[c] = top

        def careful_diagonal(c, carry):
            m_s[c] = jnp.full((1, C), HIDDEN, F32)
            l_s[c] = jnp.zeros((8, C), F32)
            careful(c, full_blocks(c))
            return carry

        def careful_plain(n, carry):
            careful(plain_c[n], plain_b[n])
            return carry

        lax.fori_loop(0, NC, careful_diagonal, 0)
        lax.fori_loop(0, n_plain, careful_plain, 0)

    def put_logsum(c, carry):
        logsum = m_s[c] + jnp.log2(jnp.sum(l_s[c], axis=0, keepdims=True))
        rest = logsum * (1.0 / EXP_SCALE)
        rows = []
        for _ in range(3):
            part = rest.astype(BF16).astype(F32)
            rows.append(-part)
            rest = rest - part
        put_shift(c, *rows)
        return carry

    lax.fori_loop(0, NC, put_logsum, 0, unroll=4)
    for copy in value_copies:
        copy.wait()

    def grad_step(items, masked):
        made = []
        for c, b in items:
            weights = weights_of(c, b, masked)
            above = jnp.dot(block_of(v_s, b), ga_s[c], preferred_element_type=F32)
            made.append((weights.astype(BF16), (weights * above).astype(BF16)))
        for (c, b), (weights, score_grad) in zip(items, made):
            for ref, term in (
                (dv_s, jnp.dot(weights, do_s[c], preferred_element_type=F32)),
                (dk_s, jnp.dot(score_grad, q_s[c], preferred_element_type=F32)),
            ):
                ref[pl.ds(2 * b, 2)] += term.reshape(2, 2, 2, R, D)
            dq_s[c] += jnp.dot(kt_s[b], score_grad, preferred_element_type=F32)

    grad_step([(c, full_blocks(c)) for c in range(NC)], True)
    each_plain(grad_step, GRAD_WIDTHS)

    def finish(c, carry):
        dq = (dq_s[c] * SCALE).T.astype(BF16)
        dq_out[2 * c] = dq[:QR]
        dq_out[2 * c + 1] = dq[QR:]
        return carry

    lax.fori_loop(0, NC, finish, 0, unroll=4)

    for from_core, group in (
        (core, ((0, keep_0, 0), (1, keep_1, 0), (3, keep_3, 0), (2, sum_a, 0), (2, sum_b, 1))),
        (1 - core, ((0, give_0, 0), (1, give_1, 0), (3, give_3, 0), (2, far_give, 0))),
    ):
        for dy, out, first_xh in group:
            for at in range(out.shape[0] // 2):
                rank = place(dy, first_xh + at // 4, at // 2 % 2, at % 2)
                rows = slice(2 * at, 2 * at + 2)
                out[rows, :R] = (dk_s[rank, :, from_core] * SCALE).astype(BF16)
                out[rows, R:] = dv_s[rank, :, from_core].astype(BF16)


def far_sum_kernel(sum_a, sum_b, got, out_a, out_b):
    out_a[...] = (sum_a[...].astype(F32) + got[:8].astype(F32)).astype(BF16)
    out_b[...] = (sum_b[...].astype(F32) + got[8:].astype(F32)).astype(BF16)


def near_sum_kernel(sum_1, got_1, sum_3, got_3, from_1, from_3, out_1, out_3):
    for rows, with_from in ((slice(0, 8), 3), (slice(8, 16), 1)):
        for number, keep, got, came, out in (
            (1, sum_1, got_1, from_3, out_1),
            (3, sum_3, got_3, from_1, out_3),
        ):
            total = keep[rows].astype(F32) + got[rows].astype(F32)
            if number == with_from:
                total = total + came[...].astype(F32)
            out[rows] = total.astype(BF16)


def last_sum_kernel(keep, got, near_1, near_3, dq, sums, query_grad):
    total = keep[...].astype(F32) + got[...].astype(F32)
    total = total + (near_1[...].astype(F32) + near_3[...].astype(F32))
    sums[...] = total.astype(BF16)
    for g in range(8):
        for half in range(2):
            rows = slice(half * HR, (half + 1) * HR)
            for h in range(G):
                query_grad[rows, head_columns(g, h)] = dq[spread_to(g, half), h * HR : (h + 1) * HR]


def unpack_kernel(got, key_grad, value_grad):
    for g in range(8):
        for start, out in ((0, key_grad), (R, value_grad)):
            total = got[spread_to(g, 0), start : start + R].astype(F32)
            total = total + got[spread_to(g, 1), start : start + R].astype(F32)
            out[:, g * D : (g + 1) * D] = total.astype(BF16)


def bf16(*shape):
    return jax.ShapeDtypeStruct(shape, BF16)


def on_vmem(kernel, outs, *args):
    return pl.pallas_call(
        kernel,
        out_shape=outs,
        compiler_params=pltpu.CompilerParams(vmem_limit_bytes=16 << 20),
    )(*args)


IN_SMEM = pl.BlockSpec(memory_space=pltpu.SMEM)
IN_VMEM = pl.BlockSpec(memory_space=pltpu.VMEM)
ANYWHERE = pl.BlockSpec(memory_space=pl.ANY)


def exchange(array):
    return lax.all_to_all(array, SPREAD, split_axis=0, concat_axis=0, tiled=True)


def flip(array):
    return lax.ppermute(array, "core", [(0, 1), (1, 0)])


def swap(array, distance):
    return lax.ppermute(array, "y", [(i, i ^ distance) for i in range(4)])


def body(queries, keys, values, attn_out, out_grad, segment, span_order):
    kv_packed = pl.pallas_call(
        pack_kv_kernel,
        out_shape=bf16(16, 2 * R, D),
        in_specs=[pl.BlockSpec(memory_space=pltpu.HBM)] * 2,
        scratch_shapes=[pltpu.SemaphoreType.DMA],
        compiler_params=pltpu.CompilerParams(vmem_limit_bytes=60 << 20),
    )(keys, values)
    own = exchange(kv_packed)
    q_packed, counts = pl.pallas_call(
        pack_q_kernel,
        out_shape=[bf16(16, 2 * QR + 16, D), jax.ShapeDtypeStruct((2,), jnp.int32)],
        in_specs=[IN_VMEM] * 4 + [ANYWHERE],
        out_specs=[pl.BlockSpec(memory_space=pltpu.HBM), IN_SMEM],
        scratch_shapes=[pltpu.VMEM((16, 2 * QR + 16, D), BF16), pltpu.SemaphoreType.DMA],
        compiler_params=pltpu.CompilerParams(vmem_limit_bytes=16 << 20),
    )(queries, attn_out, out_grad, segment.reshape(64, 128), own)
    qpay = exchange(q_packed)

    near_1 = swap(own, 1)
    near_3 = swap(own, 3)
    far_a = swap(near_3[:8], 1)
    far_b = swap(near_1[8:], 3)
    mine = (own, near_1, near_3, far_a, far_b)
    group = bf16(16, 2 * R, D)
    half = bf16(8, 2 * R, D)
    dq, keep_0, keep_1, keep_3, sum_a, sum_b, give_0, give_1, give_3, far_give = pl.pallas_call(
        attention_kernel,
        out_shape=[bf16(16, QR, D)] + [group] * 3 + [half] * 2 + [group] * 4,
        in_specs=[IN_SMEM] * 2 + [ANYWHERE] * 11,
        scratch_shapes=[
            pltpu.SMEM((NC * NT // 2 + REST,), jnp.int32),
            pltpu.SMEM((NC * NT // 2 + REST,), jnp.int32),
            pltpu.VMEM((NC + 1, C, D), BF16),
            pltpu.VMEM((NC + 1, C, D), BF16),
            pltpu.VMEM((16, 16, D), BF16),
            pltpu.VMEM((NT, 2, 2, R, 2 * D), BF16),
            pltpu.VMEM((NT, 2, 2, R, 2 * D), BF16),
            pltpu.VMEM((NT // 2, D, KB), BF16),
            pltpu.VMEM((NC + 1, 2 * D, C), BF16),
            pltpu.VMEM((NC + 1, 2 * D, C), BF16),
            pltpu.VMEM((NC, 1, C), F32),
            pltpu.VMEM((NC + 1, 8, C), F32),
            pltpu.VMEM((NT, 2, 2, R, D), F32),
            pltpu.VMEM((NT, 2, 2, R, D), F32),
            pltpu.VMEM((NC + 1, D, C), F32),
            pltpu.SemaphoreType.DMA,
            pltpu.SemaphoreType.DMA,
        ],
        compiler_params=pltpu.CompilerParams(vmem_limit_bytes=40 << 20),
    )(span_order, counts, qpay, *mine, *[flip(array) for array in mine])
    far_sum_a, far_sum_b = on_vmem(far_sum_kernel, [half, half], sum_a, sum_b, flip(far_give))
    from_1 = swap(far_sum_a, 1)
    from_3 = swap(far_sum_b, 3)
    to_1, to_3 = on_vmem(
        near_sum_kernel, [group] * 2, keep_1, flip(give_1), keep_3, flip(give_3), from_1, from_3
    )
    sums, query_grad = on_vmem(
        last_sum_kernel,
        [group, bf16(R, 8 * G * D)],
        keep_0,
        flip(give_0),
        swap(to_1, 1),
        swap(to_3, 3),
        exchange(dq),
    )
    key_grad, value_grad = on_vmem(unpack_kernel, [bf16(R, 8 * D)] * 2, exchange(sums))
    return query_grad, key_grad, value_grad


def solution(mesh):
    fine = Mesh(mesh.devices.reshape(4, 2, 2, 2, 4), AXES)
    rows = P(AXES, None)
    return jax.shard_map(
        body,
        mesh=fine,
        in_specs=(rows,) * 5 + (P(), P()),
        out_specs=(rows,) * 3,
        check_vma=False,
    )
```

```python
import math

import jax
import jax.numpy as jnp
from jax import lax
from jax.experimental import pallas as pl
from jax.experimental.pallas import tpu as pltpu
from jax.sharding import Mesh, PartitionSpec as P

D = 128
G = 4
R = 64
HR = R // 2
SPAN = 256
NT = 32
KB = 2 * SPAN
QR = G * HR
C = 2 * QR
NC = 8
REST = 2
STATS_WIDTHS = (16, 4, REST)
GRAD_WIDTHS = (8, 4, REST)
SCALE = D**-0.5
EXP_SCALE = SCALE * math.log2(math.e)
HIDDEN = -1e30
LARGE = 2.0**90
F32 = jnp.float32
BF16 = jnp.bfloat16
AXES = ("z", "core", "xh", "xl", "y")
SPREAD = ("xh", "xl", "z")
NT_DIMS = (((1,), (1,)), ((), ()))


def spread_to(g, xl):
    return (g // 4 * 2 + xl) * 4 + g % 4


def head_columns(g, h):
    return slice((g * G + h) * D, (g * G + h + 1) * D)


def pack_kv_kernel(keys, values, out, sem):
    copies = []
    for g in range(8):
        for xl in range(2):
            for part, array in enumerate((keys, values)):
                copies.append(
                    pltpu.make_async_copy(
                        array.at[:, pl.ds(g * D, D)],
                        out.at[spread_to(g, xl), pl.ds(part * R, R)],
                        sem,
                    )
                )
    for copy in copies:
        copy.start()
    for copy in copies:
        copy.wait()


def pack_q_kernel(queries, saved, grads, segment, after, out, counts):
    del after
    counts[0] = jnp.sum((segment[...] == 0).astype(jnp.int32))
    counts[1] = jnp.sum((segment[...] != 2).astype(jnp.int32))
    ones = jnp.ones((8, D), BF16)
    row = lax.broadcasted_iota(jnp.int32, (16, D), 0)
    for g in range(8):
        for half in range(2):
            dest = spread_to(g, half)
            rows = slice(half * HR, (half + 1) * HR)
            prods = []
            for h in range(G):
                cols = head_columns(g, h)
                grad = grads[rows, cols]
                out[dest, h * HR : (h + 1) * HR] = queries[rows, cols]
                out[dest, QR + h * HR : QR + (h + 1) * HR] = grad
                prods.append(grad.astype(F32) * saved[rows, cols].astype(F32))
            prod = jnp.concatenate(prods, axis=0)
            high = prod.astype(BF16)
            low = (prod - high.astype(F32)).astype(BF16)
            dot = lax.dot_general(ones, high, NT_DIMS, preferred_element_type=F32)
            dot = dot + lax.dot_general(ones, low, NT_DIMS, preferred_element_type=F32)
            both = jnp.concatenate([dot, dot], axis=0)
            rounded = both.astype(BF16).astype(F32)
            out[dest, 2 * QR :] = jnp.where(row == 0, rounded, both - rounded).astype(BF16)


def span_id(xh, xl, y, zh):
    return ((xh * 2 + xl) * 4 + y) * 2 + zh


def attention_kernel(order, counts, qpay, *refs):
    pieces = refs[:10]
    dq_out, keep_0, keep_1, keep_3, sum_a, sum_b, give_0, give_1, give_3, far_give = refs[10:20]
    plain_c, plain_b, q_s, do_s, d_s, k_s, v_s, kt_s, qa_s, ga_s = refs[20:30]
    m_s, l_s, dk_s, dv_s, dq_s, sem, value_sem = refs[30:]
    n0 = counts[0]
    n1 = counts[1]
    xl = lax.axis_index("xl")
    y = lax.axis_index("y")
    core = lax.axis_index("core")

    def place(dy, xh, xl, zh):
        return order[span_id(xh, xl, y ^ dy, zh)]

    copies = []
    value_copies = []
    for s in range(16):
        for part, dst in ((0, q_s), (1, do_s)):
            copies.append(
                pltpu.make_async_copy(
                    qpay.at[s, pl.ds(part * QR, QR)], dst.at[s // 2, pl.ds((s % 2) * QR, QR)], sem
                )
            )
    copies.append(pltpu.make_async_copy(qpay.at[:, pl.ds(2 * QR, 16)], d_s, sem))
    for number, piece in enumerate(pieces):
        from_core = core if number < 5 else 1 - core
        dy = (0, 1, 3, 2, 2)[number % 5]
        halves = ((0, 1), (0, 1), (0, 1), (0,), (1,))[number % 5]
        for at in range(4 * len(halves)):
            rank = place(dy, halves[at // 4], at // 2 % 2, at % 2)
            rows = piece.at[pl.ds(2 * at, 2)]
            copies.append(
                pltpu.make_async_copy(
                    rows.at[:, pl.ds(0, R)], k_s.at[rank, :, from_core, :, pl.ds(0, D)], sem
                )
            )
            value_copies.append(
                pltpu.make_async_copy(
                    rows.at[:, pl.ds(R, R)], v_s.at[rank, :, from_core, :, pl.ds(0, D)], value_sem
                )
            )
    for copy in copies + value_copies:
        copy.start()

    column = lax.broadcasted_iota(jnp.int32, (SPAN, D), 1)
    row = lax.broadcasted_iota(jnp.int32, (SPAN, D), 0)

    def put_beside(i, carry):
        chosen = (i * SPAN + row >= n0) & (i * SPAN + row < n1)
        beside = jnp.where((column < 3) | ((column == 3) & chosen), 1.0, 0.0).astype(BF16)
        beside = beside.reshape(1, 2, 2, R, D)
        k_s[pl.ds(i, 1), :, :, :, D:] = beside
        v_s[pl.ds(i, 1), :, :, :, D:] = beside
        return carry

    lax.fori_loop(0, NT, put_beside, 0, unroll=4)
    dk_s[...] = jnp.zeros_like(dk_s)
    dv_s[...] = jnp.zeros_like(dv_s)
    dq_s[...] = jnp.zeros_like(dq_s)

    def span_of(c):
        return order[span_id(c // 4, c // 2 % 2, y, c % 2)]

    def full_blocks(c):
        return span_of(c) // 2

    def list_chunk(c, size):
        all_second = span_of(c) * SPAN >= n1
        skip_at = (n0 + (KB - 1)) // KB
        skip_to = jnp.where(all_second, n1 // KB, 0)

        def put(b, n):
            hidden = (b >= skip_at) & (b < skip_to)
            plain_c[n] = c
            plain_b[n] = b
            return jnp.where(hidden, n, n + 1)

        return lax.fori_loop(0, full_blocks(c), put, size)

    n_plain = lax.fori_loop(0, NC, list_chunk, jnp.int32(0))
    for i in range(REST - 1):
        plain_c[n_plain + i] = NC
        plain_b[n_plain + i] = 0

    for copy in copies:
        copy.wait()

    def block_of(ref, b):
        return ref[pl.ds(2 * b, 2)].reshape(KB, 2 * D)

    def keys_of(b):
        return k_s[pl.ds(2 * b, 2), :, :, :, :D].reshape(KB, D)

    def turn_keys(b, carry):
        kt_s[b] = keys_of(b).T
        return carry

    lax.fori_loop(0, NT // 2, turn_keys, 0, unroll=4)

    def put_under(ref, c, *rows):
        number = lax.broadcasted_iota(jnp.int32, (D, C), 0)
        block = jnp.zeros((D, C), F32)
        for i, values in enumerate(rows):
            block = jnp.where(number == i, values, block)
        ref[c, D:] = block.astype(BF16)

    def turn_rows(c, carry):
        qa_s[c, :D] = q_s[c].T
        ga_s[c, :D] = do_s[c].T
        halves = [d_s[2 * c + half].astype(F32) for half in range(2)]
        put_under(
            ga_s,
            c,
            -jnp.concatenate([half[0:1] for half in halves], axis=1),
            -jnp.concatenate([half[1:2] for half in halves], axis=1),
        )
        return carry

    lax.fori_loop(0, NC, turn_rows, 0, unroll=4)
    qa_s[NC, :D] = jnp.zeros((D, C), BF16)
    put_under(qa_s, NC, jnp.full((1, C), HIDDEN, F32))
    ga_s[NC] = jnp.zeros((2 * D, C), BF16)
    q_s[NC] = jnp.zeros((C, D), BF16)
    do_s[NC] = jnp.zeros((C, D), BF16)
    l_s[NC] = jnp.zeros((8, C), F32)

    def query_positions(c):
        lane = lax.broadcasted_iota(jnp.int32, (1, C), 1)
        start = span_of(c) * SPAN + core * R + xl * HR
        return start + (lane // QR) * (2 * R) + lane % HR

    def key_positions(b):
        return b * KB + lax.broadcasted_iota(jnp.int32, (KB, 1), 0)

    def seen(c, b):
        query_pos, key_pos = query_positions(c), key_positions(b)
        low = jnp.where(query_pos >= n1, n0, n1)
        return (key_pos <= query_pos) & ((key_pos < low) | (key_pos >= n1))

    def add_up(weights):
        return jnp.sum(weights.reshape(KB // 8, 8, C), axis=0)

    def raw_scores(c, b):
        return jnp.dot(keys_of(b), qa_s[c, :D], preferred_element_type=F32)

    def put_shift(c, *rows):
        rows = (rows + (jnp.zeros((1, C), F32),) * 3)[:3]
        hide = jnp.where(query_positions(c) >= n1, HIDDEN, 0.0)
        put_under(qa_s, c, *rows, hide)

    def weights_of(c, b, masked):
        scores = jnp.dot(block_of(k_s, b), qa_s[c], preferred_element_type=F32)
        if masked:
            scores = jnp.where(key_positions(b) <= query_positions(c), scores, HIDDEN)
        return jnp.exp2(scores * EXP_SCALE)

    found = []
    for c in range(NC):
        b = full_blocks(c)
        scores = jnp.where(seen(c, b), raw_scores(c, b), HIDDEN)
        top = jnp.max(scores, axis=0, keepdims=True).astype(BF16).astype(F32)
        found.append((top, add_up(jnp.exp2((scores - top) * EXP_SCALE))))
    for c, (top, total) in enumerate(found):
        put_shift(c, -top)
        m_s[c] = top * EXP_SCALE
        l_s[c] = total

    def add_weights(items, masked):
        parts = [add_up(weights_of(c, b, masked)) for c, b in items]
        for (c, b), part in zip(items, parts):
            l_s[c] += part

    def each_plain(step, widths):
        done = jnp.int32(0)
        for width in widths:

            def some(i, carry, width=width, done=done):
                at = [done + width * i + k for k in range(width)]
                step([(plain_c[n], plain_b[n]) for n in at], False)
                return carry

            left = n_plain - done
            count = (left + (REST - 1)) // width if width == REST else left // width
            lax.fori_loop(0, count, some, 0)
            done = done + count * width

    each_plain(add_weights, STATS_WIDTHS)

    @pl.when(jnp.logical_not(jnp.max(l_s[...]) < LARGE))
    def _():
        def careful(c, b):
            scores = jnp.where(seen(c, b), raw_scores(c, b) * EXP_SCALE, HIDDEN)
            old = m_s[c]
            top = jnp.maximum(old, jnp.max(scores, axis=0, keepdims=True))
            l_s[c] = l_s[c] * jnp.exp2(old - top) + add_up(jnp.exp2(scores - top))
            m_s[c] = top

        def careful_diagonal(c, carry):
            m_s[c] = jnp.full((1, C), HIDDEN, F32)
            l_s[c] = jnp.zeros((8, C), F32)
            careful(c, full_blocks(c))
            return carry

        def careful_plain(n, carry):
            careful(plain_c[n], plain_b[n])
            return carry

        lax.fori_loop(0, NC, careful_diagonal, 0)
        lax.fori_loop(0, n_plain, careful_plain, 0)

    def put_logsum(c, carry):
        logsum = m_s[c] + jnp.log2(jnp.sum(l_s[c], axis=0, keepdims=True))
        rest = logsum * (1.0 / EXP_SCALE)
        rows = []
        for _ in range(3):
            part = rest.astype(BF16).astype(F32)
            rows.append(-part)
            rest = rest - part
        put_shift(c, *rows)
        return carry

    lax.fori_loop(0, NC, put_logsum, 0, unroll=4)
    for copy in value_copies:
        copy.wait()

    def grad_step(items, masked):
        made = []
        for c, b in items:
            weights = weights_of(c, b, masked)
            above = jnp.dot(block_of(v_s, b), ga_s[c], preferred_element_type=F32)
            made.append((weights.astype(BF16), (weights * above).astype(BF16)))
        for (c, b), (weights, score_grad) in zip(items, made):
            for ref, term in (
                (dv_s, jnp.dot(weights, do_s[c], preferred_element_type=F32)),
                (dk_s, jnp.dot(score_grad, q_s[c], preferred_element_type=F32)),
            ):
                ref[pl.ds(2 * b, 2)] += term.reshape(2, 2, 2, R, D)
            dq_s[c] += jnp.dot(kt_s[b], score_grad, preferred_element_type=F32)

    grad_step([(c, full_blocks(c)) for c in range(NC)], True)
    each_plain(grad_step, GRAD_WIDTHS)

    def finish(c, carry):
        dq = (dq_s[c] * SCALE).T.astype(BF16)
        dq_out[2 * c] = dq[:QR]
        dq_out[2 * c + 1] = dq[QR:]
        return carry

    lax.fori_loop(0, NC, finish, 0, unroll=4)

    for from_core, group in (
        (core, ((0, keep_0, 0), (1, keep_1, 0), (3, keep_3, 0), (2, sum_a, 0), (2, sum_b, 1))),
        (1 - core, ((0, give_0, 0), (1, give_1, 0), (3, give_3, 0), (2, far_give, 0))),
    ):
        for dy, out, first_xh in group:
            for at in range(out.shape[0] // 2):
                rank = place(dy, first_xh + at // 4, at // 2 % 2, at % 2)
                rows = slice(2 * at, 2 * at + 2)
                out[rows, :R] = (dk_s[rank, :, from_core] * SCALE).astype(BF16)
                out[rows, R:] = dv_s[rank, :, from_core].astype(BF16)


def far_sum_kernel(sum_a, sum_b, got, out_a, out_b):
    out_a[...] = (sum_a[...].astype(F32) + got[:8].astype(F32)).astype(BF16)
    out_b[...] = (sum_b[...].astype(F32) + got[8:].astype(F32)).astype(BF16)


def near_sum_kernel(sum_1, got_1, sum_3, got_3, from_1, from_3, out_1, out_3):
    for rows, with_from in ((slice(0, 8), 3), (slice(8, 16), 1)):
        for number, keep, got, came, out in (
            (1, sum_1, got_1, from_3, out_1),
            (3, sum_3, got_3, from_1, out_3),
        ):
            total = keep[rows].astype(F32) + got[rows].astype(F32)
            if number == with_from:
                total = total + came[...].astype(F32)
            out[rows] = total.astype(BF16)


def last_sum_kernel(keep, got, near_1, near_3, dq, sums, query_grad):
    total = keep[...].astype(F32) + got[...].astype(F32)
    total = total + (near_1[...].astype(F32) + near_3[...].astype(F32))
    sums[...] = total.astype(BF16)
    for g in range(8):
        for half in range(2):
            rows = slice(half * HR, (half + 1) * HR)
            for h in range(G):
                query_grad[rows, head_columns(g, h)] = dq[spread_to(g, half), h * HR : (h + 1) * HR]


def unpack_kernel(got, key_grad, value_grad):
    for g in range(8):
        for start, out in ((0, key_grad), (R, value_grad)):
            total = got[spread_to(g, 0), start : start + R].astype(F32)
            total = total + got[spread_to(g, 1), start : start + R].astype(F32)
            out[:, g * D : (g + 1) * D] = total.astype(BF16)


def bf16(*shape):
    return jax.ShapeDtypeStruct(shape, BF16)


def on_vmem(kernel, outs, *args):
    return pl.pallas_call(
        kernel,
        out_shape=outs,
        compiler_params=pltpu.CompilerParams(vmem_limit_bytes=16 << 20),
    )(*args)


IN_SMEM = pl.BlockSpec(memory_space=pltpu.SMEM)
IN_VMEM = pl.BlockSpec(memory_space=pltpu.VMEM)
ANYWHERE = pl.BlockSpec(memory_space=pl.ANY)


def exchange(array):
    return lax.all_to_all(array, SPREAD, split_axis=0, concat_axis=0, tiled=True)


def flip(array):
    return lax.ppermute(array, "core", [(0, 1), (1, 0)])


def swap(array, distance):
    return lax.ppermute(array, "y", [(i, i ^ distance) for i in range(4)])


def body(queries, keys, values, attn_out, out_grad, segment, span_order):
    kv_packed = pl.pallas_call(
        pack_kv_kernel,
        out_shape=bf16(16, 2 * R, D),
        in_specs=[pl.BlockSpec(memory_space=pltpu.HBM)] * 2,
        scratch_shapes=[pltpu.SemaphoreType.DMA],
        compiler_params=pltpu.CompilerParams(vmem_limit_bytes=60 << 20),
    )(keys, values)
    own = exchange(kv_packed)
    q_packed, counts = pl.pallas_call(
        pack_q_kernel,
        out_shape=[bf16(16, 2 * QR + 16, D), jax.ShapeDtypeStruct((2,), jnp.int32)],
        in_specs=[IN_VMEM] * 4 + [ANYWHERE],
        out_specs=[IN_VMEM, IN_SMEM],
        compiler_params=pltpu.CompilerParams(vmem_limit_bytes=16 << 20),
    )(queries, attn_out, out_grad, segment.reshape(64, 128), own)
    qpay = exchange(q_packed)

    near_1 = swap(own, 1)
    near_3 = swap(own, 3)
    far_a = swap(near_3[:8], 1)
    far_b = swap(near_1[8:], 3)
    mine = (own, near_1, near_3, far_a, far_b)
    group = bf16(16, 2 * R, D)
    half = bf16(8, 2 * R, D)
    dq, keep_0, keep_1, keep_3, sum_a, sum_b, give_0, give_1, give_3, far_give = pl.pallas_call(
        attention_kernel,
        out_shape=[bf16(16, QR, D)] + [group] * 3 + [half] * 2 + [group] * 4,
        in_specs=[IN_SMEM] * 2 + [ANYWHERE] * 11,
        scratch_shapes=[
            pltpu.SMEM((NC * NT // 2 + REST,), jnp.int32),
            pltpu.SMEM((NC * NT // 2 + REST,), jnp.int32),
            pltpu.VMEM((NC + 1, C, D), BF16),
            pltpu.VMEM((NC + 1, C, D), BF16),
            pltpu.VMEM((16, 16, D), BF16),
            pltpu.VMEM((NT, 2, 2, R, 2 * D), BF16),
            pltpu.VMEM((NT, 2, 2, R, 2 * D), BF16),
            pltpu.VMEM((NT // 2, D, KB), BF16),
            pltpu.VMEM((NC + 1, 2 * D, C), BF16),
            pltpu.VMEM((NC + 1, 2 * D, C), BF16),
            pltpu.VMEM((NC, 1, C), F32),
            pltpu.VMEM((NC + 1, 8, C), F32),
            pltpu.VMEM((NT, 2, 2, R, D), F32),
            pltpu.VMEM((NT, 2, 2, R, D), F32),
            pltpu.VMEM((NC + 1, D, C), F32),
            pltpu.SemaphoreType.DMA,
            pltpu.SemaphoreType.DMA,
        ],
        compiler_params=pltpu.CompilerParams(vmem_limit_bytes=40 << 20),
    )(span_order, counts, qpay, *mine, *[flip(array) for array in mine])
    far_sum_a, far_sum_b = on_vmem(far_sum_kernel, [half, half], sum_a, sum_b, flip(far_give))
    from_1 = swap(far_sum_a, 1)
    from_3 = swap(far_sum_b, 3)
    to_1, to_3 = on_vmem(
        near_sum_kernel, [group] * 2, keep_1, flip(give_1), keep_3, flip(give_3), from_1, from_3
    )
    sums, query_grad = on_vmem(
        last_sum_kernel,
        [group, bf16(R, 8 * G * D)],
        keep_0,
        flip(give_0),
        swap(to_1, 1),
        swap(to_3, 3),
        exchange(dq),
    )
    key_grad, value_grad = on_vmem(unpack_kernel, [bf16(R, 8 * D)] * 2, exchange(sums))
    return query_grad, key_grad, value_grad


def solution(mesh):
    fine = Mesh(mesh.devices.reshape(4, 2, 2, 2, 4), AXES)
    rows = P(AXES, None)
    return jax.shard_map(
        body,
        mesh=fine,
        in_specs=(rows,) * 5 + (P(), P()),
        out_specs=(rows,) * 3,
        check_vma=False,
    )
```

```python
import math

import jax
import jax.numpy as jnp
from jax import lax
from jax.experimental import pallas as pl
from jax.experimental.pallas import tpu as pltpu
from jax.sharding import Mesh, PartitionSpec as P

D = 128
G = 4
R = 64
HR = R // 2
SPAN = 256
NT = 32
KB = 2 * SPAN
QR = G * HR
C = 2 * QR
NC = 8
WIDTHS = (8, 2)
REST = WIDTHS[-1]
SCALE = D**-0.5
EXP_SCALE = SCALE * math.log2(math.e)
HIDDEN = -1e30
LARGE = 2.0**90
F32 = jnp.float32
BF16 = jnp.bfloat16
AXES = ("z", "core", "xh", "xl", "y")
SPREAD = ("xh", "xl", "z")
NT_DIMS = (((1,), (1,)), ((), ()))


def spread_to(g, xl):
    return (g // 4 * 2 + xl) * 4 + g % 4


def head_columns(g, h):
    return slice((g * G + h) * D, (g * G + h + 1) * D)


def pack_kv_kernel(keys, values, out, sem):
    copies = []
    for g in range(8):
        for xl in range(2):
            for part, array in enumerate((keys, values)):
                copies.append(
                    pltpu.make_async_copy(
                        array.at[:, pl.ds(g * D, D)],
                        out.at[spread_to(g, xl), pl.ds(part * R, R)],
                        sem,
                    )
                )
    for copy in copies:
        copy.start()
    for copy in copies:
        copy.wait()


def pack_q_kernel(queries, saved, grads, segment, after, out, counts):
    del after
    counts[0] = jnp.sum((segment[...] == 0).astype(jnp.int32))
    counts[1] = jnp.sum((segment[...] != 2).astype(jnp.int32))
    ones = jnp.ones((8, D), BF16)
    row = lax.broadcasted_iota(jnp.int32, (16, D), 0)
    for g in range(8):
        for half in range(2):
            dest = spread_to(g, half)
            rows = slice(half * HR, (half + 1) * HR)
            prods = []
            for h in range(G):
                cols = head_columns(g, h)
                grad = grads[rows, cols]
                out[dest, h * HR : (h + 1) * HR] = queries[rows, cols]
                out[dest, QR + h * HR : QR + (h + 1) * HR] = grad
                prods.append(grad.astype(F32) * saved[rows, cols].astype(F32))
            prod = jnp.concatenate(prods, axis=0)
            high = prod.astype(BF16)
            low = (prod - high.astype(F32)).astype(BF16)
            dot = lax.dot_general(ones, high, NT_DIMS, preferred_element_type=F32)
            dot = dot + lax.dot_general(ones, low, NT_DIMS, preferred_element_type=F32)
            both = jnp.concatenate([dot, dot], axis=0)
            rounded = both.astype(BF16).astype(F32)
            out[dest, 2 * QR :] = jnp.where(row == 0, rounded, both - rounded).astype(BF16)


def span_id(xh, xl, y, zh):
    return ((xh * 2 + xl) * 4 + y) * 2 + zh


def attention_kernel(order, counts, qpay, *refs):
    pieces = refs[:10]
    dq_out, keep_0, keep_1, keep_3, sum_a, sum_b, give_0, give_1, give_3, far_give = refs[10:20]
    plain_c, plain_b, q_s, do_s, d_s, k_s, v_s, kt_s, qa_s, ga_s = refs[20:30]
    m_s, l_s, dk_s, dv_s, dq_s, sem, value_sem = refs[30:]
    n0 = counts[0]
    n1 = counts[1]
    xl = lax.axis_index("xl")
    y = lax.axis_index("y")
    core = lax.axis_index("core")

    def place(dy, xh, xl, zh):
        return order[span_id(xh, xl, y ^ dy, zh)]

    copies = []
    value_copies = []
    for s in range(16):
        for part, dst in ((0, q_s), (1, do_s)):
            copies.append(
                pltpu.make_async_copy(
                    qpay.at[s, pl.ds(part * QR, QR)], dst.at[s // 2, pl.ds((s % 2) * QR, QR)], sem
                )
            )
    copies.append(pltpu.make_async_copy(qpay.at[:, pl.ds(2 * QR, 16)], d_s, sem))
    for number, piece in enumerate(pieces):
        from_core = core if number < 5 else 1 - core
        dy = (0, 1, 3, 2, 2)[number % 5]
        halves = ((0, 1), (0, 1), (0, 1), (0,), (1,))[number % 5]
        for at in range(4 * len(halves)):
            rank = place(dy, halves[at // 4], at // 2 % 2, at % 2)
            rows = piece.at[pl.ds(2 * at, 2)]
            copies.append(
                pltpu.make_async_copy(
                    rows.at[:, pl.ds(0, R)], k_s.at[rank, :, from_core, :, pl.ds(0, D)], sem
                )
            )
            value_copies.append(
                pltpu.make_async_copy(
                    rows.at[:, pl.ds(R, R)], v_s.at[rank, :, from_core, :, pl.ds(0, D)], value_sem
                )
            )
    for copy in copies + value_copies:
        copy.start()

    column = lax.broadcasted_iota(jnp.int32, (SPAN, D), 1)
    row = lax.broadcasted_iota(jnp.int32, (SPAN, D), 0)

    def put_beside(i, carry):
        chosen = (i * SPAN + row >= n0) & (i * SPAN + row < n1)
        beside = jnp.where((column < 3) | ((column == 3) & chosen), 1.0, 0.0).astype(BF16)
        beside = beside.reshape(1, 2, 2, R, D)
        k_s[pl.ds(i, 1), :, :, :, D:] = beside
        v_s[pl.ds(i, 1), :, :, :, D:] = beside
        return carry

    lax.fori_loop(0, NT, put_beside, 0, unroll=4)
    dk_s[...] = jnp.zeros_like(dk_s)
    dv_s[...] = jnp.zeros_like(dv_s)
    dq_s[...] = jnp.zeros_like(dq_s)

    def span_of(c):
        return order[span_id(c // 4, c // 2 % 2, y, c % 2)]

    def full_blocks(c):
        return span_of(c) // 2

    def list_chunk(c, size):
        all_second = span_of(c) * SPAN >= n1
        skip_at = (n0 + (KB - 1)) // KB
        skip_to = jnp.where(all_second, n1 // KB, 0)

        def put(b, n):
            hidden = (b >= skip_at) & (b < skip_to)
            plain_c[n] = c
            plain_b[n] = b
            return jnp.where(hidden, n, n + 1)

        return lax.fori_loop(0, full_blocks(c), put, size)

    n_plain = lax.fori_loop(0, NC, list_chunk, jnp.int32(0))
    for i in range(REST - 1):
        plain_c[n_plain + i] = NC
        plain_b[n_plain + i] = 0

    for copy in copies:
        copy.wait()

    def block_of(ref, b):
        return ref[pl.ds(2 * b, 2)].reshape(KB, 2 * D)

    def keys_of(b):
        return k_s[pl.ds(2 * b, 2), :, :, :, :D].reshape(KB, D)

    def turn_keys(b, carry):
        kt_s[b] = keys_of(b).T
        return carry

    lax.fori_loop(0, NT // 2, turn_keys, 0, unroll=4)

    def put_under(ref, c, *rows):
        number = lax.broadcasted_iota(jnp.int32, (D, C), 0)
        block = jnp.zeros((D, C), F32)
        for i, values in enumerate(rows):
            block = jnp.where(number == i, values, block)
        ref[c, D:] = block.astype(BF16)

    def turn_rows(c, carry):
        qa_s[c, :D] = q_s[c].T
        ga_s[c, :D] = do_s[c].T
        halves = [d_s[2 * c + half].astype(F32) for half in range(2)]
        put_under(
            ga_s,
            c,
            -jnp.concatenate([half[0:1] for half in halves], axis=1),
            -jnp.concatenate([half[1:2] for half in halves], axis=1),
        )
        return carry

    lax.fori_loop(0, NC, turn_rows, 0, unroll=4)
    qa_s[NC, :D] = jnp.zeros((D, C), BF16)
    put_under(qa_s, NC, jnp.full((1, C), HIDDEN, F32))
    ga_s[NC] = jnp.zeros((2 * D, C), BF16)
    q_s[NC] = jnp.zeros((C, D), BF16)
    do_s[NC] = jnp.zeros((C, D), BF16)
    l_s[NC] = jnp.zeros((8, C), F32)

    def query_positions(c):
        lane = lax.broadcasted_iota(jnp.int32, (1, C), 1)
        start = span_of(c) * SPAN + core * R + xl * HR
        return start + (lane // QR) * (2 * R) + lane % HR

    def key_positions(b):
        return b * KB + lax.broadcasted_iota(jnp.int32, (KB, 1), 0)

    def seen(c, b):
        query_pos, key_pos = query_positions(c), key_positions(b)
        low = jnp.where(query_pos >= n1, n0, n1)
        return (key_pos <= query_pos) & ((key_pos < low) | (key_pos >= n1))

    def add_up(weights):
        return jnp.sum(weights.reshape(KB // 8, 8, C), axis=0)

    def raw_scores(c, b):
        return jnp.dot(keys_of(b), qa_s[c, :D], preferred_element_type=F32)

    def put_shift(c, *rows):
        rows = (rows + (jnp.zeros((1, C), F32),) * 3)[:3]
        hide = jnp.where(query_positions(c) >= n1, HIDDEN, 0.0)
        put_under(qa_s, c, *rows, hide)

    def weights_of(c, b, masked):
        scores = jnp.dot(block_of(k_s, b), qa_s[c], preferred_element_type=F32)
        if masked:
            scores = jnp.where(key_positions(b) <= query_positions(c), scores, HIDDEN)
        return jnp.exp2(scores * EXP_SCALE)

    found = []
    for c in range(NC):
        b = full_blocks(c)
        scores = jnp.where(seen(c, b), raw_scores(c, b), HIDDEN)
        top = jnp.max(scores, axis=0, keepdims=True).astype(BF16).astype(F32)
        found.append((top, add_up(jnp.exp2((scores - top) * EXP_SCALE))))
    for c, (top, total) in enumerate(found):
        put_shift(c, -top)
        m_s[c] = top * EXP_SCALE
        l_s[c] = total

    def add_weights(items, masked):
        parts = [add_up(weights_of(c, b, masked)) for c, b in items]
        for (c, b), part in zip(items, parts):
            l_s[c] += part

    def each_plain(step):
        done = jnp.int32(0)
        for width in WIDTHS:

            def some(i, carry, width=width, done=done):
                at = [done + width * i + k for k in range(width)]
                step([(plain_c[n], plain_b[n]) for n in at], False)
                return carry

            left = n_plain - done
            count = (left + (REST - 1)) // width if width == REST else left // width
            lax.fori_loop(0, count, some, 0)
            done = done + count * width

    each_plain(add_weights)

    @pl.when(jnp.logical_not(jnp.max(l_s[...]) < LARGE))
    def _():
        def careful(c, b):
            scores = jnp.where(seen(c, b), raw_scores(c, b) * EXP_SCALE, HIDDEN)
            old = m_s[c]
            top = jnp.maximum(old, jnp.max(scores, axis=0, keepdims=True))
            l_s[c] = l_s[c] * jnp.exp2(old - top) + add_up(jnp.exp2(scores - top))
            m_s[c] = top

        def careful_diagonal(c, carry):
            m_s[c] = jnp.full((1, C), HIDDEN, F32)
            l_s[c] = jnp.zeros((8, C), F32)
            careful(c, full_blocks(c))
            return carry

        def careful_plain(n, carry):
            careful(plain_c[n], plain_b[n])
            return carry

        lax.fori_loop(0, NC, careful_diagonal, 0)
        lax.fori_loop(0, n_plain, careful_plain, 0)

    def put_logsum(c, carry):
        logsum = m_s[c] + jnp.log2(jnp.sum(l_s[c], axis=0, keepdims=True))
        rest = logsum * (1.0 / EXP_SCALE)
        rows = []
        for _ in range(3):
            part = rest.astype(BF16).astype(F32)
            rows.append(-part)
            rest = rest - part
        put_shift(c, *rows)
        return carry

    lax.fori_loop(0, NC, put_logsum, 0, unroll=4)
    for copy in value_copies:
        copy.wait()

    def grad_step(items, masked):
        made = []
        for c, b in items:
            weights = weights_of(c, b, masked)
            above = jnp.dot(block_of(v_s, b), ga_s[c], preferred_element_type=F32)
            made.append((weights.astype(BF16), (weights * above).astype(BF16)))
        for which, ref, rows in ((0, dv_s, do_s), (1, dk_s, q_s)):
            for (c, b), factors in zip(items, made):
                term = jnp.dot(factors[which], rows[c], preferred_element_type=F32)
                ref[pl.ds(2 * b, 2)] += term.reshape(2, 2, 2, R, D)
        for (c, b), (_, score_grad) in zip(items, made):
            dq_s[c] += jnp.dot(kt_s[b], score_grad, preferred_element_type=F32)

    grad_step([(c, full_blocks(c)) for c in range(NC)], True)
    each_plain(grad_step)

    def finish(c, carry):
        dq = (dq_s[c] * SCALE).T.astype(BF16)
        dq_out[2 * c] = dq[:QR]
        dq_out[2 * c + 1] = dq[QR:]
        return carry

    lax.fori_loop(0, NC, finish, 0, unroll=4)

    for from_core, group in (
        (core, ((0, keep_0, 0), (1, keep_1, 0), (3, keep_3, 0), (2, sum_a, 0), (2, sum_b, 1))),
        (1 - core, ((0, give_0, 0), (1, give_1, 0), (3, give_3, 0), (2, far_give, 0))),
    ):
        for dy, out, first_xh in group:
            for at in range(out.shape[0] // 2):
                rank = place(dy, first_xh + at // 4, at // 2 % 2, at % 2)
                rows = slice(2 * at, 2 * at + 2)
                out[rows, :R] = (dk_s[rank, :, from_core] * SCALE).astype(BF16)
                out[rows, R:] = dv_s[rank, :, from_core].astype(BF16)


def far_sum_kernel(sum_a, sum_b, got, out_a, out_b):
    out_a[...] = (sum_a[...].astype(F32) + got[:8].astype(F32)).astype(BF16)
    out_b[...] = (sum_b[...].astype(F32) + got[8:].astype(F32)).astype(BF16)


def near_sum_kernel(sum_1, got_1, sum_3, got_3, from_1, from_3, out_1, out_3):
    for rows, with_from in ((slice(0, 8), 3), (slice(8, 16), 1)):
        for number, keep, got, came, out in (
            (1, sum_1, got_1, from_3, out_1),
            (3, sum_3, got_3, from_1, out_3),
        ):
            total = keep[rows].astype(F32) + got[rows].astype(F32)
            if number == with_from:
                total = total + came[...].astype(F32)
            out[rows] = total.astype(BF16)


def last_sum_kernel(keep, got, near_1, near_3, dq, sums, query_grad):
    total = keep[...].astype(F32) + got[...].astype(F32)
    total = total + (near_1[...].astype(F32) + near_3[...].astype(F32))
    sums[...] = total.astype(BF16)
    for g in range(8):
        for half in range(2):
            rows = slice(half * HR, (half + 1) * HR)
            for h in range(G):
                query_grad[rows, head_columns(g, h)] = dq[spread_to(g, half), h * HR : (h + 1) * HR]


def unpack_kernel(got, key_grad, value_grad):
    for g in range(8):
        for start, out in ((0, key_grad), (R, value_grad)):
            total = got[spread_to(g, 0), start : start + R].astype(F32)
            total = total + got[spread_to(g, 1), start : start + R].astype(F32)
            out[:, g * D : (g + 1) * D] = total.astype(BF16)


def bf16(*shape):
    return jax.ShapeDtypeStruct(shape, BF16)


def on_vmem(kernel, outs, *args):
    return pl.pallas_call(
        kernel,
        out_shape=outs,
        compiler_params=pltpu.CompilerParams(vmem_limit_bytes=16 << 20),
    )(*args)


IN_SMEM = pl.BlockSpec(memory_space=pltpu.SMEM)
IN_VMEM = pl.BlockSpec(memory_space=pltpu.VMEM)
ANYWHERE = pl.BlockSpec(memory_space=pl.ANY)


def exchange(array):
    return lax.all_to_all(array, SPREAD, split_axis=0, concat_axis=0, tiled=True)


def flip(array):
    return lax.ppermute(array, "core", [(0, 1), (1, 0)])


def swap(array, distance):
    return lax.ppermute(array, "y", [(i, i ^ distance) for i in range(4)])


def body(queries, keys, values, attn_out, out_grad, segment, span_order):
    kv_packed = pl.pallas_call(
        pack_kv_kernel,
        out_shape=bf16(16, 2 * R, D),
        in_specs=[pl.BlockSpec(memory_space=pltpu.HBM)] * 2,
        scratch_shapes=[pltpu.SemaphoreType.DMA],
        compiler_params=pltpu.CompilerParams(vmem_limit_bytes=60 << 20),
    )(keys, values)
    own = exchange(kv_packed)
    q_packed, counts = pl.pallas_call(
        pack_q_kernel,
        out_shape=[bf16(16, 2 * QR + 16, D), jax.ShapeDtypeStruct((2,), jnp.int32)],
        in_specs=[IN_VMEM] * 4 + [ANYWHERE],
        out_specs=[IN_VMEM, IN_SMEM],
        compiler_params=pltpu.CompilerParams(vmem_limit_bytes=16 << 20),
    )(queries, attn_out, out_grad, segment.reshape(64, 128), own)
    qpay = exchange(q_packed)

    near_1 = swap(own, 1)
    near_3 = swap(own, 3)
    far_a = swap(near_3[:8], 1)
    far_b = swap(near_1[8:], 3)
    mine = (own, near_1, near_3, far_a, far_b)
    group = bf16(16, 2 * R, D)
    half = bf16(8, 2 * R, D)
    dq, keep_0, keep_1, keep_3, sum_a, sum_b, give_0, give_1, give_3, far_give = pl.pallas_call(
        attention_kernel,
        out_shape=[bf16(16, QR, D)] + [group] * 3 + [half] * 2 + [group] * 4,
        in_specs=[IN_SMEM] * 2 + [ANYWHERE] * 11,
        scratch_shapes=[
            pltpu.SMEM((NC * NT // 2 + REST,), jnp.int32),
            pltpu.SMEM((NC * NT // 2 + REST,), jnp.int32),
            pltpu.VMEM((NC + 1, C, D), BF16),
            pltpu.VMEM((NC + 1, C, D), BF16),
            pltpu.VMEM((16, 16, D), BF16),
            pltpu.VMEM((NT, 2, 2, R, 2 * D), BF16),
            pltpu.VMEM((NT, 2, 2, R, 2 * D), BF16),
            pltpu.VMEM((NT // 2, D, KB), BF16),
            pltpu.VMEM((NC + 1, 2 * D, C), BF16),
            pltpu.VMEM((NC + 1, 2 * D, C), BF16),
            pltpu.VMEM((NC, 1, C), F32),
            pltpu.VMEM((NC + 1, 8, C), F32),
            pltpu.VMEM((NT, 2, 2, R, D), F32),
            pltpu.VMEM((NT, 2, 2, R, D), F32),
            pltpu.VMEM((NC + 1, D, C), F32),
            pltpu.SemaphoreType.DMA,
            pltpu.SemaphoreType.DMA,
        ],
        compiler_params=pltpu.CompilerParams(vmem_limit_bytes=40 << 20),
    )(span_order, counts, qpay, *mine, *[flip(array) for array in mine])
    far_sum_a, far_sum_b = on_vmem(far_sum_kernel, [half, half], sum_a, sum_b, flip(far_give))
    from_1 = swap(far_sum_a, 1)
    from_3 = swap(far_sum_b, 3)
    to_1, to_3 = on_vmem(
        near_sum_kernel, [group] * 2, keep_1, flip(give_1), keep_3, flip(give_3), from_1, from_3
    )
    sums, query_grad = on_vmem(
        last_sum_kernel,
        [group, bf16(R, 8 * G * D)],
        keep_0,
        flip(give_0),
        swap(to_1, 1),
        swap(to_3, 3),
        exchange(dq),
    )
    key_grad, value_grad = on_vmem(unpack_kernel, [bf16(R, 8 * D)] * 2, exchange(sums))
    return query_grad, key_grad, value_grad


def solution(mesh):
    fine = Mesh(mesh.devices.reshape(4, 2, 2, 2, 4), AXES)
    rows = P(AXES, None)
    return jax.shard_map(
        body,
        mesh=fine,
        in_specs=(rows,) * 5 + (P(), P()),
        out_specs=(rows,) * 3,
        check_vma=False,
    )
```
